32 devices in a mesh: batch: 2 (over y), gy: 4 (over z), gx: 4 (over x, core).
Axes of the slice: x: 2, y: 2, z: 4, core: 2. Of those that a mesh axis runs over, the one named last changes fastest.
Arguments:
- x_fine: bfloat16 [2, 32, 128, 256], P('batch', 'gy', 'gx'), may hold values from -6 to 6
- dy_fine: bfloat16 [2, 32, 128, 256], P('batch', 'gy', 'gx'), may hold values from -6 to 6
- x_coarse: bfloat16 [2, 16, 16, 1024], P('batch', 'gy', 'gx'), may hold values from -6 to 6
- dy_coarse: bfloat16 [2, 16, 16, 1024], P('batch', 'gy', 'gx'), may hold values from -6 to 6
- timestep: int32 [2], P('batch'), may hold values from 0 to 999
- fine_gain: float32 [256], replicated, may hold values from 0.5 to 2.5, as said below
- coarse_gain: float32 [1024], replicated, may hold values from 0.5 to 2.5, as said below
- fine_qkv: bfloat16 [256, 768], replicated, may hold values from -0.375 to 0.375
- fine_out: bfloat16 [256, 256], replicated, may hold values from -0.375 to 0.375
- coarse_qkv: bfloat16 [3, 1024, 1024], P(None, ('gy', 'gx')), may hold values from -0.1875 to 0.1875
- coarse_out: bfloat16 [1024, 1024], P(('gy', 'gx')), may hold values from -0.1875 to 0.1875
Outputs:
- dx_fine: bfloat16 [2, 32, 128, 256], P('batch', 'gy', 'gx')
- dx_coarse: bfloat16 [2, 16, 16, 1024], P('batch', 'gy', 'gx')
- grad_fine_qkv: bfloat16 [256, 768], replicated
- grad_fine_out: bfloat16 [256, 256], replicated
- grad_coarse_qkv: bfloat16 [3, 1024, 1024], P(None, ('gy', 'gx'))
- grad_coarse_out: bfloat16 [1024, 1024], P(('gy', 'gx'))
The draws below stay inside these ranges and needn't reach their ends.
Inputs may be any that keep to these rules, and one draw needn't show every extreme that they name: `fine_gain`: the norm gains are positive. `coarse_gain`: the norm gains are positive.
All inputs are finite; a program needn't handle non-finite values.
Results may differ from the reference program's by a relative error of at most 0.017.
The reference program's roundings to bfloat16 on the way count: a program that leaves them out, or rounds other values in their place, can miss the bound.
Values may be sent and summed in bfloat16 or wider, within the bound.
No kernel may reach another device: no remote copies, remote signals or barrier semaphores. Data moves between devices by JAX's collectives and lax.ppermute only.
A program may use at most 64 MiB of HBM per device.

```python
import math
import jax
import jax.numpy as jnp
from jax import lax

D_F = 256
H_F = 4
D_C = 1024
H_C = 16
HD = 64
RAD = 3
BATCH = 2
ROWS_F = 32
COLS_F = 128
ROWS_C = 16
COLS_C = 16


def gain_law(key, channels):
    return jnp.clip(1.0 + 0.15 * jax.random.normal(key, (channels,), jnp.float32), 0.5, 1.5)


def draw_fine_gain(key, part):
    return gain_law(jax.random.fold_in(key, 11), D_F)


def draw_coarse_gain(key, part):
    return gain_law(jax.random.fold_in(key, 23), D_C)


def shard_levels(key, shape, cuts, smallest, high):
    gain = 1.0
    for dim, blocks in cuts:
        heights = jax.random.uniform(jax.random.fold_in(jax.random.fold_in(key, 6), dim), (blocks,), jnp.float32, smallest / len(cuts), high / len(cuts))
        gain = gain * jnp.repeat(jnp.exp(heights), shape[dim] // blocks).reshape((-1,) + (1,) * (len(shape) - 1 - dim))
    return gain


def scatter_about(key, dims, spread, reach, shards=(), kind=jnp.bfloat16):
    factor_of = shard_levels(key, dims, shards, -0.22, 0.18) if shards else 1.0
    array = jax.random.normal(key, dims, jnp.float32) * spread * factor_of
    return jnp.minimum(jnp.maximum(array, -reach), reach).astype(kind)


def setup_inputs(seed: int = 0) -> dict:
    key_list = jax.random.split(jax.random.key(seed), 12)
    return {
        "x_fine": scatter_about(key_list[0], (BATCH, ROWS_F, COLS_F, D_F), 1.0, 6.0, ((0, 2), (1, 4), (2, 4))),
        "dy_fine": scatter_about(key_list[1], (BATCH, ROWS_F, COLS_F, D_F), 1.0, 6.0, ((0, 2), (1, 4), (2, 4))),
        "x_coarse": scatter_about(key_list[2], (BATCH, ROWS_C, COLS_C, D_C), 1.0, 6.0, ((0, 2), (1, 4), (2, 4))),
        "dy_coarse": scatter_about(key_list[3], (BATCH, ROWS_C, COLS_C, D_C), 1.0, 6.0, ((0, 2), (1, 4), (2, 4))),
        "timestep": jax.random.randint(key_list[4], (BATCH,), 0, 1000).astype(jnp.int32),
        "fine_gain": draw_fine_gain(jax.random.fold_in(key_list[11], 71), 0),
        "coarse_gain": draw_coarse_gain(jax.random.fold_in(key_list[11], 71), 0),
        "fine_qkv": scatter_about(key_list[7], (D_F, 3 * D_F), D_F ** -0.5, 0.375),
        "fine_out": scatter_about(key_list[8], (D_F, D_F), D_F ** -0.5, 0.375),
        "coarse_qkv": scatter_about(key_list[9], (3, D_C, D_C), D_C ** -0.5, 0.1875, ((1, 16),)),
        "coarse_out": scatter_about(key_list[10], (D_C, D_C), D_C ** -0.5, 0.1875, ((0, 16),)),
    }


eps = 1e-06
log_span = math.log(1000.0)
block_side = 8

def contract(pattern, first_op, second_op):
    return jnp.einsum(pattern, first_op.astype(jnp.float32), second_op.astype(jnp.float32))

def score_scale():
    return 1.0 / math.sqrt(HD)

def time_gain(gains, step_value):
    channels = gains.shape[0]
    frequency = jnp.exp(-log_span * jnp.arange(channels, dtype=jnp.float32) / channels)
    return gains * (1.0 + 0.5 * jnp.cos(step_value.astype(jnp.float32) * frequency))

def norm_forward(source, factor):
    floats = source.astype(jnp.float32)
    inverse = lax.rsqrt(lax.optimization_barrier(jnp.mean(floats * floats, axis=-1, keepdims=True)) + eps)
    return ((floats * inverse * factor).astype(jnp.bfloat16), inverse)

def norm_backward(source, inverse, factor, upstream):
    floats = source.astype(jnp.float32)
    scaled = upstream * factor
    middle = lax.optimization_barrier(jnp.mean(floats * scaled, axis=-1, keepdims=True))
    return (inverse * scaled - floats * inverse * inverse * inverse * middle).astype(jnp.bfloat16)

def to_tiles(planar):
    height, breadth, channels = planar.shape
    pieces = planar.reshape(height // block_side, block_side, breadth // block_side, block_side, channels)
    return pieces.transpose(0, 2, 1, 3, 4).reshape(-1, block_side * block_side, channels)

def from_tiles(blocks, height, breadth):
    channels = blocks.shape[-1]
    pieces = blocks.reshape(height // block_side, breadth // block_side, block_side, block_side, channels)
    return pieces.transpose(0, 2, 1, 3, 4).reshape(height, breadth, channels)

def windows(padded, height, breadth):
    extent = block_side + 2 * RAD
    block_rows = height // block_side
    across = breadth // block_side
    channels = padded.shape[-1]
    widened = jnp.pad(padded, ((0, (block_rows + 1) * block_side - padded.shape[0]), (0, (across + 1) * block_side - padded.shape[1]), (0, 0)))
    blocks_grid = widened.reshape(block_rows + 1, block_side, across + 1, block_side, channels).transpose(0, 2, 1, 3, 4)
    upper_pair = jnp.concatenate([blocks_grid[:-1, :-1], blocks_grid[:-1, 1:]], axis=3)
    lower_pair = jnp.concatenate([blocks_grid[1:, :-1], blocks_grid[1:, 1:]], axis=3)
    square = jnp.concatenate([upper_pair, lower_pair], axis=2)
    return square[:, :, :extent, :extent].reshape(block_rows * across, extent * extent, channels)

def intersection_add(windowed, height, breadth):
    extent = block_side + 2 * RAD
    block_rows = height // block_side
    across = breadth // block_side
    channels = windowed.shape[-1]
    layout = windowed.reshape(block_rows, across, extent, extent, channels)
    layout = jnp.pad(layout, ((0, 0), (0, 0), (0, 2 * block_side - extent), (0, 2 * block_side - extent), (0, 0)))
    summed = jnp.zeros((block_rows + 1, across + 1, block_side, block_side, channels), jnp.float32)
    for row_half in range(2):
        for col_half in range(2):
            quarter = layout[:, :, row_half * block_side:(row_half + 1) * block_side, col_half * block_side:(col_half + 1) * block_side]
            summed = summed + jnp.pad(quarter, ((row_half, 1 - row_half), (col_half, 1 - col_half), (0, 0), (0, 0), (0, 0)))
    merged = summed.transpose(0, 2, 1, 3, 4).reshape((block_rows + 1) * block_side, (across + 1) * block_side, channels)
    return merged[:height + 2 * RAD, :breadth + 2 * RAD]

def pair_mask():
    extent = block_side + 2 * RAD
    inner_pos = jnp.arange(block_side * block_side)
    outer_pos = jnp.arange(extent * extent)
    row_gap = outer_pos[None, :] // extent - inner_pos[:, None] // block_side
    col_gap = outer_pos[None, :] % extent - inner_pos[:, None] % block_side
    return (row_gap >= 0) & (row_gap <= 2 * RAD) & (col_gap >= 0) & (col_gap <= 2 * RAD)

def fine_forward(queries, key_values, valid_pad):
    height, breadth, channels = queries.shape
    query_blocks = to_tiles(queries)
    block_count = query_blocks.shape[0]
    query_heads = query_blocks.reshape(block_count, -1, H_F, HD)
    key_windows = windows(key_values, height, breadth)
    key_heads = key_windows[..., :channels].reshape(block_count, -1, H_F, HD)
    value_heads = key_windows[..., channels:].reshape(block_count, -1, H_F, HD)
    allowed = pair_mask()[None, None] & windows(valid_pad[..., None], height, breadth)[:, None, None, :, 0]
    scores = contract('bqhe,bkhe->bhqk', query_heads, key_heads) * score_scale()
    scores = jnp.where(allowed, scores, -1e+30)
    peak = lax.optimization_barrier(jnp.max(scores, axis=-1, keepdims=True))
    log_total = peak + jnp.log(lax.optimization_barrier(jnp.sum(jnp.exp(scores - peak), axis=-1, keepdims=True)))
    shares = jnp.where(allowed, jnp.exp(scores - log_total), 0.0)
    weights = shares.astype(jnp.bfloat16)
    mixed = contract('bhqk,bkhe->bqhe', weights, value_heads).astype(jnp.bfloat16)
    attended = from_tiles(mixed.reshape(block_count, -1, channels), height, breadth)
    return (attended, query_heads, key_heads, value_heads, shares, weights, log_total)

def fine_query_backward(upstream, query_heads, key_heads, value_heads, shares, height, breadth):
    block_count = query_heads.shape[0]
    upward_heads = to_tiles(upstream).reshape(block_count, -1, H_F, HD)
    products = contract('bqhe,bkhe->bhqk', upward_heads, value_heads)
    centre = lax.optimization_barrier(jnp.sum(shares * products, axis=-1, keepdims=True))
    slopes = (shares * (products - centre)).astype(jnp.bfloat16)
    grad_query = contract('bhqk,bkhe->bqhe', slopes, key_heads) * score_scale()
    grad_query = from_tiles(grad_query.reshape(block_count, -1, H_F * HD), height, breadth)
    return (grad_query, upward_heads, slopes, centre)

def key_grads_windows(slopes, weights, query_heads, upward_heads):
    block_count = query_heads.shape[0]
    grad_key = contract('bhqk,bqhe->bkhe', slopes, query_heads).reshape(block_count, -1, D_F)
    grad_value = contract('bhqk,bqhe->bkhe', weights, upward_heads).reshape(block_count, -1, D_F)
    return jnp.concatenate([grad_key, grad_value], axis=-1)

def fine_image(picture, cotangent, step_value, gains, fine_qkv, fine_out):
    height, breadth = (picture.shape[0], picture.shape[1])
    factor = time_gain(gains, step_value)
    normed, inverse = norm_forward(picture, factor)
    flat_normed = normed.reshape(-1, D_F)
    projected = jnp.dot(flat_normed, fine_qkv, preferred_element_type=jnp.float32).astype(jnp.bfloat16).reshape(height, breadth, 3 * D_F)
    queries = projected[..., :D_F]
    key_values = jnp.pad(projected[..., D_F:], ((RAD, RAD), (RAD, RAD), (0, 0)))
    valid_pad = jnp.pad(jnp.ones((height, breadth), dtype=jnp.bool_), RAD)
    attended, query_heads, key_heads, value_heads, shares, weights, log_total = fine_forward(queries, key_values, valid_pad)
    flat_cot = cotangent.reshape(-1, D_F)
    grad_out = jnp.dot(attended.reshape(-1, D_F).T, flat_cot, preferred_element_type=jnp.float32)
    upstream = jnp.dot(flat_cot, fine_out.T, preferred_element_type=jnp.float32).astype(jnp.bfloat16).reshape(height, breadth, D_F)
    grad_query, upward_heads, slopes, centre = fine_query_backward(upstream, query_heads, key_heads, value_heads, shares, height, breadth)
    padded_grads = intersection_add(key_grads_windows(slopes, weights, query_heads, upward_heads), height, breadth)
    key_grads = padded_grads[RAD:RAD + height, RAD:RAD + breadth]
    grad_proj = jnp.concatenate([grad_query, key_grads[..., :D_F] * score_scale(), key_grads[..., D_F:]], axis=-1).astype(jnp.bfloat16).reshape(-1, 3 * D_F)
    grad_qkv = jnp.dot(flat_normed.T, grad_proj, preferred_element_type=jnp.float32)
    down_grad = jnp.dot(grad_proj, fine_qkv.T, preferred_element_type=jnp.float32).reshape(height, breadth, D_F)
    return (norm_backward(picture, inverse, factor, down_grad), grad_qkv, grad_out)

def coarse_image(picture, cotangent, step_value, gains, coarse_qkv, coarse_out):
    tokens = picture.reshape(-1, D_C)
    factor = time_gain(gains, step_value)
    normed, inverse = norm_forward(tokens, factor)
    qkv_heads = coarse_qkv.reshape(3, H_C, HD, D_C)
    out_heads = coarse_out.reshape(H_C, HD, D_C)
    projected = contract('td,khed->khte', normed, qkv_heads).astype(jnp.bfloat16)
    queries, keys, values = (projected[0], projected[1], projected[2])
    scores = contract('hte,hse->hts', queries, keys) * score_scale()
    peak = lax.optimization_barrier(jnp.max(scores, axis=-1, keepdims=True))
    log_total = peak + jnp.log(lax.optimization_barrier(jnp.sum(jnp.exp(scores - peak), axis=-1, keepdims=True)))
    shares = jnp.exp(scores - log_total)
    weights = shares.astype(jnp.bfloat16)
    mixed = contract('hts,hse->hte', weights, values).astype(jnp.bfloat16)
    flat_cot = cotangent.reshape(-1, D_C)
    upstream = contract('td,hed->hte', flat_cot, out_heads).astype(jnp.bfloat16)
    grad_out = contract('hte,td->hed', mixed, flat_cot).reshape(D_C, D_C)
    products = contract('hte,hse->hts', upstream, values)
    centre = lax.optimization_barrier(jnp.sum(shares * products, axis=-1, keepdims=True))
    slopes = (shares * (products - centre)).astype(jnp.bfloat16)
    grad_query = (contract('hts,hse->hte', slopes, keys) * score_scale()).astype(jnp.bfloat16)
    grad_key = (contract('hts,hte->hse', slopes, queries) * score_scale()).astype(jnp.bfloat16)
    grad_value = contract('hts,hte->hse', weights, upstream).astype(jnp.bfloat16)
    stacked = jnp.stack([grad_query, grad_key, grad_value])
    grad_qkv = contract('khte,td->khed', stacked, normed).reshape(3, D_C, D_C)
    head_parts = contract('khte,khed->htd', stacked, qkv_heads).astype(jnp.bfloat16)
    down_grad = lax.optimization_barrier(jnp.sum(head_parts.astype(jnp.float32), axis=0))
    return (norm_backward(tokens, inverse, factor, down_grad).reshape(picture.shape), grad_qkv, grad_out)

def reference(x_fine, dy_fine, x_coarse, dy_coarse, timestep, fine_gain, coarse_gain, fine_qkv, fine_out, coarse_qkv, coarse_out):

    def one_image(running, inputs):
        picture, cotangent, coarse_picture, coarse_cot, step_value = inputs
        dx_picture, grad_fq, grad_fo = fine_image(picture, cotangent, step_value, fine_gain, fine_qkv, fine_out)
        dx_coarse_pic, grad_cq, grad_co = coarse_image(coarse_picture, coarse_cot, step_value, coarse_gain, coarse_qkv, coarse_out)
        updated = (running[0] + grad_fq, running[1] + grad_fo, running[2] + grad_cq, running[3] + grad_co)
        return (updated, (dx_picture, dx_coarse_pic))
    start = (jnp.zeros((D_F, 3 * D_F), jnp.float32), jnp.zeros((D_F, D_F), jnp.float32), jnp.zeros((3, D_C, D_C), jnp.float32), jnp.zeros((D_C, D_C), jnp.float32))
    sums, outputs = lax.scan(one_image, start, (x_fine, dy_fine, x_coarse, dy_coarse, timestep))
    return (outputs[0], outputs[1], sums[0].astype(jnp.bfloat16), sums[1].astype(jnp.bfloat16), sums[2].astype(jnp.bfloat16), sums[3].astype(jnp.bfloat16))
```

```python
import math

import jax
import jax.numpy as jnp
from jax import lax
from jax.sharding import PartitionSpec as P

D_F = 256
H_F = 4
D_C = 1024
HD = 64
RAD = 3


eps = 1e-06
log_span = math.log(1000.0)
block_side = 8


def padded_2(array, sides, width):
    for axis, dim in sides:
        peers, length = (lax.axis_size(axis), array.shape[dim])
        up = [(i, (i + 1) % peers) for i in range(peers - 1)]
        down = [(j, i) for i, j in up]
        last = lax.slice_in_dim(array, length - width, length, axis=dim)
        leading = lax.slice_in_dim(array, 0, width, axis=dim)
        before = lax.ppermute(last, axis, up)
        after = lax.ppermute(leading, axis, down)
        array = jnp.concatenate([before, array, after], axis=dim)
    return array


def shifted(value, axis, steps):
    count = lax.axis_size(axis)
    leading, last = (max(0, -steps), min(count, count - steps))
    return lax.ppermute(value, axis, [(source, source + steps) for source in range(leading, last)])


def contract(pattern, first_op, second_op):
    return jnp.einsum(pattern, first_op, second_op, preferred_element_type=jnp.float32)


def score_scale():
    return 1.0 / math.sqrt(HD)


def time_gain(gains, step_value):
    channels = gains.shape[0]
    frequency = jnp.exp(-log_span * jnp.arange(channels, dtype=jnp.float32) / channels)
    return gains * (1.0 + 0.5 * jnp.cos(step_value.astype(jnp.float32) * frequency))


def norm_forward(source, factor):
    floats = source.astype(jnp.float32)
    inverse = lax.rsqrt(jnp.mean(floats * floats, axis=-1, keepdims=True) + eps)
    return ((floats * inverse * factor).astype(jnp.bfloat16), inverse)


def norm_backward(source, inverse, factor, upstream):
    floats = source.astype(jnp.float32)
    scaled = upstream * factor
    middle = jnp.mean(floats * scaled, axis=-1, keepdims=True)
    return (inverse * scaled - floats * inverse * inverse * inverse * middle).astype(jnp.bfloat16)


def to_tiles(planar):
    height, breadth, channels = planar.shape
    pieces = planar.reshape(
        height // block_side, block_side, breadth // block_side, block_side, channels
    )
    return pieces.transpose(0, 2, 1, 3, 4).reshape(-1, block_side * block_side, channels)


def from_tiles(blocks, height, breadth):
    channels = blocks.shape[-1]
    pieces = blocks.reshape(
        height // block_side, breadth // block_side, block_side, block_side, channels
    )
    return pieces.transpose(0, 2, 1, 3, 4).reshape(height, breadth, channels)


def windows(padded, height, breadth):
    extent = block_side + 2 * RAD
    block_rows = height // block_side
    across = breadth // block_side
    channels = padded.shape[-1]
    widened = jnp.pad(
        padded,
        (
            (0, (block_rows + 1) * block_side - padded.shape[0]),
            (0, (across + 1) * block_side - padded.shape[1]),
            (0, 0),
        ),
    )
    blocks_grid = widened.reshape(
        block_rows + 1, block_side, across + 1, block_side, channels
    ).transpose(0, 2, 1, 3, 4)
    upper_pair = jnp.concatenate([blocks_grid[:-1, :-1], blocks_grid[:-1, 1:]], axis=3)
    lower_pair = jnp.concatenate([blocks_grid[1:, :-1], blocks_grid[1:, 1:]], axis=3)
    square = jnp.concatenate([upper_pair, lower_pair], axis=2)
    return square[:, :, :extent, :extent].reshape(block_rows * across, extent * extent, channels)


def intersection_add(windowed, height, breadth):
    extent = block_side + 2 * RAD
    block_rows = height // block_side
    across = breadth // block_side
    channels = windowed.shape[-1]
    layout = windowed.reshape(block_rows, across, extent, extent, channels)
    layout = jnp.pad(
        layout, ((0, 0), (0, 0), (0, 2 * block_side - extent), (0, 2 * block_side - extent), (0, 0))
    )
    summed = jnp.zeros((block_rows + 1, across + 1, block_side, block_side, channels), jnp.float32)
    for row_half in range(2):
        for col_half in range(2):
            quarter = layout[
                :,
                :,
                row_half * block_side : (row_half + 1) * block_side,
                col_half * block_side : (col_half + 1) * block_side,
            ]
            summed = summed + jnp.pad(
                quarter,
                ((row_half, 1 - row_half), (col_half, 1 - col_half), (0, 0), (0, 0), (0, 0)),
            )
    merged = summed.transpose(0, 2, 1, 3, 4).reshape(
        (block_rows + 1) * block_side, (across + 1) * block_side, channels
    )
    return merged[: height + 2 * RAD, : breadth + 2 * RAD]


def pair_mask():
    extent = block_side + 2 * RAD
    inner_pos = jnp.arange(block_side * block_side)
    outer_pos = jnp.arange(extent * extent)
    row_gap = outer_pos[None, :] // extent - inner_pos[:, None] // block_side
    col_gap = outer_pos[None, :] % extent - inner_pos[:, None] % block_side
    return (row_gap >= 0) & (row_gap <= 2 * RAD) & (col_gap >= 0) & (col_gap <= 2 * RAD)


def fine_forward(queries, key_values, valid_pad):
    height, breadth, channels = queries.shape
    query_blocks = to_tiles(queries)
    block_count = query_blocks.shape[0]
    query_heads = query_blocks.reshape(block_count, -1, H_F, HD)
    key_windows = windows(key_values, height, breadth)
    key_heads = key_windows[..., :channels].reshape(block_count, -1, H_F, HD)
    value_heads = key_windows[..., channels:].reshape(block_count, -1, H_F, HD)
    allowed = (
        pair_mask()[None, None]
        & windows(valid_pad[..., None], height, breadth)[:, None, None, :, 0]
    )
    scores = contract("bqhe,bkhe->bhqk", query_heads, key_heads) * score_scale()
    scores = jnp.where(allowed, scores, -1e30)
    peak = jnp.max(scores, axis=-1, keepdims=True)
    log_total = peak + jnp.log(jnp.sum(jnp.exp(scores - peak), axis=-1, keepdims=True))
    shares = jnp.where(allowed, jnp.exp(scores - log_total), 0.0)
    weights = shares.astype(jnp.bfloat16)
    mixed = contract("bhqk,bkhe->bqhe", weights, value_heads).astype(jnp.bfloat16)
    attended = from_tiles(mixed.reshape(block_count, -1, channels), height, breadth)
    return (attended, query_heads, key_heads, value_heads, shares, weights, log_total)


def fine_query_backward(upstream, query_heads, key_heads, value_heads, shares, height, breadth):
    block_count = query_heads.shape[0]
    upward_heads = to_tiles(upstream).reshape(block_count, -1, H_F, HD)
    products = contract("bqhe,bkhe->bhqk", upward_heads, value_heads)
    centre = jnp.sum(shares * products, axis=-1, keepdims=True)
    slopes = (shares * (products - centre)).astype(jnp.bfloat16)
    grad_query = contract("bhqk,bkhe->bqhe", slopes, key_heads) * score_scale()
    grad_query = from_tiles(grad_query.reshape(block_count, -1, H_F * HD), height, breadth)
    return (grad_query, upward_heads, slopes, centre)


def key_grads_windows(slopes, weights, query_heads, upward_heads):
    block_count = query_heads.shape[0]
    grad_key = contract("bhqk,bqhe->bkhe", slopes, query_heads).reshape(block_count, -1, D_F)
    grad_value = contract("bhqk,bqhe->bkhe", weights, upward_heads).reshape(block_count, -1, D_F)
    return jnp.concatenate([grad_key, grad_value], axis=-1)


def batch_sum(partial):
    images = lax.axis_size("batch")
    if images != 2:
        return lax.psum(partial, "batch")
    other = lax.ppermute(partial, "batch", [(0, 1), (1, 0)])
    return partial.astype(jnp.float32) + other.astype(jnp.float32)


def local(
    x_fine,
    dy_fine,
    x_coarse,
    dy_coarse,
    timestep,
    fine_gain,
    coarse_gain,
    fine_qkv,
    fine_out,
    coarse_qkv,
    coarse_out,
):
    step_value = timestep[0]
    picture = x_fine[0]
    height, breadth = (picture.shape[0], picture.shape[1])
    factor = time_gain(fine_gain, step_value)
    normed, inverse = norm_forward(picture, factor)
    flat_normed = normed.reshape(-1, D_F)
    projected = (
        jnp.dot(flat_normed, fine_qkv, preferred_element_type=jnp.float32)
        .astype(jnp.bfloat16)
        .reshape(height, breadth, 3 * D_F)
    )
    queries = projected[..., :D_F]
    key_values = projected[..., D_F:]
    kv_pad = padded_2(key_values[None], (("gy", 1), ("gx", 2)), RAD)[0]
    row_first = lax.axis_index("gy") * height - RAD
    col_first = lax.axis_index("gx") * breadth - RAD
    pad_rows = row_first + jnp.arange(height + 2 * RAD, dtype=jnp.int32)
    pad_cols = col_first + jnp.arange(breadth + 2 * RAD, dtype=jnp.int32)
    rows_inside = (pad_rows >= 0) & (pad_rows < height * lax.axis_size("gy"))
    cols_inside = (pad_cols >= 0) & (pad_cols < breadth * lax.axis_size("gx"))
    valid_pad = rows_inside[:, None] & cols_inside[None, :]
    attended, query_heads, key_heads, value_heads, shares, weights, log_total = fine_forward(
        queries, kv_pad, valid_pad
    )
    flat_cot = dy_fine[0].reshape(-1, D_F)
    grad_out_local = lax.dot_general(
        attended.reshape(-1, D_F),
        flat_cot,
        (((0,), (0,)), ((), ())),
        preferred_element_type=jnp.float32,
    )
    upstream = (
        lax.dot_general(
            flat_cot, fine_out, (((1,), (1,)), ((), ())), preferred_element_type=jnp.float32
        )
        .astype(jnp.bfloat16)
        .reshape(height, breadth, D_F)
    )
    grad_query, upward_heads, slopes, centre = fine_query_backward(
        upstream, query_heads, key_heads, value_heads, shares, height, breadth
    )
    summed = intersection_add(
        key_grads_windows(slopes, weights, query_heads, upward_heads), height, breadth
    )
    from_left = shifted(summed[:, breadth + RAD :], "gx", 1)
    from_right = shifted(summed[:, :RAD], "gx", -1)
    middle = summed[:, RAD : breadth + RAD]
    middle = middle.at[:, :RAD].add(from_left)
    middle = middle.at[:, breadth - RAD :].add(from_right)
    from_above = shifted(middle[height + RAD :], "gy", 1)
    from_below = shifted(middle[:RAD], "gy", -1)
    key_grads = middle[RAD : height + RAD]
    key_grads = key_grads.at[:RAD].add(from_above)
    key_grads = key_grads.at[height - RAD :].add(from_below)
    grad_proj = (
        jnp.concatenate(
            [grad_query, key_grads[..., :D_F] * score_scale(), key_grads[..., D_F:]], axis=-1
        )
        .astype(jnp.bfloat16)
        .reshape(-1, 3 * D_F)
    )
    grad_qkv_local = lax.dot_general(
        flat_normed, grad_proj, (((0,), (0,)), ((), ())), preferred_element_type=jnp.float32
    )
    down_grad = lax.dot_general(
        grad_proj, fine_qkv, (((1,), (1,)), ((), ())), preferred_element_type=jnp.float32
    ).reshape(height, breadth, D_F)
    dx_picture = norm_backward(picture, inverse, factor, down_grad)
    coarse_tokens = x_coarse[0].reshape(-1, D_C)
    coarse_factor = time_gain(coarse_gain, step_value)
    own = jnp.concatenate([coarse_tokens, dy_coarse[0].reshape(-1, D_C)], axis=1)
    everyone = lax.all_gather(own, ("gy", "gx"), axis=0, tiled=True)
    all_normed, _ = norm_forward(everyone[:, :D_C], coarse_factor)
    all_cot = everyone[:, D_C:]
    _, coarse_inverse = norm_forward(coarse_tokens, coarse_factor)
    coarse_proj = contract("td,khd->kth", all_normed, coarse_qkv).astype(jnp.bfloat16)
    head_queries, head_keys, head_values = (coarse_proj[0], coarse_proj[1], coarse_proj[2])
    coarse_scores = contract("te,se->ts", head_queries, head_keys) * score_scale()
    coarse_peak = jnp.max(coarse_scores, axis=-1, keepdims=True)
    coarse_log = coarse_peak + jnp.log(
        jnp.sum(jnp.exp(coarse_scores - coarse_peak), axis=-1, keepdims=True)
    )
    coarse_shares = jnp.exp(coarse_scores - coarse_log)
    coarse_weights = coarse_shares.astype(jnp.bfloat16)
    head_mixed = contract("ts,se->te", coarse_weights, head_values).astype(jnp.bfloat16)
    head_upstream = contract("td,ed->te", all_cot, coarse_out).astype(jnp.bfloat16)
    coarse_out_local = contract("te,td->ed", head_mixed, all_cot)
    coarse_products = contract("te,se->ts", head_upstream, head_values)
    coarse_centre = jnp.sum(coarse_shares * coarse_products, axis=-1, keepdims=True)
    coarse_slopes = (coarse_shares * (coarse_products - coarse_centre)).astype(jnp.bfloat16)
    head_grad_query = (contract("ts,se->te", coarse_slopes, head_keys) * score_scale()).astype(
        jnp.bfloat16
    )
    head_grad_key = (contract("ts,te->se", coarse_slopes, head_queries) * score_scale()).astype(
        jnp.bfloat16
    )
    head_grad_value = contract("ts,te->se", coarse_weights, head_upstream).astype(jnp.bfloat16)
    stacked = jnp.stack([head_grad_query, head_grad_key, head_grad_value])
    coarse_qkv_local = contract("kte,td->ked", stacked, all_normed)
    head_part = contract("kte,ked->td", stacked, coarse_qkv)
    shares_out = lax.all_to_all(
        head_part.astype(jnp.bfloat16), ("gy", "gx"), split_axis=0, concat_axis=0, tiled=True
    )
    ranks = lax.axis_size(("gy", "gx"))
    coarse_down = jnp.sum(
        shares_out.reshape(ranks, -1, D_C).astype(jnp.float32), axis=0
    )
    dx_coarse_tok = norm_backward(coarse_tokens, coarse_inverse, coarse_factor, coarse_down)
    fine_local = jnp.concatenate([grad_qkv_local, grad_out_local], axis=1).astype(jnp.bfloat16)
    everywhere = ("batch", "gy", "gx")
    if D_F % lax.axis_size(everywhere) == 0:
        fine_part = lax.psum_scatter(fine_local, everywhere, scatter_dimension=0, tiled=True)
        fine_all = lax.all_gather(fine_part, everywhere, axis=0, tiled=True)
    else:
        fine_all = lax.psum(fine_local, everywhere)
    fine_qkv_sum, fine_out_sum = fine_all[:, : 3 * D_F], fine_all[:, 3 * D_F :]
    coarse_local = jnp.concatenate([coarse_qkv_local, coarse_out_local[None]], axis=0)
    coarse_sum = batch_sum(coarse_local.astype(jnp.bfloat16))
    coarse_qkv_sum, coarse_out_sum = coarse_sum[:3], coarse_sum[3]
    return (
        dx_picture[None],
        dx_coarse_tok.reshape(x_coarse.shape),
        fine_qkv_sum.astype(jnp.bfloat16),
        fine_out_sum.astype(jnp.bfloat16),
        coarse_qkv_sum.astype(jnp.bfloat16),
        coarse_out_sum.astype(jnp.bfloat16),
    )


def solution(mesh):
    placed = (
        P("batch", "gy", "gx", None),
        P("batch", "gy", "gx", None),
        P("batch", "gy", "gx", None),
        P("batch", "gy", "gx", None),
        P("batch"),
        P(),
        P(),
        P(),
        P(),
        P(None, ("gy", "gx"), None),
        P(("gy", "gx"), None),
    )
    return jax.shard_map(
        local,
        mesh=mesh,
        in_specs=placed,
        out_specs=(
            P("batch", "gy", "gx", None),
            P("batch", "gy", "gx", None),
            P(),
            P(),
            P(None, ("gy", "gx"), None),
            P(("gy", "gx"), None),
        ),
        check_vma=False,
    )
```

```python
import math

import jax
import jax.numpy as jnp
from jax import lax
from jax.experimental import pallas as pl
from jax.experimental.pallas import tpu as pltpu
from jax.sharding import PartitionSpec as P

D_F = 256
H_F = 4
D_C = 1024
HD = 64
RAD = 3
HALO = 2 * RAD

eps = 1e-06
log_span = math.log(1000.0)
side = 8
extent = side + 2 * RAD
lanes_wide = 16
scale = 1.0 / math.sqrt(HD)
vmem_bytes = 48 * 1024 * 1024


def dot(first, second, dims=((1,), (0,))):
    return lax.dot_general(first, second, (dims, ((), ())), preferred_element_type=jnp.float32)


def time_gain(gains, step_value):
    channels = gains.shape[0]
    frequency = jnp.exp(-log_span * jnp.arange(channels, dtype=jnp.float32) / channels)
    return gains * (1.0 + 0.5 * jnp.cos(step_value.astype(jnp.float32) * frequency))


def inverse_rms(floats):
    return lax.rsqrt(jnp.mean(floats * floats, axis=-1, keepdims=True) + eps)


def norm_backward(floats, inverse, factor, upstream):
    scaled = upstream * factor
    middle = jnp.mean(floats * scaled, axis=-1, keepdims=True)
    return (inverse * scaled - floats * inverse * inverse * inverse * middle).astype(jnp.bfloat16)


def round_up(value, multiple):
    return -(-value // multiple) * multiple


def fine_body(
    limits,
    x_ref,
    dy_ref,
    above_ref,
    below_ref,
    left_ref,
    right_ref,
    factor_ref,
    qkv_ref,
    out_ref,
    dx_ref,
    grads_ref,
    x_grid,
    dy_grid,
    k_grid,
    v_grid,
    q_grid,
    u_grid,
    dk_grid,
    dv_grid,
    dq_grid,
    a_grid,
    bias_ref,
):
    height, breadth = x_ref.shape[0], x_ref.shape[1]
    grid_rows, grid_cols = x_grid.shape[0], x_grid.shape[1]
    query_rows = dy_grid.shape[0]
    floats = jnp.float32
    factor = factor_ref[...]

    x_grid[...] = jnp.zeros_like(x_grid)
    dy_grid[...] = jnp.zeros_like(dy_grid)
    dk_grid[...] = jnp.zeros_like(dk_grid)
    dv_grid[...] = jnp.zeros_like(dv_grid)
    inner = slice(HALO, HALO + breadth)
    x_grid[0:HALO, inner] = above_ref[0:HALO].astype(floats)
    x_grid[HALO : HALO + height, inner] = x_ref[...].astype(floats)
    x_grid[HALO + height : HALO + height + HALO, inner] = below_ref[0:HALO].astype(floats)
    dy_grid[0:RAD, inner] = above_ref[HALO : HALO + RAD].astype(floats)
    dy_grid[RAD : RAD + height, inner] = dy_ref[...].astype(floats)
    dy_grid[RAD + height : RAD + height + RAD, inner] = below_ref[HALO : HALO + RAD].astype(floats)
    for strip, first in ((left_ref, 0), (right_ref, HALO + breadth)):
        span = slice(first, first + HALO)
        at = 0
        for grid, begin, count in (
            (x_grid, 0, HALO),
            (dy_grid, 0, RAD),
            (x_grid, HALO, height),
            (dy_grid, RAD, height),
            (x_grid, HALO + height, HALO),
            (dy_grid, RAD + height, RAD),
        ):
            grid[begin : begin + count, span] = strip[at : at + count].astype(floats)
            at += count

    tokens = x_grid[...].reshape(grid_rows * grid_cols, D_F)
    normed = (tokens * inverse_rms(tokens) * factor).astype(jnp.bfloat16)
    key_values = dot(normed, qkv_ref[:, D_F:]).astype(jnp.bfloat16).astype(floats)
    k_grid[...] = key_values[:, :D_F].reshape(grid_rows, grid_cols, D_F)
    v_grid[...] = key_values[:, D_F:].reshape(grid_rows, grid_cols, D_F)
    query_tokens = normed[RAD * grid_cols : (RAD + query_rows) * grid_cols]
    queries = dot(query_tokens, qkv_ref[:, :D_F]).astype(jnp.bfloat16).astype(floats) * scale
    q_grid[...] = queries.reshape(query_rows, grid_cols, D_F)
    cotangents = dy_grid[...].reshape(query_rows * grid_cols, D_F).astype(jnp.bfloat16)
    ups = dot(cotangents, out_ref[...], ((1,), (1,))).astype(jnp.bfloat16).astype(floats)
    u_grid[...] = ups.reshape(query_rows, grid_cols, D_F)

    keys_count, heads_count = extent * lanes_wide, H_F * side * side
    key_at = lax.broadcasted_iota(jnp.int32, (keys_count, heads_count), 0)
    query_at = lax.broadcasted_iota(jnp.int32, (keys_count, heads_count), 1)
    row_gap = (key_at // lanes_wide) - ((query_at // side) % side)
    col_gap = (key_at % lanes_wide) - (query_at % side)
    near = (row_gap >= 0) & (row_gap <= 2 * RAD) & (col_gap >= 0) & (col_gap <= 2 * RAD)
    bias_ref[...] = jnp.where(near, 0.0, -1e30)
    row_low, row_high, col_low, col_high = limits[0], limits[1], limits[2], limits[3]
    lone = lax.broadcasted_iota(jnp.int32, (keys_count, 1), 0)
    head_of = lax.broadcasted_iota(jnp.int32, (side * side, D_F), 1) // HD

    def spread(block):
        return jnp.concatenate(
            [jnp.where(head_of == h, block, 0.0).astype(jnp.bfloat16) for h in range(H_F)], axis=0
        )

    def collect(full):
        total = jnp.where(head_of == 0, full[: side * side], 0.0)
        for h in range(1, H_F):
            piece = full[h * side * side : (h + 1) * side * side]
            total = jnp.where(head_of == h, piece, total)
        return total.reshape(side, side, D_F)

    for block_row in range(query_rows // side):
        top = block_row * side
        for block_col in range((grid_cols - side) // side):
            start = block_col * side
            window = (slice(top, top + extent), slice(start, start + lanes_wide))
            keys = k_grid[window].reshape(keys_count, D_F).astype(jnp.bfloat16)
            values = v_grid[window].reshape(keys_count, D_F).astype(jnp.bfloat16)
            place = (slice(top, top + side), slice(start + RAD, start + RAD + side))
            wide_queries = spread(q_grid[place].reshape(side * side, D_F))
            wide_ups = spread(u_grid[place].reshape(side * side, D_F))
            key_row = lone // lanes_wide + top
            key_col = lone % lanes_wide + start
            inside = (
                (key_row >= row_low)
                & (key_row < row_high)
                & (key_col >= col_low)
                & (key_col < col_high)
            )
            scores = dot(keys, wide_queries, ((1,), (1,)))
            scores = scores + (bias_ref[...] + jnp.where(inside, 0.0, -1e30))
            raised = jnp.exp(scores - jnp.max(scores, axis=0, keepdims=True))
            shares = raised * (1.0 / jnp.sum(raised, axis=0, keepdims=True))
            products = dot(values, wide_ups, ((1,), (1,)))
            centre = jnp.sum(shares * products, axis=0, keepdims=True)
            slopes = (shares * (products - centre)).astype(jnp.bfloat16)
            weights = shares.astype(jnp.bfloat16)
            dv_grid[window] += dot(weights, wide_ups).reshape(extent, lanes_wide, D_F)
            dk_grid[window] += dot(slopes, wide_queries).reshape(extent, lanes_wide, D_F)
            block = (slice(top, top + side), slice(start, start + side))
            a_grid[block] = collect(dot(weights, values, ((0,), (0,))))
            dq_grid[block] = collect(dot(slopes, keys, ((0,), (0,))))

    count = height * breadth
    own_queries = (slice(RAD, RAD + height), slice(RAD, RAD + breadth))
    own_keys = (slice(HALO, HALO + height), inner)
    attended = a_grid[own_queries].reshape(count, D_F).astype(jnp.bfloat16)
    grad_q = (dq_grid[own_queries].reshape(count, D_F) * scale).astype(jnp.bfloat16)
    grad_k = dk_grid[own_keys].reshape(count, D_F).astype(jnp.bfloat16)
    grad_v = dv_grid[own_keys].reshape(count, D_F).astype(jnp.bfloat16)
    grad_proj = jnp.concatenate([grad_q, grad_k, grad_v], axis=1)
    picture = x_ref[...].reshape(count, D_F).astype(floats)
    inverse = inverse_rms(picture)
    own_normed = (picture * inverse * factor).astype(jnp.bfloat16)
    flat_cot = dy_ref[...].reshape(count, D_F)
    grads_ref[:, : 3 * D_F] = dot(own_normed, grad_proj, ((0,), (0,))).astype(grads_ref.dtype)
    grads_ref[:, 3 * D_F :] = dot(attended, flat_cot, ((0,), (0,))).astype(grads_ref.dtype)
    down = dot(grad_proj, qkv_ref[...], ((1,), (1,)))
    dx_ref[...] = norm_backward(picture, inverse, factor, down).reshape(height, breadth, D_F)


def fine_block(limits, picture, cotangent, above, below, left, right, factor, fine_qkv, fine_out):
    height, breadth = picture.shape[0], picture.shape[1]
    query_rows = round_up(height + 2 * RAD, side)
    query_cols = round_up(breadth + 2 * RAD, side)
    grid_rows, grid_cols = query_rows + 2 * RAD, query_cols + side
    vmem = pl.BlockSpec(memory_space=pltpu.VMEM)
    wide = pltpu.VMEM((grid_rows, grid_cols, D_F), jnp.float32)
    middle = pltpu.VMEM((query_rows, grid_cols, D_F), jnp.float32)
    small = pltpu.VMEM((query_rows, query_cols, D_F), jnp.float32)
    return pl.pallas_call(
        fine_body,
        out_shape=(
            jax.ShapeDtypeStruct((height, breadth, D_F), jnp.bfloat16),
            jax.ShapeDtypeStruct((D_F, 4 * D_F), jnp.bfloat16),
        ),
        in_specs=[pl.BlockSpec(memory_space=pltpu.SMEM)] + [vmem] * 9,
        out_specs=(vmem, vmem),
        scratch_shapes=[
            wide,
            middle,
            wide,
            wide,
            middle,
            middle,
            wide,
            wide,
            small,
            small,
            pltpu.VMEM((extent * lanes_wide, H_F * side * side), jnp.float32),
        ],
        compiler_params=pltpu.CompilerParams(vmem_limit_bytes=vmem_bytes),
        name="fine_block",
    )(limits, picture, cotangent, above, below, left, right, factor, fine_qkv, fine_out)


def coarse_body(x_ref, dy_ref, factor_ref, qkv_ref, out_ref, parts_ref, grads_ref):
    tokens = x_ref[...].astype(jnp.float32)
    normed = (tokens * inverse_rms(tokens) * factor_ref[...]).astype(jnp.bfloat16)
    cot = dy_ref[...]
    flat_qkv = qkv_ref[...].reshape(3 * HD, D_C)
    out_rows = out_ref[...]
    projected = dot(normed, flat_qkv, ((1,), (1,))).astype(jnp.bfloat16)
    queries, keys, values = projected[:, :HD], projected[:, HD : 2 * HD], projected[:, 2 * HD :]
    ups = dot(cot, out_rows, ((1,), (1,))).astype(jnp.bfloat16)
    scores = dot(queries, keys, ((1,), (1,))) * scale
    raised = jnp.exp(scores - jnp.max(scores, axis=-1, keepdims=True))
    shares = raised * (1.0 / jnp.sum(raised, axis=-1, keepdims=True))
    weights = shares.astype(jnp.bfloat16)
    mixed = dot(weights, values).astype(jnp.bfloat16)
    products = dot(ups, values, ((1,), (1,)))
    centre = jnp.sum(shares * products, axis=-1, keepdims=True)
    slopes = (shares * (products - centre)).astype(jnp.bfloat16)
    grad_q = (dot(slopes, keys) * scale).astype(jnp.bfloat16)
    grad_k = (dot(slopes, queries, ((0,), (0,))) * scale).astype(jnp.bfloat16)
    grad_v = dot(weights, ups, ((0,), (0,))).astype(jnp.bfloat16)
    stacked = jnp.concatenate([grad_q, grad_k, grad_v], axis=1)
    parts_ref[...] = dot(stacked, flat_qkv).astype(jnp.bfloat16)
    grads_ref[: 3 * HD] = dot(stacked, normed, ((0,), (0,))).astype(grads_ref.dtype)
    grads_ref[3 * HD :] = dot(mixed, cot, ((0,), (0,))).astype(grads_ref.dtype)


def coarse_block(tokens, cotangents, factor, head_qkv, head_out):
    count = tokens.shape[0]
    vmem = pl.BlockSpec(memory_space=pltpu.VMEM)
    return pl.pallas_call(
        coarse_body,
        out_shape=(
            jax.ShapeDtypeStruct((count, D_C), jnp.bfloat16),
            jax.ShapeDtypeStruct((4 * HD, D_C), jnp.bfloat16),
        ),
        in_specs=[vmem] * 5,
        out_specs=(vmem, vmem),
        compiler_params=pltpu.CompilerParams(vmem_limit_bytes=vmem_bytes),
        name="coarse_block",
    )(tokens, cotangents, factor, head_qkv, head_out)


def neighbours(low_edge, high_edge, axis):
    peers = lax.axis_size(axis)
    up = [(i, i + 1) for i in range(peers - 1)]
    down = [(i + 1, i) for i in range(peers - 1)]
    return lax.ppermute(high_edge, axis, up), lax.ppermute(low_edge, axis, down)


def batch_sum(partial):
    images = lax.axis_size("batch")
    if images != 2:
        return lax.psum(partial, "batch")
    other = lax.ppermute(partial, "batch", [(0, 1), (1, 0)])
    return partial.astype(jnp.float32) + other.astype(jnp.float32)


def scattered_sum(whole, axes):
    ranks = lax.axis_size(axes)
    pieces = lax.all_to_all(whole, axes, split_axis=0, concat_axis=0, tiled=True)
    pieces = pieces.reshape(ranks, whole.shape[0] // ranks, whole.shape[1])
    return jnp.sum(pieces.astype(jnp.float32), axis=0)


def local(
    x_fine,
    dy_fine,
    x_coarse,
    dy_coarse,
    timestep,
    fine_gain,
    coarse_gain,
    fine_qkv,
    fine_out,
    coarse_qkv,
    coarse_out,
):
    plane = ("gy", "gx")
    step_value = timestep[0]
    picture, cotangent = x_fine[0], dy_fine[0]
    height, breadth = picture.shape[0], picture.shape[1]

    coarse_tokens = x_coarse[0].reshape(-1, D_C)
    own = jnp.concatenate([coarse_tokens, dy_coarse[0].reshape(-1, D_C)], axis=1)
    everyone = lax.all_gather(own, plane, axis=0, tiled=True)

    low = jnp.concatenate([picture[:HALO], cotangent[:RAD]], axis=0)
    high = jnp.concatenate([picture[height - HALO :], cotangent[height - RAD :]], axis=0)
    above, below = neighbours(low, high, "gy")
    column = jnp.concatenate([above, picture, cotangent, below], axis=0)
    left, right = neighbours(column[:, :HALO], column[:, breadth - HALO :], "gx")

    row_first = lax.axis_index("gy") * height - HALO
    col_first = lax.axis_index("gx") * breadth - HALO
    limits = jnp.stack(
        [
            -row_first,
            lax.axis_size("gy") * height - row_first,
            -col_first,
            lax.axis_size("gx") * breadth - col_first,
        ]
    ).astype(jnp.int32)
    factor = time_gain(fine_gain, step_value)[None]
    dx_picture, fine_partial = fine_block(
        limits, picture, cotangent, above, below, left, right, factor, fine_qkv, fine_out
    )
    fine_piece = batch_sum(scattered_sum(fine_partial, plane))
    fine_all = lax.all_gather(fine_piece.astype(jnp.bfloat16), plane, axis=0, tiled=True)

    coarse_factor = time_gain(coarse_gain, step_value)[None]
    parts, coarse_partial = coarse_block(
        everyone[:, :D_C], everyone[:, D_C:], coarse_factor, coarse_qkv, coarse_out
    )
    coarse_down = scattered_sum(parts, plane)
    coarse_sum = batch_sum(coarse_partial).astype(jnp.bfloat16)
    coarse_floats = coarse_tokens.astype(jnp.float32)
    dx_coarse = norm_backward(
        coarse_floats, inverse_rms(coarse_floats), coarse_factor, coarse_down
    )
    return (
        dx_picture[None],
        dx_coarse.reshape(x_coarse.shape),
        fine_all[:, : 3 * D_F],
        fine_all[:, 3 * D_F :],
        coarse_sum[: 3 * HD].reshape(coarse_qkv.shape),
        coarse_sum[3 * HD :],
    )


def solution(mesh):
    placed = (
        P("batch", "gy", "gx", None),
        P("batch", "gy", "gx", None),
        P("batch", "gy", "gx", None),
        P("batch", "gy", "gx", None),
        P("batch"),
        P(),
        P(),
        P(),
        P(),
        P(None, plane_spec, None),
        P(plane_spec, None),
    )
    return jax.shard_map(
        local,
        mesh=mesh,
        in_specs=placed,
        out_specs=(
            P("batch", "gy", "gx", None),
            P("batch", "gy", "gx", None),
            P(),
            P(),
            P(None, plane_spec, None),
            P(plane_spec, None),
        ),
        check_vma=False,
    )


plane_spec = ("gy", "gx")
```

```python
import math

import jax
import jax.numpy as jnp
from jax import lax
from jax.experimental import pallas as pl
from jax.experimental.pallas import tpu as pltpu
from jax.sharding import PartitionSpec as P

D_F = 256
H_F = 4
D_C = 1024
HD = 64
RAD = 3
HALO = 2 * RAD

eps = 1e-06
log_span = math.log(1000.0)
side = 8
extent = side + 2 * RAD
lanes_wide = 16
scale = 1.0 / math.sqrt(HD)
vmem_bytes = 48 * 1024 * 1024


def dot(first, second, dims=((1,), (0,))):
    return lax.dot_general(first, second, (dims, ((), ())), preferred_element_type=jnp.float32)


def time_gain(gains, step_value):
    channels = gains.shape[0]
    frequency = jnp.exp(-log_span * jnp.arange(channels, dtype=jnp.float32) / channels)
    return gains * (1.0 + 0.5 * jnp.cos(step_value.astype(jnp.float32) * frequency))


def inverse_rms(floats):
    return lax.rsqrt(jnp.mean(floats * floats, axis=-1, keepdims=True) + eps)


def norm_backward(floats, inverse, factor, upstream):
    scaled = upstream * factor
    middle = jnp.mean(floats * scaled, axis=-1, keepdims=True)
    return (inverse * scaled - floats * inverse * inverse * inverse * middle).astype(jnp.bfloat16)


def round_up(value, multiple):
    return -(-value // multiple) * multiple


def fine_body(
    limits,
    x_ref,
    dy_ref,
    above_ref,
    below_ref,
    left_ref,
    right_ref,
    factor_ref,
    qkv_ref,
    out_ref,
    dx_ref,
    grads_ref,
    x_grid,
    dy_grid,
    k_grid,
    v_grid,
    q_grid,
    u_grid,
    dk_grid,
    dv_grid,
    dq_grid,
    a_grid,
    bias_ref,
):
    height, breadth = x_ref.shape[0], x_ref.shape[1]
    grid_rows, grid_cols = x_grid.shape[0], x_grid.shape[1]
    query_rows = dy_grid.shape[0]
    floats = jnp.float32
    factor = factor_ref[...]

    x_grid[...] = jnp.zeros_like(x_grid)
    dy_grid[...] = jnp.zeros_like(dy_grid)
    dk_grid[...] = jnp.zeros_like(dk_grid)
    dv_grid[...] = jnp.zeros_like(dv_grid)
    inner = slice(HALO, HALO + breadth)
    x_grid[0:HALO, inner] = above_ref[0:HALO].astype(floats)
    x_grid[HALO : HALO + height, inner] = x_ref[...].astype(floats)
    x_grid[HALO + height : HALO + height + HALO, inner] = below_ref[0:HALO].astype(floats)
    dy_grid[0:RAD, inner] = above_ref[HALO : HALO + RAD].astype(floats)
    dy_grid[RAD : RAD + height, inner] = dy_ref[...].astype(floats)
    dy_grid[RAD + height : RAD + height + RAD, inner] = below_ref[HALO : HALO + RAD].astype(floats)
    for strip, first in ((left_ref, 0), (right_ref, HALO + breadth)):
        span = slice(first, first + HALO)
        at = 0
        for grid, begin, count in (
            (x_grid, 0, HALO),
            (dy_grid, 0, RAD),
            (x_grid, HALO, height),
            (dy_grid, RAD, height),
            (x_grid, HALO + height, HALO),
            (dy_grid, RAD + height, RAD),
        ):
            grid[begin : begin + count, span] = strip[at : at + count].astype(floats)
            at += count

    tokens = x_grid[...].reshape(grid_rows * grid_cols, D_F)
    normed = (tokens * inverse_rms(tokens) * factor).astype(jnp.bfloat16)
    key_values = dot(normed, qkv_ref[:, D_F:]).astype(jnp.bfloat16).astype(floats)
    k_grid[...] = key_values[:, :D_F].reshape(grid_rows, grid_cols, D_F)
    v_grid[...] = key_values[:, D_F:].reshape(grid_rows, grid_cols, D_F)
    query_tokens = normed[RAD * grid_cols : (RAD + query_rows) * grid_cols]
    queries = dot(query_tokens, qkv_ref[:, :D_F]).astype(jnp.bfloat16).astype(floats) * scale
    q_grid[...] = queries.reshape(query_rows, grid_cols, D_F)
    cotangents = dy_grid[...].reshape(query_rows * grid_cols, D_F).astype(jnp.bfloat16)
    ups = dot(cotangents, out_ref[...], ((1,), (1,))).astype(jnp.bfloat16).astype(floats)
    u_grid[...] = ups.reshape(query_rows, grid_cols, D_F)

    keys_count, heads_count = extent * lanes_wide, H_F * side * side
    key_at = lax.broadcasted_iota(jnp.int32, (keys_count, heads_count), 0)
    query_at = lax.broadcasted_iota(jnp.int32, (keys_count, heads_count), 1)
    row_gap = (key_at // lanes_wide) - ((query_at // side) % side)
    col_gap = (key_at % lanes_wide) - (query_at % side)
    near = (row_gap >= 0) & (row_gap <= 2 * RAD) & (col_gap >= 0) & (col_gap <= 2 * RAD)
    bias_ref[...] = jnp.where(near, 0.0, -1e30)
    row_low, row_high, col_low, col_high = limits[0], limits[1], limits[2], limits[3]
    lone = lax.broadcasted_iota(jnp.int32, (keys_count, 1), 0)
    head_of = lax.broadcasted_iota(jnp.int32, (side * side, D_F), 1) // HD

    def spread(block):
        return jnp.concatenate(
            [jnp.where(head_of == h, block, 0.0).astype(jnp.bfloat16) for h in range(H_F)], axis=0
        )

    def collect(full):
        total = jnp.where(head_of == 0, full[: side * side], 0.0)
        for h in range(1, H_F):
            piece = full[h * side * side : (h + 1) * side * side]
            total = jnp.where(head_of == h, piece, total)
        return total.reshape(side, side, D_F)

    for block_row in range(query_rows // side):
        top = block_row * side
        for block_col in range((grid_cols - side) // side):
            start = block_col * side
            window = (slice(top, top + extent), slice(start, start + lanes_wide))
            keys = k_grid[window].reshape(keys_count, D_F).astype(jnp.bfloat16)
            values = v_grid[window].reshape(keys_count, D_F).astype(jnp.bfloat16)
            place = (slice(top, top + side), slice(start + RAD, start + RAD + side))
            wide_queries = spread(q_grid[place].reshape(side * side, D_F))
            wide_ups = spread(u_grid[place].reshape(side * side, D_F))
            key_row = lone // lanes_wide + top
            key_col = lone % lanes_wide + start
            inside = (
                (key_row >= row_low)
                & (key_row < row_high)
                & (key_col >= col_low)
                & (key_col < col_high)
            )
            scores = dot(keys, wide_queries, ((1,), (1,)))
            scores = scores + (bias_ref[...] + jnp.where(inside, 0.0, -1e30))
            raised = jnp.exp(scores - jnp.max(scores, axis=0, keepdims=True))
            shares = raised * (1.0 / jnp.sum(raised, axis=0, keepdims=True))
            products = dot(values, wide_ups, ((1,), (1,)))
            centre = jnp.sum(shares * products, axis=0, keepdims=True)
            slopes = (shares * (products - centre)).astype(jnp.bfloat16)
            weights = shares.astype(jnp.bfloat16)
            dv_grid[window] += dot(weights, wide_ups).reshape(extent, lanes_wide, D_F)
            dk_grid[window] += dot(slopes, wide_queries).reshape(extent, lanes_wide, D_F)
            block = (slice(top, top + side), slice(start, start + side))
            a_grid[block] = collect(dot(weights, values, ((0,), (0,))))
            dq_grid[block] = collect(dot(slopes, keys, ((0,), (0,))))

    count = height * breadth
    own_queries = (slice(RAD, RAD + height), slice(RAD, RAD + breadth))
    own_keys = (slice(HALO, HALO + height), inner)
    attended = a_grid[own_queries].reshape(count, D_F).astype(jnp.bfloat16)
    grad_q = (dq_grid[own_queries].reshape(count, D_F) * scale).astype(jnp.bfloat16)
    grad_k = dk_grid[own_keys].reshape(count, D_F).astype(jnp.bfloat16)
    grad_v = dv_grid[own_keys].reshape(count, D_F).astype(jnp.bfloat16)
    grad_proj = jnp.concatenate([grad_q, grad_k, grad_v], axis=1)
    picture = x_ref[...].reshape(count, D_F).astype(floats)
    inverse = inverse_rms(picture)
    own_normed = (picture * inverse * factor).astype(jnp.bfloat16)
    flat_cot = dy_ref[...].reshape(count, D_F)
    grads_ref[:, : 3 * D_F] = dot(own_normed, grad_proj, ((0,), (0,))).astype(grads_ref.dtype)
    grads_ref[:, 3 * D_F :] = dot(attended, flat_cot, ((0,), (0,))).astype(grads_ref.dtype)
    down = dot(grad_proj, qkv_ref[...], ((1,), (1,)))
    dx_ref[...] = norm_backward(picture, inverse, factor, down).reshape(height, breadth, D_F)


def fine_block(limits, picture, cotangent, above, below, left, right, factor, fine_qkv, fine_out):
    height, breadth = picture.shape[0], picture.shape[1]
    query_rows = round_up(height + 2 * RAD, side)
    query_cols = round_up(breadth + 2 * RAD, side)
    grid_rows, grid_cols = query_rows + 2 * RAD, query_cols + side
    vmem = pl.BlockSpec(memory_space=pltpu.VMEM)
    wide = pltpu.VMEM((grid_rows, grid_cols, D_F), jnp.float32)
    middle = pltpu.VMEM((query_rows, grid_cols, D_F), jnp.float32)
    small = pltpu.VMEM((query_rows, query_cols, D_F), jnp.float32)
    return pl.pallas_call(
        fine_body,
        out_shape=(
            jax.ShapeDtypeStruct((height, breadth, D_F), jnp.bfloat16),
            jax.ShapeDtypeStruct((D_F, 4 * D_F), jnp.bfloat16),
        ),
        in_specs=[pl.BlockSpec(memory_space=pltpu.SMEM)] + [vmem] * 9,
        out_specs=(vmem, vmem),
        scratch_shapes=[
            wide,
            middle,
            wide,
            wide,
            middle,
            middle,
            wide,
            wide,
            small,
            small,
            pltpu.VMEM((extent * lanes_wide, H_F * side * side), jnp.float32),
        ],
        compiler_params=pltpu.CompilerParams(vmem_limit_bytes=vmem_bytes),
        name="fine_block",
    )(limits, picture, cotangent, above, below, left, right, factor, fine_qkv, fine_out)


def coarse_body(x_ref, dy_ref, factor_ref, qkv_ref, out_ref, parts_ref, grads_ref):
    tokens = x_ref[...].astype(jnp.float32)
    normed = (tokens * inverse_rms(tokens) * factor_ref[...]).astype(jnp.bfloat16)
    cot = dy_ref[...]
    flat_qkv = qkv_ref[...].reshape(3 * HD, D_C)
    out_rows = out_ref[...]
    projected = dot(normed, flat_qkv, ((1,), (1,))).astype(jnp.bfloat16)
    queries, keys, values = projected[:, :HD], projected[:, HD : 2 * HD], projected[:, 2 * HD :]
    ups = dot(cot, out_rows, ((1,), (1,))).astype(jnp.bfloat16)
    scores = dot(queries, keys, ((1,), (1,))) * scale
    raised = jnp.exp(scores - jnp.max(scores, axis=-1, keepdims=True))
    shares = raised * (1.0 / jnp.sum(raised, axis=-1, keepdims=True))
    weights = shares.astype(jnp.bfloat16)
    mixed = dot(weights, values).astype(jnp.bfloat16)
    products = dot(ups, values, ((1,), (1,)))
    centre = jnp.sum(shares * products, axis=-1, keepdims=True)
    slopes = (shares * (products - centre)).astype(jnp.bfloat16)
    grad_q = (dot(slopes, keys) * scale).astype(jnp.bfloat16)
    grad_k = (dot(slopes, queries, ((0,), (0,))) * scale).astype(jnp.bfloat16)
    grad_v = dot(weights, ups, ((0,), (0,))).astype(jnp.bfloat16)
    stacked = jnp.concatenate([grad_q, grad_k, grad_v], axis=1)
    parts_ref[...] = dot(stacked, flat_qkv).astype(jnp.bfloat16)
    grads_ref[: 3 * HD] = dot(stacked, normed, ((0,), (0,))).astype(grads_ref.dtype)
    grads_ref[3 * HD :] = dot(mixed, cot, ((0,), (0,))).astype(grads_ref.dtype)


def coarse_block(tokens, cotangents, factor, head_qkv, head_out):
    count = tokens.shape[0]
    vmem = pl.BlockSpec(memory_space=pltpu.VMEM)
    return pl.pallas_call(
        coarse_body,
        out_shape=(
            jax.ShapeDtypeStruct((count, D_C), jnp.bfloat16),
            jax.ShapeDtypeStruct((4 * HD, D_C), jnp.bfloat16),
        ),
        in_specs=[vmem] * 5,
        out_specs=(vmem, vmem),
        compiler_params=pltpu.CompilerParams(vmem_limit_bytes=vmem_bytes),
        name="coarse_block",
    )(tokens, cotangents, factor, head_qkv, head_out)


def neighbours(low_edge, high_edge, axis):
    peers = lax.axis_size(axis)
    up = [(i, i + 1) for i in range(peers - 1)]
    down = [(i + 1, i) for i in range(peers - 1)]
    return lax.ppermute(high_edge, axis, up), lax.ppermute(low_edge, axis, down)


def batch_sum(partial):
    images = lax.axis_size("batch")
    if images != 2:
        return lax.psum(partial, "batch")
    other = lax.ppermute(partial, "batch", [(0, 1), (1, 0)])
    return partial.astype(jnp.float32) + other.astype(jnp.float32)


def scattered_sum(whole, axes):
    ranks = lax.axis_size(axes)
    pieces = lax.all_to_all(whole, axes, split_axis=0, concat_axis=0, tiled=True)
    pieces = pieces.reshape(ranks, whole.shape[0] // ranks, whole.shape[1])
    return jnp.sum(pieces.astype(jnp.float32), axis=0)


def gathered(piece, axes):
    ranks = lax.axis_size(axes)
    copies = jnp.broadcast_to(piece[None], (ranks,) + piece.shape)
    copies = copies.reshape((ranks * piece.shape[0],) + piece.shape[1:])
    return lax.all_to_all(copies, axes, split_axis=0, concat_axis=0, tiled=True)


def tied(*arrays):
    return lax.optimization_barrier(arrays)


def local(
    x_fine,
    dy_fine,
    x_coarse,
    dy_coarse,
    timestep,
    fine_gain,
    coarse_gain,
    fine_qkv,
    fine_out,
    coarse_qkv,
    coarse_out,
):
    step_value = timestep[0]
    picture, cotangent = x_fine[0], dy_fine[0]
    height, breadth = picture.shape[0], picture.shape[1]

    coarse_tokens = x_coarse[0].reshape(-1, D_C)
    own = jnp.concatenate([coarse_tokens, dy_coarse[0].reshape(-1, D_C)], axis=1)
    row_group = gathered(own, "gy")
    low = jnp.concatenate([picture[:HALO], cotangent[:RAD]], axis=0)
    high = jnp.concatenate([picture[height - HALO :], cotangent[height - RAD :]], axis=0)
    above, below = neighbours(low, high, "gy")
    column = jnp.concatenate([above, picture, cotangent, below], axis=0)
    column, row_group = tied(column, row_group)
    left, right = neighbours(column[:, :HALO], column[:, breadth - HALO :], "gx")
    everyone = gathered(row_group, "gx")

    row_first = lax.axis_index("gy") * height - HALO
    col_first = lax.axis_index("gx") * breadth - HALO
    limits = jnp.stack(
        [
            -row_first,
            lax.axis_size("gy") * height - row_first,
            -col_first,
            lax.axis_size("gx") * breadth - col_first,
        ]
    ).astype(jnp.int32)
    factor = time_gain(fine_gain, step_value)[None]
    coarse_factor = time_gain(coarse_gain, step_value)[None]
    dx_picture, fine_partial = fine_block(
        limits, picture, cotangent, above, below, left, right, factor, fine_qkv, fine_out
    )
    fine_partial, everyone = tied(fine_partial, everyone)

    parts, coarse_partial = coarse_block(
        everyone[:, :D_C], everyone[:, D_C:], coarse_factor, coarse_qkv, coarse_out
    )
    fine_share = scattered_sum(fine_partial, "gx").astype(jnp.bfloat16)
    fine_share, parts, coarse_partial = tied(fine_share, parts, coarse_partial)

    coarse_sum = batch_sum(coarse_partial).astype(jnp.bfloat16)
    coarse_share = scattered_sum(parts, "gx").astype(jnp.bfloat16)
    others = ("batch", "gy")
    if fine_share.shape[0] % (8 * lax.axis_size(others)) == 0:
        fine_piece = scattered_sum(fine_share, others).astype(jnp.bfloat16)
        fine_piece, coarse_share = tied(fine_piece, coarse_share)
        fine_share = gathered(fine_piece, others)
    else:
        fine_share = lax.psum(fine_share, others)
    coarse_down = scattered_sum(coarse_share, "gy")
    fine_share, coarse_down = tied(fine_share, coarse_down)
    fine_all = gathered(fine_share, "gx")

    coarse_floats = coarse_tokens.astype(jnp.float32)
    dx_coarse = norm_backward(
        coarse_floats, inverse_rms(coarse_floats), coarse_factor, coarse_down
    )
    return (
        dx_picture[None],
        dx_coarse.reshape(x_coarse.shape),
        fine_all[:, : 3 * D_F],
        fine_all[:, 3 * D_F :],
        coarse_sum[: 3 * HD].reshape(coarse_qkv.shape),
        coarse_sum[3 * HD :],
    )


def solution(mesh):
    placed = (
        P("batch", "gy", "gx", None),
        P("batch", "gy", "gx", None),
        P("batch", "gy", "gx", None),
        P("batch", "gy", "gx", None),
        P("batch"),
        P(),
        P(),
        P(),
        P(),
        P(None, plane_spec, None),
        P(plane_spec, None),
    )
    return jax.shard_map(
        local,
        mesh=mesh,
        in_specs=placed,
        out_specs=(
            P("batch", "gy", "gx", None),
            P("batch", "gy", "gx", None),
            P(),
            P(),
            P(None, plane_spec, None),
            P(plane_spec, None),
        ),
        check_vma=False,
    )


plane_spec = ("gy", "gx")
```

```python
import math

import jax
import jax.numpy as jnp
from jax import lax
from jax.experimental import pallas as pl
from jax.experimental.pallas import tpu as pltpu
from jax.sharding import PartitionSpec as P

D_F = 256
H_F = 4
D_C = 1024
HD = 64
RAD = 3
HALO = 2 * RAD

eps = 1e-06
log_span = math.log(1000.0)
side = 8
extent = side + 2 * RAD
lanes_wide = 16
scale = 1.0 / math.sqrt(HD)
vmem_bytes = 48 * 1024 * 1024


def dot(first, second, dims=((1,), (0,))):
    return lax.dot_general(first, second, (dims, ((), ())), preferred_element_type=jnp.float32)


def time_gain(gains, step_value):
    channels = gains.shape[0]
    frequency = jnp.exp(-log_span * jnp.arange(channels, dtype=jnp.float32) / channels)
    return gains * (1.0 + 0.5 * jnp.cos(step_value.astype(jnp.float32) * frequency))


def inverse_rms(floats):
    return lax.rsqrt(jnp.mean(floats * floats, axis=-1, keepdims=True) + eps)


def norm_backward(floats, inverse, factor, upstream):
    scaled = upstream * factor
    middle = jnp.mean(floats * scaled, axis=-1, keepdims=True)
    return (inverse * scaled - floats * inverse * inverse * inverse * middle).astype(jnp.bfloat16)


def round_up(value, multiple):
    return -(-value // multiple) * multiple


def fine_body(
    limits,
    x_ref,
    dy_ref,
    above_ref,
    below_ref,
    left_ref,
    right_ref,
    factor_ref,
    qkv_ref,
    out_ref,
    dx_ref,
    keep_ref,
    send_ref,
    x_grid,
    dy_grid,
    k_grid,
    v_grid,
    q_grid,
    u_grid,
    dk_grid,
    dv_grid,
    dq_grid,
    a_grid,
    bias_ref,
    total_ref,
):
    height, breadth = x_ref.shape[0], x_ref.shape[1]
    grid_rows, grid_cols = x_grid.shape[0], x_grid.shape[1]
    query_rows = dy_grid.shape[0]
    floats = jnp.float32
    factor = factor_ref[...]

    x_grid[...] = jnp.zeros_like(x_grid)
    dy_grid[...] = jnp.zeros_like(dy_grid)
    dk_grid[...] = jnp.zeros_like(dk_grid)
    dv_grid[...] = jnp.zeros_like(dv_grid)
    inner = slice(HALO, HALO + breadth)
    x_grid[0:HALO, inner] = above_ref[0:HALO].astype(floats)
    x_grid[HALO : HALO + height, inner] = x_ref[...].astype(floats)
    x_grid[HALO + height : HALO + height + HALO, inner] = below_ref[0:HALO].astype(floats)
    dy_grid[0:RAD, inner] = above_ref[HALO : HALO + RAD].astype(floats)
    dy_grid[RAD : RAD + height, inner] = dy_ref[...].astype(floats)
    dy_grid[RAD + height : RAD + height + RAD, inner] = below_ref[HALO : HALO + RAD].astype(floats)
    for strip, first in ((left_ref, 0), (right_ref, HALO + breadth)):
        span = slice(first, first + HALO)
        at = 0
        for grid, begin, count in (
            (x_grid, 0, HALO),
            (dy_grid, 0, RAD),
            (x_grid, HALO, height),
            (dy_grid, RAD, height),
            (x_grid, HALO + height, HALO),
            (dy_grid, RAD + height, RAD),
        ):
            grid[begin : begin + count, span] = strip[at : at + count].astype(floats)
            at += count

    tokens = x_grid[...].reshape(grid_rows * grid_cols, D_F)
    normed = (tokens * inverse_rms(tokens) * factor).astype(jnp.bfloat16)
    key_values = dot(normed, qkv_ref[:, D_F:]).astype(jnp.bfloat16).astype(floats)
    k_grid[...] = key_values[:, :D_F].reshape(grid_rows, grid_cols, D_F)
    v_grid[...] = key_values[:, D_F:].reshape(grid_rows, grid_cols, D_F)
    query_tokens = normed[RAD * grid_cols : (RAD + query_rows) * grid_cols]
    queries = dot(query_tokens, qkv_ref[:, :D_F]).astype(jnp.bfloat16).astype(floats) * scale
    q_grid[...] = queries.reshape(query_rows, grid_cols, D_F)
    cotangents = dy_grid[...].reshape(query_rows * grid_cols, D_F).astype(jnp.bfloat16)
    ups = dot(cotangents, out_ref[...], ((1,), (1,))).astype(jnp.bfloat16).astype(floats)
    u_grid[...] = ups.reshape(query_rows, grid_cols, D_F)

    keys_count, heads_count = extent * lanes_wide, H_F * side * side
    key_at = lax.broadcasted_iota(jnp.int32, (keys_count, heads_count), 0)
    query_at = lax.broadcasted_iota(jnp.int32, (keys_count, heads_count), 1)
    row_gap = (key_at // lanes_wide) - ((query_at // side) % side)
    col_gap = (key_at % lanes_wide) - (query_at % side)
    near = (row_gap >= 0) & (row_gap <= 2 * RAD) & (col_gap >= 0) & (col_gap <= 2 * RAD)
    bias_ref[...] = jnp.where(near, 0.0, -1e30)
    row_low, row_high, col_low, col_high = limits[0], limits[1], limits[2], limits[3]
    lone = lax.broadcasted_iota(jnp.int32, (keys_count, 1), 0)
    head_of = lax.broadcasted_iota(jnp.int32, (side * side, D_F), 1) // HD

    def spread(block):
        return jnp.concatenate(
            [jnp.where(head_of == h, block, 0.0).astype(jnp.bfloat16) for h in range(H_F)], axis=0
        )

    def collect(full):
        total = jnp.where(head_of == 0, full[: side * side], 0.0)
        for h in range(1, H_F):
            piece = full[h * side * side : (h + 1) * side * side]
            total = jnp.where(head_of == h, piece, total)
        return total.reshape(side, side, D_F)

    for block_row in range(query_rows // side):
        top = block_row * side
        for block_col in range((grid_cols - side) // side):
            start = block_col * side
            window = (slice(top, top + extent), slice(start, start + lanes_wide))
            keys = k_grid[window].reshape(keys_count, D_F).astype(jnp.bfloat16)
            values = v_grid[window].reshape(keys_count, D_F).astype(jnp.bfloat16)
            place = (slice(top, top + side), slice(start + RAD, start + RAD + side))
            wide_queries = spread(q_grid[place].reshape(side * side, D_F))
            wide_ups = spread(u_grid[place].reshape(side * side, D_F))
            key_row = lone // lanes_wide + top
            key_col = lone % lanes_wide + start
            inside = (
                (key_row >= row_low)
                & (key_row < row_high)
                & (key_col >= col_low)
                & (key_col < col_high)
            )
            scores = dot(keys, wide_queries, ((1,), (1,)))
            scores = scores + (bias_ref[...] + jnp.where(inside, 0.0, -1e30))
            raised = jnp.exp(scores - jnp.max(scores, axis=0, keepdims=True))
            shares = raised * (1.0 / jnp.sum(raised, axis=0, keepdims=True))
            products = dot(values, wide_ups, ((1,), (1,)))
            centre = jnp.sum(shares * products, axis=0, keepdims=True)
            slopes = (shares * (products - centre)).astype(jnp.bfloat16)
            weights = shares.astype(jnp.bfloat16)
            dv_grid[window] += dot(weights, wide_ups).reshape(extent, lanes_wide, D_F)
            dk_grid[window] += dot(slopes, wide_queries).reshape(extent, lanes_wide, D_F)
            block = (slice(top, top + side), slice(start, start + side))
            a_grid[block] = collect(dot(weights, values, ((0,), (0,))))
            dq_grid[block] = collect(dot(slopes, keys, ((0,), (0,))))

    count = height * breadth
    own_queries = (slice(RAD, RAD + height), slice(RAD, RAD + breadth))
    own_keys = (slice(HALO, HALO + height), inner)
    attended = a_grid[own_queries].reshape(count, D_F).astype(jnp.bfloat16)
    grad_q = (dq_grid[own_queries].reshape(count, D_F) * scale).astype(jnp.bfloat16)
    grad_k = dk_grid[own_keys].reshape(count, D_F).astype(jnp.bfloat16)
    grad_v = dv_grid[own_keys].reshape(count, D_F).astype(jnp.bfloat16)
    grad_proj = jnp.concatenate([grad_q, grad_k, grad_v], axis=1)
    picture = x_ref[...].reshape(count, D_F).astype(floats)
    inverse = inverse_rms(picture)
    own_normed = (picture * inverse * factor).astype(jnp.bfloat16)
    flat_cot = dy_ref[...].reshape(count, D_F)
    grads = jnp.concatenate(
        [
            dot(own_normed, grad_proj, ((0,), (0,))),
            dot(attended, flat_cot, ((0,), (0,))),
        ],
        axis=1,
    )
    half, columns = keep_ref.shape[0], keep_ref.shape[1]
    total_ref[...] = grads.reshape(total_ref.shape)
    for low in range(2):
        target = (keep_ref, send_ref)[low]
        for high in range(half):
            for row in range(columns):
                block = (limits[4] ^ (2 * high + low)) * columns + (limits[5] ^ row)
                target[high, row] = total_ref[block].astype(target.dtype)
    down = dot(grad_proj, qkv_ref[...], ((1,), (1,)))
    dx_ref[...] = norm_backward(picture, inverse, factor, down).reshape(height, breadth, D_F)


def fine_block(peers, limits, picture, cotangent, above, below, left, right, factor, fine_qkv, fine_out):
    height, breadth = picture.shape[0], picture.shape[1]
    query_rows = round_up(height + 2 * RAD, side)
    query_cols = round_up(breadth + 2 * RAD, side)
    grid_rows, grid_cols = query_rows + 2 * RAD, query_cols + side
    across, down = peers
    rows = D_F // (across * down)
    halves = (across // 2, down, rows, 4 * D_F)
    vmem = pl.BlockSpec(memory_space=pltpu.VMEM)
    wide = pltpu.VMEM((grid_rows, grid_cols, D_F), jnp.float32)
    middle = pltpu.VMEM((query_rows, grid_cols, D_F), jnp.float32)
    small = pltpu.VMEM((query_rows, query_cols, D_F), jnp.float32)
    return pl.pallas_call(
        fine_body,
        out_shape=(
            jax.ShapeDtypeStruct((height, breadth, D_F), jnp.bfloat16),
            jax.ShapeDtypeStruct(halves, jnp.float32),
            jax.ShapeDtypeStruct(halves, jnp.bfloat16),
        ),
        in_specs=[pl.BlockSpec(memory_space=pltpu.SMEM)] + [vmem] * 9,
        out_specs=(vmem, vmem, vmem),
        scratch_shapes=[
            wide,
            middle,
            wide,
            wide,
            middle,
            middle,
            wide,
            wide,
            small,
            small,
            pltpu.VMEM((extent * lanes_wide, H_F * side * side), jnp.float32),
            pltpu.VMEM((across * down, rows, 4 * D_F), jnp.float32),
        ],
        compiler_params=pltpu.CompilerParams(vmem_limit_bytes=vmem_bytes),
        name="fine_block",
    )(limits, picture, cotangent, above, below, left, right, factor, fine_qkv, fine_out)


def coarse_body(x_ref, dy_ref, factor_ref, qkv_ref, out_ref, parts_ref, grads_ref):
    tokens = x_ref[...].astype(jnp.float32)
    normed = (tokens * inverse_rms(tokens) * factor_ref[...]).astype(jnp.bfloat16)
    cot = dy_ref[...]
    flat_qkv = qkv_ref[...].reshape(3 * HD, D_C)
    out_rows = out_ref[...]
    projected = dot(normed, flat_qkv, ((1,), (1,))).astype(jnp.bfloat16)
    queries, keys, values = projected[:, :HD], projected[:, HD : 2 * HD], projected[:, 2 * HD :]
    ups = dot(cot, out_rows, ((1,), (1,))).astype(jnp.bfloat16)
    scores = dot(queries, keys, ((1,), (1,))) * scale
    raised = jnp.exp(scores - jnp.max(scores, axis=-1, keepdims=True))
    shares = raised * (1.0 / jnp.sum(raised, axis=-1, keepdims=True))
    weights = shares.astype(jnp.bfloat16)
    mixed = dot(weights, values).astype(jnp.bfloat16)
    products = dot(ups, values, ((1,), (1,)))
    centre = jnp.sum(shares * products, axis=-1, keepdims=True)
    slopes = (shares * (products - centre)).astype(jnp.bfloat16)
    grad_q = (dot(slopes, keys) * scale).astype(jnp.bfloat16)
    grad_k = (dot(slopes, queries, ((0,), (0,))) * scale).astype(jnp.bfloat16)
    grad_v = dot(weights, ups, ((0,), (0,))).astype(jnp.bfloat16)
    stacked = jnp.concatenate([grad_q, grad_k, grad_v], axis=1)
    parts_ref[...] = dot(stacked, flat_qkv).astype(jnp.bfloat16)
    grads_ref[: 3 * HD] = dot(stacked, normed, ((0,), (0,))).astype(grads_ref.dtype)
    grads_ref[3 * HD :] = dot(mixed, cot, ((0,), (0,))).astype(grads_ref.dtype)


def coarse_block(tokens, cotangents, factor, head_qkv, head_out):
    count = tokens.shape[0]
    vmem = pl.BlockSpec(memory_space=pltpu.VMEM)
    return pl.pallas_call(
        coarse_body,
        out_shape=(
            jax.ShapeDtypeStruct((count, D_C), jnp.bfloat16),
            jax.ShapeDtypeStruct((4 * HD, D_C), jnp.bfloat16),
        ),
        in_specs=[vmem] * 5,
        out_specs=(vmem, vmem),
        compiler_params=pltpu.CompilerParams(vmem_limit_bytes=vmem_bytes),
        name="coarse_block",
    )(tokens, cotangents, factor, head_qkv, head_out)


def place_body(place, near_ref, far_ref, qkv_ref, out_ref):
    highs, downs, rows = near_ref.shape[0], near_ref.shape[1], near_ref.shape[2]
    for low in range(2):
        for high in range(highs):
            for row in range(downs):
                block = (place[0] ^ (2 * high + low)) * downs + (place[1] ^ row)
                at = pl.ds(pl.multiple_of(block * rows, rows), rows)
                piece = (near_ref, far_ref)[low][high, row]
                qkv_ref[at] = piece[:, : 3 * D_F]
                out_ref[at] = piece[:, 3 * D_F :]


def place_blocks(place, near, far):
    vmem = pl.BlockSpec(memory_space=pltpu.VMEM)
    return pl.pallas_call(
        place_body,
        out_shape=(
            jax.ShapeDtypeStruct((D_F, 3 * D_F), jnp.bfloat16),
            jax.ShapeDtypeStruct((D_F, D_F), jnp.bfloat16),
        ),
        in_specs=[pl.BlockSpec(memory_space=pltpu.SMEM), vmem, vmem],
        out_specs=(vmem, vmem),
        compiler_params=pltpu.CompilerParams(vmem_limit_bytes=vmem_bytes),
        name="place_blocks",
    )(place, near, far)


def neighbours(low_edge, high_edge, axis):
    peers = lax.axis_size(axis)
    up = [(i, i + 1) for i in range(peers - 1)]
    down = [(i + 1, i) for i in range(peers - 1)]
    return lax.ppermute(high_edge, axis, up), lax.ppermute(low_edge, axis, down)


def swapped(value, axis, mask):
    return lax.ppermute(value, axis, [(i, i ^ mask) for i in range(lax.axis_size(axis))])


def tied(*arrays):
    return lax.optimization_barrier(arrays)


def batch_sum(partial):
    images = lax.axis_size("batch")
    if images != 2:
        return lax.psum(partial, "batch").astype(jnp.float32)
    other = lax.ppermute(partial, "batch", [(0, 1), (1, 0)])
    return partial.astype(jnp.float32) + other.astype(jnp.float32)


def wide(value):
    return value.astype(jnp.float32)


def narrow(value):
    return value.astype(jnp.bfloat16)


def all_rows(piece):
    downs = lax.axis_size("gy")
    return jnp.stack([piece] + [swapped(piece, "gy", row) for row in range(1, downs)])


def row_sum(pieces):
    total = wide(pieces[0])
    for row in range(1, pieces.shape[0]):
        total = total + wide(swapped(narrow(pieces[row]), "gy", row))
    return total


def local(
    x_fine,
    dy_fine,
    x_coarse,
    dy_coarse,
    timestep,
    fine_gain,
    coarse_gain,
    fine_qkv,
    fine_out,
    coarse_qkv,
    coarse_out,
):
    step_value = timestep[0]
    picture, cotangent = x_fine[0], dy_fine[0]
    height, breadth = picture.shape[0], picture.shape[1]
    across, downs = lax.axis_size("gx"), lax.axis_size("gy")
    assert across == 4 and downs & (downs - 1) == 0
    gx, gy = lax.axis_index("gx"), lax.axis_index("gy")

    low = jnp.concatenate([picture[:HALO], cotangent[:RAD]], axis=0)
    high = jnp.concatenate([picture[height - HALO :], cotangent[height - RAD :]], axis=0)
    above, below = neighbours(low, high, "gy")
    coarse_tokens = x_coarse[0].reshape(-1, D_C)
    own = jnp.concatenate([coarse_tokens, dy_coarse[0].reshape(-1, D_C)], axis=1)
    count = own.shape[0]
    row_group = all_rows(own)
    column = jnp.concatenate([above, picture, cotangent, below], axis=0)
    column, row_group = tied(column, row_group)
    left, right = neighbours(column[:, :HALO], column[:, breadth - HALO :], "gx")
    left, right, row_group = tied(left, right, row_group)
    pair = jnp.stack([row_group, swapped(row_group, "gx", 2)])

    row_first = gy * height - HALO
    col_first = gx * breadth - HALO
    limits = jnp.stack(
        [
            -row_first,
            downs * height - row_first,
            -col_first,
            across * breadth - col_first,
            gx,
            gy,
        ]
    ).astype(jnp.int32)
    factor = time_gain(fine_gain, step_value)[None]
    coarse_factor = time_gain(coarse_gain, step_value)[None]
    dx_picture, fine_keep, fine_send = fine_block(
        (across, downs),
        limits,
        picture,
        cotangent,
        above,
        below,
        left,
        right,
        factor,
        fine_qkv,
        fine_out,
    )
    fine_send, pair = tied(fine_send, pair)

    fine_half = fine_keep + wide(swapped(fine_send, "gx", 1))
    other_pair = swapped(pair, "gx", 1)
    fine_half, other_pair = tied(fine_half, other_pair)

    everyone = jnp.stack([pair, other_pair]).reshape(-1, 2 * D_C)
    fine_quarter = fine_half[0] + wide(swapped(narrow(fine_half[1]), "gx", 2))
    parts, coarse_partial = coarse_block(
        everyone[:, :D_C], everyone[:, D_C:], coarse_factor, coarse_qkv, coarse_out
    )
    fine_quarter, parts, coarse_partial = tied(fine_quarter, parts, coarse_partial)

    coarse_sum = narrow(batch_sum(coarse_partial))
    parts = parts.reshape(2, 2, downs, count, D_C)
    fine_piece = row_sum(fine_quarter)
    coarse_half = wide(parts[0]) + wide(swapped(parts[1], "gx", 1))
    fine_piece, coarse_half = tied(fine_piece, coarse_half)

    fine_piece = narrow(batch_sum(fine_piece))
    coarse_quarter = wide(coarse_half[0]) + wide(swapped(narrow(coarse_half[1]), "gx", 2))
    fine_piece, coarse_quarter = tied(fine_piece, coarse_quarter)

    fine_rows = all_rows(fine_piece)
    coarse_down = row_sum(coarse_quarter)
    fine_rows, coarse_down = tied(fine_rows, coarse_down)

    fine_pair = jnp.stack([fine_rows, swapped(fine_rows, "gx", 2)])
    coarse_floats = wide(coarse_tokens)
    dx_coarse = norm_backward(
        coarse_floats, inverse_rms(coarse_floats), coarse_factor, coarse_down
    )
    fine_pair, dx_coarse, coarse_sum = tied(fine_pair, dx_coarse, coarse_sum)
    grad_qkv, grad_out = place_blocks(
        jnp.stack([gx, gy]).astype(jnp.int32), fine_pair, swapped(fine_pair, "gx", 1)
    )
    return (
        dx_picture[None],
        dx_coarse.reshape(x_coarse.shape),
        grad_qkv,
        grad_out,
        coarse_sum[: 3 * HD].reshape(coarse_qkv.shape),
        coarse_sum[3 * HD :],
    )


def solution(mesh):
    placed = (
        P("batch", "gy", "gx", None),
        P("batch", "gy", "gx", None),
        P("batch", "gy", "gx", None),
        P("batch", "gy", "gx", None),
        P("batch"),
        P(),
        P(),
        P(),
        P(),
        P(None, plane_spec, None),
        P(plane_spec, None),
    )
    return jax.shard_map(
        local,
        mesh=mesh,
        in_specs=placed,
        out_specs=(
            P("batch", "gy", "gx", None),
            P("batch", "gy", "gx", None),
            P(),
            P(),
            P(None, plane_spec, None),
            P(plane_spec, None),
        ),
        check_vma=False,
    )


plane_spec = ("gy", "gx")
```

```python
import math

import jax
import jax.numpy as jnp
from jax import lax
from jax.experimental import pallas as pl
from jax.experimental.pallas import tpu as pltpu
from jax.sharding import PartitionSpec as P

D_F = 256
H_F = 4
D_C = 1024
HD = 64
RAD = 3
HALO = 2 * RAD

eps = 1e-06
log_span = math.log(1000.0)
side = 8
extent = side + 2 * RAD
lanes_wide = 16
scale = 1.0 / math.sqrt(HD)
vmem_bytes = 48 * 1024 * 1024


def dot(first, second, dims=((1,), (0,))):
    return lax.dot_general(first, second, (dims, ((), ())), preferred_element_type=jnp.float32)


def time_gain(gains, step_value):
    channels = gains.shape[0]
    frequency = jnp.exp(-log_span * jnp.arange(channels, dtype=jnp.float32) / channels)
    return gains * (1.0 + 0.5 * jnp.cos(step_value.astype(jnp.float32) * frequency))


def inverse_rms(floats):
    return lax.rsqrt(jnp.mean(floats * floats, axis=-1, keepdims=True) + eps)


def norm_backward(floats, inverse, factor, upstream):
    scaled = upstream * factor
    middle = jnp.mean(floats * scaled, axis=-1, keepdims=True)
    return (inverse * scaled - floats * inverse * inverse * inverse * middle).astype(jnp.bfloat16)


def round_up(value, multiple):
    return -(-value // multiple) * multiple


def fine_body(
    limits,
    x_ref,
    dy_ref,
    above_ref,
    below_ref,
    left_ref,
    right_ref,
    factor_ref,
    qkv_ref,
    out_ref,
    dx_ref,
    keep_ref,
    send_ref,
    x_grid,
    dy_grid,
    k_grid,
    v_grid,
    q_grid,
    u_grid,
    dk_grid,
    dv_grid,
    dq_grid,
    a_grid,
    bias_ref,
    total_ref,
):
    height, breadth = x_ref.shape[0], x_ref.shape[1]
    grid_rows, grid_cols = x_grid.shape[0], x_grid.shape[1]
    query_rows = dy_grid.shape[0]
    floats = jnp.float32
    factor = factor_ref[...]

    x_grid[...] = jnp.zeros_like(x_grid)
    dy_grid[...] = jnp.zeros_like(dy_grid)
    dk_grid[...] = jnp.zeros_like(dk_grid)
    dv_grid[...] = jnp.zeros_like(dv_grid)
    inner = slice(HALO, HALO + breadth)
    x_grid[0:HALO, inner] = above_ref[0:HALO].astype(floats)
    x_grid[HALO : HALO + height, inner] = x_ref[...].astype(floats)
    x_grid[HALO + height : HALO + height + HALO, inner] = below_ref[0:HALO].astype(floats)
    dy_grid[0:RAD, inner] = above_ref[HALO : HALO + RAD].astype(floats)
    dy_grid[RAD : RAD + height, inner] = dy_ref[...].astype(floats)
    dy_grid[RAD + height : RAD + height + RAD, inner] = below_ref[HALO : HALO + RAD].astype(floats)
    for strip, first in ((left_ref, 0), (right_ref, HALO + breadth)):
        span = slice(first, first + HALO)
        at = 0
        for grid, begin, count in (
            (x_grid, 0, HALO),
            (dy_grid, 0, RAD),
            (x_grid, HALO, height),
            (dy_grid, RAD, height),
            (x_grid, HALO + height, HALO),
            (dy_grid, RAD + height, RAD),
        ):
            grid[begin : begin + count, span] = strip[at : at + count].astype(floats)
            at += count

    tokens = x_grid[...].reshape(grid_rows * grid_cols, D_F)
    normed = (tokens * inverse_rms(tokens) * factor).astype(jnp.bfloat16)
    key_values = dot(normed, qkv_ref[:, D_F:]).astype(jnp.bfloat16).astype(floats)
    k_grid[...] = key_values[:, :D_F].reshape(grid_rows, grid_cols, D_F)
    v_grid[...] = key_values[:, D_F:].reshape(grid_rows, grid_cols, D_F)
    query_tokens = normed[RAD * grid_cols : (RAD + query_rows) * grid_cols]
    queries = dot(query_tokens, qkv_ref[:, :D_F]).astype(jnp.bfloat16).astype(floats) * scale
    q_grid[...] = queries.reshape(query_rows, grid_cols, D_F)
    cotangents = dy_grid[...].reshape(query_rows * grid_cols, D_F).astype(jnp.bfloat16)
    ups = dot(cotangents, out_ref[...], ((1,), (1,))).astype(jnp.bfloat16).astype(floats)
    u_grid[...] = ups.reshape(query_rows, grid_cols, D_F)

    keys_count, heads_count = extent * lanes_wide, H_F * side * side
    key_at = lax.broadcasted_iota(jnp.int32, (keys_count, heads_count), 0)
    query_at = lax.broadcasted_iota(jnp.int32, (keys_count, heads_count), 1)
    row_gap = (key_at // lanes_wide) - ((query_at // side) % side)
    col_gap = (key_at % lanes_wide) - (query_at % side)
    near = (row_gap >= 0) & (row_gap <= 2 * RAD) & (col_gap >= 0) & (col_gap <= 2 * RAD)
    bias_ref[...] = jnp.where(near, 0.0, -1e30)
    row_low, row_high, col_low, col_high = limits[0], limits[1], limits[2], limits[3]
    lone = lax.broadcasted_iota(jnp.int32, (keys_count, 1), 0)
    head_of = lax.broadcasted_iota(jnp.int32, (side * side, D_F), 1) // HD

    def spread(block):
        return jnp.concatenate(
            [jnp.where(head_of == h, block, 0.0).astype(jnp.bfloat16) for h in range(H_F)], axis=0
        )

    def collect(full):
        total = jnp.where(head_of == 0, full[: side * side], 0.0)
        for h in range(1, H_F):
            piece = full[h * side * side : (h + 1) * side * side]
            total = jnp.where(head_of == h, piece, total)
        return total.reshape(side, side, D_F)

    for block_row in range(query_rows // side):
        top = block_row * side
        for block_col in range((grid_cols - side) // side):
            start = block_col * side
            window = (slice(top, top + extent), slice(start, start + lanes_wide))
            keys = k_grid[window].reshape(keys_count, D_F).astype(jnp.bfloat16)
            values = v_grid[window].reshape(keys_count, D_F).astype(jnp.bfloat16)
            place = (slice(top, top + side), slice(start + RAD, start + RAD + side))
            wide_queries = spread(q_grid[place].reshape(side * side, D_F))
            wide_ups = spread(u_grid[place].reshape(side * side, D_F))
            key_row = lone // lanes_wide + top
            key_col = lone % lanes_wide + start
            inside = (
                (key_row >= row_low)
                & (key_row < row_high)
                & (key_col >= col_low)
                & (key_col < col_high)
            )
            scores = dot(keys, wide_queries, ((1,), (1,)))
            scores = scores + (bias_ref[...] + jnp.where(inside, 0.0, -1e30))
            raised = jnp.exp(scores - jnp.max(scores, axis=0, keepdims=True))
            shares = raised * (1.0 / jnp.sum(raised, axis=0, keepdims=True))
            products = dot(values, wide_ups, ((1,), (1,)))
            centre = jnp.sum(shares * products, axis=0, keepdims=True)
            slopes = (shares * (products - centre)).astype(jnp.bfloat16)
            weights = shares.astype(jnp.bfloat16)
            dv_grid[window] += dot(weights, wide_ups).reshape(extent, lanes_wide, D_F)
            dk_grid[window] += dot(slopes, wide_queries).reshape(extent, lanes_wide, D_F)
            block = (slice(top, top + side), slice(start, start + side))
            a_grid[block] = collect(dot(weights, values, ((0,), (0,))))
            dq_grid[block] = collect(dot(slopes, keys, ((0,), (0,))))

    count = height * breadth
    own_queries = (slice(RAD, RAD + height), slice(RAD, RAD + breadth))
    own_keys = (slice(HALO, HALO + height), inner)
    attended = a_grid[own_queries].reshape(count, D_F).astype(jnp.bfloat16)
    grad_q = (dq_grid[own_queries].reshape(count, D_F) * scale).astype(jnp.bfloat16)
    grad_k = dk_grid[own_keys].reshape(count, D_F).astype(jnp.bfloat16)
    grad_v = dv_grid[own_keys].reshape(count, D_F).astype(jnp.bfloat16)
    grad_proj = jnp.concatenate([grad_q, grad_k, grad_v], axis=1)
    picture = x_ref[...].reshape(count, D_F).astype(floats)
    inverse = inverse_rms(picture)
    own_normed = (picture * inverse * factor).astype(jnp.bfloat16)
    flat_cot = dy_ref[...].reshape(count, D_F)
    grads = jnp.concatenate(
        [
            dot(own_normed, grad_proj, ((0,), (0,))),
            dot(attended, flat_cot, ((0,), (0,))),
        ],
        axis=1,
    )
    half, columns = keep_ref.shape[0], keep_ref.shape[1]
    total_ref[...] = grads.reshape(total_ref.shape)
    for low in range(2):
        target = (keep_ref, send_ref)[low]
        for high in range(half):
            for row in range(columns):
                block = (limits[4] ^ (2 * high + low)) * columns + row
                target[high, row] = total_ref[block].astype(target.dtype)
    down = dot(grad_proj, qkv_ref[...], ((1,), (1,)))
    dx_ref[...] = norm_backward(picture, inverse, factor, down).reshape(height, breadth, D_F)


def fine_block(peers, limits, picture, cotangent, above, below, left, right, factor, fine_qkv, fine_out):
    height, breadth = picture.shape[0], picture.shape[1]
    query_rows = round_up(height + 2 * RAD, side)
    query_cols = round_up(breadth + 2 * RAD, side)
    grid_rows, grid_cols = query_rows + 2 * RAD, query_cols + side
    across, down = peers
    rows = D_F // (across * down)
    halves = (across // 2, down, rows, 4 * D_F)
    vmem = pl.BlockSpec(memory_space=pltpu.VMEM)
    wide = pltpu.VMEM((grid_rows, grid_cols, D_F), jnp.float32)
    middle = pltpu.VMEM((query_rows, grid_cols, D_F), jnp.float32)
    small = pltpu.VMEM((query_rows, query_cols, D_F), jnp.float32)
    return pl.pallas_call(
        fine_body,
        out_shape=(
            jax.ShapeDtypeStruct((height, breadth, D_F), jnp.bfloat16),
            jax.ShapeDtypeStruct(halves, jnp.float32),
            jax.ShapeDtypeStruct(halves, jnp.bfloat16),
        ),
        in_specs=[pl.BlockSpec(memory_space=pltpu.SMEM)] + [vmem] * 9,
        out_specs=(vmem, vmem, vmem),
        scratch_shapes=[
            wide,
            middle,
            wide,
            wide,
            middle,
            middle,
            wide,
            wide,
            small,
            small,
            pltpu.VMEM((extent * lanes_wide, H_F * side * side), jnp.float32),
            pltpu.VMEM((across * down, rows, 4 * D_F), jnp.float32),
        ],
        compiler_params=pltpu.CompilerParams(vmem_limit_bytes=vmem_bytes),
        name="fine_block",
    )(limits, picture, cotangent, above, below, left, right, factor, fine_qkv, fine_out)


def coarse_body(
    x_ref,
    dy_ref,
    factor_ref,
    qkv_hbm,
    out_hbm,
    parts_ref,
    grads_ref,
    qkv_ref,
    out_ref,
    arrived,
):
    fetches = [
        pltpu.make_async_copy(qkv_hbm, qkv_ref, arrived.at[0]),
        pltpu.make_async_copy(out_hbm, out_ref, arrived.at[1]),
    ]
    for fetch in fetches:
        fetch.start()
    tokens = x_ref[...].astype(jnp.float32)
    normed = (tokens * inverse_rms(tokens) * factor_ref[...]).astype(jnp.bfloat16)
    cot = dy_ref[...]
    for fetch in fetches:
        fetch.wait()
    flat_qkv = qkv_ref[...].reshape(3 * HD, D_C)
    out_rows = out_ref[...]
    projected = dot(normed, flat_qkv, ((1,), (1,))).astype(jnp.bfloat16)
    queries, keys, values = projected[:, :HD], projected[:, HD : 2 * HD], projected[:, 2 * HD :]
    ups = dot(cot, out_rows, ((1,), (1,))).astype(jnp.bfloat16)
    scores = dot(queries, keys, ((1,), (1,))) * scale
    raised = jnp.exp(scores - jnp.max(scores, axis=-1, keepdims=True))
    shares = raised * (1.0 / jnp.sum(raised, axis=-1, keepdims=True))
    weights = shares.astype(jnp.bfloat16)
    mixed = dot(weights, values).astype(jnp.bfloat16)
    products = dot(ups, values, ((1,), (1,)))
    centre = jnp.sum(shares * products, axis=-1, keepdims=True)
    slopes = (shares * (products - centre)).astype(jnp.bfloat16)
    grad_q = (dot(slopes, keys) * scale).astype(jnp.bfloat16)
    grad_k = (dot(slopes, queries, ((0,), (0,))) * scale).astype(jnp.bfloat16)
    grad_v = dot(weights, ups, ((0,), (0,))).astype(jnp.bfloat16)
    stacked = jnp.concatenate([grad_q, grad_k, grad_v], axis=1)
    parts_ref[...] = dot(stacked, flat_qkv).astype(jnp.bfloat16)
    grads_ref[: 3 * HD] = dot(stacked, normed, ((0,), (0,))).astype(grads_ref.dtype)
    grads_ref[3 * HD :] = dot(mixed, cot, ((0,), (0,))).astype(grads_ref.dtype)


def coarse_block(tokens, cotangents, factor, head_qkv, head_out):
    count = tokens.shape[0]
    vmem = pl.BlockSpec(memory_space=pltpu.VMEM)
    return pl.pallas_call(
        coarse_body,
        out_shape=(
            jax.ShapeDtypeStruct((count, D_C), jnp.bfloat16),
            jax.ShapeDtypeStruct((4 * HD, D_C), jnp.bfloat16),
        ),
        in_specs=[vmem] * 3 + [pl.BlockSpec(memory_space=pl.ANY)] * 2,
        out_specs=(vmem, vmem),
        scratch_shapes=[
            pltpu.VMEM(head_qkv.shape, jnp.bfloat16),
            pltpu.VMEM(head_out.shape, jnp.bfloat16),
            pltpu.SemaphoreType.DMA((2,)),
        ],
        compiler_params=pltpu.CompilerParams(vmem_limit_bytes=vmem_bytes),
        name="coarse_block",
    )(tokens, cotangents, factor, head_qkv, head_out)


def pack_body(first, second, x_ref, dy_ref, own_ref):
    own_ref[:, :D_C] = x_ref[...].astype(jnp.float32).reshape(-1, D_C).astype(jnp.bfloat16)
    own_ref[:, D_C:] = dy_ref[...].astype(jnp.float32).reshape(-1, D_C).astype(jnp.bfloat16)


def packed(after, tokens, cotangents):
    vmem = pl.BlockSpec(memory_space=pltpu.VMEM)
    count = tokens.shape[0] * tokens.shape[1]
    return pl.pallas_call(
        pack_body,
        out_shape=jax.ShapeDtypeStruct((count, 2 * D_C), jnp.bfloat16),
        in_specs=[pl.BlockSpec(memory_space=pl.ANY)] * 2 + [vmem] * 2,
        out_specs=vmem,
        name="pack_coarse",
    )(*after, tokens, cotangents)


def pair_sum_body(first, second, qkv_ref, out_ref):
    total = (first[...].astype(jnp.float32) + second[...].astype(jnp.float32)).astype(jnp.bfloat16)
    qkv_ref[...] = total[: 3 * HD].reshape(qkv_ref.shape)
    out_ref[...] = total[3 * HD :]


def pair_sum(first, second):
    vmem = pl.BlockSpec(memory_space=pltpu.VMEM)
    return pl.pallas_call(
        pair_sum_body,
        out_shape=(
            jax.ShapeDtypeStruct((3, HD, D_C), jnp.bfloat16),
            jax.ShapeDtypeStruct((HD, D_C), jnp.bfloat16),
        ),
        in_specs=[vmem, vmem],
        out_specs=(vmem, vmem),
        name="pair_sum",
    )(first, second)


def place_body(place, near_ref, far_ref, qkv_ref, out_ref):
    highs, downs, rows = near_ref.shape[0], near_ref.shape[1], near_ref.shape[2]
    for low in range(2):
        for high in range(highs):
            for row in range(downs):
                block = (place[0] ^ (2 * high + low)) * downs + row
                at = pl.ds(pl.multiple_of(block * rows, rows), rows)
                piece = (near_ref, far_ref)[low][high, row]
                qkv_ref[at] = piece[:, : 3 * D_F]
                out_ref[at] = piece[:, 3 * D_F :]


def place_blocks(place, near, far):
    vmem = pl.BlockSpec(memory_space=pltpu.VMEM)
    return pl.pallas_call(
        place_body,
        out_shape=(
            jax.ShapeDtypeStruct((D_F, 3 * D_F), jnp.bfloat16),
            jax.ShapeDtypeStruct((D_F, D_F), jnp.bfloat16),
        ),
        in_specs=[pl.BlockSpec(memory_space=pltpu.SMEM), vmem, vmem],
        out_specs=(vmem, vmem),
        compiler_params=pltpu.CompilerParams(vmem_limit_bytes=vmem_bytes),
        name="place_blocks",
    )(place, near, far)


def neighbours(low_edge, high_edge, axis):
    peers = lax.axis_size(axis)
    up = [(i, i + 1) for i in range(peers - 1)]
    down = [(i + 1, i) for i in range(peers - 1)]
    return lax.ppermute(high_edge, axis, up), lax.ppermute(low_edge, axis, down)


def swapped(value, axis, mask):
    return lax.ppermute(value, axis, [(i, i ^ mask) for i in range(lax.axis_size(axis))])


def tied(*arrays):
    return lax.optimization_barrier(arrays)


def batch_sum(partial):
    if lax.axis_size("batch") != 2:
        return lax.psum(partial, "batch")
    return wide(partial) + wide(swapped(partial, "batch", 1))


def wide(value):
    return value.astype(jnp.float32)


def narrow(value):
    return value.astype(jnp.bfloat16)


def all_rows(piece):
    downs = lax.axis_size("gy")
    return jnp.stack([piece] + [swapped(piece, "gy", row) for row in range(1, downs)])


def row_sum(pieces):
    total = wide(pieces[0])
    for row in range(1, pieces.shape[0]):
        total = total + wide(swapped(narrow(pieces[row]), "gy", row))
    return total


def local(
    x_fine,
    dy_fine,
    x_coarse,
    dy_coarse,
    timestep,
    fine_gain,
    coarse_gain,
    fine_qkv,
    fine_out,
    coarse_qkv,
    coarse_out,
):
    step_value = timestep[0]
    picture, cotangent = x_fine[0], dy_fine[0]
    height, breadth = picture.shape[0], picture.shape[1]
    across, downs = lax.axis_size("gx"), lax.axis_size("gy")
    assert across == 4 and downs & (downs - 1) == 0
    gx, gy = lax.axis_index("gx"), lax.axis_index("gy")

    low = jnp.concatenate([picture[:HALO], cotangent[:RAD]], axis=0)
    high = jnp.concatenate([picture[height - HALO :], cotangent[height - RAD :]], axis=0)
    above, below = neighbours(low, high, "gy")
    own = packed((low, high), x_coarse[0], dy_coarse[0])
    count = own.shape[0]
    row_group = all_rows(own)

    row_first = gy * height - HALO
    col_first = gx * breadth - HALO
    limits = jnp.stack(
        [
            -row_first,
            downs * height - row_first,
            -col_first,
            across * breadth - col_first,
            gx,
            gy,
        ]
    ).astype(jnp.int32)
    factor = time_gain(fine_gain, step_value)[None]
    coarse_factor = time_gain(coarse_gain, step_value)[None]
    above, below, limits, factor, coarse_factor = tied(above, below, limits, factor, coarse_factor)
    column = jnp.concatenate([above, picture, cotangent, below], axis=0)
    left, right = neighbours(column[:, :HALO], column[:, breadth - HALO :], "gx")
    left, right, row_group = tied(left, right, row_group)
    pair = jnp.stack([row_group, swapped(row_group, "gx", 2)])
    dx_picture, fine_keep, fine_send = fine_block(
        (across, downs),
        limits,
        picture,
        cotangent,
        above,
        below,
        left,
        right,
        factor,
        fine_qkv,
        fine_out,
    )
    fine_send, pair = tied(fine_send, pair)

    fine_half = fine_keep + wide(swapped(fine_send, "gx", 1))
    other_pair = swapped(pair, "gx", 1)
    fine_half, other_pair = tied(fine_half, other_pair)

    fine_quarter = narrow(fine_half[0] + wide(swapped(narrow(fine_half[1]), "gx", 2)))
    everyone = jnp.stack([pair, other_pair]).reshape(-1, 2 * D_C)
    parts, coarse_partial = coarse_block(
        everyone[:, :D_C], everyone[:, D_C:], coarse_factor, coarse_qkv, coarse_out
    )
    fine_quarter, parts, coarse_partial = tied(fine_quarter, parts, coarse_partial)

    fine_quarter = narrow(batch_sum(fine_quarter))
    parts = parts.reshape(2, 2, downs, count, D_C)
    coarse_half = wide(parts[0]) + wide(swapped(parts[1], "gx", 1))
    coarse_quarter = wide(coarse_half[0]) + wide(swapped(narrow(coarse_half[1]), "gx", 2))
    fine_quarter, coarse_quarter, coarse_partial = tied(
        fine_quarter, coarse_quarter, coarse_partial
    )

    pair_batch = lax.axis_size("batch") == 2
    coarse_other = swapped(coarse_partial, "batch", 1) if pair_batch else coarse_partial
    mask = 1
    while mask < downs:
        fine_quarter = narrow(wide(fine_quarter) + wide(swapped(fine_quarter, "gy", mask)))
        if mask == 1:
            coarse_down = row_sum(coarse_quarter)
            fine_quarter, coarse_down = tied(fine_quarter, coarse_down)
        mask *= 2
    coarse_floats = wide(x_coarse[0].reshape(-1, D_C))
    dx_coarse = norm_backward(
        coarse_floats, inverse_rms(coarse_floats), coarse_factor, coarse_down
    ).reshape(x_coarse.shape)
    fine_quarter, dx_coarse = tied(fine_quarter, dx_coarse)

    fine_pair = jnp.stack([fine_quarter, swapped(fine_quarter, "gx", 2)])
    if pair_batch:
        grad_coarse_qkv, grad_coarse_out = pair_sum(coarse_partial, coarse_other)
    else:
        coarse_sum = narrow(batch_sum(wide(coarse_partial)))
        grad_coarse_qkv = coarse_sum[: 3 * HD].reshape(coarse_qkv.shape)
        grad_coarse_out = coarse_sum[3 * HD :]
    fine_pair, grad_coarse_qkv, grad_coarse_out = tied(fine_pair, grad_coarse_qkv, grad_coarse_out)
    grad_qkv, grad_out = place_blocks(
        jnp.stack([gx, gy]).astype(jnp.int32), fine_pair, swapped(fine_pair, "gx", 1)
    )
    return (dx_picture[None], dx_coarse, grad_qkv, grad_out, grad_coarse_qkv, grad_coarse_out)


def solution(mesh):
    placed = (
        P("batch", "gy", "gx", None),
        P("batch", "gy", "gx", None),
        P("batch", "gy", "gx", None),
        P("batch", "gy", "gx", None),
        P("batch"),
        P(),
        P(),
        P(),
        P(),
        P(None, plane_spec, None),
        P(plane_spec, None),
    )
    return jax.shard_map(
        local,
        mesh=mesh,
        in_specs=placed,
        out_specs=(
            P("batch", "gy", "gx", None),
            P("batch", "gy", "gx", None),
            P(),
            P(),
            P(None, plane_spec, None),
            P(plane_spec, None),
        ),
        check_vma=False,
    )


plane_spec = ("gy", "gx")
```

```python
import math

import jax
import jax.numpy as jnp
from jax import lax
from jax.experimental import pallas as pl
from jax.experimental.pallas import tpu as pltpu
from jax.sharding import PartitionSpec as P

D_F = 256
H_F = 4
D_C = 1024
HD = 64
RAD = 3
HALO = 2 * RAD

eps = 1e-06
log_span = math.log(1000.0)
side = 8
extent = side + 2 * RAD
lanes_wide = 16
scale = 1.0 / math.sqrt(HD)
vmem_bytes = 48 * 1024 * 1024


def dot(first, second, dims=((1,), (0,))):
    return lax.dot_general(first, second, (dims, ((), ())), preferred_element_type=jnp.float32)


def time_gain(gains, step_value):
    channels = gains.shape[0]
    frequency = jnp.exp(-log_span * jnp.arange(channels, dtype=jnp.float32) / channels)
    return gains * (1.0 + 0.5 * jnp.cos(step_value.astype(jnp.float32) * frequency))


def inverse_rms(floats):
    return lax.rsqrt(jnp.mean(floats * floats, axis=-1, keepdims=True) + eps)


def norm_backward(floats, inverse, factor, upstream):
    scaled = upstream * factor
    middle = jnp.mean(floats * scaled, axis=-1, keepdims=True)
    return (inverse * scaled - floats * inverse * inverse * inverse * middle).astype(jnp.bfloat16)


def round_up(value, multiple):
    return -(-value // multiple) * multiple


def fine_body(
    limits,
    x_ref,
    dy_ref,
    above_ref,
    below_ref,
    left_ref,
    right_ref,
    factor_ref,
    qkv_ref,
    out_ref,
    dx_ref,
    keep_ref,
    send_ref,
    x_grid,
    dy_grid,
    k_grid,
    v_grid,
    q_grid,
    u_grid,
    dk_grid,
    dv_grid,
    dq_grid,
    a_grid,
    bias_ref,
    total_ref,
):
    height, breadth = x_ref.shape[0], x_ref.shape[1]
    grid_rows, grid_cols = x_grid.shape[0], x_grid.shape[1]
    query_rows = dy_grid.shape[0]
    floats = jnp.float32
    factor = factor_ref[...]

    x_grid[...] = jnp.zeros_like(x_grid)
    dy_grid[...] = jnp.zeros_like(dy_grid)
    dk_grid[...] = jnp.zeros_like(dk_grid)
    dv_grid[...] = jnp.zeros_like(dv_grid)
    inner = slice(HALO, HALO + breadth)
    x_grid[0:HALO, inner] = above_ref[0:HALO].astype(floats)
    x_grid[HALO : HALO + height, inner] = x_ref[...].astype(floats)
    x_grid[HALO + height : HALO + height + HALO, inner] = below_ref[0:HALO].astype(floats)
    dy_grid[0:RAD, inner] = above_ref[HALO : HALO + RAD].astype(floats)
    dy_grid[RAD : RAD + height, inner] = dy_ref[...].astype(floats)
    dy_grid[RAD + height : RAD + height + RAD, inner] = below_ref[HALO : HALO + RAD].astype(floats)
    for strip, first in ((left_ref, 0), (right_ref, HALO + breadth)):
        span = slice(first, first + HALO)
        at = 0
        for grid, begin, count in (
            (x_grid, 0, HALO),
            (dy_grid, 0, RAD),
            (x_grid, HALO, height),
            (dy_grid, RAD, height),
            (x_grid, HALO + height, HALO),
            (dy_grid, RAD + height, RAD),
        ):
            grid[begin : begin + count, span] = strip[at : at + count].astype(floats)
            at += count

    tokens = x_grid[...].reshape(grid_rows * grid_cols, D_F)
    normed = (tokens * inverse_rms(tokens) * factor).astype(jnp.bfloat16)
    key_values = dot(normed, qkv_ref[:, D_F:]).astype(jnp.bfloat16).astype(floats)
    k_grid[...] = key_values[:, :D_F].reshape(grid_rows, grid_cols, D_F)
    v_grid[...] = key_values[:, D_F:].reshape(grid_rows, grid_cols, D_F)
    query_tokens = normed[RAD * grid_cols : (RAD + query_rows) * grid_cols]
    queries = dot(query_tokens, qkv_ref[:, :D_F]).astype(jnp.bfloat16).astype(floats) * scale
    q_grid[...] = queries.reshape(query_rows, grid_cols, D_F)
    cotangents = dy_grid[...].reshape(query_rows * grid_cols, D_F).astype(jnp.bfloat16)
    ups = dot(cotangents, out_ref[...], ((1,), (1,))).astype(jnp.bfloat16).astype(floats)
    u_grid[...] = ups.reshape(query_rows, grid_cols, D_F)

    keys_count, heads_count = extent * lanes_wide, H_F * side * side
    key_at = lax.broadcasted_iota(jnp.int32, (keys_count, heads_count), 0)
    query_at = lax.broadcasted_iota(jnp.int32, (keys_count, heads_count), 1)
    row_gap = (key_at // lanes_wide) - ((query_at // side) % side)
    col_gap = (key_at % lanes_wide) - (query_at % side)
    near = (row_gap >= 0) & (row_gap <= 2 * RAD) & (col_gap >= 0) & (col_gap <= 2 * RAD)
    bias_ref[...] = jnp.where(near, 0.0, -1e30)
    row_low, row_high, col_low, col_high = limits[0], limits[1], limits[2], limits[3]
    lone = lax.broadcasted_iota(jnp.int32, (keys_count, 1), 0)
    head_of = lax.broadcasted_iota(jnp.int32, (side * side, D_F), 1) // HD

    def spread(block):
        return jnp.concatenate(
            [jnp.where(head_of == h, block, 0.0).astype(jnp.bfloat16) for h in range(H_F)], axis=0
        )

    def collect(full):
        total = jnp.where(head_of == 0, full[: side * side], 0.0)
        for h in range(1, H_F):
            piece = full[h * side * side : (h + 1) * side * side]
            total = jnp.where(head_of == h, piece, total)
        return total.reshape(side, side, D_F)

    for block_row in range(query_rows // side):
        top = block_row * side
        for block_col in range((grid_cols - side) // side):
            start = block_col * side
            window = (slice(top, top + extent), slice(start, start + lanes_wide))
            keys = k_grid[window].reshape(keys_count, D_F).astype(jnp.bfloat16)
            values = v_grid[window].reshape(keys_count, D_F).astype(jnp.bfloat16)
            place = (slice(top, top + side), slice(start + RAD, start + RAD + side))
            wide_queries = spread(q_grid[place].reshape(side * side, D_F))
            wide_ups = spread(u_grid[place].reshape(side * side, D_F))
            key_row = lone // lanes_wide + top
            key_col = lone % lanes_wide + start
            inside = (
                (key_row >= row_low)
                & (key_row < row_high)
                & (key_col >= col_low)
                & (key_col < col_high)
            )
            scores = dot(keys, wide_queries, ((1,), (1,)))
            scores = scores + (bias_ref[...] + jnp.where(inside, 0.0, -1e30))
            raised = jnp.exp(scores - jnp.max(scores, axis=0, keepdims=True))
            shares = raised * (1.0 / jnp.sum(raised, axis=0, keepdims=True))
            products = dot(values, wide_ups, ((1,), (1,)))
            centre = jnp.sum(shares * products, axis=0, keepdims=True)
            slopes = (shares * (products - centre)).astype(jnp.bfloat16)
            weights = shares.astype(jnp.bfloat16)
            dv_grid[window] += dot(weights, wide_ups).reshape(extent, lanes_wide, D_F)
            dk_grid[window] += dot(slopes, wide_queries).reshape(extent, lanes_wide, D_F)
            block = (slice(top, top + side), slice(start, start + side))
            a_grid[block] = collect(dot(weights, values, ((0,), (0,))))
            dq_grid[block] = collect(dot(slopes, keys, ((0,), (0,))))

    count = height * breadth
    own_queries = (slice(RAD, RAD + height), slice(RAD, RAD + breadth))
    own_keys = (slice(HALO, HALO + height), inner)
    attended = a_grid[own_queries].reshape(count, D_F).astype(jnp.bfloat16)
    grad_q = (dq_grid[own_queries].reshape(count, D_F) * scale).astype(jnp.bfloat16)
    grad_k = dk_grid[own_keys].reshape(count, D_F).astype(jnp.bfloat16)
    grad_v = dv_grid[own_keys].reshape(count, D_F).astype(jnp.bfloat16)
    grad_proj = jnp.concatenate([grad_q, grad_k, grad_v], axis=1)
    picture = x_ref[...].reshape(count, D_F).astype(floats)
    inverse = inverse_rms(picture)
    own_normed = (picture * inverse * factor).astype(jnp.bfloat16)
    flat_cot = dy_ref[...].reshape(count, D_F)
    grads = jnp.concatenate(
        [
            dot(own_normed, grad_proj, ((0,), (0,))),
            dot(attended, flat_cot, ((0,), (0,))),
        ],
        axis=1,
    )
    half, columns = keep_ref.shape[0], keep_ref.shape[1]
    total_ref[...] = grads.reshape(total_ref.shape)
    for low in range(2):
        target = (keep_ref, send_ref)[low]
        for high in range(half):
            for row in range(columns):
                block = (limits[4] ^ (2 * high + low)) * columns + row
                target[high, row] = total_ref[block].astype(target.dtype)
    down = dot(grad_proj, qkv_ref[...], ((1,), (1,)))
    dx_ref[...] = norm_backward(picture, inverse, factor, down).reshape(height, breadth, D_F)


def fine_block(peers, limits, picture, cotangent, above, below, left, right, factor, fine_qkv, fine_out):
    height, breadth = picture.shape[0], picture.shape[1]
    query_rows = round_up(height + 2 * RAD, side)
    query_cols = round_up(breadth + 2 * RAD, side)
    grid_rows, grid_cols = query_rows + 2 * RAD, query_cols + side
    across, down = peers
    rows = D_F // (across * down)
    halves = (across // 2, down, rows, 4 * D_F)
    vmem = pl.BlockSpec(memory_space=pltpu.VMEM)
    wide = pltpu.VMEM((grid_rows, grid_cols, D_F), jnp.float32)
    middle = pltpu.VMEM((query_rows, grid_cols, D_F), jnp.float32)
    small = pltpu.VMEM((query_rows, query_cols, D_F), jnp.float32)
    return pl.pallas_call(
        fine_body,
        out_shape=(
            jax.ShapeDtypeStruct((height, breadth, D_F), jnp.bfloat16),
            jax.ShapeDtypeStruct(halves, jnp.float32),
            jax.ShapeDtypeStruct(halves, jnp.bfloat16),
        ),
        in_specs=[pl.BlockSpec(memory_space=pltpu.SMEM)] + [vmem] * 9,
        out_specs=(vmem, vmem, vmem),
        scratch_shapes=[
            wide,
            middle,
            wide,
            wide,
            middle,
            middle,
            wide,
            wide,
            small,
            small,
            pltpu.VMEM((extent * lanes_wide, H_F * side * side), jnp.float32),
            pltpu.VMEM((across * down, rows, 4 * D_F), jnp.float32),
        ],
        compiler_params=pltpu.CompilerParams(vmem_limit_bytes=vmem_bytes),
        name="fine_block",
    )(limits, picture, cotangent, above, below, left, right, factor, fine_qkv, fine_out)


def coarse_body(
    x_ref,
    dy_ref,
    factor_ref,
    qkv_hbm,
    out_hbm,
    parts_ref,
    grads_ref,
    qkv_ref,
    out_ref,
    arrived,
):
    fetches = [
        pltpu.make_async_copy(qkv_hbm, qkv_ref, arrived.at[0]),
        pltpu.make_async_copy(out_hbm, out_ref, arrived.at[1]),
    ]
    for fetch in fetches:
        fetch.start()
    tokens = x_ref[...].astype(jnp.float32)
    normed = (tokens * inverse_rms(tokens) * factor_ref[...]).astype(jnp.bfloat16)
    cot = dy_ref[...]
    for fetch in fetches:
        fetch.wait()
    flat_qkv = qkv_ref[...].reshape(3 * HD, D_C)
    out_rows = out_ref[...]
    projected = dot(normed, flat_qkv, ((1,), (1,))).astype(jnp.bfloat16)
    queries, keys, values = projected[:, :HD], projected[:, HD : 2 * HD], projected[:, 2 * HD :]
    ups = dot(cot, out_rows, ((1,), (1,))).astype(jnp.bfloat16)
    scores = dot(queries, keys, ((1,), (1,))) * scale
    raised = jnp.exp(scores - jnp.max(scores, axis=-1, keepdims=True))
    shares = raised * (1.0 / jnp.sum(raised, axis=-1, keepdims=True))
    weights = shares.astype(jnp.bfloat16)
    mixed = dot(weights, values).astype(jnp.bfloat16)
    products = dot(ups, values, ((1,), (1,)))
    centre = jnp.sum(shares * products, axis=-1, keepdims=True)
    slopes = (shares * (products - centre)).astype(jnp.bfloat16)
    grad_q = (dot(slopes, keys) * scale).astype(jnp.bfloat16)
    grad_k = (dot(slopes, queries, ((0,), (0,))) * scale).astype(jnp.bfloat16)
    grad_v = dot(weights, ups, ((0,), (0,))).astype(jnp.bfloat16)
    stacked = jnp.concatenate([grad_q, grad_k, grad_v], axis=1)
    parts_ref[...] = dot(stacked, flat_qkv).astype(jnp.bfloat16)
    grads_ref[: 3 * HD] = dot(stacked, normed, ((0,), (0,))).astype(grads_ref.dtype)
    grads_ref[3 * HD :] = dot(mixed, cot, ((0,), (0,))).astype(grads_ref.dtype)


def coarse_block(tokens, cotangents, factor, head_qkv, head_out):
    count = tokens.shape[0]
    vmem = pl.BlockSpec(memory_space=pltpu.VMEM)
    return pl.pallas_call(
        coarse_body,
        out_shape=(
            jax.ShapeDtypeStruct((count, D_C), jnp.bfloat16),
            jax.ShapeDtypeStruct((4 * HD, D_C), jnp.bfloat16),
        ),
        in_specs=[vmem] * 3 + [pl.BlockSpec(memory_space=pltpu.HBM)] * 2,
        out_specs=(vmem, vmem),
        scratch_shapes=[
            pltpu.VMEM(head_qkv.shape, jnp.bfloat16),
            pltpu.VMEM(head_out.shape, jnp.bfloat16),
            pltpu.SemaphoreType.DMA((2,)),
        ],
        compiler_params=pltpu.CompilerParams(vmem_limit_bytes=vmem_bytes),
        name="coarse_block",
    )(tokens, cotangents, factor, head_qkv, head_out)


def pack_body(x_ref, dy_ref, own_ref):
    own_ref[:, :D_C] = x_ref[...].astype(jnp.float32).reshape(-1, D_C).astype(jnp.bfloat16)
    own_ref[:, D_C:] = dy_ref[...].astype(jnp.float32).reshape(-1, D_C).astype(jnp.bfloat16)


def packed(tokens, cotangents):
    vmem = pl.BlockSpec(memory_space=pltpu.VMEM)
    count = tokens.shape[0] * tokens.shape[1]
    return pl.pallas_call(
        pack_body,
        out_shape=jax.ShapeDtypeStruct((count, 2 * D_C), jnp.bfloat16),
        in_specs=[vmem] * 2,
        out_specs=vmem,
        compiler_params=pltpu.CompilerParams(vmem_limit_bytes=vmem_bytes),
        name="pack_coarse",
    )(tokens, cotangents)


def pair_sum_body(own, first, second, qkv_ref, out_ref):
    for part in range(4):
        come = (first, second)[part // 2][(part % 2) * HD : (part % 2 + 1) * HD]
        total = own[part * HD : (part + 1) * HD].astype(jnp.float32) + come.astype(jnp.float32)
        if part < 3:
            qkv_ref[part] = total.astype(jnp.bfloat16)
        else:
            out_ref[...] = total.astype(jnp.bfloat16)


def pair_sum(own, first, second):
    vmem = pl.BlockSpec(memory_space=pltpu.VMEM)
    return pl.pallas_call(
        pair_sum_body,
        out_shape=(
            jax.ShapeDtypeStruct((3, HD, D_C), jnp.bfloat16),
            jax.ShapeDtypeStruct((HD, D_C), jnp.bfloat16),
        ),
        in_specs=[vmem] * 3,
        out_specs=(vmem, vmem),
        compiler_params=pltpu.CompilerParams(vmem_limit_bytes=vmem_bytes),
        name="pair_sum",
    )(own, first, second)


def last_body(
    place,
    near_ref,
    far_ref,
    x_ref,
    factor_ref,
    kept_ref,
    come_ref,
    qkv_hbm,
    out_hbm,
    dx_ref,
    sems,
):
    highs, rows = near_ref.shape[0], near_ref.shape[1]
    copies = []
    for low in range(2):
        for high in range(highs):
            source = (near_ref, far_ref)[low].at[high]
            block = place[0] ^ (2 * high + low)
            at = pl.ds(pl.multiple_of(block * rows, rows), rows)
            for part, target in enumerate((qkv_hbm, out_hbm)):
                lanes = (slice(0, 3 * D_F), slice(3 * D_F, 4 * D_F))[part]
                copies.append(
                    pltpu.make_async_copy(
                        source.at[:, lanes], target.at[at, :], sems.at[low, high, part]
                    )
                )
    for copy in copies:
        copy.start()
    tokens = x_ref[...].astype(jnp.float32).reshape(-1, D_C)
    upstream = kept_ref[...] + come_ref[...].astype(jnp.float32)
    grads = norm_backward(tokens, inverse_rms(tokens), factor_ref[...], upstream)
    dx_ref[...] = grads.astype(jnp.float32).reshape(dx_ref.shape).astype(jnp.bfloat16)
    for copy in copies:
        copy.wait()


def last_step(place, near, far, tokens, factor, kept, come):
    vmem = pl.BlockSpec(memory_space=pltpu.VMEM)
    hbm = pl.BlockSpec(memory_space=pltpu.HBM)
    return pl.pallas_call(
        last_body,
        out_shape=(
            jax.ShapeDtypeStruct((D_F, 3 * D_F), jnp.bfloat16),
            jax.ShapeDtypeStruct((D_F, D_F), jnp.bfloat16),
            jax.ShapeDtypeStruct(tokens.shape, jnp.bfloat16),
        ),
        in_specs=[pl.BlockSpec(memory_space=pltpu.SMEM)] + [vmem] * 6,
        out_specs=(hbm, hbm, vmem),
        scratch_shapes=[pltpu.SemaphoreType.DMA((2, near.shape[0], 2))],
        compiler_params=pltpu.CompilerParams(vmem_limit_bytes=vmem_bytes),
        name="last_step",
    )(place, near, far, tokens, factor, kept, come)


def neighbours(low_edge, high_edge, axis):
    peers = lax.axis_size(axis)
    up = [(i, i + 1) for i in range(peers - 1)]
    down = [(i + 1, i) for i in range(peers - 1)]
    return lax.ppermute(high_edge, axis, up), lax.ppermute(low_edge, axis, down)


def swapped(value, axis, mask):
    return lax.ppermute(value, axis, [(i, i ^ mask) for i in range(lax.axis_size(axis))])


def tied(*arrays):
    return lax.optimization_barrier(arrays)


def batch_sum(partial):
    if lax.axis_size("batch") != 2:
        return lax.psum(partial, "batch")
    return wide(partial) + wide(swapped(partial, "batch", 1))


def wide(value):
    return value.astype(jnp.float32)


def narrow(value):
    return value.astype(jnp.bfloat16)


def all_rows(piece):
    downs = lax.axis_size("gy")
    return jnp.stack([piece] + [swapped(piece, "gy", row) for row in range(1, downs)])


def local(
    x_fine,
    dy_fine,
    x_coarse,
    dy_coarse,
    timestep,
    fine_gain,
    coarse_gain,
    fine_qkv,
    fine_out,
    coarse_qkv,
    coarse_out,
):
    step_value = timestep[0]
    picture, cotangent = x_fine[0], dy_fine[0]
    height, breadth = picture.shape[0], picture.shape[1]
    across, downs = lax.axis_size("gx"), lax.axis_size("gy")
    assert across == 4 and downs & (downs - 1) == 0
    gx, gy = lax.axis_index("gx"), lax.axis_index("gy")

    low = jnp.concatenate([picture[:HALO], cotangent[:RAD]], axis=0)
    high = jnp.concatenate([picture[height - HALO :], cotangent[height - RAD :]], axis=0)
    above, below = neighbours(low, high, "gy")
    row_first = gy * height - HALO
    col_first = gx * breadth - HALO
    limits = jnp.stack(
        [
            -row_first,
            downs * height - row_first,
            -col_first,
            across * breadth - col_first,
            gx,
            gy,
        ]
    ).astype(jnp.int32)
    factor = time_gain(fine_gain, step_value)[None]
    coarse_factor = time_gain(coarse_gain, step_value)[None]
    place = gx.astype(jnp.int32)[None]
    coarse_picture, coarse_cot = x_coarse[0], dy_coarse[0]
    above, below, limits, place, factor, coarse_factor = tied(
        above, below, limits, place, factor, coarse_factor
    )
    column = jnp.concatenate([above, picture, cotangent, below], axis=0)
    first, final = column[:, :HALO], column[:, breadth - HALO :]
    first, final, coarse_picture, coarse_cot = tied(first, final, coarse_picture, coarse_cot)
    left, right = neighbours(first, final, "gx")
    own = packed(coarse_picture, coarse_cot)
    count = own.shape[0]
    row_group = all_rows(own)
    left, right, row_group = tied(left, right, row_group)
    pair = jnp.stack([row_group, swapped(row_group, "gx", 2)])
    dx_picture, fine_keep, fine_send = fine_block(
        (across, downs),
        limits,
        picture,
        cotangent,
        above,
        below,
        left,
        right,
        factor,
        fine_qkv,
        fine_out,
    )
    fine_send, pair = tied(fine_send, pair)

    fine_half = fine_keep + wide(swapped(fine_send, "gx", 1))
    other_pair = swapped(pair, "gx", 1)
    fine_half, other_pair = tied(fine_half, other_pair)

    fine_quarter = narrow(fine_half[0] + wide(swapped(narrow(fine_half[1]), "gx", 2)))
    everyone = jnp.stack([pair, other_pair]).reshape(-1, 2 * D_C)
    parts, coarse_partial = coarse_block(
        everyone[:, :D_C], everyone[:, D_C:], coarse_factor, coarse_qkv, coarse_out
    )
    fine_quarter, parts, coarse_partial = tied(fine_quarter, parts, coarse_partial)

    rows = D_F // across
    fine_quarter = narrow(batch_sum(fine_quarter)).reshape(rows, 4 * D_F)
    parts = parts.reshape(2, 2, downs, count, D_C)
    coarse_kept = wide(parts[0]) + wide(swapped(parts[1], "gx", 1))
    fine_quarter, coarse_kept, coarse_partial = tied(fine_quarter, coarse_kept, coarse_partial)

    pair_batch = lax.axis_size("batch") == 2
    halves = (coarse_partial[: 2 * HD], coarse_partial[2 * HD :])
    others = [swapped(half, "batch", 1) if pair_batch else half for half in halves]
    mask = 1
    while mask < downs:
        last = 2 * mask == downs
        coarse_kept = coarse_kept.reshape(2, -1, 2, count, D_C)
        sent = narrow(coarse_kept[:, :, 1]).reshape(-1, D_C)
        come = swapped(jnp.concatenate([fine_quarter, sent], axis=0), "gy", mask)
        coarse_kept = coarse_kept[:, :, 0]
        coarse_kept = coarse_kept + wide(come[rows:]).reshape(coarse_kept.shape)
        fine_quarter = narrow(wide(fine_quarter) + wide(come[:rows]))
        at = int(last)
        fine_quarter, coarse_kept, others[at] = tied(fine_quarter, coarse_kept, others[at])
        mask *= 2

    coarse_kept = coarse_kept.reshape(2, count, D_C)
    come = swapped(jnp.concatenate([fine_quarter, narrow(coarse_kept[1])], axis=0), "gx", 2)
    if pair_batch:
        grad_coarse_qkv, grad_coarse_out = pair_sum(coarse_partial, *others)
    else:
        coarse_sum = narrow(batch_sum(wide(coarse_partial)))
        grad_coarse_qkv = coarse_sum[: 3 * HD].reshape(coarse_qkv.shape)
        grad_coarse_out = coarse_sum[3 * HD :]
    come, grad_coarse_qkv, grad_coarse_out = tied(come, grad_coarse_qkv, grad_coarse_out)
    fine_pair = jnp.stack([fine_quarter, come[:rows]])
    grad_qkv, grad_out, dx_coarse = last_step(
        place,
        fine_pair,
        swapped(fine_pair, "gx", 1),
        coarse_picture,
        coarse_factor,
        coarse_kept[0],
        come[rows:],
    )
    return (
        dx_picture[None],
        dx_coarse[None],
        grad_qkv,
        grad_out,
        grad_coarse_qkv,
        grad_coarse_out,
    )


def solution(mesh):
    placed = (
        P("batch", "gy", "gx", None),
        P("batch", "gy", "gx", None),
        P("batch", "gy", "gx", None),
        P("batch", "gy", "gx", None),
        P("batch"),
        P(),
        P(),
        P(),
        P(),
        P(None, plane_spec, None),
        P(plane_spec, None),
    )
    return jax.shard_map(
        local,
        mesh=mesh,
        in_specs=placed,
        out_specs=(
            P("batch", "gy", "gx", None),
            P("batch", "gy", "gx", None),
            P(),
            P(),
            P(None, plane_spec, None),
            P(plane_spec, None),
        ),
        check_vma=False,
    )


plane_spec = ("gy", "gx")
```

```python
import math

import jax
import jax.numpy as jnp
from jax import lax
from jax.experimental import pallas as pl
from jax.experimental.pallas import tpu as pltpu
from jax.sharding import PartitionSpec as P

D_F = 256
H_F = 4
D_C = 1024
HD = 64
RAD = 3
HALO = 2 * RAD

eps = 1e-06
log_span = math.log(1000.0)
side = 8
extent = side + 2 * RAD
lanes_wide = 16
scale = 1.0 / math.sqrt(HD)
vmem_bytes = 48 * 1024 * 1024


def dot(first, second, dims=((1,), (0,))):
    return lax.dot_general(first, second, (dims, ((), ())), preferred_element_type=jnp.float32)


def time_gain(gains, step_value):
    channels = gains.shape[0]
    frequency = jnp.exp(-log_span * jnp.arange(channels, dtype=jnp.float32) / channels)
    return gains * (1.0 + 0.5 * jnp.cos(step_value.astype(jnp.float32) * frequency))


def inverse_rms(floats):
    return lax.rsqrt(jnp.mean(floats * floats, axis=-1, keepdims=True) + eps)


def norm_backward(floats, inverse, factor, upstream):
    scaled = upstream * factor
    middle = jnp.mean(floats * scaled, axis=-1, keepdims=True)
    return (inverse * scaled - floats * inverse * inverse * inverse * middle).astype(jnp.bfloat16)


def round_up(value, multiple):
    return -(-value // multiple) * multiple


def fine_body(
    limits,
    x_ref,
    dy_ref,
    above_ref,
    below_ref,
    left_ref,
    right_ref,
    factor_ref,
    qkv_ref,
    out_ref,
    dx_ref,
    keep_ref,
    send_ref,
    x_grid,
    dy_grid,
    k_grid,
    v_grid,
    q_grid,
    u_grid,
    dk_grid,
    dv_grid,
    dq_grid,
    a_grid,
    bias_ref,
    total_ref,
):
    height, breadth = x_ref.shape[0], x_ref.shape[1]
    grid_rows, grid_cols = x_grid.shape[0], x_grid.shape[1]
    query_rows = dy_grid.shape[0]
    floats = jnp.float32
    factor = factor_ref[...]

    x_grid[...] = jnp.zeros_like(x_grid)
    dy_grid[...] = jnp.zeros_like(dy_grid)
    dk_grid[...] = jnp.zeros_like(dk_grid)
    dv_grid[...] = jnp.zeros_like(dv_grid)
    inner = slice(HALO, HALO + breadth)
    x_grid[0:HALO, inner] = above_ref[0:HALO].astype(floats)
    x_grid[HALO : HALO + height, inner] = x_ref[...].astype(floats)
    x_grid[HALO + height : HALO + height + HALO, inner] = below_ref[0:HALO].astype(floats)
    dy_grid[0:RAD, inner] = above_ref[HALO : HALO + RAD].astype(floats)
    dy_grid[RAD : RAD + height, inner] = dy_ref[...].astype(floats)
    dy_grid[RAD + height : RAD + height + RAD, inner] = below_ref[HALO : HALO + RAD].astype(floats)
    for strip, first in ((left_ref, 0), (right_ref, HALO + breadth)):
        span = slice(first, first + HALO)
        at = 0
        for grid, begin, count in (
            (x_grid, 0, HALO),
            (dy_grid, 0, RAD),
            (x_grid, HALO, height),
            (dy_grid, RAD, height),
            (x_grid, HALO + height, HALO),
            (dy_grid, RAD + height, RAD),
        ):
            grid[begin : begin + count, span] = strip[at : at + count].astype(floats)
            at += count

    tokens = x_grid[...].reshape(grid_rows * grid_cols, D_F)
    normed = (tokens * inverse_rms(tokens) * factor).astype(jnp.bfloat16)
    key_values = dot(normed, qkv_ref[:, D_F:]).astype(jnp.bfloat16).astype(floats)
    k_grid[...] = key_values[:, :D_F].reshape(grid_rows, grid_cols, D_F)
    v_grid[...] = key_values[:, D_F:].reshape(grid_rows, grid_cols, D_F)
    query_tokens = normed[RAD * grid_cols : (RAD + query_rows) * grid_cols]
    queries = dot(query_tokens, qkv_ref[:, :D_F]).astype(jnp.bfloat16).astype(floats) * scale
    q_grid[...] = queries.reshape(query_rows, grid_cols, D_F)
    cotangents = dy_grid[...].reshape(query_rows * grid_cols, D_F).astype(jnp.bfloat16)
    ups = dot(cotangents, out_ref[...], ((1,), (1,))).astype(jnp.bfloat16).astype(floats)
    u_grid[...] = ups.reshape(query_rows, grid_cols, D_F)

    keys_count, heads_count = extent * lanes_wide, H_F * side * side
    key_at = lax.broadcasted_iota(jnp.int32, (keys_count, heads_count), 0)
    query_at = lax.broadcasted_iota(jnp.int32, (keys_count, heads_count), 1)
    row_gap = (key_at // lanes_wide) - ((query_at // side) % side)
    col_gap = (key_at % lanes_wide) - (query_at % side)
    near = (row_gap >= 0) & (row_gap <= 2 * RAD) & (col_gap >= 0) & (col_gap <= 2 * RAD)
    bias_ref[...] = jnp.where(near, 0.0, -1e30)
    row_low, row_high, col_low, col_high = limits[0], limits[1], limits[2], limits[3]
    lone = lax.broadcasted_iota(jnp.int32, (keys_count, 1), 0)
    head_of = lax.broadcasted_iota(jnp.int32, (side * side, D_F), 1) // HD

    def spread(block):
        return jnp.concatenate(
            [jnp.where(head_of == h, block, 0.0).astype(jnp.bfloat16) for h in range(H_F)], axis=0
        )

    def collect(full):
        total = jnp.where(head_of == 0, full[: side * side], 0.0)
        for h in range(1, H_F):
            piece = full[h * side * side : (h + 1) * side * side]
            total = jnp.where(head_of == h, piece, total)
        return total.reshape(side, side, D_F)

    for block_row in range(query_rows // side):
        top = block_row * side
        for block_col in range((grid_cols - side) // side):
            start = block_col * side
            window = (slice(top, top + extent), slice(start, start + lanes_wide))
            keys = k_grid[window].reshape(keys_count, D_F).astype(jnp.bfloat16)
            values = v_grid[window].reshape(keys_count, D_F).astype(jnp.bfloat16)
            place = (slice(top, top + side), slice(start + RAD, start + RAD + side))
            wide_queries = spread(q_grid[place].reshape(side * side, D_F))
            wide_ups = spread(u_grid[place].reshape(side * side, D_F))
            key_row = lone // lanes_wide + top
            key_col = lone % lanes_wide + start
            inside = (
                (key_row >= row_low)
                & (key_row < row_high)
                & (key_col >= col_low)
                & (key_col < col_high)
            )
            scores = dot(keys, wide_queries, ((1,), (1,)))
            scores = scores + (bias_ref[...] + jnp.where(inside, 0.0, -1e30))
            raised = jnp.exp(scores - jnp.max(scores, axis=0, keepdims=True))
            shares = raised * (1.0 / jnp.sum(raised, axis=0, keepdims=True))
            products = dot(values, wide_ups, ((1,), (1,)))
            centre = jnp.sum(shares * products, axis=0, keepdims=True)
            slopes = (shares * (products - centre)).astype(jnp.bfloat16)
            weights = shares.astype(jnp.bfloat16)
            dv_grid[window] += dot(weights, wide_ups).reshape(extent, lanes_wide, D_F)
            dk_grid[window] += dot(slopes, wide_queries).reshape(extent, lanes_wide, D_F)
            block = (slice(top, top + side), slice(start, start + side))
            a_grid[block] = collect(dot(weights, values, ((0,), (0,))))
            dq_grid[block] = collect(dot(slopes, keys, ((0,), (0,))))

    count = height * breadth
    own_queries = (slice(RAD, RAD + height), slice(RAD, RAD + breadth))
    own_keys = (slice(HALO, HALO + height), inner)
    attended = a_grid[own_queries].reshape(count, D_F).astype(jnp.bfloat16)
    grad_q = (dq_grid[own_queries].reshape(count, D_F) * scale).astype(jnp.bfloat16)
    grad_k = dk_grid[own_keys].reshape(count, D_F).astype(jnp.bfloat16)
    grad_v = dv_grid[own_keys].reshape(count, D_F).astype(jnp.bfloat16)
    grad_proj = jnp.concatenate([grad_q, grad_k, grad_v], axis=1)
    picture = x_ref[...].reshape(count, D_F).astype(floats)
    inverse = inverse_rms(picture)
    own_normed = (picture * inverse * factor).astype(jnp.bfloat16)
    flat_cot = dy_ref[...].reshape(count, D_F)
    grads = jnp.concatenate(
        [
            dot(own_normed, grad_proj, ((0,), (0,))),
            dot(attended, flat_cot, ((0,), (0,))),
        ],
        axis=1,
    )
    half, columns = keep_ref.shape[0], keep_ref.shape[1]
    total_ref[...] = grads.reshape(total_ref.shape)
    for low in range(2):
        target = (keep_ref, send_ref)[low]
        for high in range(half):
            for row in range(columns):
                block = (limits[4] ^ (2 * high + low)) * columns + row
                target[high, row] = total_ref[block].astype(target.dtype)
    down = dot(grad_proj, qkv_ref[...], ((1,), (1,)))
    dx_ref[...] = norm_backward(picture, inverse, factor, down).reshape(height, breadth, D_F)


def fine_block(peers, limits, picture, cotangent, above, below, left, right, factor, fine_qkv, fine_out):
    height, breadth = picture.shape[0], picture.shape[1]
    query_rows = round_up(height + 2 * RAD, side)
    query_cols = round_up(breadth + 2 * RAD, side)
    grid_rows, grid_cols = query_rows + 2 * RAD, query_cols + side
    across, down = peers
    rows = D_F // (across * down)
    halves = (across // 2, down, rows, 4 * D_F)
    vmem = pl.BlockSpec(memory_space=pltpu.VMEM)
    wide = pltpu.VMEM((grid_rows, grid_cols, D_F), jnp.float32)
    middle = pltpu.VMEM((query_rows, grid_cols, D_F), jnp.float32)
    small = pltpu.VMEM((query_rows, query_cols, D_F), jnp.float32)
    return pl.pallas_call(
        fine_body,
        out_shape=(
            jax.ShapeDtypeStruct((height, breadth, D_F), jnp.bfloat16),
            jax.ShapeDtypeStruct(halves, jnp.float32),
            jax.ShapeDtypeStruct(halves, jnp.bfloat16),
        ),
        in_specs=[pl.BlockSpec(memory_space=pltpu.SMEM)] + [vmem] * 9,
        out_specs=(vmem, vmem, vmem),
        scratch_shapes=[
            wide,
            middle,
            wide,
            wide,
            middle,
            middle,
            wide,
            wide,
            small,
            small,
            pltpu.VMEM((extent * lanes_wide, H_F * side * side), jnp.float32),
            pltpu.VMEM((across * down, rows, 4 * D_F), jnp.float32),
        ],
        compiler_params=pltpu.CompilerParams(vmem_limit_bytes=vmem_bytes),
        name="fine_block",
    )(limits, picture, cotangent, above, below, left, right, factor, fine_qkv, fine_out)


def coarse_body(
    x_ref,
    dy_ref,
    factor_ref,
    qkv_hbm,
    out_hbm,
    parts_ref,
    grads_ref,
    qkv_ref,
    out_ref,
    arrived,
):
    fetches = [
        pltpu.make_async_copy(qkv_hbm, qkv_ref, arrived.at[0]),
        pltpu.make_async_copy(out_hbm, out_ref, arrived.at[1]),
    ]
    for fetch in fetches:
        fetch.start()
    tokens = x_ref[...].astype(jnp.float32)
    normed = (tokens * inverse_rms(tokens) * factor_ref[...]).astype(jnp.bfloat16)
    cot = dy_ref[...]
    for fetch in fetches:
        fetch.wait()
    flat_qkv = qkv_ref[...].reshape(3 * HD, D_C)
    out_rows = out_ref[...]
    projected = dot(normed, flat_qkv, ((1,), (1,))).astype(jnp.bfloat16)
    queries, keys, values = projected[:, :HD], projected[:, HD : 2 * HD], projected[:, 2 * HD :]
    ups = dot(cot, out_rows, ((1,), (1,))).astype(jnp.bfloat16)
    scores = dot(queries, keys, ((1,), (1,))) * scale
    raised = jnp.exp(scores - jnp.max(scores, axis=-1, keepdims=True))
    shares = raised * (1.0 / jnp.sum(raised, axis=-1, keepdims=True))
    weights = shares.astype(jnp.bfloat16)
    mixed = dot(weights, values).astype(jnp.bfloat16)
    products = dot(ups, values, ((1,), (1,)))
    centre = jnp.sum(shares * products, axis=-1, keepdims=True)
    slopes = (shares * (products - centre)).astype(jnp.bfloat16)
    grad_q = (dot(slopes, keys) * scale).astype(jnp.bfloat16)
    grad_k = (dot(slopes, queries, ((0,), (0,))) * scale).astype(jnp.bfloat16)
    grad_v = dot(weights, ups, ((0,), (0,))).astype(jnp.bfloat16)
    stacked = jnp.concatenate([grad_q, grad_k, grad_v], axis=1)
    parts_ref[...] = dot(stacked, flat_qkv).astype(jnp.bfloat16)
    grads_ref[: 3 * HD] = dot(stacked, normed, ((0,), (0,))).astype(grads_ref.dtype)
    grads_ref[3 * HD :] = dot(mixed, cot, ((0,), (0,))).astype(grads_ref.dtype)


def coarse_block(tokens, cotangents, factor, head_qkv, head_out):
    count = tokens.shape[0]
    vmem = pl.BlockSpec(memory_space=pltpu.VMEM)
    return pl.pallas_call(
        coarse_body,
        out_shape=(
            jax.ShapeDtypeStruct((count, D_C), jnp.bfloat16),
            jax.ShapeDtypeStruct((4 * HD, D_C), jnp.bfloat16),
        ),
        in_specs=[vmem] * 3 + [pl.BlockSpec(memory_space=pltpu.HBM)] * 2,
        out_specs=(vmem, vmem),
        scratch_shapes=[
            pltpu.VMEM(head_qkv.shape, jnp.bfloat16),
            pltpu.VMEM(head_out.shape, jnp.bfloat16),
            pltpu.SemaphoreType.DMA((2,)),
        ],
        compiler_params=pltpu.CompilerParams(vmem_limit_bytes=vmem_bytes),
        name="coarse_block",
    )(tokens, cotangents, factor, head_qkv, head_out)


def pack_body(first, second, x_ref, dy_ref, own_ref):
    own_ref[:, :D_C] = x_ref[...].astype(jnp.float32).reshape(-1, D_C).astype(jnp.bfloat16)
    own_ref[:, D_C:] = dy_ref[...].astype(jnp.float32).reshape(-1, D_C).astype(jnp.bfloat16)


def packed(after, tokens, cotangents):
    vmem = pl.BlockSpec(memory_space=pltpu.VMEM)
    count = tokens.shape[0] * tokens.shape[1]
    return pl.pallas_call(
        pack_body,
        out_shape=jax.ShapeDtypeStruct((count, 2 * D_C), jnp.bfloat16),
        in_specs=[pl.BlockSpec(memory_space=pl.ANY)] * 2 + [vmem] * 2,
        out_specs=vmem,
        name="pack_coarse",
    )(*after, tokens, cotangents)


def pair_sum_body(own, first, second, qkv_ref, out_ref):
    for part in range(4):
        come = (first, second)[part // 2][(part % 2) * HD : (part % 2 + 1) * HD]
        total = own[part * HD : (part + 1) * HD].astype(jnp.float32) + come.astype(jnp.float32)
        if part < 3:
            qkv_ref[part] = total.astype(jnp.bfloat16)
        else:
            out_ref[...] = total.astype(jnp.bfloat16)


def pair_sum(own, first, second):
    vmem = pl.BlockSpec(memory_space=pltpu.VMEM)
    return pl.pallas_call(
        pair_sum_body,
        out_shape=(
            jax.ShapeDtypeStruct((3, HD, D_C), jnp.bfloat16),
            jax.ShapeDtypeStruct((HD, D_C), jnp.bfloat16),
        ),
        in_specs=[vmem] * 3,
        out_specs=(vmem, vmem),
        compiler_params=pltpu.CompilerParams(vmem_limit_bytes=vmem_bytes),
        name="pair_sum",
    )(own, first, second)


def last_body(
    place,
    near_ref,
    far_ref,
    x_ref,
    factor_ref,
    kept_ref,
    come_ref,
    qkv_hbm,
    out_hbm,
    dx_ref,
    sems,
):
    highs, rows = near_ref.shape[0], near_ref.shape[1]
    copies = []
    for low in range(2):
        for high in range(highs):
            source = (near_ref, far_ref)[low].at[high]
            block = place[0] ^ (2 * high + low)
            at = pl.ds(pl.multiple_of(block * rows, rows), rows)
            for part, target in enumerate((qkv_hbm, out_hbm)):
                lanes = (slice(0, 3 * D_F), slice(3 * D_F, 4 * D_F))[part]
                copies.append(
                    pltpu.make_async_copy(
                        source.at[:, lanes], target.at[at, :], sems.at[low, high, part]
                    )
                )
    for copy in copies:
        copy.start()
    tokens = x_ref[...].astype(jnp.float32).reshape(-1, D_C)
    upstream = kept_ref[...] + come_ref[...].astype(jnp.float32)
    grads = norm_backward(tokens, inverse_rms(tokens), factor_ref[...], upstream)
    dx_ref[...] = grads.astype(jnp.float32).reshape(dx_ref.shape).astype(jnp.bfloat16)
    for copy in copies:
        copy.wait()


def last_step(place, near, far, tokens, factor, kept, come):
    vmem = pl.BlockSpec(memory_space=pltpu.VMEM)
    hbm = pl.BlockSpec(memory_space=pltpu.HBM)
    return pl.pallas_call(
        last_body,
        out_shape=(
            jax.ShapeDtypeStruct((D_F, 3 * D_F), jnp.bfloat16),
            jax.ShapeDtypeStruct((D_F, D_F), jnp.bfloat16),
            jax.ShapeDtypeStruct(tokens.shape, jnp.bfloat16),
        ),
        in_specs=[pl.BlockSpec(memory_space=pltpu.SMEM)] + [vmem] * 6,
        out_specs=(hbm, hbm, vmem),
        scratch_shapes=[pltpu.SemaphoreType.DMA((2, near.shape[0], 2))],
        compiler_params=pltpu.CompilerParams(vmem_limit_bytes=vmem_bytes),
        name="last_step",
    )(place, near, far, tokens, factor, kept, come)


def neighbours(low_edge, high_edge, axis):
    peers = lax.axis_size(axis)
    odd = lax.axis_index(axis) & 1 == 1
    near = [(i, i ^ 1) for i in range(peers)]
    far = [(i, i + 1 if i % 2 else i - 1) for i in range(1, peers - 1)]
    to_near, to_far = jnp.where(odd, low_edge, high_edge), jnp.where(odd, high_edge, low_edge)
    second = lax.ppermute(to_far, axis, far)
    first = lax.ppermute(to_near, axis, near)
    return jnp.where(odd, first, second), jnp.where(odd, second, first), (to_near, to_far)


def swapped(value, axis, mask):
    return lax.ppermute(value, axis, [(i, i ^ mask) for i in range(lax.axis_size(axis))])


def tied(*arrays):
    return lax.optimization_barrier(arrays)


def batch_sum(partial):
    if lax.axis_size("batch") != 2:
        return lax.psum(partial, "batch")
    return wide(partial) + wide(swapped(partial, "batch", 1))


def wide(value):
    return value.astype(jnp.float32)


def narrow(value):
    return value.astype(jnp.bfloat16)


def all_rows(piece):
    downs = lax.axis_size("gy")
    return jnp.stack([piece] + [swapped(piece, "gy", row) for row in range(1, downs)])


def local(
    x_fine,
    dy_fine,
    x_coarse,
    dy_coarse,
    timestep,
    fine_gain,
    coarse_gain,
    fine_qkv,
    fine_out,
    coarse_qkv,
    coarse_out,
):
    step_value = timestep[0]
    picture, cotangent = x_fine[0], dy_fine[0]
    height, breadth = picture.shape[0], picture.shape[1]
    across, downs = lax.axis_size("gx"), lax.axis_size("gy")
    assert across == 4 and downs & (downs - 1) == 0
    gx, gy = lax.axis_index("gx"), lax.axis_index("gy")

    low = jnp.concatenate([picture[:HALO], cotangent[:RAD]], axis=0)
    high = jnp.concatenate([picture[height - HALO :], cotangent[height - RAD :]], axis=0)
    above, below, payloads = neighbours(low, high, "gy")
    own = packed(payloads, x_coarse[0], dy_coarse[0])
    row_first = gy * height - HALO
    col_first = gx * breadth - HALO
    limits = jnp.stack(
        [
            -row_first,
            downs * height - row_first,
            -col_first,
            across * breadth - col_first,
            gx,
            gy,
        ]
    ).astype(jnp.int32)
    factor = time_gain(fine_gain, step_value)[None]
    coarse_factor = time_gain(coarse_gain, step_value)[None]
    place = gx.astype(jnp.int32)[None]
    above, below, limits, place, factor, coarse_factor = tied(
        above, below, limits, place, factor, coarse_factor
    )
    column = jnp.concatenate([above, picture, cotangent, below], axis=0)
    first, final = column[:, :HALO], column[:, breadth - HALO :]
    left, right, _ = neighbours(first, final, "gx")
    count = own.shape[0]
    row_group = all_rows(own)
    left, right, row_group = tied(left, right, row_group)
    pair = jnp.stack([row_group, swapped(row_group, "gx", 2)])
    dx_picture, fine_keep, fine_send = fine_block(
        (across, downs),
        limits,
        picture,
        cotangent,
        above,
        below,
        left,
        right,
        factor,
        fine_qkv,
        fine_out,
    )
    fine_send, pair = tied(fine_send, pair)

    fine_half = fine_keep + wide(swapped(fine_send, "gx", 1))
    other_pair = swapped(pair, "gx", 1)
    fine_half, other_pair = tied(fine_half, other_pair)

    fine_quarter = narrow(fine_half[0] + wide(swapped(narrow(fine_half[1]), "gx", 2)))
    everyone = jnp.stack([pair, other_pair]).reshape(-1, 2 * D_C)
    parts, coarse_partial = coarse_block(
        everyone[:, :D_C], everyone[:, D_C:], coarse_factor, coarse_qkv, coarse_out
    )
    fine_quarter, parts, coarse_partial = tied(fine_quarter, parts, coarse_partial)

    rows = D_F // across
    fine_quarter = narrow(batch_sum(fine_quarter)).reshape(rows, 4 * D_F)
    parts = parts.reshape(2, 2, downs, count, D_C)
    coarse_kept = wide(parts[0]) + wide(swapped(parts[1], "gx", 1))
    fine_quarter, coarse_kept, coarse_partial = tied(fine_quarter, coarse_kept, coarse_partial)

    pair_batch = lax.axis_size("batch") == 2
    halves = (coarse_partial[: 2 * HD], coarse_partial[2 * HD :])
    others = [swapped(half, "batch", 1) if pair_batch else half for half in halves]
    mask = 1
    while mask < downs:
        last = 2 * mask == downs
        coarse_kept = coarse_kept.reshape(2, -1, 2, count, D_C)
        sent = narrow(coarse_kept[:, :, 1]).reshape(-1, D_C)
        come = swapped(jnp.concatenate([fine_quarter, sent], axis=0), "gy", mask)
        coarse_kept = coarse_kept[:, :, 0]
        coarse_kept = coarse_kept + wide(come[rows:]).reshape(coarse_kept.shape)
        fine_quarter = narrow(wide(fine_quarter) + wide(come[:rows]))
        at = int(last)
        fine_quarter, coarse_kept, others[at] = tied(fine_quarter, coarse_kept, others[at])
        mask *= 2

    coarse_kept = coarse_kept.reshape(2, count, D_C)
    come = swapped(jnp.concatenate([fine_quarter, narrow(coarse_kept[1])], axis=0), "gx", 2)
    if pair_batch:
        grad_coarse_qkv, grad_coarse_out = pair_sum(coarse_partial, *others)
    else:
        coarse_sum = narrow(batch_sum(wide(coarse_partial)))
        grad_coarse_qkv = coarse_sum[: 3 * HD].reshape(coarse_qkv.shape)
        grad_coarse_out = coarse_sum[3 * HD :]
    come, grad_coarse_qkv, grad_coarse_out = tied(come, grad_coarse_qkv, grad_coarse_out)
    fine_pair = jnp.stack([fine_quarter, come[:rows]])
    grad_qkv, grad_out, dx_coarse = last_step(
        place,
        fine_pair,
        swapped(fine_pair, "gx", 1),
        x_coarse[0],
        coarse_factor,
        coarse_kept[0],
        come[rows:],
    )
    return (
        dx_picture[None],
        dx_coarse[None],
        grad_qkv,
        grad_out,
        grad_coarse_qkv,
        grad_coarse_out,
    )


def solution(mesh):
    placed = (
        P("batch", "gy", "gx", None),
        P("batch", "gy", "gx", None),
        P("batch", "gy", "gx", None),
        P("batch", "gy", "gx", None),
        P("batch"),
        P(),
        P(),
        P(),
        P(),
        P(None, plane_spec, None),
        P(plane_spec, None),
    )
    return jax.shard_map(
        local,
        mesh=mesh,
        in_specs=placed,
        out_specs=(
            P("batch", "gy", "gx", None),
            P("batch", "gy", "gx", None),
            P(),
            P(),
            P(None, plane_spec, None),
            P(plane_spec, None),
        ),
        check_vma=False,
    )


plane_spec = ("gy", "gx")
```

```python
import math

import jax
import jax.numpy as jnp
import numpy as np
from jax import lax
from jax.experimental import pallas as pl
from jax.experimental.pallas import tpu as pltpu
from jax.sharding import PartitionSpec as P

D_F = 256
H_F = 4
D_C = 1024
HD = 64
RAD = 3
HALO = 2 * RAD

eps = 1e-06
log_span = math.log(1000.0)
side = 8
extent = side + 2 * RAD
lanes_wide = 16
scale = 1.0 / math.sqrt(HD)
vmem_bytes = 48 * 1024 * 1024


def dot(first, second, dims=((1,), (0,))):
    return lax.dot_general(first, second, (dims, ((), ())), preferred_element_type=jnp.float32)


def frequencies(channels):
    steps = np.float32(-log_span) * np.arange(channels, dtype=np.float32) / np.float32(channels)
    return np.exp(steps)[None]


def odd_rank(axis):
    return lax.axis_index(axis) & 1 == 1


def inverse_rms(floats):
    return lax.rsqrt(jnp.mean(floats * floats, axis=-1, keepdims=True) + eps)


def norm_backward(floats, inverse, factor, upstream):
    scaled = upstream * factor
    middle = jnp.mean(floats * scaled, axis=-1, keepdims=True)
    return (inverse * scaled - floats * inverse * inverse * inverse * middle).astype(jnp.bfloat16)


def round_up(value, multiple):
    return -(-value // multiple) * multiple


def in_order(axis, near, far):
    odd = odd_rank(axis)
    first, second = near[...].astype(jnp.float32), far[...].astype(jnp.float32)
    return jnp.where(odd, first, second), jnp.where(odd, second, first)


def fine_body(
    x_ref,
    dy_ref,
    row_near_ref,
    row_far_ref,
    col_near_ref,
    col_far_ref,
    factor_ref,
    qkv_ref,
    out_ref,
    dx_ref,
    keep_ref,
    send_ref,
    x_grid,
    dy_grid,
    k_grid,
    v_grid,
    q_grid,
    u_grid,
    dk_grid,
    dv_grid,
    dq_grid,
    a_grid,
    bias_ref,
    total_ref,
):
    height, breadth = x_ref.shape[0], x_ref.shape[1]
    grid_rows, grid_cols = x_grid.shape[0], x_grid.shape[1]
    query_rows = dy_grid.shape[0]
    floats = jnp.float32
    factor = factor_ref[...]

    x_grid[...] = jnp.zeros_like(x_grid)
    dy_grid[...] = jnp.zeros_like(dy_grid)
    dk_grid[...] = jnp.zeros_like(dk_grid)
    dv_grid[...] = jnp.zeros_like(dv_grid)
    inner = slice(HALO, HALO + breadth)
    above, below = in_order("gy", row_near_ref, row_far_ref)
    left, right = in_order("gx", col_near_ref, col_far_ref)
    x_grid[0:HALO, inner] = above[0:HALO]
    x_grid[HALO : HALO + height, inner] = x_ref[...].astype(floats)
    x_grid[HALO + height : HALO + height + HALO, inner] = below[0:HALO]
    dy_grid[0:RAD, inner] = above[HALO : HALO + RAD]
    dy_grid[RAD : RAD + height, inner] = dy_ref[...].astype(floats)
    dy_grid[RAD + height : RAD + height + RAD, inner] = below[HALO : HALO + RAD]
    left, right = left[:, left.shape[1] - HALO :], right[:, :HALO]
    for strip, first in ((left, 0), (right, HALO + breadth)):
        span = slice(first, first + HALO)
        at = 0
        for grid, begin, count in (
            (x_grid, 0, HALO),
            (dy_grid, 0, RAD),
            (x_grid, HALO, height),
            (dy_grid, RAD, height),
            (x_grid, HALO + height, HALO),
            (dy_grid, RAD + height, RAD),
        ):
            grid[begin : begin + count, span] = strip[at : at + count]
            at += count

    tokens = x_grid[...].reshape(grid_rows * grid_cols, D_F)
    normed = (tokens * inverse_rms(tokens) * factor).astype(jnp.bfloat16)
    key_values = dot(normed, qkv_ref[:, D_F:]).astype(jnp.bfloat16).astype(floats)
    k_grid[...] = key_values[:, :D_F].reshape(grid_rows, grid_cols, D_F)
    v_grid[...] = key_values[:, D_F:].reshape(grid_rows, grid_cols, D_F)
    query_tokens = normed[RAD * grid_cols : (RAD + query_rows) * grid_cols]
    queries = dot(query_tokens, qkv_ref[:, :D_F]).astype(jnp.bfloat16).astype(floats) * scale
    q_grid[...] = queries.reshape(query_rows, grid_cols, D_F)
    cotangents = dy_grid[...].reshape(query_rows * grid_cols, D_F).astype(jnp.bfloat16)
    ups = dot(cotangents, out_ref[...], ((1,), (1,))).astype(jnp.bfloat16).astype(floats)
    u_grid[...] = ups.reshape(query_rows, grid_cols, D_F)

    keys_count, heads_count = extent * lanes_wide, H_F * side * side
    key_at = lax.broadcasted_iota(jnp.int32, (keys_count, heads_count), 0)
    query_at = lax.broadcasted_iota(jnp.int32, (keys_count, heads_count), 1)
    row_gap = (key_at // lanes_wide) - ((query_at // side) % side)
    col_gap = (key_at % lanes_wide) - (query_at % side)
    near = (row_gap >= 0) & (row_gap <= 2 * RAD) & (col_gap >= 0) & (col_gap <= 2 * RAD)
    bias_ref[...] = jnp.where(near, 0.0, -1e30)
    gx, gy = lax.axis_index("gx"), lax.axis_index("gy")
    row_low, col_low = HALO - gy * height, HALO - gx * breadth
    row_high = row_low + lax.axis_size("gy") * height
    col_high = col_low + lax.axis_size("gx") * breadth
    lone = lax.broadcasted_iota(jnp.int32, (keys_count, 1), 0)
    head_of = lax.broadcasted_iota(jnp.int32, (side * side, D_F), 1) // HD

    def spread(block):
        return jnp.concatenate(
            [jnp.where(head_of == h, block, 0.0).astype(jnp.bfloat16) for h in range(H_F)], axis=0
        )

    def collect(full):
        total = jnp.where(head_of == 0, full[: side * side], 0.0)
        for h in range(1, H_F):
            piece = full[h * side * side : (h + 1) * side * side]
            total = jnp.where(head_of == h, piece, total)
        return total.reshape(side, side, D_F)

    for block_row in range(query_rows // side):
        top = block_row * side
        for block_col in range((grid_cols - side) // side):
            start = block_col * side
            window = (slice(top, top + extent), slice(start, start + lanes_wide))
            keys = k_grid[window].reshape(keys_count, D_F).astype(jnp.bfloat16)
            values = v_grid[window].reshape(keys_count, D_F).astype(jnp.bfloat16)
            place = (slice(top, top + side), slice(start + RAD, start + RAD + side))
            wide_queries = spread(q_grid[place].reshape(side * side, D_F))
            wide_ups = spread(u_grid[place].reshape(side * side, D_F))
            key_row = lone // lanes_wide + top
            key_col = lone % lanes_wide + start
            inside = (
                (key_row >= row_low)
                & (key_row < row_high)
                & (key_col >= col_low)
                & (key_col < col_high)
            )
            scores = dot(keys, wide_queries, ((1,), (1,)))
            scores = scores + (bias_ref[...] + jnp.where(inside, 0.0, -1e30))
            raised = jnp.exp(scores - jnp.max(scores, axis=0, keepdims=True))
            shares = raised * (1.0 / jnp.sum(raised, axis=0, keepdims=True))
            products = dot(values, wide_ups, ((1,), (1,)))
            centre = jnp.sum(shares * products, axis=0, keepdims=True)
            slopes = (shares * (products - centre)).astype(jnp.bfloat16)
            weights = shares.astype(jnp.bfloat16)
            dv_grid[window] += dot(weights, wide_ups).reshape(extent, lanes_wide, D_F)
            dk_grid[window] += dot(slopes, wide_queries).reshape(extent, lanes_wide, D_F)
            block = (slice(top, top + side), slice(start, start + side))
            a_grid[block] = collect(dot(weights, values, ((0,), (0,))))
            dq_grid[block] = collect(dot(slopes, keys, ((0,), (0,))))

    count = height * breadth
    own_queries = (slice(RAD, RAD + height), slice(RAD, RAD + breadth))
    own_keys = (slice(HALO, HALO + height), inner)
    attended = a_grid[own_queries].reshape(count, D_F).astype(jnp.bfloat16)
    grad_q = (dq_grid[own_queries].reshape(count, D_F) * scale).astype(jnp.bfloat16)
    grad_k = dk_grid[own_keys].reshape(count, D_F).astype(jnp.bfloat16)
    grad_v = dv_grid[own_keys].reshape(count, D_F).astype(jnp.bfloat16)
    grad_proj = jnp.concatenate([grad_q, grad_k, grad_v], axis=1)
    picture = x_ref[...].reshape(count, D_F).astype(floats)
    inverse = inverse_rms(picture)
    own_normed = (picture * inverse * factor).astype(jnp.bfloat16)
    flat_cot = dy_ref[...].reshape(count, D_F)
    grads = jnp.concatenate(
        [
            dot(own_normed, grad_proj, ((0,), (0,))),
            dot(attended, flat_cot, ((0,), (0,))),
        ],
        axis=1,
    )
    half, columns = keep_ref.shape[0], keep_ref.shape[1]
    total_ref[...] = grads.reshape(total_ref.shape)
    for low in range(2):
        target = (keep_ref, send_ref)[low]
        for high in range(half):
            for row in range(columns):
                block = (gx ^ (2 * high + low)) * columns + row
                target[high, row] = total_ref[block].astype(target.dtype)
    down = dot(grad_proj, qkv_ref[...], ((1,), (1,)))
    dx_ref[...] = norm_backward(picture, inverse, factor, down).reshape(height, breadth, D_F)


def fine_block(peers, picture, *operands):
    height, breadth = picture.shape[0], picture.shape[1]
    query_rows = round_up(height + 2 * RAD, side)
    query_cols = round_up(breadth + 2 * RAD, side)
    grid_rows, grid_cols = query_rows + 2 * RAD, query_cols + side
    across, down = peers
    rows = D_F // (across * down)
    halves = (across // 2, down, rows, 4 * D_F)
    vmem = pl.BlockSpec(memory_space=pltpu.VMEM)
    wide = pltpu.VMEM((grid_rows, grid_cols, D_F), jnp.float32)
    middle = pltpu.VMEM((query_rows, grid_cols, D_F), jnp.float32)
    small = pltpu.VMEM((query_rows, query_cols, D_F), jnp.float32)
    return pl.pallas_call(
        fine_body,
        out_shape=(
            jax.ShapeDtypeStruct((height, breadth, D_F), jnp.bfloat16),
            jax.ShapeDtypeStruct(halves, jnp.float32),
            jax.ShapeDtypeStruct(halves, jnp.bfloat16),
        ),
        in_specs=[vmem] * 9,
        out_specs=(vmem, vmem, vmem),
        scratch_shapes=[
            wide,
            middle,
            wide,
            wide,
            middle,
            middle,
            wide,
            wide,
            small,
            small,
            pltpu.VMEM((extent * lanes_wide, H_F * side * side), jnp.float32),
            pltpu.VMEM((across * down, rows, 4 * D_F), jnp.float32),
        ],
        compiler_params=pltpu.CompilerParams(vmem_limit_bytes=vmem_bytes),
        name="fine_block",
    )(picture, *operands)


def coarse_body(
    x_ref,
    dy_ref,
    factor_ref,
    qkv_hbm,
    out_hbm,
    parts_ref,
    grads_ref,
    qkv_ref,
    out_ref,
    arrived,
):
    fetches = [
        pltpu.make_async_copy(qkv_hbm, qkv_ref, arrived.at[0]),
        pltpu.make_async_copy(out_hbm, out_ref, arrived.at[1]),
    ]
    for fetch in fetches:
        fetch.start()
    tokens = x_ref[...].astype(jnp.float32)
    normed = (tokens * inverse_rms(tokens) * factor_ref[...]).astype(jnp.bfloat16)
    cot = dy_ref[...]
    for fetch in fetches:
        fetch.wait()
    flat_qkv = qkv_ref[...].reshape(3 * HD, D_C)
    out_rows = out_ref[...]
    projected = dot(normed, flat_qkv, ((1,), (1,))).astype(jnp.bfloat16)
    queries, keys, values = projected[:, :HD], projected[:, HD : 2 * HD], projected[:, 2 * HD :]
    ups = dot(cot, out_rows, ((1,), (1,))).astype(jnp.bfloat16)
    scores = dot(queries, keys, ((1,), (1,))) * scale
    raised = jnp.exp(scores - jnp.max(scores, axis=-1, keepdims=True))
    shares = raised * (1.0 / jnp.sum(raised, axis=-1, keepdims=True))
    weights = shares.astype(jnp.bfloat16)
    mixed = dot(weights, values).astype(jnp.bfloat16)
    products = dot(ups, values, ((1,), (1,)))
    centre = jnp.sum(shares * products, axis=-1, keepdims=True)
    slopes = (shares * (products - centre)).astype(jnp.bfloat16)
    grad_q = (dot(slopes, keys) * scale).astype(jnp.bfloat16)
    grad_k = (dot(slopes, queries, ((0,), (0,))) * scale).astype(jnp.bfloat16)
    grad_v = dot(weights, ups, ((0,), (0,))).astype(jnp.bfloat16)
    stacked = jnp.concatenate([grad_q, grad_k, grad_v], axis=1)
    parts_ref[...] = dot(stacked, flat_qkv).astype(jnp.bfloat16)
    grads_ref[: 3 * HD] = dot(stacked, normed, ((0,), (0,))).astype(grads_ref.dtype)
    grads_ref[3 * HD :] = dot(mixed, cot, ((0,), (0,))).astype(grads_ref.dtype)


def coarse_block(tokens, cotangents, factor, head_qkv, head_out):
    count = tokens.shape[0]
    vmem = pl.BlockSpec(memory_space=pltpu.VMEM)
    return pl.pallas_call(
        coarse_body,
        out_shape=(
            jax.ShapeDtypeStruct((count, D_C), jnp.bfloat16),
            jax.ShapeDtypeStruct((4 * HD, D_C), jnp.bfloat16),
        ),
        in_specs=[vmem] * 3 + [pl.BlockSpec(memory_space=pltpu.HBM)] * 2,
        out_specs=(vmem, vmem),
        scratch_shapes=[
            pltpu.VMEM(head_qkv.shape, jnp.bfloat16),
            pltpu.VMEM(head_out.shape, jnp.bfloat16),
            pltpu.SemaphoreType.DMA((2,)),
        ],
        compiler_params=pltpu.CompilerParams(vmem_limit_bytes=vmem_bytes),
        name="coarse_block",
    )(tokens, cotangents, factor, head_qkv, head_out)


def row_edges_body(x_ref, dy_ref, near_ref, far_ref):
    height = x_ref.shape[0]
    odd = odd_rank("gy")

    def fill(low_ref, high_ref):
        low_ref[:HALO], low_ref[HALO:] = x_ref[:HALO], dy_ref[:RAD]
        high_ref[:HALO], high_ref[HALO:] = x_ref[height - HALO :], dy_ref[height - RAD :]

    @pl.when(odd)
    def _():
        fill(near_ref, far_ref)

    @pl.when(jnp.logical_not(odd))
    def _():
        fill(far_ref, near_ref)


def row_edges(picture, cotangent):
    vmem = pl.BlockSpec(memory_space=pltpu.VMEM)
    shape = jax.ShapeDtypeStruct((HALO + RAD,) + picture.shape[1:], jnp.bfloat16)
    return pl.pallas_call(
        row_edges_body,
        out_shape=(shape, shape),
        in_specs=[vmem, vmem],
        out_specs=(vmem, vmem),
        compiler_params=pltpu.CompilerParams(vmem_limit_bytes=vmem_bytes),
        name="row_edges",
    )(picture, cotangent)


def col_edges_body(x_ref, dy_ref, row_near_ref, row_far_ref, near_ref, far_ref):
    above, below = in_order("gy", row_near_ref, row_far_ref)
    breadth = x_ref.shape[1]
    odd = odd_rank("gx")
    at = 0
    for rows in (above, x_ref[...].astype(jnp.float32), dy_ref[...].astype(jnp.float32), below):
        first, final = rows[:, :side], rows[:, breadth - side :]
        span = slice(at, at + rows.shape[0])
        near_ref[span] = jnp.where(odd, first, final).astype(jnp.bfloat16)
        far_ref[span] = jnp.where(odd, final, first).astype(jnp.bfloat16)
        at += rows.shape[0]


def col_edges(picture, cotangent, row_near, row_far):
    vmem = pl.BlockSpec(memory_space=pltpu.VMEM)
    rows = 2 * (picture.shape[0] + row_near.shape[0])
    shape = jax.ShapeDtypeStruct((rows, side, D_F), jnp.bfloat16)
    return pl.pallas_call(
        col_edges_body,
        out_shape=(shape, shape),
        in_specs=[vmem] * 4,
        out_specs=(vmem, vmem),
        compiler_params=pltpu.CompilerParams(vmem_limit_bytes=vmem_bytes),
        name="col_edges",
    )(picture, cotangent, row_near, row_far)


def pack_body(
    first,
    second,
    step,
    x_ref,
    dy_ref,
    fine_gain,
    coarse_gain,
    fine_freq,
    coarse_freq,
    own_ref,
    fine_ref,
    coarse_ref,
):
    own_ref[:, :D_C] = x_ref[...].astype(jnp.float32).reshape(-1, D_C).astype(jnp.bfloat16)
    own_ref[:, D_C:] = dy_ref[...].astype(jnp.float32).reshape(-1, D_C).astype(jnp.bfloat16)
    time = step[0].astype(jnp.float32)
    fine_ref[...] = fine_gain[...] * (1.0 + 0.5 * jnp.cos(time * fine_freq[...]))
    coarse_ref[...] = coarse_gain[...] * (1.0 + 0.5 * jnp.cos(time * coarse_freq[...]))


def packed(after, step, tokens, cotangents, fine_gain, coarse_gain):
    vmem = pl.BlockSpec(memory_space=pltpu.VMEM)
    count = tokens.shape[0] * tokens.shape[1]
    return pl.pallas_call(
        pack_body,
        out_shape=(
            jax.ShapeDtypeStruct((count, 2 * D_C), jnp.bfloat16),
            jax.ShapeDtypeStruct((1, D_F), jnp.float32),
            jax.ShapeDtypeStruct((1, D_C), jnp.float32),
        ),
        in_specs=[pl.BlockSpec(memory_space=pl.ANY)] * 2
        + [pl.BlockSpec(memory_space=pltpu.SMEM)]
        + [vmem] * 6,
        out_specs=(vmem, vmem, vmem),
        compiler_params=pltpu.CompilerParams(vmem_limit_bytes=vmem_bytes),
        name="pack_coarse",
    )(
        *after,
        step,
        tokens,
        cotangents,
        fine_gain[None],
        coarse_gain[None],
        frequencies(D_F),
        frequencies(D_C),
    )


def pair_sum_body(own, first, second, qkv_ref, out_ref):
    for part in range(4):
        come = (first, second)[part // 2][(part % 2) * HD : (part % 2 + 1) * HD]
        total = own[part * HD : (part + 1) * HD].astype(jnp.float32) + come.astype(jnp.float32)
        if part < 3:
            qkv_ref[part] = total.astype(jnp.bfloat16)
        else:
            out_ref[...] = total.astype(jnp.bfloat16)


def pair_sum(own, first, second):
    vmem = pl.BlockSpec(memory_space=pltpu.VMEM)
    return pl.pallas_call(
        pair_sum_body,
        out_shape=(
            jax.ShapeDtypeStruct((3, HD, D_C), jnp.bfloat16),
            jax.ShapeDtypeStruct((HD, D_C), jnp.bfloat16),
        ),
        in_specs=[vmem] * 3,
        out_specs=(vmem, vmem),
        compiler_params=pltpu.CompilerParams(vmem_limit_bytes=vmem_bytes),
        name="pair_sum",
    )(own, first, second)


def last_body(
    near_ref,
    far_ref,
    x_ref,
    factor_ref,
    upstream_ref,
    qkv_hbm,
    out_hbm,
    dx_ref,
    sems,
):
    highs, rows = near_ref.shape[0], near_ref.shape[1]
    copies = []
    for low in range(2):
        for high in range(highs):
            source = (near_ref, far_ref)[low].at[high]
            block = lax.axis_index("gx") ^ (2 * high + low)
            at = pl.ds(pl.multiple_of(block * rows, rows), rows)
            for part, target in enumerate((qkv_hbm, out_hbm)):
                lanes = (slice(0, 3 * D_F), slice(3 * D_F, 4 * D_F))[part]
                copies.append(
                    pltpu.make_async_copy(
                        source.at[:, lanes], target.at[at, :], sems.at[low, high, part]
                    )
                )
    for copy in copies:
        copy.start()
    tokens = x_ref[...].astype(jnp.float32).reshape(-1, D_C)
    grads = norm_backward(tokens, inverse_rms(tokens), factor_ref[...], upstream_ref[...])
    dx_ref[...] = grads.astype(jnp.float32).reshape(dx_ref.shape).astype(jnp.bfloat16)
    for copy in copies:
        copy.wait()


def last_step(near, far, tokens, factor, upstream):
    vmem = pl.BlockSpec(memory_space=pltpu.VMEM)
    hbm = pl.BlockSpec(memory_space=pltpu.HBM)
    return pl.pallas_call(
        last_body,
        out_shape=(
            jax.ShapeDtypeStruct((D_F, 3 * D_F), jnp.bfloat16),
            jax.ShapeDtypeStruct((D_F, D_F), jnp.bfloat16),
            jax.ShapeDtypeStruct(tokens.shape, jnp.bfloat16),
        ),
        in_specs=[vmem] * 5,
        out_specs=(hbm, hbm, vmem),
        scratch_shapes=[pltpu.SemaphoreType.DMA((2, near.shape[0], 2))],
        compiler_params=pltpu.CompilerParams(vmem_limit_bytes=vmem_bytes),
        name="last_step",
    )(near, far, tokens, factor, upstream)


def neighbours(to_near, to_far, axis):
    peers = lax.axis_size(axis)
    near = [(i, i ^ 1) for i in range(peers)]
    far = [(i, i + 1 if i % 2 else i - 1) for i in range(1, peers - 1)]
    from_far = lax.ppermute(to_far, axis, far)
    return lax.ppermute(to_near, axis, near), from_far


def swapped(value, axis, mask):
    return lax.ppermute(value, axis, [(i, i ^ mask) for i in range(lax.axis_size(axis))])


def tied(*arrays):
    return lax.optimization_barrier(arrays)


def batch_sum(partial):
    if lax.axis_size("batch") != 2:
        return lax.psum(partial, "batch")
    return wide(partial) + wide(swapped(partial, "batch", 1))


def wide(value):
    return value.astype(jnp.float32)


def narrow(value):
    return value.astype(jnp.bfloat16)


def all_rows(piece):
    downs = lax.axis_size("gy")
    return jnp.stack([piece] + [swapped(piece, "gy", row) for row in range(1, downs)])


def local(
    x_fine,
    dy_fine,
    x_coarse,
    dy_coarse,
    timestep,
    fine_gain,
    coarse_gain,
    fine_qkv,
    fine_out,
    coarse_qkv,
    coarse_out,
):
    picture, cotangent = x_fine[0], dy_fine[0]
    across, downs = lax.axis_size("gx"), lax.axis_size("gy")
    assert across == 4 and downs & (downs - 1) == 0

    payloads = row_edges(picture, cotangent)
    row_near, row_far = neighbours(*payloads, "gy")
    own, factor, coarse_factor = packed(
        payloads, timestep, x_coarse[0], dy_coarse[0], fine_gain, coarse_gain
    )
    count = own.shape[0]
    row_group = all_rows(own)
    edges = col_edges(picture, cotangent, row_near, row_far)
    col_near, col_far = neighbours(*edges, "gx")
    col_near, col_far, row_group = tied(col_near, col_far, row_group)
    cross = swapped(row_group, "gx", 2)
    beside = swapped(row_group, "gx", 1)
    dx_picture, fine_keep, fine_send = fine_block(
        (across, downs),
        picture,
        cotangent,
        row_near,
        row_far,
        col_near,
        col_far,
        factor,
        fine_qkv,
        fine_out,
    )
    fine_half = fine_keep + wide(swapped(fine_send, "gx", 1))
    opposite = swapped(cross, "gx", 1)
    fine_half, opposite = tied(fine_half, opposite)

    fine_quarter = narrow(fine_half[0] + wide(swapped(narrow(fine_half[1]), "gx", 2)))
    everyone = jnp.stack([row_group, cross, beside, opposite]).reshape(-1, 2 * D_C)
    parts, coarse_partial = coarse_block(
        everyone[:, :D_C], everyone[:, D_C:], coarse_factor, coarse_qkv, coarse_out
    )
    fine_quarter, parts, coarse_partial = tied(fine_quarter, parts, coarse_partial)

    rows = D_F // across
    fine_quarter = narrow(batch_sum(fine_quarter)).reshape(rows, 4 * D_F)
    parts = parts.reshape(2, 2, downs, count, D_C)
    coarse_kept = wide(parts[0]) + wide(swapped(parts[1], "gx", 1))
    coarse_kept = coarse_kept[0] + wide(swapped(narrow(coarse_kept[1]), "gx", 2))
    fine_quarter, coarse_kept, coarse_partial = tied(fine_quarter, coarse_kept, coarse_partial)

    pair_batch = lax.axis_size("batch") == 2
    halves = (coarse_partial[: 2 * HD], coarse_partial[2 * HD :])
    others = [swapped(half, "batch", 1) if pair_batch else half for half in halves]
    mask = 1
    while mask < downs:
        last = 2 * mask == downs
        coarse_kept = coarse_kept.reshape(-1, 2, count, D_C)
        sent = narrow(coarse_kept[:, 1]).reshape(-1, D_C)
        come = swapped(jnp.concatenate([fine_quarter, sent], axis=0), "gy", mask)
        coarse_kept = coarse_kept[:, 0]
        coarse_kept = coarse_kept + wide(come[rows:]).reshape(coarse_kept.shape)
        fine_quarter = narrow(wide(fine_quarter) + wide(come[:rows]))
        at = int(last)
        fine_quarter, coarse_kept, others[at] = tied(fine_quarter, coarse_kept, others[at])
        mask *= 2

    come = swapped(fine_quarter, "gx", 2)
    if pair_batch:
        grad_coarse_qkv, grad_coarse_out = pair_sum(coarse_partial, *others)
    else:
        coarse_sum = narrow(batch_sum(wide(coarse_partial)))
        grad_coarse_qkv = coarse_sum[: 3 * HD].reshape(coarse_qkv.shape)
        grad_coarse_out = coarse_sum[3 * HD :]
    come, grad_coarse_qkv, grad_coarse_out = tied(come, grad_coarse_qkv, grad_coarse_out)
    fine_pair = jnp.stack([fine_quarter, come])
    grad_qkv, grad_out, dx_coarse = last_step(
        fine_pair,
        swapped(fine_pair, "gx", 1),
        x_coarse[0],
        coarse_factor,
        coarse_kept.reshape(count, D_C),
    )
    return (
        dx_picture[None],
        dx_coarse[None],
        grad_qkv,
        grad_out,
        grad_coarse_qkv,
        grad_coarse_out,
    )


def solution(mesh):
    placed = (
        P("batch", "gy", "gx", None),
        P("batch", "gy", "gx", None),
        P("batch", "gy", "gx", None),
        P("batch", "gy", "gx", None),
        P("batch"),
        P(),
        P(),
        P(),
        P(),
        P(None, plane_spec, None),
        P(plane_spec, None),
    )
    return jax.shard_map(
        local,
        mesh=mesh,
        in_specs=placed,
        out_specs=(
            P("batch", "gy", "gx", None),
            P("batch", "gy", "gx", None),
            P(),
            P(),
            P(None, plane_spec, None),
            P(plane_spec, None),
        ),
        check_vma=False,
    )


plane_spec = ("gy", "gx")
```

```python
import math

import jax
import jax.numpy as jnp
import numpy as np
from jax import lax
from jax.experimental import pallas as pl
from jax.experimental.pallas import tpu as pltpu
from jax.sharding import PartitionSpec as P

D_F = 256
H_F = 4
D_C = 1024
HD = 64
RAD = 3
HALO = 2 * RAD

eps = 1e-06
log_span = math.log(1000.0)
side = 8
extent = side + 2 * RAD
lanes_wide = 16
scale = 1.0 / math.sqrt(HD)
vmem_bytes = 48 * 1024 * 1024


def dot(first, second, dims=((1,), (0,))):
    return lax.dot_general(first, second, (dims, ((), ())), preferred_element_type=jnp.float32)


def frequencies(channels):
    steps = np.float32(-log_span) * np.arange(channels, dtype=np.float32) / np.float32(channels)
    return np.exp(steps)[None]


def odd_rank(axis):
    return lax.axis_index(axis) & 1 == 1


def inverse_rms(floats):
    return lax.rsqrt(jnp.mean(floats * floats, axis=-1, keepdims=True) + eps)


def norm_backward(floats, inverse, factor, upstream):
    scaled = upstream * factor
    middle = jnp.mean(floats * scaled, axis=-1, keepdims=True)
    return (inverse * scaled - floats * inverse * inverse * inverse * middle).astype(jnp.bfloat16)


def round_up(value, multiple):
    return -(-value // multiple) * multiple


def in_order(axis, near, far):
    odd = odd_rank(axis)
    first, second = near[...].astype(jnp.float32), far[...].astype(jnp.float32)
    return jnp.where(odd, first, second), jnp.where(odd, second, first)


def fine_body(
    x_ref,
    dy_ref,
    row_near_ref,
    row_far_ref,
    col_near_ref,
    col_far_ref,
    factor_ref,
    qkv_ref,
    out_ref,
    dx_ref,
    keep_ref,
    send_ref,
    x_grid,
    dy_grid,
    k_grid,
    v_grid,
    q_grid,
    u_grid,
    dk_grid,
    dv_grid,
    dq_grid,
    a_grid,
    bias_ref,
    total_ref,
):
    height, breadth = x_ref.shape[0], x_ref.shape[1]
    grid_rows, grid_cols = x_grid.shape[0], x_grid.shape[1]
    query_rows = dy_grid.shape[0]
    floats = jnp.float32
    factor = factor_ref[...]

    x_grid[...] = jnp.zeros_like(x_grid)
    dy_grid[...] = jnp.zeros_like(dy_grid)
    dk_grid[...] = jnp.zeros_like(dk_grid)
    dv_grid[...] = jnp.zeros_like(dv_grid)
    inner = slice(HALO, HALO + breadth)
    above, below = in_order("gy", row_near_ref, row_far_ref)
    left, right = in_order("gx", col_near_ref, col_far_ref)
    x_grid[0:HALO, inner] = above[0:HALO]
    x_grid[HALO : HALO + height, inner] = x_ref[...].astype(floats)
    x_grid[HALO + height : HALO + height + HALO, inner] = below[0:HALO]
    dy_grid[0:RAD, inner] = above[HALO : HALO + RAD]
    dy_grid[RAD : RAD + height, inner] = dy_ref[...].astype(floats)
    dy_grid[RAD + height : RAD + height + RAD, inner] = below[HALO : HALO + RAD]
    left, right = left[:, left.shape[1] - HALO :], right[:, :HALO]
    for strip, first in ((left, 0), (right, HALO + breadth)):
        span = slice(first, first + HALO)
        at = 0
        for grid, begin, count in (
            (x_grid, 0, HALO),
            (dy_grid, 0, RAD),
            (x_grid, HALO, height),
            (dy_grid, RAD, height),
            (x_grid, HALO + height, HALO),
            (dy_grid, RAD + height, RAD),
        ):
            grid[begin : begin + count, span] = strip[at : at + count]
            at += count

    tokens = x_grid[...].reshape(grid_rows * grid_cols, D_F)
    normed = (tokens * inverse_rms(tokens) * factor).astype(jnp.bfloat16)
    key_values = dot(normed, qkv_ref[:, D_F:]).astype(jnp.bfloat16).astype(floats)
    k_grid[...] = key_values[:, :D_F].reshape(grid_rows, grid_cols, D_F)
    v_grid[...] = key_values[:, D_F:].reshape(grid_rows, grid_cols, D_F)
    query_tokens = normed[RAD * grid_cols : (RAD + query_rows) * grid_cols]
    queries = dot(query_tokens, qkv_ref[:, :D_F]).astype(jnp.bfloat16).astype(floats) * scale
    q_grid[...] = queries.reshape(query_rows, grid_cols, D_F)
    cotangents = dy_grid[...].reshape(query_rows * grid_cols, D_F).astype(jnp.bfloat16)
    ups = dot(cotangents, out_ref[...], ((1,), (1,))).astype(jnp.bfloat16).astype(floats)
    u_grid[...] = ups.reshape(query_rows, grid_cols, D_F)

    keys_count, heads_count = extent * lanes_wide, H_F * side * side
    key_at = lax.broadcasted_iota(jnp.int32, (keys_count, heads_count), 0)
    query_at = lax.broadcasted_iota(jnp.int32, (keys_count, heads_count), 1)
    row_gap = (key_at // lanes_wide) - ((query_at // side) % side)
    col_gap = (key_at % lanes_wide) - (query_at % side)
    near = (row_gap >= 0) & (row_gap <= 2 * RAD) & (col_gap >= 0) & (col_gap <= 2 * RAD)
    bias_ref[...] = jnp.where(near, 0.0, -1e30)
    gx, gy = lax.axis_index("gx"), lax.axis_index("gy")
    row_low, col_low = HALO - gy * height, HALO - gx * breadth
    row_high = row_low + lax.axis_size("gy") * height
    col_high = col_low + lax.axis_size("gx") * breadth
    lone = lax.broadcasted_iota(jnp.int32, (keys_count, 1), 0)
    head_of = lax.broadcasted_iota(jnp.int32, (side * side, D_F), 1) // HD

    def spread(block):
        return jnp.concatenate(
            [jnp.where(head_of == h, block, 0.0).astype(jnp.bfloat16) for h in range(H_F)], axis=0
        )

    def collect(full):
        total = jnp.where(head_of == 0, full[: side * side], 0.0)
        for h in range(1, H_F):
            piece = full[h * side * side : (h + 1) * side * side]
            total = jnp.where(head_of == h, piece, total)
        return total.reshape(side, side, D_F)

    for block_row in range(query_rows // side):
        top = block_row * side
        for block_col in range((grid_cols - side) // side):
            start = block_col * side
            window = (slice(top, top + extent), slice(start, start + lanes_wide))
            keys = k_grid[window].reshape(keys_count, D_F).astype(jnp.bfloat16)
            values = v_grid[window].reshape(keys_count, D_F).astype(jnp.bfloat16)
            place = (slice(top, top + side), slice(start + RAD, start + RAD + side))
            wide_queries = spread(q_grid[place].reshape(side * side, D_F))
            wide_ups = spread(u_grid[place].reshape(side * side, D_F))
            key_row = lone // lanes_wide + top
            key_col = lone % lanes_wide + start
            inside = (
                (key_row >= row_low)
                & (key_row < row_high)
                & (key_col >= col_low)
                & (key_col < col_high)
            )
            scores = dot(keys, wide_queries, ((1,), (1,)))
            scores = scores + (bias_ref[...] + jnp.where(inside, 0.0, -1e30))
            raised = jnp.exp(scores - jnp.max(scores, axis=0, keepdims=True))
            shares = raised * (1.0 / jnp.sum(raised, axis=0, keepdims=True))
            products = dot(values, wide_ups, ((1,), (1,)))
            centre = jnp.sum(shares * products, axis=0, keepdims=True)
            slopes = (shares * (products - centre)).astype(jnp.bfloat16)
            weights = shares.astype(jnp.bfloat16)
            dv_grid[window] += dot(weights, wide_ups).reshape(extent, lanes_wide, D_F)
            dk_grid[window] += dot(slopes, wide_queries).reshape(extent, lanes_wide, D_F)
            block = (slice(top, top + side), slice(start, start + side))
            a_grid[block] = collect(dot(weights, values, ((0,), (0,))))
            dq_grid[block] = collect(dot(slopes, keys, ((0,), (0,))))

    count = height * breadth
    own_queries = (slice(RAD, RAD + height), slice(RAD, RAD + breadth))
    own_keys = (slice(HALO, HALO + height), inner)
    attended = a_grid[own_queries].reshape(count, D_F).astype(jnp.bfloat16)
    grad_q = (dq_grid[own_queries].reshape(count, D_F) * scale).astype(jnp.bfloat16)
    grad_k = dk_grid[own_keys].reshape(count, D_F).astype(jnp.bfloat16)
    grad_v = dv_grid[own_keys].reshape(count, D_F).astype(jnp.bfloat16)
    grad_proj = jnp.concatenate([grad_q, grad_k, grad_v], axis=1)
    picture = x_ref[...].reshape(count, D_F).astype(floats)
    inverse = inverse_rms(picture)
    own_normed = (picture * inverse * factor).astype(jnp.bfloat16)
    flat_cot = dy_ref[...].reshape(count, D_F)
    grads = jnp.concatenate(
        [
            dot(own_normed, grad_proj, ((0,), (0,))),
            dot(attended, flat_cot, ((0,), (0,))),
        ],
        axis=1,
    )
    half, columns = keep_ref.shape[0], keep_ref.shape[1]
    total_ref[...] = grads.reshape(total_ref.shape)
    for low in range(2):
        target = (keep_ref, send_ref)[low]
        for high in range(half):
            for row in range(columns):
                block = (gx ^ (2 * high + low)) * columns + row
                target[high, row] = total_ref[block].astype(target.dtype)
    down = dot(grad_proj, qkv_ref[...], ((1,), (1,)))
    dx_ref[...] = norm_backward(picture, inverse, factor, down).reshape(height, breadth, D_F)


def fine_block(peers, picture, *operands):
    height, breadth = picture.shape[0], picture.shape[1]
    query_rows = round_up(height + 2 * RAD, side)
    query_cols = round_up(breadth + 2 * RAD, side)
    grid_rows, grid_cols = query_rows + 2 * RAD, query_cols + side
    across, down = peers
    rows = D_F // (across * down)
    halves = (across // 2, down, rows, 4 * D_F)
    vmem = pl.BlockSpec(memory_space=pltpu.VMEM)
    wide = pltpu.VMEM((grid_rows, grid_cols, D_F), jnp.float32)
    middle = pltpu.VMEM((query_rows, grid_cols, D_F), jnp.float32)
    small = pltpu.VMEM((query_rows, query_cols, D_F), jnp.float32)
    return pl.pallas_call(
        fine_body,
        out_shape=(
            jax.ShapeDtypeStruct((height, breadth, D_F), jnp.bfloat16),
            jax.ShapeDtypeStruct(halves, jnp.float32),
            jax.ShapeDtypeStruct(halves, jnp.bfloat16),
        ),
        in_specs=[vmem] * 9,
        out_specs=(vmem, vmem, vmem),
        scratch_shapes=[
            wide,
            middle,
            wide,
            wide,
            middle,
            middle,
            wide,
            wide,
            small,
            small,
            pltpu.VMEM((extent * lanes_wide, H_F * side * side), jnp.float32),
            pltpu.VMEM((across * down, rows, 4 * D_F), jnp.float32),
        ],
        compiler_params=pltpu.CompilerParams(vmem_limit_bytes=vmem_bytes),
        name="fine_block",
    )(picture, *operands)


def coarse_body(
    x_ref,
    dy_ref,
    factor_ref,
    qkv_hbm,
    out_hbm,
    parts_ref,
    grads_ref,
    qkv_ref,
    out_ref,
    arrived,
):
    fetches = [
        pltpu.make_async_copy(qkv_hbm, qkv_ref, arrived.at[0]),
        pltpu.make_async_copy(out_hbm, out_ref, arrived.at[1]),
    ]
    for fetch in fetches:
        fetch.start()
    tokens = x_ref[...].astype(jnp.float32)
    normed = (tokens * inverse_rms(tokens) * factor_ref[...]).astype(jnp.bfloat16)
    cot = dy_ref[...]
    for fetch in fetches:
        fetch.wait()
    flat_qkv = qkv_ref[...].reshape(3 * HD, D_C)
    out_rows = out_ref[...]
    projected = dot(normed, flat_qkv, ((1,), (1,))).astype(jnp.bfloat16)
    queries, keys, values = projected[:, :HD], projected[:, HD : 2 * HD], projected[:, 2 * HD :]
    ups = dot(cot, out_rows, ((1,), (1,))).astype(jnp.bfloat16)
    scores = dot(queries, keys, ((1,), (1,))) * scale
    raised = jnp.exp(scores - jnp.max(scores, axis=-1, keepdims=True))
    shares = raised * (1.0 / jnp.sum(raised, axis=-1, keepdims=True))
    weights = shares.astype(jnp.bfloat16)
    mixed = dot(weights, values).astype(jnp.bfloat16)
    products = dot(ups, values, ((1,), (1,)))
    centre = jnp.sum(shares * products, axis=-1, keepdims=True)
    slopes = (shares * (products - centre)).astype(jnp.bfloat16)
    grad_q = (dot(slopes, keys) * scale).astype(jnp.bfloat16)
    grad_k = (dot(slopes, queries, ((0,), (0,))) * scale).astype(jnp.bfloat16)
    grad_v = dot(weights, ups, ((0,), (0,))).astype(jnp.bfloat16)
    stacked = jnp.concatenate([grad_q, grad_k, grad_v], axis=1)
    parts_ref[...] = dot(stacked, flat_qkv).astype(jnp.bfloat16)
    grads_ref[: 3 * HD] = dot(stacked, normed, ((0,), (0,))).astype(grads_ref.dtype)
    grads_ref[3 * HD :] = dot(mixed, cot, ((0,), (0,))).astype(grads_ref.dtype)


def coarse_block(tokens, cotangents, factor, head_qkv, head_out):
    count = tokens.shape[0]
    vmem = pl.BlockSpec(memory_space=pltpu.VMEM)
    return pl.pallas_call(
        coarse_body,
        out_shape=(
            jax.ShapeDtypeStruct((count, D_C), jnp.bfloat16),
            jax.ShapeDtypeStruct((4 * HD, D_C), jnp.bfloat16),
        ),
        in_specs=[vmem] * 3 + [pl.BlockSpec(memory_space=pltpu.HBM)] * 2,
        out_specs=(vmem, vmem),
        scratch_shapes=[
            pltpu.VMEM(head_qkv.shape, jnp.bfloat16),
            pltpu.VMEM(head_out.shape, jnp.bfloat16),
            pltpu.SemaphoreType.DMA((2,)),
        ],
        compiler_params=pltpu.CompilerParams(vmem_limit_bytes=vmem_bytes),
        name="coarse_block",
    )(tokens, cotangents, factor, head_qkv, head_out)


def row_edges_body(x_ref, dy_ref, near_ref, far_ref):
    height = x_ref.shape[0]
    odd = odd_rank("gy")

    def fill(low_ref, high_ref):
        low_ref[:HALO], low_ref[HALO:] = x_ref[:HALO], dy_ref[:RAD]
        high_ref[:HALO], high_ref[HALO:] = x_ref[height - HALO :], dy_ref[height - RAD :]

    @pl.when(odd)
    def _():
        fill(near_ref, far_ref)

    @pl.when(jnp.logical_not(odd))
    def _():
        fill(far_ref, near_ref)


def row_edges(picture, cotangent):
    vmem = pl.BlockSpec(memory_space=pltpu.VMEM)
    shape = jax.ShapeDtypeStruct((HALO + RAD,) + picture.shape[1:], jnp.bfloat16)
    return pl.pallas_call(
        row_edges_body,
        out_shape=(shape, shape),
        in_specs=[vmem, vmem],
        out_specs=(vmem, vmem),
        compiler_params=pltpu.CompilerParams(vmem_limit_bytes=vmem_bytes),
        name="row_edges",
    )(picture, cotangent)


def col_edges_body(x_ref, dy_ref, row_near_ref, row_far_ref, near_ref, far_ref):
    above, below = in_order("gy", row_near_ref, row_far_ref)
    breadth = x_ref.shape[1]
    odd = odd_rank("gx")
    at = 0
    for rows in (above, x_ref[...].astype(jnp.float32), dy_ref[...].astype(jnp.float32), below):
        first, final = rows[:, :side], rows[:, breadth - side :]
        span = slice(at, at + rows.shape[0])
        near_ref[span] = jnp.where(odd, first, final).astype(jnp.bfloat16)
        far_ref[span] = jnp.where(odd, final, first).astype(jnp.bfloat16)
        at += rows.shape[0]


def col_edges(picture, cotangent, row_near, row_far):
    vmem = pl.BlockSpec(memory_space=pltpu.VMEM)
    rows = 2 * (picture.shape[0] + row_near.shape[0])
    shape = jax.ShapeDtypeStruct((rows, side, D_F), jnp.bfloat16)
    return pl.pallas_call(
        col_edges_body,
        out_shape=(shape, shape),
        in_specs=[vmem] * 4,
        out_specs=(vmem, vmem),
        compiler_params=pltpu.CompilerParams(vmem_limit_bytes=vmem_bytes),
        name="col_edges",
    )(picture, cotangent, row_near, row_far)


def pack_body(
    first,
    second,
    step,
    x_ref,
    dy_ref,
    fine_gain,
    coarse_gain,
    fine_freq,
    coarse_freq,
    own_ref,
    fine_ref,
    coarse_ref,
):
    own_ref[:, :D_C] = x_ref[...].astype(jnp.float32).reshape(-1, D_C).astype(jnp.bfloat16)
    own_ref[:, D_C:] = dy_ref[...].astype(jnp.float32).reshape(-1, D_C).astype(jnp.bfloat16)
    time = step[0].astype(jnp.float32)
    fine_ref[...] = fine_gain[...] * (1.0 + 0.5 * jnp.cos(time * fine_freq[...]))
    coarse_ref[...] = coarse_gain[...] * (1.0 + 0.5 * jnp.cos(time * coarse_freq[...]))


def packed(after, step, tokens, cotangents, fine_gain, coarse_gain):
    vmem = pl.BlockSpec(memory_space=pltpu.VMEM)
    count = tokens.shape[0] * tokens.shape[1]
    return pl.pallas_call(
        pack_body,
        out_shape=(
            jax.ShapeDtypeStruct((count, 2 * D_C), jnp.bfloat16),
            jax.ShapeDtypeStruct((1, D_F), jnp.float32),
            jax.ShapeDtypeStruct((1, D_C), jnp.float32),
        ),
        in_specs=[pl.BlockSpec(memory_space=pl.ANY)] * 2
        + [pl.BlockSpec(memory_space=pltpu.SMEM)]
        + [vmem] * 6,
        out_specs=(vmem, vmem, vmem),
        compiler_params=pltpu.CompilerParams(vmem_limit_bytes=vmem_bytes),
        name="pack_coarse",
    )(
        *after,
        step,
        tokens,
        cotangents,
        fine_gain[None],
        coarse_gain[None],
        frequencies(D_F),
        frequencies(D_C),
    )


def pair_sum_body(own, first, second, qkv_ref, out_ref):
    for part in range(4):
        come = (first, second)[part // 2][(part % 2) * HD : (part % 2 + 1) * HD]
        total = own[part * HD : (part + 1) * HD].astype(jnp.float32) + come.astype(jnp.float32)
        if part < 3:
            qkv_ref[part] = total.astype(jnp.bfloat16)
        else:
            out_ref[...] = total.astype(jnp.bfloat16)


def pair_sum(own, first, second):
    vmem = pl.BlockSpec(memory_space=pltpu.VMEM)
    return pl.pallas_call(
        pair_sum_body,
        out_shape=(
            jax.ShapeDtypeStruct((3, HD, D_C), jnp.bfloat16),
            jax.ShapeDtypeStruct((HD, D_C), jnp.bfloat16),
        ),
        in_specs=[vmem] * 3,
        out_specs=(vmem, vmem),
        compiler_params=pltpu.CompilerParams(vmem_limit_bytes=vmem_bytes),
        name="pair_sum",
    )(own, first, second)


def last_body(
    near_ref,
    far_ref,
    x_ref,
    factor_ref,
    kept_ref,
    come_ref,
    qkv_hbm,
    out_hbm,
    dx_ref,
    sems,
):
    highs, rows = near_ref.shape[0], near_ref.shape[1]
    copies = []
    for low in range(2):
        for high in range(highs):
            source = (near_ref, far_ref)[low].at[high]
            block = lax.axis_index("gx") ^ (2 * high + low)
            at = pl.ds(pl.multiple_of(block * rows, rows), rows)
            for part, target in enumerate((qkv_hbm, out_hbm)):
                lanes = (slice(0, 3 * D_F), slice(3 * D_F, 4 * D_F))[part]
                copies.append(
                    pltpu.make_async_copy(
                        source.at[:, lanes], target.at[at, :], sems.at[low, high, part]
                    )
                )
    for copy in copies:
        copy.start()
    tokens = x_ref[...].astype(jnp.float32).reshape(-1, D_C)
    upstream = kept_ref[...] + come_ref[...].astype(jnp.float32)
    grads = norm_backward(tokens, inverse_rms(tokens), factor_ref[...], upstream)
    dx_ref[...] = grads.astype(jnp.float32).reshape(dx_ref.shape).astype(jnp.bfloat16)
    for copy in copies:
        copy.wait()


def last_step(near, far, tokens, factor, kept, come):
    vmem = pl.BlockSpec(memory_space=pltpu.VMEM)
    hbm = pl.BlockSpec(memory_space=pltpu.HBM)
    return pl.pallas_call(
        last_body,
        out_shape=(
            jax.ShapeDtypeStruct((D_F, 3 * D_F), jnp.bfloat16),
            jax.ShapeDtypeStruct((D_F, D_F), jnp.bfloat16),
            jax.ShapeDtypeStruct(tokens.shape, jnp.bfloat16),
        ),
        in_specs=[vmem] * 6,
        out_specs=(hbm, hbm, vmem),
        scratch_shapes=[pltpu.SemaphoreType.DMA((2, near.shape[0], 2))],
        compiler_params=pltpu.CompilerParams(vmem_limit_bytes=vmem_bytes),
        name="last_step",
    )(near, far, tokens, factor, kept, come)


def neighbours(to_near, to_far, axis):
    peers = lax.axis_size(axis)
    near = [(i, i ^ 1) for i in range(peers)]
    far = [(i, i + 1 if i % 2 else i - 1) for i in range(1, peers - 1)]
    from_far = lax.ppermute(to_far, axis, far)
    return lax.ppermute(to_near, axis, near), from_far


def swapped(value, axis, mask):
    return lax.ppermute(value, axis, [(i, i ^ mask) for i in range(lax.axis_size(axis))])


def tied(*arrays):
    return lax.optimization_barrier(arrays)


def batch_sum(partial):
    if lax.axis_size("batch") != 2:
        return lax.psum(partial, "batch")
    return wide(partial) + wide(swapped(partial, "batch", 1))


def wide(value):
    return value.astype(jnp.float32)


def narrow(value):
    return value.astype(jnp.bfloat16)


def all_rows(piece):
    downs = lax.axis_size("gy")
    return jnp.stack([piece] + [swapped(piece, "gy", row) for row in range(1, downs)])


def local(
    x_fine,
    dy_fine,
    x_coarse,
    dy_coarse,
    timestep,
    fine_gain,
    coarse_gain,
    fine_qkv,
    fine_out,
    coarse_qkv,
    coarse_out,
):
    picture, cotangent = x_fine[0], dy_fine[0]
    across, downs = lax.axis_size("gx"), lax.axis_size("gy")
    assert across == 4 and downs & (downs - 1) == 0

    payloads = row_edges(picture, cotangent)
    row_near, row_far = neighbours(*payloads, "gy")
    own, factor, coarse_factor = packed(
        payloads, timestep, x_coarse[0], dy_coarse[0], fine_gain, coarse_gain
    )
    row_near, own, factor, coarse_factor = tied(row_near, own, factor, coarse_factor)
    count = own.shape[0]
    edges = col_edges(picture, cotangent, row_near, row_far)
    col_near, col_far = neighbours(*edges, "gx")
    col_near, own = tied(col_near, own)
    pieces = [own] + [swapped(own, "gy", row) for row in range(1, downs)]
    col_near, col_far, *pieces = tied(col_near, col_far, *pieces)
    row_group = jnp.stack(pieces)
    cross = swapped(row_group, "gx", 2)
    beside = swapped(row_group, "gx", 1)
    dx_picture, fine_keep, fine_send = fine_block(
        (across, downs),
        picture,
        cotangent,
        row_near,
        row_far,
        col_near,
        col_far,
        factor,
        fine_qkv,
        fine_out,
    )
    fine_half = fine_keep + wide(swapped(fine_send, "gx", 1))
    opposite = swapped(cross, "gx", 1)
    fine_half, opposite = tied(fine_half, opposite)

    fine_quarter = narrow(fine_half[0] + wide(swapped(narrow(fine_half[1]), "gx", 2)))
    everyone = jnp.stack([row_group, cross, beside, opposite]).reshape(-1, 2 * D_C)
    parts, coarse_partial = coarse_block(
        everyone[:, :D_C], everyone[:, D_C:], coarse_factor, coarse_qkv, coarse_out
    )
    fine_quarter, parts, coarse_partial = tied(fine_quarter, parts, coarse_partial)

    rows = D_F // across
    fine_quarter = narrow(batch_sum(fine_quarter)).reshape(rows, 4 * D_F)
    parts = parts.reshape(2, 2, downs, count, D_C)
    coarse_kept = wide(parts[0]) + wide(swapped(parts[1], "gx", 1))
    fine_quarter, coarse_kept, coarse_partial = tied(fine_quarter, coarse_kept, coarse_partial)

    pair_batch = lax.axis_size("batch") == 2
    halves = (coarse_partial[: 2 * HD], coarse_partial[2 * HD :])
    others = [swapped(half, "batch", 1) if pair_batch else half for half in halves]
    mask = 1
    while mask < downs:
        last = 2 * mask == downs
        coarse_kept = coarse_kept.reshape(2, -1, 2, count, D_C)
        sent = narrow(coarse_kept[:, :, 1]).reshape(-1, D_C)
        come = swapped(jnp.concatenate([fine_quarter, sent], axis=0), "gy", mask)
        coarse_kept = coarse_kept[:, :, 0]
        coarse_kept = coarse_kept + wide(come[rows:]).reshape(coarse_kept.shape)
        fine_quarter = narrow(wide(fine_quarter) + wide(come[:rows]))
        at = int(last)
        fine_quarter, coarse_kept, others[at] = tied(fine_quarter, coarse_kept, others[at])
        mask *= 2

    coarse_kept = coarse_kept.reshape(2, count, D_C)
    come = swapped(jnp.concatenate([fine_quarter, narrow(coarse_kept[1])], axis=0), "gx", 2)
    if pair_batch:
        grad_coarse_qkv, grad_coarse_out = pair_sum(coarse_partial, *others)
    else:
        coarse_sum = narrow(batch_sum(wide(coarse_partial)))
        grad_coarse_qkv = coarse_sum[: 3 * HD].reshape(coarse_qkv.shape)
        grad_coarse_out = coarse_sum[3 * HD :]
    come, grad_coarse_qkv, grad_coarse_out = tied(come, grad_coarse_qkv, grad_coarse_out)
    fine_pair = jnp.stack([fine_quarter, come[:rows]])
    grad_qkv, grad_out, dx_coarse = last_step(
        fine_pair,
        swapped(fine_pair, "gx", 1),
        x_coarse[0],
        coarse_factor,
        coarse_kept[0],
        come[rows:],
    )
    return (
        dx_picture[None],
        dx_coarse[None],
        grad_qkv,
        grad_out,
        grad_coarse_qkv,
        grad_coarse_out,
    )


def solution(mesh):
    placed = (
        P("batch", "gy", "gx", None),
        P("batch", "gy", "gx", None),
        P("batch", "gy", "gx", None),
        P("batch", "gy", "gx", None),
        P("batch"),
        P(),
        P(),
        P(),
        P(),
        P(None, plane_spec, None),
        P(plane_spec, None),
    )
    return jax.shard_map(
        local,
        mesh=mesh,
        in_specs=placed,
        out_specs=(
            P("batch", "gy", "gx", None),
            P("batch", "gy", "gx", None),
            P(),
            P(),
            P(None, plane_spec, None),
            P(plane_spec, None),
        ),
        check_vma=False,
    )


plane_spec = ("gy", "gx")
```

```python
import math

import jax
import jax.numpy as jnp
import numpy as np
from jax import lax
from jax.experimental import pallas as pl
from jax.experimental.pallas import tpu as pltpu
from jax.sharding import PartitionSpec as P

D_F = 256
H_F = 4
D_C = 1024
HD = 64
RAD = 3
HALO = 2 * RAD

eps = 1e-06
log_span = math.log(1000.0)
side = 8
extent = side + 2 * RAD
lanes_wide = 16
scale = 1.0 / math.sqrt(HD)
vmem_bytes = 48 * 1024 * 1024


def dot(first, second, dims=((1,), (0,))):
    return lax.dot_general(first, second, (dims, ((), ())), preferred_element_type=jnp.float32)


def frequencies(channels):
    steps = np.float32(-log_span) * np.arange(channels, dtype=np.float32) / np.float32(channels)
    return np.exp(steps)[None]


def odd_rank(axis):
    return lax.axis_index(axis) & 1 == 1


def inverse_rms(floats):
    return lax.rsqrt(jnp.mean(floats * floats, axis=-1, keepdims=True) + eps)


def norm_backward(floats, inverse, factor, upstream):
    scaled = upstream * factor
    middle = jnp.mean(floats * scaled, axis=-1, keepdims=True)
    return (inverse * scaled - floats * inverse * inverse * inverse * middle).astype(jnp.bfloat16)


def round_up(value, multiple):
    return -(-value // multiple) * multiple


def in_order(axis, near, far):
    odd = odd_rank(axis)
    first, second = near[...].astype(jnp.float32), far[...].astype(jnp.float32)
    return jnp.where(odd, first, second), jnp.where(odd, second, first)


def fine_body(
    x_ref,
    dy_ref,
    row_far_ref,
    row_near_ref,
    col_far_ref,
    col_near_ref,
    factor_ref,
    qkv_ref,
    out_ref,
    dx_ref,
    keep_ref,
    send_ref,
    x_grid,
    dy_grid,
    k_grid,
    v_grid,
    q_grid,
    u_grid,
    dk_grid,
    dv_grid,
    dq_grid,
    a_grid,
    bias_ref,
    total_ref,
):
    height, breadth = x_ref.shape[0], x_ref.shape[1]
    grid_rows, grid_cols = x_grid.shape[0], x_grid.shape[1]
    query_rows = dy_grid.shape[0]
    floats = jnp.float32
    factor = factor_ref[...]

    x_grid[...] = jnp.zeros_like(x_grid)
    dy_grid[...] = jnp.zeros_like(dy_grid)
    dk_grid[...] = jnp.zeros_like(dk_grid)
    dv_grid[...] = jnp.zeros_like(dv_grid)
    inner = slice(HALO, HALO + breadth)
    above, below = in_order("gy", row_near_ref, row_far_ref)
    left, right = in_order("gx", col_near_ref, col_far_ref)
    x_grid[0:HALO, inner] = above[0:HALO]
    x_grid[HALO : HALO + height, inner] = x_ref[...].astype(floats)
    x_grid[HALO + height : HALO + height + HALO, inner] = below[0:HALO]
    dy_grid[0:RAD, inner] = above[HALO : HALO + RAD]
    dy_grid[RAD : RAD + height, inner] = dy_ref[...].astype(floats)
    dy_grid[RAD + height : RAD + height + RAD, inner] = below[HALO : HALO + RAD]
    left, right = left[:, left.shape[1] - HALO :], right[:, :HALO]
    for strip, first in ((left, 0), (right, HALO + breadth)):
        span = slice(first, first + HALO)
        at = 0
        for grid, begin, count in (
            (x_grid, 0, HALO),
            (dy_grid, 0, RAD),
            (x_grid, HALO, height),
            (dy_grid, RAD, height),
            (x_grid, HALO + height, HALO),
            (dy_grid, RAD + height, RAD),
        ):
            grid[begin : begin + count, span] = strip[at : at + count]
            at += count

    tokens = x_grid[...].reshape(grid_rows * grid_cols, D_F)
    normed = (tokens * inverse_rms(tokens) * factor).astype(jnp.bfloat16)
    key_values = dot(normed, qkv_ref[:, D_F:]).astype(jnp.bfloat16).astype(floats)
    k_grid[...] = key_values[:, :D_F].reshape(grid_rows, grid_cols, D_F)
    v_grid[...] = key_values[:, D_F:].reshape(grid_rows, grid_cols, D_F)
    query_tokens = normed[RAD * grid_cols : (RAD + query_rows) * grid_cols]
    queries = dot(query_tokens, qkv_ref[:, :D_F]).astype(jnp.bfloat16).astype(floats) * scale
    q_grid[...] = queries.reshape(query_rows, grid_cols, D_F)
    cotangents = dy_grid[...].reshape(query_rows * grid_cols, D_F).astype(jnp.bfloat16)
    ups = dot(cotangents, out_ref[...], ((1,), (1,))).astype(jnp.bfloat16).astype(floats)
    u_grid[...] = ups.reshape(query_rows, grid_cols, D_F)

    keys_count, heads_count = extent * lanes_wide, H_F * side * side
    key_at = lax.broadcasted_iota(jnp.int32, (keys_count, heads_count), 0)
    query_at = lax.broadcasted_iota(jnp.int32, (keys_count, heads_count), 1)
    row_gap = (key_at // lanes_wide) - ((query_at // side) % side)
    col_gap = (key_at % lanes_wide) - (query_at % side)
    near = (row_gap >= 0) & (row_gap <= 2 * RAD) & (col_gap >= 0) & (col_gap <= 2 * RAD)
    bias_ref[...] = jnp.where(near, 0.0, -1e30)
    gx, gy = lax.axis_index("gx"), lax.axis_index("gy")
    row_low, col_low = HALO - gy * height, HALO - gx * breadth
    row_high = row_low + lax.axis_size("gy") * height
    col_high = col_low + lax.axis_size("gx") * breadth
    lone = lax.broadcasted_iota(jnp.int32, (keys_count, 1), 0)
    head_of = lax.broadcasted_iota(jnp.int32, (side * side, D_F), 1) // HD

    def spread(block):
        return jnp.concatenate(
            [jnp.where(head_of == h, block, 0.0).astype(jnp.bfloat16) for h in range(H_F)], axis=0
        )

    def collect(full):
        total = jnp.where(head_of == 0, full[: side * side], 0.0)
        for h in range(1, H_F):
            piece = full[h * side * side : (h + 1) * side * side]
            total = jnp.where(head_of == h, piece, total)
        return total.reshape(side, side, D_F)

    for block_row in range(query_rows // side):
        top = block_row * side
        for block_col in range((grid_cols - side) // side):
            start = block_col * side
            window = (slice(top, top + extent), slice(start, start + lanes_wide))
            keys = k_grid[window].reshape(keys_count, D_F).astype(jnp.bfloat16)
            values = v_grid[window].reshape(keys_count, D_F).astype(jnp.bfloat16)
            place = (slice(top, top + side), slice(start + RAD, start + RAD + side))
            wide_queries = spread(q_grid[place].reshape(side * side, D_F))
            wide_ups = spread(u_grid[place].reshape(side * side, D_F))
            key_row = lone // lanes_wide + top
            key_col = lone % lanes_wide + start
            inside = (
                (key_row >= row_low)
                & (key_row < row_high)
                & (key_col >= col_low)
                & (key_col < col_high)
            )
            scores = dot(keys, wide_queries, ((1,), (1,)))
            scores = scores + (bias_ref[...] + jnp.where(inside, 0.0, -1e30))
            raised = jnp.exp(scores - jnp.max(scores, axis=0, keepdims=True))
            shares = raised * (1.0 / jnp.sum(raised, axis=0, keepdims=True))
            products = dot(values, wide_ups, ((1,), (1,)))
            centre = jnp.sum(shares * products, axis=0, keepdims=True)
            slopes = (shares * (products - centre)).astype(jnp.bfloat16)
            weights = shares.astype(jnp.bfloat16)
            dv_grid[window] += dot(weights, wide_ups).reshape(extent, lanes_wide, D_F)
            dk_grid[window] += dot(slopes, wide_queries).reshape(extent, lanes_wide, D_F)
            block = (slice(top, top + side), slice(start, start + side))
            a_grid[block] = collect(dot(weights, values, ((0,), (0,))))
            dq_grid[block] = collect(dot(slopes, keys, ((0,), (0,))))

    count = height * breadth
    own_queries = (slice(RAD, RAD + height), slice(RAD, RAD + breadth))
    own_keys = (slice(HALO, HALO + height), inner)
    attended = a_grid[own_queries].reshape(count, D_F).astype(jnp.bfloat16)
    grad_q = (dq_grid[own_queries].reshape(count, D_F) * scale).astype(jnp.bfloat16)
    grad_k = dk_grid[own_keys].reshape(count, D_F).astype(jnp.bfloat16)
    grad_v = dv_grid[own_keys].reshape(count, D_F).astype(jnp.bfloat16)
    grad_proj = jnp.concatenate([grad_q, grad_k, grad_v], axis=1)
    picture = x_ref[...].reshape(count, D_F).astype(floats)
    inverse = inverse_rms(picture)
    own_normed = (picture * inverse * factor).astype(jnp.bfloat16)
    flat_cot = dy_ref[...].reshape(count, D_F)
    grads = jnp.concatenate(
        [
            dot(own_normed, grad_proj, ((0,), (0,))),
            dot(attended, flat_cot, ((0,), (0,))),
        ],
        axis=1,
    )
    half, columns = keep_ref.shape[0], keep_ref.shape[1]
    total_ref[...] = grads.reshape(total_ref.shape)
    for low in range(2):
        target = (keep_ref, send_ref)[low]
        for high in range(half):
            for row in range(columns):
                block = (gx ^ (2 * high + low)) * columns + row
                target[high, row] = total_ref[block].astype(target.dtype)
    down = dot(grad_proj, qkv_ref[...], ((1,), (1,)))
    dx_ref[...] = norm_backward(picture, inverse, factor, down).reshape(height, breadth, D_F)


def fine_block(peers, picture, *operands):
    height, breadth = picture.shape[0], picture.shape[1]
    query_rows = round_up(height + 2 * RAD, side)
    query_cols = round_up(breadth + 2 * RAD, side)
    grid_rows, grid_cols = query_rows + 2 * RAD, query_cols + side
    across, down = peers
    rows = D_F // (across * down)
    halves = (across // 2, down, rows, 4 * D_F)
    vmem = pl.BlockSpec(memory_space=pltpu.VMEM)
    wide = pltpu.VMEM((grid_rows, grid_cols, D_F), jnp.float32)
    middle = pltpu.VMEM((query_rows, grid_cols, D_F), jnp.float32)
    small = pltpu.VMEM((query_rows, query_cols, D_F), jnp.float32)
    return pl.pallas_call(
        fine_body,
        out_shape=(
            jax.ShapeDtypeStruct((height, breadth, D_F), jnp.bfloat16),
            jax.ShapeDtypeStruct(halves, jnp.float32),
            jax.ShapeDtypeStruct(halves, jnp.bfloat16),
        ),
        in_specs=[vmem] * 9,
        out_specs=(vmem, vmem, vmem),
        scratch_shapes=[
            wide,
            middle,
            wide,
            wide,
            middle,
            middle,
            wide,
            wide,
            small,
            small,
            pltpu.VMEM((extent * lanes_wide, H_F * side * side), jnp.float32),
            pltpu.VMEM((across * down, rows, 4 * D_F), jnp.float32),
        ],
        compiler_params=pltpu.CompilerParams(vmem_limit_bytes=vmem_bytes),
        name="fine_block",
    )(picture, *operands)


def coarse_body(
    x_ref,
    dy_ref,
    factor_ref,
    qkv_hbm,
    out_hbm,
    parts_ref,
    grads_ref,
    qkv_ref,
    out_ref,
    arrived,
):
    fetches = [
        pltpu.make_async_copy(qkv_hbm, qkv_ref, arrived.at[0]),
        pltpu.make_async_copy(out_hbm, out_ref, arrived.at[1]),
    ]
    for fetch in fetches:
        fetch.start()
    tokens = x_ref[...].astype(jnp.float32)
    normed = (tokens * inverse_rms(tokens) * factor_ref[...]).astype(jnp.bfloat16)
    cot = dy_ref[...]
    for fetch in fetches:
        fetch.wait()
    flat_qkv = qkv_ref[...].reshape(3 * HD, D_C)
    out_rows = out_ref[...]
    projected = dot(normed, flat_qkv, ((1,), (1,))).astype(jnp.bfloat16)
    queries, keys, values = projected[:, :HD], projected[:, HD : 2 * HD], projected[:, 2 * HD :]
    ups = dot(cot, out_rows, ((1,), (1,))).astype(jnp.bfloat16)
    scores = dot(queries, keys, ((1,), (1,))) * scale
    raised = jnp.exp(scores - jnp.max(scores, axis=-1, keepdims=True))
    shares = raised * (1.0 / jnp.sum(raised, axis=-1, keepdims=True))
    weights = shares.astype(jnp.bfloat16)
    mixed = dot(weights, values).astype(jnp.bfloat16)
    products = dot(ups, values, ((1,), (1,)))
    centre = jnp.sum(shares * products, axis=-1, keepdims=True)
    slopes = (shares * (products - centre)).astype(jnp.bfloat16)
    grad_q = (dot(slopes, keys) * scale).astype(jnp.bfloat16)
    grad_k = (dot(slopes, queries, ((0,), (0,))) * scale).astype(jnp.bfloat16)
    grad_v = dot(weights, ups, ((0,), (0,))).astype(jnp.bfloat16)
    stacked = jnp.concatenate([grad_q, grad_k, grad_v], axis=1)
    parts_ref[...] = dot(stacked, flat_qkv).astype(jnp.bfloat16)
    grads_ref[: 3 * HD] = dot(stacked, normed, ((0,), (0,))).astype(grads_ref.dtype)
    grads_ref[3 * HD :] = dot(mixed, cot, ((0,), (0,))).astype(grads_ref.dtype)


def coarse_block(tokens, cotangents, factor, head_qkv, head_out):
    count = tokens.shape[0]
    vmem = pl.BlockSpec(memory_space=pltpu.VMEM)
    return pl.pallas_call(
        coarse_body,
        out_shape=(
            jax.ShapeDtypeStruct((count, D_C), jnp.bfloat16),
            jax.ShapeDtypeStruct((4 * HD, D_C), jnp.bfloat16),
        ),
        in_specs=[vmem] * 3 + [pl.BlockSpec(memory_space=pltpu.HBM)] * 2,
        out_specs=(vmem, vmem),
        scratch_shapes=[
            pltpu.VMEM(head_qkv.shape, jnp.bfloat16),
            pltpu.VMEM(head_out.shape, jnp.bfloat16),
            pltpu.SemaphoreType.DMA((2,)),
        ],
        compiler_params=pltpu.CompilerParams(vmem_limit_bytes=vmem_bytes),
        name="coarse_block",
    )(tokens, cotangents, factor, head_qkv, head_out)


def row_edges_body(x_ref, dy_ref, near_ref, far_ref):
    height = x_ref.shape[0]
    odd = odd_rank("gy")

    def fill(low_ref, high_ref):
        low_ref[:HALO], low_ref[HALO:] = x_ref[:HALO], dy_ref[:RAD]
        high_ref[:HALO], high_ref[HALO:] = x_ref[height - HALO :], dy_ref[height - RAD :]

    @pl.when(odd)
    def _():
        fill(near_ref, far_ref)

    @pl.when(jnp.logical_not(odd))
    def _():
        fill(far_ref, near_ref)


def row_edges(picture, cotangent):
    vmem = pl.BlockSpec(memory_space=pltpu.VMEM)
    shape = jax.ShapeDtypeStruct((HALO + RAD,) + picture.shape[1:], jnp.bfloat16)
    return pl.pallas_call(
        row_edges_body,
        out_shape=(shape, shape),
        in_specs=[vmem, vmem],
        out_specs=(vmem, vmem),
        compiler_params=pltpu.CompilerParams(vmem_limit_bytes=vmem_bytes),
        name="row_edges",
    )(picture, cotangent)


def col_edges_body(x_ref, dy_ref, row_far_ref, row_near_ref, near_ref, far_ref):
    above, below = in_order("gy", row_near_ref, row_far_ref)
    breadth = x_ref.shape[1]
    odd = odd_rank("gx")
    at = 0
    for rows in (above, x_ref[...].astype(jnp.float32), dy_ref[...].astype(jnp.float32), below):
        first, final = rows[:, :side], rows[:, breadth - side :]
        span = slice(at, at + rows.shape[0])
        near_ref[span] = jnp.where(odd, first, final).astype(jnp.bfloat16)
        far_ref[span] = jnp.where(odd, final, first).astype(jnp.bfloat16)
        at += rows.shape[0]


def col_edges(picture, cotangent, row_far, row_near):
    vmem = pl.BlockSpec(memory_space=pltpu.VMEM)
    rows = 2 * (picture.shape[0] + row_near.shape[0])
    shape = jax.ShapeDtypeStruct((rows, side, D_F), jnp.bfloat16)
    return pl.pallas_call(
        col_edges_body,
        out_shape=(shape, shape),
        in_specs=[vmem] * 4,
        out_specs=(vmem, vmem),
        compiler_params=pltpu.CompilerParams(vmem_limit_bytes=vmem_bytes),
        name="col_edges",
    )(picture, cotangent, row_far, row_near)


def pack_body(
    first,
    second,
    step,
    x_ref,
    dy_ref,
    fine_gain,
    coarse_gain,
    fine_freq,
    coarse_freq,
    own_ref,
    fine_ref,
    coarse_ref,
):
    own_ref[:, :D_C] = x_ref[...].astype(jnp.float32).reshape(-1, D_C).astype(jnp.bfloat16)
    own_ref[:, D_C:] = dy_ref[...].astype(jnp.float32).reshape(-1, D_C).astype(jnp.bfloat16)
    time = step[0].astype(jnp.float32)
    fine_ref[...] = fine_gain[...] * (1.0 + 0.5 * jnp.cos(time * fine_freq[...]))
    coarse_ref[...] = coarse_gain[...] * (1.0 + 0.5 * jnp.cos(time * coarse_freq[...]))


def packed(after, step, tokens, cotangents, fine_gain, coarse_gain):
    vmem = pl.BlockSpec(memory_space=pltpu.VMEM)
    count = tokens.shape[0] * tokens.shape[1]
    return pl.pallas_call(
        pack_body,
        out_shape=(
            jax.ShapeDtypeStruct((count, 2 * D_C), jnp.bfloat16),
            jax.ShapeDtypeStruct((1, D_F), jnp.float32),
            jax.ShapeDtypeStruct((1, D_C), jnp.float32),
        ),
        in_specs=[pl.BlockSpec(memory_space=pl.ANY)] * 2
        + [pl.BlockSpec(memory_space=pltpu.SMEM)]
        + [vmem] * 6,
        out_specs=(vmem, vmem, vmem),
        compiler_params=pltpu.CompilerParams(vmem_limit_bytes=vmem_bytes),
        name="pack_coarse",
    )(
        *after,
        step,
        tokens,
        cotangents,
        fine_gain[None],
        coarse_gain[None],
        frequencies(D_F),
        frequencies(D_C),
    )


def pair_sum_body(own, first, second, qkv_ref, out_ref):
    for part in range(4):
        come = (first, second)[part // 2][(part % 2) * HD : (part % 2 + 1) * HD]
        total = own[part * HD : (part + 1) * HD].astype(jnp.float32) + come.astype(jnp.float32)
        if part < 3:
            qkv_ref[part] = total.astype(jnp.bfloat16)
        else:
            out_ref[...] = total.astype(jnp.bfloat16)


def pair_sum(own, first, second):
    vmem = pl.BlockSpec(memory_space=pltpu.VMEM)
    return pl.pallas_call(
        pair_sum_body,
        out_shape=(
            jax.ShapeDtypeStruct((3, HD, D_C), jnp.bfloat16),
            jax.ShapeDtypeStruct((HD, D_C), jnp.bfloat16),
        ),
        in_specs=[vmem] * 3,
        out_specs=(vmem, vmem),
        compiler_params=pltpu.CompilerParams(vmem_limit_bytes=vmem_bytes),
        name="pair_sum",
    )(own, first, second)


def last_body(
    near_ref,
    far_ref,
    x_ref,
    factor_ref,
    kept_ref,
    come_ref,
    qkv_hbm,
    out_hbm,
    dx_ref,
    sems,
):
    highs, rows = near_ref.shape[0], near_ref.shape[1]
    copies = []
    for low in range(2):
        for high in range(highs):
            source = (near_ref, far_ref)[low].at[high]
            block = lax.axis_index("gx") ^ (2 * high + low)
            at = pl.ds(pl.multiple_of(block * rows, rows), rows)
            for part, target in enumerate((qkv_hbm, out_hbm)):
                lanes = (slice(0, 3 * D_F), slice(3 * D_F, 4 * D_F))[part]
                copies.append(
                    pltpu.make_async_copy(
                        source.at[:, lanes], target.at[at, :], sems.at[low, high, part]
                    )
                )
    for copy in copies:
        copy.start()
    tokens = x_ref[...].astype(jnp.float32).reshape(-1, D_C)
    upstream = kept_ref[...] + come_ref[...].astype(jnp.float32)
    grads = norm_backward(tokens, inverse_rms(tokens), factor_ref[...], upstream)
    dx_ref[...] = grads.astype(jnp.float32).reshape(dx_ref.shape).astype(jnp.bfloat16)
    for copy in copies:
        copy.wait()


def last_step(near, far, tokens, factor, kept, come):
    vmem = pl.BlockSpec(memory_space=pltpu.VMEM)
    hbm = pl.BlockSpec(memory_space=pltpu.HBM)
    return pl.pallas_call(
        last_body,
        out_shape=(
            jax.ShapeDtypeStruct((D_F, 3 * D_F), jnp.bfloat16),
            jax.ShapeDtypeStruct((D_F, D_F), jnp.bfloat16),
            jax.ShapeDtypeStruct(tokens.shape, jnp.bfloat16),
        ),
        in_specs=[vmem] * 6,
        out_specs=(hbm, hbm, vmem),
        scratch_shapes=[pltpu.SemaphoreType.DMA((2, near.shape[0], 2))],
        compiler_params=pltpu.CompilerParams(vmem_limit_bytes=vmem_bytes),
        name="last_step",
    )(near, far, tokens, factor, kept, come)


def neighbours(to_near, to_far, axis):
    peers = lax.axis_size(axis)
    near = [(i, i ^ 1) for i in range(peers)]
    far = [(i, i + 1 if i % 2 else i - 1) for i in range(1, peers - 1)]
    from_far = lax.ppermute(to_far, axis, far)
    return lax.ppermute(to_near, axis, near), from_far


def swapped(value, axis, mask):
    return lax.ppermute(value, axis, [(i, i ^ mask) for i in range(lax.axis_size(axis))])


def tied(*arrays):
    return lax.optimization_barrier(arrays)


def batch_sum(partial):
    if lax.axis_size("batch") != 2:
        return lax.psum(partial, "batch")
    return wide(partial) + wide(swapped(partial, "batch", 1))


def wide(value):
    return value.astype(jnp.float32)


def narrow(value):
    return value.astype(jnp.bfloat16)


def all_rows(piece):
    downs = lax.axis_size("gy")
    return jnp.stack([piece] + [swapped(piece, "gy", row) for row in range(1, downs)])


def local(
    x_fine,
    dy_fine,
    x_coarse,
    dy_coarse,
    timestep,
    fine_gain,
    coarse_gain,
    fine_qkv,
    fine_out,
    coarse_qkv,
    coarse_out,
):
    picture, cotangent = x_fine[0], dy_fine[0]
    across, downs = lax.axis_size("gx"), lax.axis_size("gy")
    assert across == 4 and downs & (downs - 1) == 0

    payloads = row_edges(picture, cotangent)
    row_near, row_far = neighbours(*payloads, "gy")
    own, factor, coarse_factor = packed(
        payloads, timestep, x_coarse[0], dy_coarse[0], fine_gain, coarse_gain
    )
    count = own.shape[0]
    row_group = all_rows(own)
    edges = col_edges(picture, cotangent, row_far, row_near)
    col_near, col_far = neighbours(*edges, "gx")
    col_far, col_near, row_group = tied(col_far, col_near, row_group)
    cross = swapped(row_group, "gx", 2)
    beside = swapped(row_group, "gx", 1)
    dx_picture, fine_keep, fine_send = fine_block(
        (across, downs),
        picture,
        cotangent,
        row_far,
        row_near,
        col_far,
        col_near,
        factor,
        fine_qkv,
        fine_out,
    )
    fine_half = fine_keep + wide(swapped(fine_send, "gx", 1))
    opposite = swapped(cross, "gx", 1)
    fine_half, opposite = tied(fine_half, opposite)

    fine_quarter = narrow(fine_half[0] + wide(swapped(narrow(fine_half[1]), "gx", 2)))
    everyone = jnp.stack([row_group, cross, beside, opposite]).reshape(-1, 2 * D_C)
    parts, coarse_partial = coarse_block(
        everyone[:, :D_C], everyone[:, D_C:], coarse_factor, coarse_qkv, coarse_out
    )
    fine_quarter, parts, coarse_partial = tied(fine_quarter, parts, coarse_partial)

    rows = D_F // across
    fine_quarter = narrow(batch_sum(fine_quarter)).reshape(rows, 4 * D_F)
    parts = parts.reshape(2, 2, downs, count, D_C)
    coarse_kept = wide(parts[0]) + wide(swapped(parts[1], "gx", 1))
    fine_quarter, coarse_kept, coarse_partial = tied(fine_quarter, coarse_kept, coarse_partial)

    pair_batch = lax.axis_size("batch") == 2
    halves = (coarse_partial[: 2 * HD], coarse_partial[2 * HD :])
    others = [swapped(half, "batch", 1) if pair_batch else half for half in halves]
    mask = 1
    while mask < downs:
        last = 2 * mask == downs
        coarse_kept = coarse_kept.reshape(2, -1, 2, count, D_C)
        sent = narrow(coarse_kept[:, :, 1]).reshape(-1, D_C)
        come = swapped(jnp.concatenate([fine_quarter, sent], axis=0), "gy", mask)
        coarse_kept = coarse_kept[:, :, 0]
        coarse_kept = coarse_kept + wide(come[rows:]).reshape(coarse_kept.shape)
        fine_quarter = narrow(wide(fine_quarter) + wide(come[:rows]))
        at = int(last)
        fine_quarter, coarse_kept, others[at] = tied(fine_quarter, coarse_kept, others[at])
        mask *= 2

    coarse_kept = coarse_kept.reshape(2, count, D_C)
    come = swapped(jnp.concatenate([fine_quarter, narrow(coarse_kept[1])], axis=0), "gx", 2)
    if pair_batch:
        grad_coarse_qkv, grad_coarse_out = pair_sum(coarse_partial, *others)
    else:
        coarse_sum = narrow(batch_sum(wide(coarse_partial)))
        grad_coarse_qkv = coarse_sum[: 3 * HD].reshape(coarse_qkv.shape)
        grad_coarse_out = coarse_sum[3 * HD :]
    come, grad_coarse_qkv, grad_coarse_out = tied(come, grad_coarse_qkv, grad_coarse_out)
    fine_pair = jnp.stack([fine_quarter, come[:rows]])
    grad_qkv, grad_out, dx_coarse = last_step(
        fine_pair,
        swapped(fine_pair, "gx", 1),
        x_coarse[0],
        coarse_factor,
        coarse_kept[0],
        come[rows:],
    )
    return (
        dx_picture[None],
        dx_coarse[None],
        grad_qkv,
        grad_out,
        grad_coarse_qkv,
        grad_coarse_out,
    )


def solution(mesh):
    placed = (
        P("batch", "gy", "gx", None),
        P("batch", "gy", "gx", None),
        P("batch", "gy", "gx", None),
        P("batch", "gy", "gx", None),
        P("batch"),
        P(),
        P(),
        P(),
        P(),
        P(None, plane_spec, None),
        P(plane_spec, None),
    )
    return jax.shard_map(
        local,
        mesh=mesh,
        in_specs=placed,
        out_specs=(
            P("batch", "gy", "gx", None),
            P("batch", "gy", "gx", None),
            P(),
            P(),
            P(None, plane_spec, None),
            P(plane_spec, None),
        ),
        check_vma=False,
    )


plane_spec = ("gy", "gx")
```

```python
import math

import jax
import jax.numpy as jnp
import numpy as np
from jax import lax
from jax.experimental import pallas as pl
from jax.experimental.pallas import tpu as pltpu
from jax.sharding import PartitionSpec as P

D_F = 256
H_F = 4
D_C = 1024
HD = 64
RAD = 3
HALO = 2 * RAD

eps = 1e-06
log_span = math.log(1000.0)
side = 8
extent = side + 2 * RAD
lanes_wide = 16
scale = 1.0 / math.sqrt(HD)
vmem_bytes = 48 * 1024 * 1024


def dot(first, second, dims=((1,), (0,))):
    return lax.dot_general(first, second, (dims, ((), ())), preferred_element_type=jnp.float32)


def frequencies(channels):
    steps = np.float32(-log_span) * np.arange(channels, dtype=np.float32) / np.float32(channels)
    return np.exp(steps)[None]


def odd_rank(axis):
    return lax.axis_index(axis) & 1 == 1


def inverse_rms(floats):
    return lax.rsqrt(jnp.mean(floats * floats, axis=-1, keepdims=True) + eps)


def norm_backward(floats, inverse, factor, upstream):
    scaled = upstream * factor
    middle = jnp.mean(floats * scaled, axis=-1, keepdims=True)
    return (inverse * scaled - floats * inverse * inverse * inverse * middle).astype(jnp.bfloat16)


def round_up(value, multiple):
    return -(-value // multiple) * multiple


def in_order(axis, near, far):
    odd = odd_rank(axis)
    first, second = near[...].astype(jnp.float32), far[...].astype(jnp.float32)
    return jnp.where(odd, first, second), jnp.where(odd, second, first)


def fine_body(
    x_ref,
    dy_ref,
    row_far_ref,
    row_near_ref,
    col_far_ref,
    col_near_ref,
    factor_ref,
    qkv_ref,
    out_ref,
    dx_ref,
    keep_ref,
    send_ref,
    x_grid,
    dy_grid,
    k_grid,
    v_grid,
    q_grid,
    u_grid,
    dk_grid,
    dv_grid,
    dq_grid,
    a_grid,
    bias_ref,
    total_ref,
):
    height, breadth = x_ref.shape[0], x_ref.shape[1]
    grid_rows, grid_cols = x_grid.shape[0], x_grid.shape[1]
    query_rows = dy_grid.shape[0]
    floats = jnp.float32
    factor = factor_ref[...]

    x_grid[...] = jnp.zeros_like(x_grid)
    dy_grid[...] = jnp.zeros_like(dy_grid)
    dk_grid[...] = jnp.zeros_like(dk_grid)
    dv_grid[...] = jnp.zeros_like(dv_grid)
    inner = slice(HALO, HALO + breadth)
    above, below = in_order("gy", row_near_ref, row_far_ref)
    left, right = in_order("gx", col_near_ref, col_far_ref)
    x_grid[0:HALO, inner] = above[0:HALO]
    x_grid[HALO : HALO + height, inner] = x_ref[...].astype(floats)
    x_grid[HALO + height : HALO + height + HALO, inner] = below[0:HALO]
    dy_grid[0:RAD, inner] = above[HALO : HALO + RAD]
    dy_grid[RAD : RAD + height, inner] = dy_ref[...].astype(floats)
    dy_grid[RAD + height : RAD + height + RAD, inner] = below[HALO : HALO + RAD]
    left, right = left[:, left.shape[1] - HALO :], right[:, :HALO]
    for strip, first in ((left, 0), (right, HALO + breadth)):
        span = slice(first, first + HALO)
        at = 0
        for grid, begin, count in (
            (x_grid, 0, HALO),
            (dy_grid, 0, RAD),
            (x_grid, HALO, height),
            (dy_grid, RAD, height),
            (x_grid, HALO + height, HALO),
            (dy_grid, RAD + height, RAD),
        ):
            grid[begin : begin + count, span] = strip[at : at + count]
            at += count

    tokens = x_grid[...].reshape(grid_rows * grid_cols, D_F)
    normed = (tokens * inverse_rms(tokens) * factor).astype(jnp.bfloat16)
    key_values = dot(normed, qkv_ref[:, D_F:]).astype(jnp.bfloat16).astype(floats)
    k_grid[...] = key_values[:, :D_F].reshape(grid_rows, grid_cols, D_F)
    v_grid[...] = key_values[:, D_F:].reshape(grid_rows, grid_cols, D_F)
    query_tokens = normed[RAD * grid_cols : (RAD + query_rows) * grid_cols]
    queries = dot(query_tokens, qkv_ref[:, :D_F]).astype(jnp.bfloat16).astype(floats) * scale
    q_grid[...] = queries.reshape(query_rows, grid_cols, D_F)
    cotangents = dy_grid[...].reshape(query_rows * grid_cols, D_F).astype(jnp.bfloat16)
    ups = dot(cotangents, out_ref[...], ((1,), (1,))).astype(jnp.bfloat16).astype(floats)
    u_grid[...] = ups.reshape(query_rows, grid_cols, D_F)

    keys_count, heads_count = extent * lanes_wide, H_F * side * side
    key_at = lax.broadcasted_iota(jnp.int32, (keys_count, heads_count), 0)
    query_at = lax.broadcasted_iota(jnp.int32, (keys_count, heads_count), 1)
    row_gap = (key_at // lanes_wide) - ((query_at // side) % side)
    col_gap = (key_at % lanes_wide) - (query_at % side)
    near = (row_gap >= 0) & (row_gap <= 2 * RAD) & (col_gap >= 0) & (col_gap <= 2 * RAD)
    bias_ref[...] = jnp.where(near, 0.0, -1e30)
    gx, gy = lax.axis_index("gx"), lax.axis_index("gy")
    row_low, col_low = HALO - gy * height, HALO - gx * breadth
    row_high = row_low + lax.axis_size("gy") * height
    col_high = col_low + lax.axis_size("gx") * breadth
    lone = lax.broadcasted_iota(jnp.int32, (keys_count, 1), 0)
    head_of = lax.broadcasted_iota(jnp.int32, (side * side, D_F), 1) // HD

    def spread(block):
        return jnp.concatenate(
            [jnp.where(head_of == h, block, 0.0).astype(jnp.bfloat16) for h in range(H_F)], axis=0
        )

    def collect(full):
        total = jnp.where(head_of == 0, full[: side * side], 0.0)
        for h in range(1, H_F):
            piece = full[h * side * side : (h + 1) * side * side]
            total = jnp.where(head_of == h, piece, total)
        return total.reshape(side, side, D_F)

    for block_row in range(query_rows // side):
        top = block_row * side
        for block_col in range((grid_cols - side) // side):
            start = block_col * side
            window = (slice(top, top + extent), slice(start, start + lanes_wide))
            keys = k_grid[window].reshape(keys_count, D_F).astype(jnp.bfloat16)
            values = v_grid[window].reshape(keys_count, D_F).astype(jnp.bfloat16)
            place = (slice(top, top + side), slice(start + RAD, start + RAD + side))
            wide_queries = spread(q_grid[place].reshape(side * side, D_F))
            wide_ups = spread(u_grid[place].reshape(side * side, D_F))
            key_row = lone // lanes_wide + top
            key_col = lone % lanes_wide + start
            inside = (
                (key_row >= row_low)
                & (key_row < row_high)
                & (key_col >= col_low)
                & (key_col < col_high)
            )
            scores = dot(keys, wide_queries, ((1,), (1,)))
            scores = scores + (bias_ref[...] + jnp.where(inside, 0.0, -1e30))
            raised = jnp.exp(scores - jnp.max(scores, axis=0, keepdims=True))
            shares = raised * (1.0 / jnp.sum(raised, axis=0, keepdims=True))
            products = dot(values, wide_ups, ((1,), (1,)))
            centre = jnp.sum(shares * products, axis=0, keepdims=True)
            slopes = (shares * (products - centre)).astype(jnp.bfloat16)
            weights = shares.astype(jnp.bfloat16)
            dv_grid[window] += dot(weights, wide_ups).reshape(extent, lanes_wide, D_F)
            dk_grid[window] += dot(slopes, wide_queries).reshape(extent, lanes_wide, D_F)
            block = (slice(top, top + side), slice(start, start + side))
            a_grid[block] = collect(dot(weights, values, ((0,), (0,))))
            dq_grid[block] = collect(dot(slopes, keys, ((0,), (0,))))

    count = height * breadth
    own_queries = (slice(RAD, RAD + height), slice(RAD, RAD + breadth))
    own_keys = (slice(HALO, HALO + height), inner)
    attended = a_grid[own_queries].reshape(count, D_F).astype(jnp.bfloat16)
    grad_q = (dq_grid[own_queries].reshape(count, D_F) * scale).astype(jnp.bfloat16)
    grad_k = dk_grid[own_keys].reshape(count, D_F).astype(jnp.bfloat16)
    grad_v = dv_grid[own_keys].reshape(count, D_F).astype(jnp.bfloat16)
    grad_proj = jnp.concatenate([grad_q, grad_k, grad_v], axis=1)
    picture = x_ref[...].reshape(count, D_F).astype(floats)
    inverse = inverse_rms(picture)
    own_normed = (picture * inverse * factor).astype(jnp.bfloat16)
    flat_cot = dy_ref[...].reshape(count, D_F)
    grads = jnp.concatenate(
        [
            dot(own_normed, grad_proj, ((0,), (0,))),
            dot(attended, flat_cot, ((0,), (0,))),
        ],
        axis=1,
    )
    half, columns = keep_ref.shape[0], keep_ref.shape[1]
    total_ref[...] = grads.reshape(total_ref.shape)
    for low in range(2):
        target = (keep_ref, send_ref)[low]
        for high in range(half):
            for row in range(columns):
                block = (gx ^ (2 * high + low)) * columns + row
                target[high, row] = total_ref[block].astype(target.dtype)
    down = dot(grad_proj, qkv_ref[...], ((1,), (1,)))
    dx_ref[...] = norm_backward(picture, inverse, factor, down).reshape(height, breadth, D_F)


def fine_block(peers, picture, *operands):
    height, breadth = picture.shape[0], picture.shape[1]
    query_rows = round_up(height + 2 * RAD, side)
    query_cols = round_up(breadth + 2 * RAD, side)
    grid_rows, grid_cols = query_rows + 2 * RAD, query_cols + side
    across, down = peers
    rows = D_F // (across * down)
    halves = (across // 2, down, rows, 4 * D_F)
    vmem = pl.BlockSpec(memory_space=pltpu.VMEM)
    wide = pltpu.VMEM((grid_rows, grid_cols, D_F), jnp.float32)
    middle = pltpu.VMEM((query_rows, grid_cols, D_F), jnp.float32)
    small = pltpu.VMEM((query_rows, query_cols, D_F), jnp.float32)
    return pl.pallas_call(
        fine_body,
        out_shape=(
            jax.ShapeDtypeStruct((height, breadth, D_F), jnp.bfloat16),
            jax.ShapeDtypeStruct(halves, jnp.float32),
            jax.ShapeDtypeStruct(halves, jnp.bfloat16),
        ),
        in_specs=[vmem] * 9,
        out_specs=(vmem, vmem, vmem),
        scratch_shapes=[
            wide,
            middle,
            wide,
            wide,
            middle,
            middle,
            wide,
            wide,
            small,
            small,
            pltpu.VMEM((extent * lanes_wide, H_F * side * side), jnp.float32),
            pltpu.VMEM((across * down, rows, 4 * D_F), jnp.float32),
        ],
        compiler_params=pltpu.CompilerParams(vmem_limit_bytes=vmem_bytes),
        name="fine_block",
    )(picture, *operands)


def coarse_body(
    x_ref,
    dy_ref,
    factor_ref,
    qkv_hbm,
    out_hbm,
    parts_ref,
    grads_ref,
    qkv_ref,
    out_ref,
    arrived,
):
    fetches = [
        pltpu.make_async_copy(qkv_hbm, qkv_ref, arrived.at[0]),
        pltpu.make_async_copy(out_hbm, out_ref, arrived.at[1]),
    ]
    for fetch in fetches:
        fetch.start()
    tokens = x_ref[...].astype(jnp.float32)
    normed = (tokens * inverse_rms(tokens) * factor_ref[...]).astype(jnp.bfloat16)
    cot = dy_ref[...]
    for fetch in fetches:
        fetch.wait()
    flat_qkv = qkv_ref[...].reshape(3 * HD, D_C)
    out_rows = out_ref[...]
    projected = dot(normed, flat_qkv, ((1,), (1,))).astype(jnp.bfloat16)
    queries, keys, values = projected[:, :HD], projected[:, HD : 2 * HD], projected[:, 2 * HD :]
    ups = dot(cot, out_rows, ((1,), (1,))).astype(jnp.bfloat16)
    scores = dot(queries, keys, ((1,), (1,))) * scale
    raised = jnp.exp(scores - jnp.max(scores, axis=-1, keepdims=True))
    shares = raised * (1.0 / jnp.sum(raised, axis=-1, keepdims=True))
    weights = shares.astype(jnp.bfloat16)
    mixed = dot(weights, values).astype(jnp.bfloat16)
    products = dot(ups, values, ((1,), (1,)))
    centre = jnp.sum(shares * products, axis=-1, keepdims=True)
    slopes = (shares * (products - centre)).astype(jnp.bfloat16)
    grad_q = (dot(slopes, keys) * scale).astype(jnp.bfloat16)
    grad_k = (dot(slopes, queries, ((0,), (0,))) * scale).astype(jnp.bfloat16)
    grad_v = dot(weights, ups, ((0,), (0,))).astype(jnp.bfloat16)
    stacked = jnp.concatenate([grad_q, grad_k, grad_v], axis=1)
    parts_ref[...] = dot(stacked, flat_qkv).astype(jnp.bfloat16)
    grads_ref[: 3 * HD] = dot(stacked, normed, ((0,), (0,))).astype(grads_ref.dtype)
    grads_ref[3 * HD :] = dot(mixed, cot, ((0,), (0,))).astype(grads_ref.dtype)


def coarse_block(tokens, cotangents, factor, head_qkv, head_out):
    count = tokens.shape[0]
    vmem = pl.BlockSpec(memory_space=pltpu.VMEM)
    return pl.pallas_call(
        coarse_body,
        out_shape=(
            jax.ShapeDtypeStruct((count, D_C), jnp.bfloat16),
            jax.ShapeDtypeStruct((4 * HD, D_C), jnp.bfloat16),
        ),
        in_specs=[vmem] * 3 + [pl.BlockSpec(memory_space=pltpu.HBM)] * 2,
        out_specs=(vmem, vmem),
        scratch_shapes=[
            pltpu.VMEM(head_qkv.shape, jnp.bfloat16),
            pltpu.VMEM(head_out.shape, jnp.bfloat16),
            pltpu.SemaphoreType.DMA((2,)),
        ],
        compiler_params=pltpu.CompilerParams(vmem_limit_bytes=vmem_bytes),
        name="coarse_block",
    )(tokens, cotangents, factor, head_qkv, head_out)


def row_edges_body(x_ref, dy_ref, near_ref, far_ref):
    height = x_ref.shape[0]
    odd = odd_rank("gy")

    def fill(low_ref, high_ref):
        low_ref[:HALO], low_ref[HALO:] = x_ref[:HALO], dy_ref[:RAD]
        high_ref[:HALO], high_ref[HALO:] = x_ref[height - HALO :], dy_ref[height - RAD :]

    @pl.when(odd)
    def _():
        fill(near_ref, far_ref)

    @pl.when(jnp.logical_not(odd))
    def _():
        fill(far_ref, near_ref)


def row_edges(picture, cotangent):
    vmem = pl.BlockSpec(memory_space=pltpu.VMEM)
    shape = jax.ShapeDtypeStruct((HALO + RAD,) + picture.shape[1:], jnp.bfloat16)
    return pl.pallas_call(
        row_edges_body,
        out_shape=(shape, shape),
        in_specs=[vmem, vmem],
        out_specs=(vmem, vmem),
        compiler_params=pltpu.CompilerParams(vmem_limit_bytes=vmem_bytes),
        name="row_edges",
    )(picture, cotangent)


def col_edges_body(x_ref, dy_ref, row_far_ref, row_near_ref, near_ref, far_ref):
    above, below = in_order("gy", row_near_ref, row_far_ref)
    breadth = x_ref.shape[1]
    odd = odd_rank("gx")
    at = 0
    for rows in (above, x_ref[...].astype(jnp.float32), dy_ref[...].astype(jnp.float32), below):
        first, final = rows[:, :side], rows[:, breadth - side :]
        span = slice(at, at + rows.shape[0])
        near_ref[span] = jnp.where(odd, first, final).astype(jnp.bfloat16)
        far_ref[span] = jnp.where(odd, final, first).astype(jnp.bfloat16)
        at += rows.shape[0]


def col_edges(picture, cotangent, row_far, row_near):
    vmem = pl.BlockSpec(memory_space=pltpu.VMEM)
    rows = 2 * (picture.shape[0] + row_near.shape[0])
    shape = jax.ShapeDtypeStruct((rows, side, D_F), jnp.bfloat16)
    return pl.pallas_call(
        col_edges_body,
        out_shape=(shape, shape),
        in_specs=[vmem] * 4,
        out_specs=(vmem, vmem),
        compiler_params=pltpu.CompilerParams(vmem_limit_bytes=vmem_bytes),
        name="col_edges",
    )(picture, cotangent, row_far, row_near)


def pack_body(first, second, x_ref, dy_ref, own_ref):
    own_ref[:, :D_C] = x_ref[...].astype(jnp.float32).reshape(-1, D_C).astype(jnp.bfloat16)
    own_ref[:, D_C:] = dy_ref[...].astype(jnp.float32).reshape(-1, D_C).astype(jnp.bfloat16)


def packed(after, tokens, cotangents):
    vmem = pl.BlockSpec(memory_space=pltpu.VMEM)
    count = tokens.shape[0] * tokens.shape[1]
    return pl.pallas_call(
        pack_body,
        out_shape=jax.ShapeDtypeStruct((count, 2 * D_C), jnp.bfloat16),
        in_specs=[pl.BlockSpec(memory_space=pl.ANY)] * 2 + [vmem] * 2,
        out_specs=vmem,
        compiler_params=pltpu.CompilerParams(vmem_limit_bytes=vmem_bytes),
        name="pack_coarse",
    )(*after, tokens, cotangents)


def factors_body(step, fine_gain, coarse_gain, fine_freq, coarse_freq, fine_ref, coarse_ref):
    time = step[0].astype(jnp.float32)
    fine_ref[...] = fine_gain[...] * (1.0 + 0.5 * jnp.cos(time * fine_freq[...]))
    coarse_ref[...] = coarse_gain[...] * (1.0 + 0.5 * jnp.cos(time * coarse_freq[...]))


def time_factors(step, fine_gain, coarse_gain):
    vmem = pl.BlockSpec(memory_space=pltpu.VMEM)
    return pl.pallas_call(
        factors_body,
        out_shape=(
            jax.ShapeDtypeStruct((1, D_F), jnp.float32),
            jax.ShapeDtypeStruct((1, D_C), jnp.float32),
        ),
        in_specs=[pl.BlockSpec(memory_space=pltpu.SMEM)] + [vmem] * 4,
        out_specs=(vmem, vmem),
        compiler_params=pltpu.CompilerParams(vmem_limit_bytes=vmem_bytes),
        name="time_factors",
    )(step, fine_gain[None], coarse_gain[None], frequencies(D_F), frequencies(D_C))


def pair_sum_body(own, *refs):
    qkv_ref, out_ref = refs[-2:]
    come = jnp.concatenate([ref[...] for ref in refs[:-2]], axis=0)
    for part in range(4):
        rows = slice(part * HD, (part + 1) * HD)
        total = own[rows].astype(jnp.float32) + come[rows].astype(jnp.float32)
        if part < 3:
            qkv_ref[part] = total.astype(jnp.bfloat16)
        else:
            out_ref[...] = total.astype(jnp.bfloat16)


def pair_sum(own, *come):
    vmem = pl.BlockSpec(memory_space=pltpu.VMEM)
    return pl.pallas_call(
        pair_sum_body,
        out_shape=(
            jax.ShapeDtypeStruct((3, HD, D_C), jnp.bfloat16),
            jax.ShapeDtypeStruct((HD, D_C), jnp.bfloat16),
        ),
        in_specs=[vmem] * (1 + len(come)),
        out_specs=(vmem, vmem),
        compiler_params=pltpu.CompilerParams(vmem_limit_bytes=vmem_bytes),
        name="pair_sum",
    )(own, *come)


def last_body(
    near_ref,
    far_ref,
    x_ref,
    factor_ref,
    kept_ref,
    come_ref,
    qkv_hbm,
    out_hbm,
    dx_ref,
    sems,
):
    highs, rows = near_ref.shape[0], near_ref.shape[1]
    copies = []
    for low in range(2):
        for high in range(highs):
            source = (near_ref, far_ref)[low].at[high]
            block = lax.axis_index("gx") ^ (2 * high + low)
            at = pl.ds(pl.multiple_of(block * rows, rows), rows)
            for part, target in enumerate((qkv_hbm, out_hbm)):
                lanes = (slice(0, 3 * D_F), slice(3 * D_F, 4 * D_F))[part]
                copies.append(
                    pltpu.make_async_copy(
                        source.at[:, lanes], target.at[at, :], sems.at[low, high, part]
                    )
                )
    for copy in copies:
        copy.start()
    tokens = x_ref[...].astype(jnp.float32).reshape(-1, D_C)
    upstream = kept_ref[...] + come_ref[...].astype(jnp.float32)
    grads = norm_backward(tokens, inverse_rms(tokens), factor_ref[...], upstream)
    dx_ref[...] = grads.astype(jnp.float32).reshape(dx_ref.shape).astype(jnp.bfloat16)
    for copy in copies:
        copy.wait()


def last_step(near, far, tokens, factor, kept, come):
    vmem = pl.BlockSpec(memory_space=pltpu.VMEM)
    hbm = pl.BlockSpec(memory_space=pltpu.HBM)
    return pl.pallas_call(
        last_body,
        out_shape=(
            jax.ShapeDtypeStruct((D_F, 3 * D_F), jnp.bfloat16),
            jax.ShapeDtypeStruct((D_F, D_F), jnp.bfloat16),
            jax.ShapeDtypeStruct(tokens.shape, jnp.bfloat16),
        ),
        in_specs=[vmem] * 6,
        out_specs=(hbm, hbm, vmem),
        scratch_shapes=[pltpu.SemaphoreType.DMA((2, near.shape[0], 2))],
        compiler_params=pltpu.CompilerParams(vmem_limit_bytes=vmem_bytes),
        name="last_step",
    )(near, far, tokens, factor, kept, come)


def neighbours(to_near, to_far, axis):
    peers = lax.axis_size(axis)
    near = [(i, i ^ 1) for i in range(peers)]
    far = [(i, i + 1 if i % 2 else i - 1) for i in range(1, peers - 1)]
    from_far = lax.ppermute(to_far, axis, far)
    return lax.ppermute(to_near, axis, near), from_far


def swapped(value, axis, mask):
    return lax.ppermute(value, axis, [(i, i ^ mask) for i in range(lax.axis_size(axis))])


def tied(*arrays):
    return lax.optimization_barrier(arrays)


def batch_sum(partial):
    if lax.axis_size("batch") != 2:
        return lax.psum(partial, "batch")
    return wide(partial) + wide(swapped(partial, "batch", 1))


def wide(value):
    return value.astype(jnp.float32)


def narrow(value):
    return value.astype(jnp.bfloat16)


def all_rows(piece):
    downs = lax.axis_size("gy")
    return jnp.stack([piece] + [swapped(piece, "gy", row) for row in range(1, downs)])


def row_halved(kept, mask):
    columns, count = kept.shape[0], kept.shape[-2]
    kept = kept.reshape(columns, -1, 2, count, D_C)
    come = swapped(narrow(kept[:, :, 1]), "gy", mask)
    return kept[:, :, 0] + wide(come)


def local(
    x_fine,
    dy_fine,
    x_coarse,
    dy_coarse,
    timestep,
    fine_gain,
    coarse_gain,
    fine_qkv,
    fine_out,
    coarse_qkv,
    coarse_out,
):
    picture, cotangent = x_fine[0], dy_fine[0]
    across, downs = lax.axis_size("gx"), lax.axis_size("gy")
    assert across == 4 and downs & (downs - 1) == 0

    payloads = row_edges(picture, cotangent)
    row_near, row_far = neighbours(*payloads, "gy")
    own = packed(payloads, x_coarse[0], dy_coarse[0])
    count = own.shape[0]
    row_group = all_rows(own)
    edges = col_edges(picture, cotangent, row_far, row_near)
    *edges, step, gain_f, gain_c = tied(*edges, timestep, fine_gain, coarse_gain)
    col_near, col_far = neighbours(*edges, "gx")
    factor, coarse_factor = time_factors(step, gain_f, gain_c)
    col_far, col_near, row_group, factor = tied(col_far, col_near, row_group, factor)
    cross = swapped(row_group, "gx", 2)
    beside = swapped(row_group, "gx", 1)
    dx_picture, fine_keep, fine_send = fine_block(
        (across, downs),
        picture,
        cotangent,
        row_far,
        row_near,
        col_far,
        col_near,
        factor,
        fine_qkv,
        fine_out,
    )
    fine_half = fine_keep + wide(swapped(fine_send, "gx", 1))
    opposite = swapped(cross, "gx", 1)
    fine_half, opposite = tied(fine_half, opposite)

    fine_quarter = narrow(fine_half[0] + wide(swapped(narrow(fine_half[1]), "gx", 2)))
    everyone = jnp.stack([row_group, cross, beside, opposite]).reshape(-1, 2 * D_C)
    parts, coarse_partial = coarse_block(
        everyone[:, :D_C], everyone[:, D_C:], coarse_factor, coarse_qkv, coarse_out
    )
    parts = parts.reshape(2, 2, downs, count, D_C)
    coarse_kept = wide(parts[0]) + wide(swapped(parts[1], "gx", 1))
    fine_quarter, coarse_kept, coarse_partial = tied(fine_quarter, coarse_kept, coarse_partial)

    rows = D_F // across
    fine_quarter = narrow(batch_sum(fine_quarter)).reshape(rows, 4 * D_F)
    masks = [1 << bit for bit in range(downs.bit_length() - 1)]
    coarse_kept = row_halved(coarse_kept, masks[0])
    fine_quarter, coarse_kept, coarse_partial = tied(fine_quarter, coarse_kept, coarse_partial)

    pair_batch = lax.axis_size("batch") == 2
    cut = 5 * HD // 4
    halves = (coarse_partial[:cut], coarse_partial[cut:])
    others = [swapped(half, "batch", 1) if pair_batch else half for half in halves]
    for turn, mask in enumerate(masks):
        last = turn + 1 == len(masks)
        sent = fine_quarter
        if turn:
            coarse_kept = coarse_kept.reshape(2, -1, 2, count, D_C)
            extra = narrow(coarse_kept[:, :, 1]).reshape(-1, D_C)
            sent = jnp.concatenate([fine_quarter, extra], axis=0)
        come = swapped(sent, "gy", mask)
        fine_quarter = narrow(wide(fine_quarter) + wide(come[:rows]))
        if turn:
            coarse_kept = coarse_kept[:, :, 0]
            coarse_kept = coarse_kept + wide(come[rows:]).reshape(coarse_kept.shape)
        at = int(last)
        fine_quarter, coarse_kept, others[at] = tied(fine_quarter, coarse_kept, others[at])

    coarse_kept = coarse_kept.reshape(2, count, D_C)
    come = swapped(jnp.concatenate([fine_quarter, narrow(coarse_kept[1])], axis=0), "gx", 2)
    if pair_batch:
        grad_coarse_qkv, grad_coarse_out = pair_sum(coarse_partial, *others)
    else:
        coarse_sum = narrow(batch_sum(wide(coarse_partial)))
        grad_coarse_qkv = coarse_sum[: 3 * HD].reshape(coarse_qkv.shape)
        grad_coarse_out = coarse_sum[3 * HD :]
    come, grad_coarse_qkv, grad_coarse_out = tied(come, grad_coarse_qkv, grad_coarse_out)
    fine_pair = jnp.stack([fine_quarter, come[:rows]])
    grad_qkv, grad_out, dx_coarse = last_step(
        fine_pair,
        swapped(fine_pair, "gx", 1),
        x_coarse[0],
        coarse_factor,
        coarse_kept[0],
        come[rows:],
    )
    return (
        dx_picture[None],
        dx_coarse[None],
        grad_qkv,
        grad_out,
        grad_coarse_qkv,
        grad_coarse_out,
    )


def solution(mesh):
    placed = (
        P("batch", "gy", "gx", None),
        P("batch", "gy", "gx", None),
        P("batch", "gy", "gx", None),
        P("batch", "gy", "gx", None),
        P("batch"),
        P(),
        P(),
        P(),
        P(),
        P(None, plane_spec, None),
        P(plane_spec, None),
    )
    return jax.shard_map(
        local,
        mesh=mesh,
        in_specs=placed,
        out_specs=(
            P("batch", "gy", "gx", None),
            P("batch", "gy", "gx", None),
            P(),
            P(),
            P(None, plane_spec, None),
            P(plane_spec, None),
        ),
        check_vma=False,
    )


plane_spec = ("gy", "gx")
```

```python
import math

import jax
import jax.numpy as jnp
import numpy as np
from jax import lax
from jax.experimental import pallas as pl
from jax.experimental.pallas import tpu as pltpu
from jax.sharding import PartitionSpec as P

D_F = 256
H_F = 4
D_C = 1024
HD = 64
RAD = 3
HALO = 2 * RAD

eps = 1e-06
log_span = math.log(1000.0)
side = 8
extent = side + 2 * RAD
lanes_wide = 16
scale = 1.0 / math.sqrt(HD)
vmem_bytes = 48 * 1024 * 1024


def dot(first, second, dims=((1,), (0,))):
    return lax.dot_general(first, second, (dims, ((), ())), preferred_element_type=jnp.float32)


def frequencies(channels):
    steps = np.float32(-log_span) * np.arange(channels, dtype=np.float32) / np.float32(channels)
    return np.exp(steps)[None]


def odd_rank(axis):
    return lax.axis_index(axis) & 1 == 1


def inverse_rms(floats):
    return lax.rsqrt(jnp.mean(floats * floats, axis=-1, keepdims=True) + eps)


def norm_backward(floats, inverse, factor, upstream):
    scaled = upstream * factor
    middle = jnp.mean(floats * scaled, axis=-1, keepdims=True)
    return (inverse * scaled - floats * inverse * inverse * inverse * middle).astype(jnp.bfloat16)


def round_up(value, multiple):
    return -(-value // multiple) * multiple


def in_order(axis, near, far):
    odd = odd_rank(axis)
    first, second = near[...].astype(jnp.float32), far[...].astype(jnp.float32)
    return jnp.where(odd, first, second), jnp.where(odd, second, first)


def fine_body(
    x_ref,
    dy_ref,
    row_far_ref,
    row_near_ref,
    col_far_ref,
    col_near_ref,
    factor_ref,
    qkv_ref,
    out_ref,
    dx_ref,
    keep_ref,
    send_ref,
    x_grid,
    dy_grid,
    k_grid,
    v_grid,
    q_grid,
    u_grid,
    dk_grid,
    dv_grid,
    dq_grid,
    a_grid,
    bias_ref,
    total_ref,
):
    height, breadth = x_ref.shape[0], x_ref.shape[1]
    grid_rows, grid_cols = x_grid.shape[0], x_grid.shape[1]
    query_rows = dy_grid.shape[0]
    floats = jnp.float32
    factor = factor_ref[...]

    x_grid[...] = jnp.zeros_like(x_grid)
    dy_grid[...] = jnp.zeros_like(dy_grid)
    dk_grid[...] = jnp.zeros_like(dk_grid)
    dv_grid[...] = jnp.zeros_like(dv_grid)
    inner = slice(HALO, HALO + breadth)
    above, below = in_order("gy", row_near_ref, row_far_ref)
    left, right = in_order("gx", col_near_ref, col_far_ref)
    x_grid[0:HALO, inner] = above[0:HALO]
    x_grid[HALO : HALO + height, inner] = x_ref[...].astype(floats)
    x_grid[HALO + height : HALO + height + HALO, inner] = below[0:HALO]
    dy_grid[0:RAD, inner] = above[HALO : HALO + RAD]
    dy_grid[RAD : RAD + height, inner] = dy_ref[...].astype(floats)
    dy_grid[RAD + height : RAD + height + RAD, inner] = below[HALO : HALO + RAD]
    left, right = left[:, left.shape[1] - HALO :], right[:, :HALO]
    for strip, first in ((left, 0), (right, HALO + breadth)):
        span = slice(first, first + HALO)
        at = 0
        for grid, begin, count in (
            (x_grid, 0, HALO),
            (dy_grid, 0, RAD),
            (x_grid, HALO, height),
            (dy_grid, RAD, height),
            (x_grid, HALO + height, HALO),
            (dy_grid, RAD + height, RAD),
        ):
            grid[begin : begin + count, span] = strip[at : at + count]
            at += count

    tokens = x_grid[...].reshape(grid_rows * grid_cols, D_F)
    normed = (tokens * inverse_rms(tokens) * factor).astype(jnp.bfloat16)
    key_values = dot(normed, qkv_ref[:, D_F:]).astype(jnp.bfloat16).astype(floats)
    k_grid[...] = key_values[:, :D_F].reshape(grid_rows, grid_cols, D_F)
    v_grid[...] = key_values[:, D_F:].reshape(grid_rows, grid_cols, D_F)
    query_tokens = normed[RAD * grid_cols : (RAD + query_rows) * grid_cols]
    queries = dot(query_tokens, qkv_ref[:, :D_F]).astype(jnp.bfloat16).astype(floats) * scale
    q_grid[...] = queries.reshape(query_rows, grid_cols, D_F)
    cotangents = dy_grid[...].reshape(query_rows * grid_cols, D_F).astype(jnp.bfloat16)
    ups = dot(cotangents, out_ref[...], ((1,), (1,))).astype(jnp.bfloat16).astype(floats)
    u_grid[...] = ups.reshape(query_rows, grid_cols, D_F)

    keys_count, heads_count = extent * lanes_wide, H_F * side * side
    key_at = lax.broadcasted_iota(jnp.int32, (keys_count, heads_count), 0)
    query_at = lax.broadcasted_iota(jnp.int32, (keys_count, heads_count), 1)
    row_gap = (key_at // lanes_wide) - ((query_at // side) % side)
    col_gap = (key_at % lanes_wide) - (query_at % side)
    near = (row_gap >= 0) & (row_gap <= 2 * RAD) & (col_gap >= 0) & (col_gap <= 2 * RAD)
    bias_ref[...] = jnp.where(near, 0.0, -1e30)
    gx, gy = lax.axis_index("gx"), lax.axis_index("gy")
    row_low, col_low = HALO - gy * height, HALO - gx * breadth
    row_high = row_low + lax.axis_size("gy") * height
    col_high = col_low + lax.axis_size("gx") * breadth
    lone = lax.broadcasted_iota(jnp.int32, (keys_count, 1), 0)
    head_of = lax.broadcasted_iota(jnp.int32, (side * side, D_F), 1) // HD

    def spread(block):
        return jnp.concatenate(
            [jnp.where(head_of == h, block, 0.0).astype(jnp.bfloat16) for h in range(H_F)], axis=0
        )

    def collect(full):
        total = jnp.where(head_of == 0, full[: side * side], 0.0)
        for h in range(1, H_F):
            piece = full[h * side * side : (h + 1) * side * side]
            total = jnp.where(head_of == h, piece, total)
        return total.reshape(side, side, D_F)

    for block_row in range(query_rows // side):
        top = block_row * side
        for block_col in range((grid_cols - side) // side):
            start = block_col * side
            window = (slice(top, top + extent), slice(start, start + lanes_wide))
            keys = k_grid[window].reshape(keys_count, D_F).astype(jnp.bfloat16)
            values = v_grid[window].reshape(keys_count, D_F).astype(jnp.bfloat16)
            place = (slice(top, top + side), slice(start + RAD, start + RAD + side))
            wide_queries = spread(q_grid[place].reshape(side * side, D_F))
            wide_ups = spread(u_grid[place].reshape(side * side, D_F))
            key_row = lone // lanes_wide + top
            key_col = lone % lanes_wide + start
            inside = (
                (key_row >= row_low)
                & (key_row < row_high)
                & (key_col >= col_low)
                & (key_col < col_high)
            )
            scores = dot(keys, wide_queries, ((1,), (1,)))
            scores = scores + (bias_ref[...] + jnp.where(inside, 0.0, -1e30))
            raised = jnp.exp(scores - jnp.max(scores, axis=0, keepdims=True))
            shares = raised * (1.0 / jnp.sum(raised, axis=0, keepdims=True))
            products = dot(values, wide_ups, ((1,), (1,)))
            centre = jnp.sum(shares * products, axis=0, keepdims=True)
            slopes = (shares * (products - centre)).astype(jnp.bfloat16)
            weights = shares.astype(jnp.bfloat16)
            dv_grid[window] += dot(weights, wide_ups).reshape(extent, lanes_wide, D_F)
            dk_grid[window] += dot(slopes, wide_queries).reshape(extent, lanes_wide, D_F)
            block = (slice(top, top + side), slice(start, start + side))
            a_grid[block] = collect(dot(weights, values, ((0,), (0,))))
            dq_grid[block] = collect(dot(slopes, keys, ((0,), (0,))))

    count = height * breadth
    own_queries = (slice(RAD, RAD + height), slice(RAD, RAD + breadth))
    own_keys = (slice(HALO, HALO + height), inner)
    attended = a_grid[own_queries].reshape(count, D_F).astype(jnp.bfloat16)
    grad_q = (dq_grid[own_queries].reshape(count, D_F) * scale).astype(jnp.bfloat16)
    grad_k = dk_grid[own_keys].reshape(count, D_F).astype(jnp.bfloat16)
    grad_v = dv_grid[own_keys].reshape(count, D_F).astype(jnp.bfloat16)
    grad_proj = jnp.concatenate([grad_q, grad_k, grad_v], axis=1)
    picture = x_ref[...].reshape(count, D_F).astype(floats)
    inverse = inverse_rms(picture)
    own_normed = (picture * inverse * factor).astype(jnp.bfloat16)
    flat_cot = dy_ref[...].reshape(count, D_F)
    grads = jnp.concatenate(
        [
            dot(own_normed, grad_proj, ((0,), (0,))),
            dot(attended, flat_cot, ((0,), (0,))),
        ],
        axis=1,
    )
    half, columns = keep_ref.shape[0], keep_ref.shape[1]
    total_ref[...] = grads.reshape(total_ref.shape)
    for low in range(2):
        target = (keep_ref, send_ref)[low]
        for high in range(half):
            for row in range(columns):
                block = (gx ^ (2 * high + low)) * columns + row
                target[high, row] = total_ref[block].astype(target.dtype)
    down = dot(grad_proj, qkv_ref[...], ((1,), (1,)))
    dx_ref[...] = norm_backward(picture, inverse, factor, down).reshape(height, breadth, D_F)


def fine_block(peers, picture, *operands):
    height, breadth = picture.shape[0], picture.shape[1]
    query_rows = round_up(height + 2 * RAD, side)
    query_cols = round_up(breadth + 2 * RAD, side)
    grid_rows, grid_cols = query_rows + 2 * RAD, query_cols + side
    across, down = peers
    rows = D_F // (across * down)
    halves = (across // 2, down, rows, 4 * D_F)
    vmem = pl.BlockSpec(memory_space=pltpu.VMEM)
    wide = pltpu.VMEM((grid_rows, grid_cols, D_F), jnp.float32)
    middle = pltpu.VMEM((query_rows, grid_cols, D_F), jnp.float32)
    small = pltpu.VMEM((query_rows, query_cols, D_F), jnp.float32)
    return pl.pallas_call(
        fine_body,
        out_shape=(
            jax.ShapeDtypeStruct((height, breadth, D_F), jnp.bfloat16),
            jax.ShapeDtypeStruct(halves, jnp.float32),
            jax.ShapeDtypeStruct(halves, jnp.bfloat16),
        ),
        in_specs=[vmem] * 9,
        out_specs=(vmem, vmem, vmem),
        scratch_shapes=[
            wide,
            middle,
            wide,
            wide,
            middle,
            middle,
            wide,
            wide,
            small,
            small,
            pltpu.VMEM((extent * lanes_wide, H_F * side * side), jnp.float32),
            pltpu.VMEM((across * down, rows, 4 * D_F), jnp.float32),
        ],
        compiler_params=pltpu.CompilerParams(vmem_limit_bytes=vmem_bytes),
        name="fine_block",
    )(picture, *operands)


def coarse_body(
    x_ref,
    dy_ref,
    factor_ref,
    qkv_hbm,
    out_hbm,
    parts_ref,
    grads_ref,
    qkv_ref,
    out_ref,
    arrived,
):
    fetches = [
        pltpu.make_async_copy(qkv_hbm, qkv_ref, arrived.at[0]),
        pltpu.make_async_copy(out_hbm, out_ref, arrived.at[1]),
    ]
    for fetch in fetches:
        fetch.start()
    tokens = x_ref[...].astype(jnp.float32)
    normed = (tokens * inverse_rms(tokens) * factor_ref[...]).astype(jnp.bfloat16)
    cot = dy_ref[...]
    for fetch in fetches:
        fetch.wait()
    flat_qkv = qkv_ref[...].reshape(3 * HD, D_C)
    out_rows = out_ref[...]
    projected = dot(normed, flat_qkv, ((1,), (1,))).astype(jnp.bfloat16)
    queries, keys, values = projected[:, :HD], projected[:, HD : 2 * HD], projected[:, 2 * HD :]
    ups = dot(cot, out_rows, ((1,), (1,))).astype(jnp.bfloat16)
    scores = dot(queries, keys, ((1,), (1,))) * scale
    raised = jnp.exp(scores - jnp.max(scores, axis=-1, keepdims=True))
    shares = raised * (1.0 / jnp.sum(raised, axis=-1, keepdims=True))
    weights = shares.astype(jnp.bfloat16)
    mixed = dot(weights, values).astype(jnp.bfloat16)
    products = dot(ups, values, ((1,), (1,)))
    centre = jnp.sum(shares * products, axis=-1, keepdims=True)
    slopes = (shares * (products - centre)).astype(jnp.bfloat16)
    grad_q = (dot(slopes, keys) * scale).astype(jnp.bfloat16)
    grad_k = (dot(slopes, queries, ((0,), (0,))) * scale).astype(jnp.bfloat16)
    grad_v = dot(weights, ups, ((0,), (0,))).astype(jnp.bfloat16)
    stacked = jnp.concatenate([grad_q, grad_k, grad_v], axis=1)
    parts_ref[...] = dot(stacked, flat_qkv).astype(jnp.bfloat16)
    grads_ref[: 3 * HD] = dot(stacked, normed, ((0,), (0,))).astype(grads_ref.dtype)
    grads_ref[3 * HD :] = dot(mixed, cot, ((0,), (0,))).astype(grads_ref.dtype)


def coarse_block(tokens, cotangents, factor, head_qkv, head_out):
    count = tokens.shape[0]
    vmem = pl.BlockSpec(memory_space=pltpu.VMEM)
    return pl.pallas_call(
        coarse_body,
        out_shape=(
            jax.ShapeDtypeStruct((count, D_C), jnp.bfloat16),
            jax.ShapeDtypeStruct((4 * HD, D_C), jnp.bfloat16),
        ),
        in_specs=[vmem] * 3 + [pl.BlockSpec(memory_space=pltpu.HBM)] * 2,
        out_specs=(vmem, vmem),
        scratch_shapes=[
            pltpu.VMEM(head_qkv.shape, jnp.bfloat16),
            pltpu.VMEM(head_out.shape, jnp.bfloat16),
            pltpu.SemaphoreType.DMA((2,)),
        ],
        compiler_params=pltpu.CompilerParams(vmem_limit_bytes=vmem_bytes),
        name="coarse_block",
    )(tokens, cotangents, factor, head_qkv, head_out)


def row_edges_body(x_low, x_high, dy_low, dy_high, near_ref, far_ref):
    odd = odd_rank("gy")

    def fill(low_ref, high_ref):
        low_ref[:HALO], low_ref[HALO:] = x_low[...], dy_low[...]
        high_ref[:HALO], high_ref[HALO:] = x_high[...], dy_high[...]

    @pl.when(odd)
    def _():
        fill(near_ref, far_ref)

    @pl.when(jnp.logical_not(odd))
    def _():
        fill(far_ref, near_ref)


def row_edges(picture, cotangent):
    vmem = pl.BlockSpec(memory_space=pltpu.VMEM)
    height = picture.shape[0]
    shape = jax.ShapeDtypeStruct((HALO + RAD,) + picture.shape[1:], jnp.bfloat16)
    return pl.pallas_call(
        row_edges_body,
        out_shape=(shape, shape),
        in_specs=[vmem] * 4,
        out_specs=(vmem, vmem),
        compiler_params=pltpu.CompilerParams(vmem_limit_bytes=vmem_bytes),
        name="row_edges",
    )(picture[:HALO], picture[height - HALO :], cotangent[:RAD], cotangent[height - RAD :])


def col_edges_body(x_ref, dy_ref, row_far_ref, row_near_ref, near_ref, far_ref):
    above, below = in_order("gy", row_near_ref, row_far_ref)
    breadth = x_ref.shape[1]
    odd = odd_rank("gx")
    at = 0
    for rows in (above, x_ref[...].astype(jnp.float32), dy_ref[...].astype(jnp.float32), below):
        first, final = rows[:, :side], rows[:, breadth - side :]
        span = slice(at, at + rows.shape[0])
        near_ref[span] = jnp.where(odd, first, final).astype(jnp.bfloat16)
        far_ref[span] = jnp.where(odd, final, first).astype(jnp.bfloat16)
        at += rows.shape[0]


def col_edges(picture, cotangent, row_far, row_near):
    vmem = pl.BlockSpec(memory_space=pltpu.VMEM)
    rows = 2 * (picture.shape[0] + row_near.shape[0])
    shape = jax.ShapeDtypeStruct((rows, side, D_F), jnp.bfloat16)
    return pl.pallas_call(
        col_edges_body,
        out_shape=(shape, shape),
        in_specs=[vmem] * 4,
        out_specs=(vmem, vmem),
        compiler_params=pltpu.CompilerParams(vmem_limit_bytes=vmem_bytes),
        name="col_edges",
    )(picture, cotangent, row_far, row_near)


def pack_body(first, second, x_ref, dy_ref, own_ref):
    own_ref[:, :D_C] = x_ref[...].astype(jnp.float32).reshape(-1, D_C).astype(jnp.bfloat16)
    own_ref[:, D_C:] = dy_ref[...].astype(jnp.float32).reshape(-1, D_C).astype(jnp.bfloat16)


def packed(after, tokens, cotangents):
    vmem = pl.BlockSpec(memory_space=pltpu.VMEM)
    count = tokens.shape[0] * tokens.shape[1]
    return pl.pallas_call(
        pack_body,
        out_shape=jax.ShapeDtypeStruct((count, 2 * D_C), jnp.bfloat16),
        in_specs=[pl.BlockSpec(memory_space=pl.ANY)] * 2 + [vmem] * 2,
        out_specs=vmem,
        compiler_params=pltpu.CompilerParams(vmem_limit_bytes=vmem_bytes),
        name="pack_coarse",
    )(*after, tokens, cotangents)


def factors_body(step, fine_gain, coarse_gain, fine_freq, coarse_freq, fine_ref, coarse_ref):
    time = step[0].astype(jnp.float32)
    fine_ref[...] = fine_gain[...] * (1.0 + 0.5 * jnp.cos(time * fine_freq[...]))
    coarse_ref[...] = coarse_gain[...] * (1.0 + 0.5 * jnp.cos(time * coarse_freq[...]))


def time_factors(step, fine_gain, coarse_gain):
    vmem = pl.BlockSpec(memory_space=pltpu.VMEM)
    return pl.pallas_call(
        factors_body,
        out_shape=(
            jax.ShapeDtypeStruct((1, D_F), jnp.float32),
            jax.ShapeDtypeStruct((1, D_C), jnp.float32),
        ),
        in_specs=[pl.BlockSpec(memory_space=pltpu.SMEM)] + [vmem] * 4,
        out_specs=(vmem, vmem),
        compiler_params=pltpu.CompilerParams(vmem_limit_bytes=vmem_bytes),
        name="time_factors",
    )(step, fine_gain[None], coarse_gain[None], frequencies(D_F), frequencies(D_C))


def pair_sum_body(own, first, second, qkv_ref, out_ref):
    for part in range(4):
        come = (first, second)[part // 2][(part % 2) * HD : (part % 2 + 1) * HD]
        total = own[part * HD : (part + 1) * HD].astype(jnp.float32) + come.astype(jnp.float32)
        if part < 3:
            qkv_ref[part] = total.astype(jnp.bfloat16)
        else:
            out_ref[...] = total.astype(jnp.bfloat16)


def pair_sum(own, first, second):
    vmem = pl.BlockSpec(memory_space=pltpu.VMEM)
    return pl.pallas_call(
        pair_sum_body,
        out_shape=(
            jax.ShapeDtypeStruct((3, HD, D_C), jnp.bfloat16),
            jax.ShapeDtypeStruct((HD, D_C), jnp.bfloat16),
        ),
        in_specs=[vmem] * 3,
        out_specs=(vmem, vmem),
        compiler_params=pltpu.CompilerParams(vmem_limit_bytes=vmem_bytes),
        name="pair_sum",
    )(own, first, second)


def block_copies(near_ref, low, qkv_hbm, out_hbm, sems):
    highs, rows = near_ref.shape[0], near_ref.shape[1]
    copies = []
    for high in range(highs):
        block = lax.axis_index("gx") ^ (2 * high + low)
        at = pl.ds(pl.multiple_of(block * rows, rows), rows)
        for part, target in enumerate((qkv_hbm, out_hbm)):
            lanes = (slice(0, 3 * D_F), slice(3 * D_F, 4 * D_F))[part]
            copies.append(
                pltpu.make_async_copy(
                    near_ref.at[high, :, lanes], target.at[at, :], sems.at[high, part]
                )
            )
    for copy in copies:
        copy.start()
    return copies


def near_body(near_ref, x_ref, factor_ref, kept_ref, come_ref, qkv_hbm, out_hbm, dx_ref, sems):
    copies = block_copies(near_ref, 0, qkv_hbm, out_hbm, sems)
    tokens = x_ref[...].astype(jnp.float32).reshape(-1, D_C)
    upstream = kept_ref[...] + come_ref[...].astype(jnp.float32)
    grads = norm_backward(tokens, inverse_rms(tokens), factor_ref[...], upstream)
    dx_ref[...] = grads.astype(jnp.float32).reshape(dx_ref.shape).astype(jnp.bfloat16)
    for copy in copies:
        copy.wait()


def far_body(far_ref, qkv_in, out_in, qkv_hbm, out_hbm, sems):
    for copy in block_copies(far_ref, 1, qkv_hbm, out_hbm, sems):
        copy.wait()


def near_step(near, tokens, *operands):
    vmem = pl.BlockSpec(memory_space=pltpu.VMEM)
    hbm = pl.BlockSpec(memory_space=pltpu.HBM)
    return pl.pallas_call(
        near_body,
        out_shape=(
            jax.ShapeDtypeStruct((D_F, 3 * D_F), jnp.bfloat16),
            jax.ShapeDtypeStruct((D_F, D_F), jnp.bfloat16),
            jax.ShapeDtypeStruct(tokens.shape, jnp.bfloat16),
        ),
        in_specs=[vmem] * 5,
        out_specs=(hbm, hbm, vmem),
        scratch_shapes=[pltpu.SemaphoreType.DMA((near.shape[0], 2))],
        compiler_params=pltpu.CompilerParams(vmem_limit_bytes=vmem_bytes),
        name="near_step",
    )(near, tokens, *operands)


def far_step(far, qkv, out):
    vmem = pl.BlockSpec(memory_space=pltpu.VMEM)
    hbm = pl.BlockSpec(memory_space=pltpu.HBM)
    return pl.pallas_call(
        far_body,
        out_shape=(
            jax.ShapeDtypeStruct(qkv.shape, qkv.dtype),
            jax.ShapeDtypeStruct(out.shape, out.dtype),
        ),
        in_specs=[vmem, hbm, hbm],
        out_specs=(hbm, hbm),
        input_output_aliases={1: 0, 2: 1},
        scratch_shapes=[pltpu.SemaphoreType.DMA((far.shape[0], 2))],
        compiler_params=pltpu.CompilerParams(vmem_limit_bytes=vmem_bytes),
        name="far_step",
    )(far, qkv, out)


def neighbours(to_near, to_far, axis):
    peers = lax.axis_size(axis)
    near = [(i, i ^ 1) for i in range(peers)]
    far = [(i, i + 1 if i % 2 else i - 1) for i in range(1, peers - 1)]
    from_far = lax.ppermute(to_far, axis, far)
    return lax.ppermute(to_near, axis, near), from_far


def swapped(value, axis, mask):
    return lax.ppermute(value, axis, [(i, i ^ mask) for i in range(lax.axis_size(axis))])


def tied(*arrays):
    return lax.optimization_barrier(arrays)


def batch_sum(partial):
    if lax.axis_size("batch") != 2:
        return lax.psum(partial, "batch")
    return wide(partial) + wide(swapped(partial, "batch", 1))


def wide(value):
    return value.astype(jnp.float32)


def narrow(value):
    return value.astype(jnp.bfloat16)


def all_rows(piece):
    downs = lax.axis_size("gy")
    return jnp.stack([piece] + [swapped(piece, "gy", row) for row in range(1, downs)])


def local(
    x_fine,
    dy_fine,
    x_coarse,
    dy_coarse,
    timestep,
    fine_gain,
    coarse_gain,
    fine_qkv,
    fine_out,
    coarse_qkv,
    coarse_out,
):
    picture, cotangent = x_fine[0], dy_fine[0]
    across, downs = lax.axis_size("gx"), lax.axis_size("gy")
    assert across == 4 and downs & (downs - 1) == 0

    payloads = row_edges(picture, cotangent)
    row_near, row_far = neighbours(*payloads, "gy")
    own = packed(payloads, x_coarse[0], dy_coarse[0])
    count = own.shape[0]
    row_group = all_rows(own)
    edges = col_edges(picture, cotangent, row_far, row_near)
    *edges, step, gain_f, gain_c = tied(*edges, timestep, fine_gain, coarse_gain)
    col_near, col_far = neighbours(*edges, "gx")
    factor, coarse_factor = time_factors(step, gain_f, gain_c)
    cross = swapped(row_group, "gx", 2)
    beside = swapped(row_group, "gx", 1)
    col_far, col_near, row_group, factor = tied(col_far, col_near, row_group, factor)
    dx_picture, fine_keep, fine_send = fine_block(
        (across, downs),
        picture,
        cotangent,
        row_far,
        row_near,
        col_far,
        col_near,
        factor,
        fine_qkv,
        fine_out,
    )
    fine_half = fine_keep + wide(swapped(fine_send, "gx", 1))
    opposite = swapped(cross, "gx", 1)
    fine_half, opposite = tied(fine_half, opposite)

    fine_quarter = narrow(fine_half[0] + wide(swapped(narrow(fine_half[1]), "gx", 2)))
    everyone = jnp.stack([row_group, cross, beside, opposite]).reshape(-1, 2 * D_C)
    parts, coarse_partial = coarse_block(
        everyone[:, :D_C], everyone[:, D_C:], coarse_factor, coarse_qkv, coarse_out
    )
    fine_quarter, parts, coarse_partial = tied(fine_quarter, parts, coarse_partial)

    rows = D_F // across
    fine_quarter = narrow(batch_sum(fine_quarter)).reshape(rows, 4 * D_F)
    parts = parts.reshape(2, 2, downs, count, D_C)
    coarse_kept = wide(parts[0]) + wide(swapped(parts[1], "gx", 1))
    fine_quarter, coarse_kept, coarse_partial = tied(fine_quarter, coarse_kept, coarse_partial)

    pair_batch = lax.axis_size("batch") == 2
    halves = (coarse_partial[: 2 * HD], coarse_partial[2 * HD :])
    others = [swapped(half, "batch", 1) if pair_batch else half for half in halves]
    mask = 1
    while mask < downs:
        last = 2 * mask == downs
        coarse_kept = coarse_kept.reshape(2, -1, 2, count, D_C)
        sent = narrow(coarse_kept[:, :, 1]).reshape(-1, D_C)
        come = swapped(jnp.concatenate([fine_quarter, sent], axis=0), "gy", mask)
        coarse_kept = coarse_kept[:, :, 0]
        coarse_kept = coarse_kept + wide(come[rows:]).reshape(coarse_kept.shape)
        fine_quarter = narrow(wide(fine_quarter) + wide(come[:rows]))
        at = int(last)
        fine_quarter, coarse_kept, others[at] = tied(fine_quarter, coarse_kept, others[at])
        mask *= 2

    coarse_kept = coarse_kept.reshape(2, count, D_C)
    come = swapped(jnp.concatenate([fine_quarter, narrow(coarse_kept[1])], axis=0), "gx", 2)
    if pair_batch:
        grad_coarse_qkv, grad_coarse_out = pair_sum(coarse_partial, *others)
    else:
        coarse_sum = narrow(batch_sum(wide(coarse_partial)))
        grad_coarse_qkv = coarse_sum[: 3 * HD].reshape(coarse_qkv.shape)
        grad_coarse_out = coarse_sum[3 * HD :]
    come, grad_coarse_qkv, grad_coarse_out = tied(come, grad_coarse_qkv, grad_coarse_out)
    fine_pair = jnp.stack([fine_quarter, come[:rows]])
    near_qkv, near_out, dx_coarse = near_step(
        fine_pair, x_coarse[0], coarse_factor, coarse_kept[0], come[rows:]
    )
    far_pair = swapped(fine_pair, "gx", 1)
    far_pair, near_qkv, near_out = tied(far_pair, near_qkv, near_out)
    grad_qkv, grad_out = far_step(far_pair, near_qkv, near_out)
    return (
        dx_picture[None],
        dx_coarse[None],
        grad_qkv,
        grad_out,
        grad_coarse_qkv,
        grad_coarse_out,
    )


def solution(mesh):
    placed = (
        P("batch", "gy", "gx", None),
        P("batch", "gy", "gx", None),
        P("batch", "gy", "gx", None),
        P("batch", "gy", "gx", None),
        P("batch"),
        P(),
        P(),
        P(),
        P(),
        P(None, plane_spec, None),
        P(plane_spec, None),
    )
    return jax.shard_map(
        local,
        mesh=mesh,
        in_specs=placed,
        out_specs=(
            P("batch", "gy", "gx", None),
            P("batch", "gy", "gx", None),
            P(),
            P(),
            P(None, plane_spec, None),
            P(plane_spec, None),
        ),
        check_vma=False,
    )


plane_spec = ("gy", "gx")
```

```python
import math

import jax
import jax.numpy as jnp
import numpy as np
from jax import lax
from jax.experimental import pallas as pl
from jax.experimental.pallas import tpu as pltpu
from jax.sharding import PartitionSpec as P

D_F = 256
H_F = 4
D_C = 1024
HD = 64
RAD = 3
HALO = 2 * RAD

eps = 1e-06
log_span = math.log(1000.0)
side = 8
extent = side + 2 * RAD
lanes_wide = 16
thin = 4
scale = 1.0 / math.sqrt(HD)
vmem_bytes = 48 * 1024 * 1024


def dot(first, second, dims=((1,), (0,))):
    return lax.dot_general(first, second, (dims, ((), ())), preferred_element_type=jnp.float32)


def frequencies(channels):
    steps = np.float32(-log_span) * np.arange(channels, dtype=np.float32) / np.float32(channels)
    return np.exp(steps)[None]


def time_gain(step_ref, gain_ref, freq_ref):
    return gain_ref[...] * (1.0 + 0.5 * jnp.cos(step_ref[...].astype(jnp.float32) * freq_ref[...]))


def odd_rank(axis):
    return lax.axis_index(axis) & 1 == 1


def inverse_rms(floats):
    return lax.rsqrt(jnp.mean(floats * floats, axis=-1, keepdims=True) + eps)


def norm_backward(floats, inverse, factor, upstream):
    scaled = upstream * factor
    middle = jnp.mean(floats * scaled, axis=-1, keepdims=True)
    return (inverse * scaled - floats * inverse * inverse * inverse * middle).astype(jnp.bfloat16)


def round_up(value, multiple):
    return -(-value // multiple) * multiple


def in_order(axis, near, far):
    odd = odd_rank(axis)
    first, second = near[...].astype(jnp.float32), far[...].astype(jnp.float32)
    return jnp.where(odd, first, second), jnp.where(odd, second, first)


def fine_body(
    x_ref,
    dy_ref,
    row_far_ref,
    row_near_ref,
    col_far_ref,
    col_near_ref,
    step_ref,
    gain_ref,
    freq_ref,
    qkv_ref,
    out_ref,
    dx_ref,
    keep_ref,
    send_ref,
    x_grid,
    dy_grid,
    k_grid,
    v_grid,
    q_grid,
    u_grid,
    dk_grid,
    dv_grid,
    dq_grid,
    a_grid,
    bias_ref,
    thin_bias_ref,
    total_ref,
):
    height, breadth = x_ref.shape[0], x_ref.shape[1]
    grid_rows, grid_cols = x_grid.shape[0], x_grid.shape[1]
    query_rows = dy_grid.shape[0]
    floats = jnp.float32
    factor = time_gain(step_ref, gain_ref, freq_ref)

    for grid, rows in ((x_grid, height + 2 * HALO), (dy_grid, height + 2 * RAD)):
        grid[rows:] = jnp.zeros((grid.shape[0] - rows,) + grid.shape[1:], floats)
        cols = breadth + 2 * HALO
        grid[:rows, cols:] = jnp.zeros((rows, grid_cols - cols, D_F), floats)
    dk_grid[...] = jnp.zeros_like(dk_grid)
    dv_grid[...] = jnp.zeros_like(dv_grid)
    inner = slice(HALO, HALO + breadth)
    above, below = in_order("gy", row_near_ref, row_far_ref)
    left, right = in_order("gx", col_near_ref, col_far_ref)
    x_grid[0:HALO, inner] = above[0:HALO]
    x_grid[HALO : HALO + height, inner] = x_ref[...].astype(floats)
    x_grid[HALO + height : HALO + height + HALO, inner] = below[0:HALO]
    dy_grid[0:RAD, inner] = above[HALO : HALO + RAD]
    dy_grid[RAD : RAD + height, inner] = dy_ref[...].astype(floats)
    dy_grid[RAD + height : RAD + height + RAD, inner] = below[HALO : HALO + RAD]
    left, right = left[:, left.shape[1] - HALO :], right[:, :HALO]
    for strip, first in ((left, 0), (right, HALO + breadth)):
        span = slice(first, first + HALO)
        at = 0
        for grid, begin, count in (
            (x_grid, 0, HALO),
            (dy_grid, 0, RAD),
            (x_grid, HALO, height),
            (dy_grid, RAD, height),
            (x_grid, HALO + height, HALO),
            (dy_grid, RAD + height, RAD),
        ):
            grid[begin : begin + count, span] = strip[at : at + count]
            at += count

    tokens = x_grid[...].reshape(grid_rows * grid_cols, D_F)
    normed = (tokens * inverse_rms(tokens) * factor).astype(jnp.bfloat16)
    key_values = dot(normed, qkv_ref[:, D_F:]).astype(jnp.bfloat16).astype(floats)
    k_grid[...] = key_values[:, :D_F].reshape(grid_rows, grid_cols, D_F)
    v_grid[...] = key_values[:, D_F:].reshape(grid_rows, grid_cols, D_F)
    query_tokens = normed[RAD * grid_cols : (RAD + query_rows) * grid_cols]
    queries = dot(query_tokens, qkv_ref[:, :D_F]).astype(jnp.bfloat16).astype(floats) * scale
    q_grid[...] = queries.reshape(query_rows, grid_cols, D_F)
    cotangents = dy_grid[...].reshape(query_rows * grid_cols, D_F).astype(jnp.bfloat16)
    ups = dot(cotangents, out_ref[...], ((1,), (1,))).astype(jnp.bfloat16).astype(floats)
    u_grid[...] = ups.reshape(query_rows, grid_cols, D_F)

    gx, gy = lax.axis_index("gx"), lax.axis_index("gy")
    row_low, col_low = HALO - gy * height, HALO - gx * breadth
    row_high = row_low + lax.axis_size("gy") * height
    col_high = col_low + lax.axis_size("gx") * breadth

    def window_bias(query_rows):
        shape = ((query_rows + 2 * RAD) * lanes_wide, H_F * query_rows * side)
        key_at = lax.broadcasted_iota(jnp.int32, shape, 0)
        query_at = lax.broadcasted_iota(jnp.int32, shape, 1)
        row_gap = (key_at // lanes_wide) - ((query_at // side) % query_rows)
        col_gap = (key_at % lanes_wide) - (query_at % side)
        near = (row_gap >= 0) & (row_gap <= 2 * RAD) & (col_gap >= 0) & (col_gap <= 2 * RAD)
        return jnp.where(near, 0.0, -1e30)

    bias_ref[...] = window_bias(side)
    thin_bias_ref[...] = window_bias(thin)

    def head_of(rows):
        return lax.broadcasted_iota(jnp.int32, (rows, D_F), 1) // HD

    def spread(block):
        block = block.reshape(-1, D_F)
        heads = head_of(block.shape[0])
        return jnp.concatenate(
            [jnp.where(heads == h, block, 0.0).astype(jnp.bfloat16) for h in range(H_F)], axis=0
        )

    def collect(full):
        rows = full.shape[0] // H_F
        heads = head_of(rows)
        total = jnp.where(heads == 0, full[:rows], 0.0)
        for h in range(1, H_F):
            total = jnp.where(heads == h, full[h * rows : (h + 1) * rows], total)
        return total.reshape(rows // side, side, D_F)

    def attend(top, start, query_rows, near_bias, live):
        key_rows = query_rows + 2 * RAD
        window = (slice(top, top + key_rows), slice(start, start + lanes_wide))
        keys = k_grid[window].reshape(-1, D_F).astype(jnp.bfloat16)
        values = v_grid[window].reshape(-1, D_F).astype(jnp.bfloat16)
        place = (slice(top, top + query_rows), slice(start + RAD, start + RAD + side))
        wide_queries = spread(q_grid[place])
        ups = u_grid[place]
        if live < query_rows:
            row = lax.broadcasted_iota(jnp.int32, ups.shape, 0)
            ups = jnp.where(row < live, ups, 0.0)
        wide_ups = spread(ups)
        lone = lax.broadcasted_iota(jnp.int32, (key_rows * lanes_wide, 1), 0)
        key_row, key_col = lone // lanes_wide + top, lone % lanes_wide + start
        inside = (key_row >= row_low) & (key_row < row_high)
        inside = inside & (key_col >= col_low) & (key_col < col_high)
        scores = dot(keys, wide_queries, ((1,), (1,)))
        scores = scores + (near_bias[...] + jnp.where(inside, 0.0, -1e30))
        raised = jnp.exp(scores - jnp.max(scores, axis=0, keepdims=True))
        shares = raised * (1.0 / jnp.sum(raised, axis=0, keepdims=True))
        products = dot(values, wide_ups, ((1,), (1,)))
        centre = jnp.sum(shares * products, axis=0, keepdims=True)
        slopes = (shares * (products - centre)).astype(jnp.bfloat16)
        weights = shares.astype(jnp.bfloat16)
        first, final = max(top, HALO), min(top + key_rows, HALO + height)
        kept = slice((first - top) * lanes_wide, (final - top) * lanes_wide)
        target = (slice(first - HALO, final - HALO), slice(start, start + lanes_wide))
        shape = (final - first, lanes_wide, D_F)
        dv_grid[target] += dot(weights[kept], wide_ups).reshape(shape)
        dk_grid[target] += dot(slopes[kept], wide_queries).reshape(shape)
        return keys, values, slopes, weights

    for start in range(0, grid_cols - side, side):
        for top in range(RAD, RAD + height, side):
            keys, values, slopes, weights = attend(top, start, side, bias_ref, side)
            block = (slice(top - RAD, top - RAD + side), slice(start, start + side))
            a_grid[block] = collect(dot(weights, values, ((0,), (0,))))
            dq_grid[block] = collect(dot(slopes, keys, ((0,), (0,))))
        attend(0, start, thin, thin_bias_ref, RAD)
        attend(RAD + height, start, thin, thin_bias_ref, RAD)

    count = height * breadth
    own_queries = (slice(0, height), slice(RAD, RAD + breadth))
    own_keys = (slice(0, height), inner)
    attended = a_grid[own_queries].reshape(count, D_F).astype(jnp.bfloat16)
    grad_q = (dq_grid[own_queries].reshape(count, D_F) * scale).astype(jnp.bfloat16)
    grad_k = dk_grid[own_keys].reshape(count, D_F).astype(jnp.bfloat16)
    grad_v = dv_grid[own_keys].reshape(count, D_F).astype(jnp.bfloat16)
    grad_proj = jnp.concatenate([grad_q, grad_k, grad_v], axis=1)
    picture = x_ref[...].reshape(count, D_F).astype(floats)
    inverse = inverse_rms(picture)
    own_normed = (picture * inverse * factor).astype(jnp.bfloat16)
    flat_cot = dy_ref[...].reshape(count, D_F)
    grads = jnp.concatenate(
        [
            dot(own_normed, grad_proj, ((0,), (0,))),
            dot(attended, flat_cot, ((0,), (0,))),
        ],
        axis=1,
    )
    half, columns = keep_ref.shape[0], keep_ref.shape[1]
    total_ref[...] = grads.reshape(total_ref.shape)
    for low in range(2):
        target = (keep_ref, send_ref)[low]
        for high in range(half):
            for row in range(columns):
                block = (gx ^ (2 * high + low)) * columns + row
                target[high, row] = total_ref[block].astype(target.dtype)
    down = dot(grad_proj, qkv_ref[...], ((1,), (1,)))
    dx_ref[...] = norm_backward(picture, inverse, factor, down).reshape(height, breadth, D_F)


def fine_block(peers, picture, *operands):
    height, breadth = picture.shape[0], picture.shape[1]
    query_rows = RAD + height + thin
    query_cols = round_up(breadth + 2 * RAD, side)
    grid_rows, grid_cols = query_rows + 2 * RAD, query_cols + side
    across, down = peers
    rows = D_F // (across * down)
    halves = (across // 2, down, rows, 4 * D_F)
    vmem = pl.BlockSpec(memory_space=pltpu.VMEM)
    wide = pltpu.VMEM((grid_rows, grid_cols, D_F), jnp.float32)
    middle = pltpu.VMEM((query_rows, grid_cols, D_F), jnp.float32)
    small = pltpu.VMEM((height, query_cols, D_F), jnp.float32)
    strip = pltpu.VMEM((height, grid_cols, D_F), jnp.float32)
    return pl.pallas_call(
        fine_body,
        out_shape=(
            jax.ShapeDtypeStruct((height, breadth, D_F), jnp.bfloat16),
            jax.ShapeDtypeStruct(halves, jnp.float32),
            jax.ShapeDtypeStruct(halves, jnp.bfloat16),
        ),
        in_specs=[vmem] * 11,
        out_specs=(vmem, vmem, vmem),
        scratch_shapes=[
            wide,
            middle,
            wide,
            wide,
            middle,
            middle,
            strip,
            strip,
            small,
            small,
            pltpu.VMEM((extent * lanes_wide, H_F * side * side), jnp.float32),
            pltpu.VMEM(((thin + 2 * RAD) * lanes_wide, H_F * thin * side), jnp.float32),
            pltpu.VMEM((across * down, rows, 4 * D_F), jnp.float32),
        ],
        compiler_params=pltpu.CompilerParams(vmem_limit_bytes=vmem_bytes),
        name="fine_block",
    )(picture, *operands)


def coarse_body(
    x_ref,
    dy_ref,
    step_ref,
    gain_ref,
    freq_ref,
    qkv_hbm,
    out_hbm,
    parts_ref,
    grads_ref,
    factor_ref,
    qkv_ref,
    out_ref,
    arrived,
):
    fetches = [
        pltpu.make_async_copy(qkv_hbm, qkv_ref, arrived.at[0]),
        pltpu.make_async_copy(out_hbm, out_ref, arrived.at[1]),
    ]
    for fetch in fetches:
        fetch.start()
    tokens = x_ref[...].astype(jnp.float32)
    factor_ref[...] = time_gain(step_ref, gain_ref, freq_ref)
    normed = (tokens * inverse_rms(tokens) * factor_ref[...]).astype(jnp.bfloat16)
    cot = dy_ref[...]
    for fetch in fetches:
        fetch.wait()
    flat_qkv = qkv_ref[...].reshape(3 * HD, D_C)
    out_rows = out_ref[...]
    projected = dot(normed, flat_qkv, ((1,), (1,))).astype(jnp.bfloat16)
    queries, keys, values = projected[:, :HD], projected[:, HD : 2 * HD], projected[:, 2 * HD :]
    ups = dot(cot, out_rows, ((1,), (1,))).astype(jnp.bfloat16)
    scores = dot(queries, keys, ((1,), (1,))) * scale
    raised = jnp.exp(scores - jnp.max(scores, axis=-1, keepdims=True))
    shares = raised * (1.0 / jnp.sum(raised, axis=-1, keepdims=True))
    weights = shares.astype(jnp.bfloat16)
    mixed = dot(weights, values).astype(jnp.bfloat16)
    products = dot(ups, values, ((1,), (1,)))
    centre = jnp.sum(shares * products, axis=-1, keepdims=True)
    slopes = (shares * (products - centre)).astype(jnp.bfloat16)
    grad_q = (dot(slopes, keys) * scale).astype(jnp.bfloat16)
    grad_k = (dot(slopes, queries, ((0,), (0,))) * scale).astype(jnp.bfloat16)
    grad_v = dot(weights, ups, ((0,), (0,))).astype(jnp.bfloat16)
    stacked = jnp.concatenate([grad_q, grad_k, grad_v], axis=1)
    parts_ref[...] = dot(stacked, flat_qkv).astype(jnp.bfloat16)
    grads_ref[: 3 * HD] = dot(stacked, normed, ((0,), (0,))).astype(grads_ref.dtype)
    grads_ref[3 * HD :] = dot(mixed, cot, ((0,), (0,))).astype(grads_ref.dtype)


def coarse_block(tokens, cotangents, step, gain, head_qkv, head_out):
    count = tokens.shape[0]
    vmem = pl.BlockSpec(memory_space=pltpu.VMEM)
    return pl.pallas_call(
        coarse_body,
        out_shape=(
            jax.ShapeDtypeStruct((count, D_C), jnp.bfloat16),
            jax.ShapeDtypeStruct((4 * HD, D_C), jnp.bfloat16),
            jax.ShapeDtypeStruct((1, D_C), jnp.float32),
        ),
        in_specs=[vmem] * 5 + [pl.BlockSpec(memory_space=pltpu.HBM)] * 2,
        out_specs=(vmem, vmem, vmem),
        scratch_shapes=[
            pltpu.VMEM(head_qkv.shape, jnp.bfloat16),
            pltpu.VMEM(head_out.shape, jnp.bfloat16),
            pltpu.SemaphoreType.DMA((2,)),
        ],
        compiler_params=pltpu.CompilerParams(vmem_limit_bytes=vmem_bytes),
        name="coarse_block",
    )(tokens, cotangents, step, gain[None], frequencies(D_C), head_qkv, head_out)


def row_edges_body(x_low, x_high, dy_low, dy_high, near_ref, far_ref):
    odd = odd_rank("gy")

    def fill(low_ref, high_ref):
        low_ref[:HALO], low_ref[HALO:] = x_low[...], dy_low[...]
        high_ref[:HALO], high_ref[HALO:] = x_high[...], dy_high[...]

    @pl.when(odd)
    def _():
        fill(near_ref, far_ref)

    @pl.when(jnp.logical_not(odd))
    def _():
        fill(far_ref, near_ref)


def row_edges(picture, cotangent):
    vmem = pl.BlockSpec(memory_space=pltpu.VMEM)
    height = picture.shape[0]
    shape = jax.ShapeDtypeStruct((HALO + RAD,) + picture.shape[1:], jnp.bfloat16)
    return pl.pallas_call(
        row_edges_body,
        out_shape=(shape, shape),
        in_specs=[vmem] * 4,
        out_specs=(vmem, vmem),
        compiler_params=pltpu.CompilerParams(vmem_limit_bytes=vmem_bytes),
        name="row_edges",
    )(picture[:HALO], picture[height - HALO :], cotangent[:RAD], cotangent[height - RAD :])


def col_edges_body(x_ref, dy_ref, row_far_ref, row_near_ref, near_ref, far_ref):
    above, below = in_order("gy", row_near_ref, row_far_ref)
    breadth = x_ref.shape[1]
    odd = odd_rank("gx")
    at = 0
    for rows in (above, x_ref[...].astype(jnp.float32), dy_ref[...].astype(jnp.float32), below):
        first, final = rows[:, :side], rows[:, breadth - side :]
        span = slice(at, at + rows.shape[0])
        near_ref[span] = jnp.where(odd, first, final).astype(jnp.bfloat16)
        far_ref[span] = jnp.where(odd, final, first).astype(jnp.bfloat16)
        at += rows.shape[0]


def col_edges(picture, cotangent, row_far, row_near):
    vmem = pl.BlockSpec(memory_space=pltpu.VMEM)
    rows = 2 * (picture.shape[0] + row_near.shape[0])
    shape = jax.ShapeDtypeStruct((rows, side, D_F), jnp.bfloat16)
    return pl.pallas_call(
        col_edges_body,
        out_shape=(shape, shape),
        in_specs=[vmem] * 4,
        out_specs=(vmem, vmem),
        compiler_params=pltpu.CompilerParams(vmem_limit_bytes=vmem_bytes),
        name="col_edges",
    )(picture, cotangent, row_far, row_near)


def pack_body(first, second, x_ref, dy_ref, own_ref):
    own_ref[:, :D_C] = x_ref[...].astype(jnp.float32).reshape(-1, D_C).astype(jnp.bfloat16)
    own_ref[:, D_C:] = dy_ref[...].astype(jnp.float32).reshape(-1, D_C).astype(jnp.bfloat16)


def packed(after, tokens, cotangents):
    vmem = pl.BlockSpec(memory_space=pltpu.VMEM)
    count = tokens.shape[0] * tokens.shape[1]
    return pl.pallas_call(
        pack_body,
        out_shape=jax.ShapeDtypeStruct((count, 2 * D_C), jnp.bfloat16),
        in_specs=[pl.BlockSpec(memory_space=pl.ANY)] * 2 + [vmem] * 2,
        out_specs=vmem,
        compiler_params=pltpu.CompilerParams(vmem_limit_bytes=vmem_bytes),
        name="pack_coarse",
    )(*after, tokens, cotangents)


def pair_sum_body(own, *refs):
    qkv_ref, out_ref = refs[-2:]
    come = jnp.concatenate([ref[...] for ref in refs[:-2]], axis=0)
    for part in range(4):
        rows = slice(part * HD, (part + 1) * HD)
        total = own[rows].astype(jnp.float32) + come[rows].astype(jnp.float32)
        if part < 3:
            qkv_ref[part] = total.astype(jnp.bfloat16)
        else:
            out_ref[...] = total.astype(jnp.bfloat16)


def pair_sum(own, *come):
    vmem = pl.BlockSpec(memory_space=pltpu.VMEM)
    return pl.pallas_call(
        pair_sum_body,
        out_shape=(
            jax.ShapeDtypeStruct((3, HD, D_C), jnp.bfloat16),
            jax.ShapeDtypeStruct((HD, D_C), jnp.bfloat16),
        ),
        in_specs=[vmem] * (1 + len(come)),
        out_specs=(vmem, vmem),
        compiler_params=pltpu.CompilerParams(vmem_limit_bytes=vmem_bytes),
        name="pair_sum",
    )(own, *come)


def block_copies(near_ref, low, qkv_hbm, out_hbm, sems):
    highs, rows = near_ref.shape[0], near_ref.shape[1]
    copies = []
    for high in range(highs):
        block = lax.axis_index("gx") ^ (2 * high + low)
        at = pl.ds(pl.multiple_of(block * rows, rows), rows)
        for part, target in enumerate((qkv_hbm, out_hbm)):
            lanes = (slice(0, 3 * D_F), slice(3 * D_F, 4 * D_F))[part]
            copies.append(
                pltpu.make_async_copy(
                    near_ref.at[high, :, lanes], target.at[at, :], sems.at[high, part]
                )
            )
    for copy in copies:
        copy.start()
    return copies


def near_body(near_ref, x_ref, factor_ref, kept_ref, come_ref, qkv_hbm, out_hbm, dx_ref, sems):
    copies = block_copies(near_ref, 0, qkv_hbm, out_hbm, sems)
    tokens = x_ref[...].astype(jnp.float32).reshape(-1, D_C)
    upstream = kept_ref[...] + come_ref[...].astype(jnp.float32)
    grads = norm_backward(tokens, inverse_rms(tokens), factor_ref[...], upstream)
    dx_ref[...] = grads.astype(jnp.float32).reshape(dx_ref.shape).astype(jnp.bfloat16)
    for copy in copies:
        copy.wait()


def far_body(far_ref, qkv_in, out_in, qkv_hbm, out_hbm, sems):
    for copy in block_copies(far_ref, 1, qkv_hbm, out_hbm, sems):
        copy.wait()


def near_step(near, tokens, *operands):
    vmem = pl.BlockSpec(memory_space=pltpu.VMEM)
    hbm = pl.BlockSpec(memory_space=pltpu.HBM)
    return pl.pallas_call(
        near_body,
        out_shape=(
            jax.ShapeDtypeStruct((D_F, 3 * D_F), jnp.bfloat16),
            jax.ShapeDtypeStruct((D_F, D_F), jnp.bfloat16),
            jax.ShapeDtypeStruct(tokens.shape, jnp.bfloat16),
        ),
        in_specs=[vmem] * 5,
        out_specs=(hbm, hbm, vmem),
        scratch_shapes=[pltpu.SemaphoreType.DMA((near.shape[0], 2))],
        compiler_params=pltpu.CompilerParams(vmem_limit_bytes=vmem_bytes),
        name="near_step",
    )(near, tokens, *operands)


def far_step(far, qkv, out):
    vmem = pl.BlockSpec(memory_space=pltpu.VMEM)
    hbm = pl.BlockSpec(memory_space=pltpu.HBM)
    return pl.pallas_call(
        far_body,
        out_shape=(
            jax.ShapeDtypeStruct(qkv.shape, qkv.dtype),
            jax.ShapeDtypeStruct(out.shape, out.dtype),
        ),
        in_specs=[vmem, hbm, hbm],
        out_specs=(hbm, hbm),
        input_output_aliases={1: 0, 2: 1},
        scratch_shapes=[pltpu.SemaphoreType.DMA((far.shape[0], 2))],
        compiler_params=pltpu.CompilerParams(vmem_limit_bytes=vmem_bytes),
        name="far_step",
    )(far, qkv, out)


def neighbours(to_near, to_far, axis):
    peers = lax.axis_size(axis)
    near = [(i, i ^ 1) for i in range(peers)]
    far = [(i, i + 1 if i % 2 else i - 1) for i in range(1, peers - 1)]
    from_far = lax.ppermute(to_far, axis, far)
    return lax.ppermute(to_near, axis, near), from_far


def swapped(value, axis, mask):
    return lax.ppermute(value, axis, [(i, i ^ mask) for i in range(lax.axis_size(axis))])


def tied(*arrays):
    return lax.optimization_barrier(arrays)


def batch_sum(partial):
    if lax.axis_size("batch") != 2:
        return lax.psum(partial, "batch")
    return wide(partial) + wide(swapped(partial, "batch", 1))


def wide(value):
    return value.astype(jnp.float32)


def narrow(value):
    return value.astype(jnp.bfloat16)


def all_rows(piece):
    downs = lax.axis_size("gy")
    return jnp.stack([piece] + [swapped(piece, "gy", row) for row in range(1, downs)])


def local(
    x_fine,
    dy_fine,
    x_coarse,
    dy_coarse,
    timestep,
    fine_gain,
    coarse_gain,
    fine_qkv,
    fine_out,
    coarse_qkv,
    coarse_out,
):
    picture, cotangent = x_fine[0], dy_fine[0]
    across, downs = lax.axis_size("gx"), lax.axis_size("gy")
    assert across == 4 and downs & (downs - 1) == 0

    payloads = row_edges(picture, cotangent)
    row_near, row_far = neighbours(*payloads, "gy")
    own = packed(payloads, x_coarse[0], dy_coarse[0])
    count = own.shape[0]
    row_group = all_rows(own)
    edges = col_edges(picture, cotangent, row_far, row_near)
    col_near, col_far = neighbours(*edges, "gx")
    step = timestep[None]
    cross = swapped(row_group, "gx", 2)
    beside = swapped(row_group, "gx", 1)
    col_far, col_near, row_group = tied(col_far, col_near, row_group)
    dx_picture, fine_keep, fine_send = fine_block(
        (across, downs),
        picture,
        cotangent,
        row_far,
        row_near,
        col_far,
        col_near,
        step,
        fine_gain[None],
        frequencies(D_F),
        fine_qkv,
        fine_out,
    )
    fine_half = fine_keep + wide(swapped(fine_send, "gx", 1))
    opposite = swapped(cross, "gx", 1)
    fine_half, opposite = tied(fine_half, opposite)

    fine_quarter = narrow(fine_half[0] + wide(swapped(narrow(fine_half[1]), "gx", 2)))
    everyone = jnp.stack([row_group, cross, beside, opposite]).reshape(-1, 2 * D_C)
    parts, coarse_partial, coarse_factor = coarse_block(
        everyone[:, :D_C], everyone[:, D_C:], step, coarse_gain, coarse_qkv, coarse_out
    )
    fine_quarter, parts, coarse_partial = tied(fine_quarter, parts, coarse_partial)

    rows = D_F // across
    fine_quarter = narrow(batch_sum(fine_quarter)).reshape(rows, 4 * D_F)
    parts = parts.reshape(2, 2, downs, count, D_C)
    coarse_kept = wide(parts[0]) + wide(swapped(parts[1], "gx", 1))
    fine_quarter, coarse_kept, coarse_partial = tied(fine_quarter, coarse_kept, coarse_partial)

    pair_batch = lax.axis_size("batch") == 2
    cut = 7 * HD // 4
    halves = (coarse_partial[:cut], coarse_partial[cut:])
    others = [swapped(half, "batch", 1) if pair_batch else half for half in halves]
    mask = 1
    while mask < downs:
        last = 2 * mask == downs
        coarse_kept = coarse_kept.reshape(2, -1, 2, count, D_C)
        sent = narrow(coarse_kept[:, :, 1]).reshape(-1, D_C)
        come = swapped(jnp.concatenate([fine_quarter, sent], axis=0), "gy", mask)
        coarse_kept = coarse_kept[:, :, 0]
        coarse_kept = coarse_kept + wide(come[rows:]).reshape(coarse_kept.shape)
        fine_quarter = narrow(wide(fine_quarter) + wide(come[:rows]))
        at = int(last)
        fine_quarter, coarse_kept, others[at] = tied(fine_quarter, coarse_kept, others[at])
        mask *= 2

    coarse_kept = coarse_kept.reshape(2, count, D_C)
    come = swapped(jnp.concatenate([fine_quarter, narrow(coarse_kept[1])], axis=0), "gx", 2)
    if pair_batch:
        grad_coarse_qkv, grad_coarse_out = pair_sum(coarse_partial, *others)
    else:
        coarse_sum = narrow(batch_sum(wide(coarse_partial)))
        grad_coarse_qkv = coarse_sum[: 3 * HD].reshape(coarse_qkv.shape)
        grad_coarse_out = coarse_sum[3 * HD :]
    come, grad_coarse_qkv, grad_coarse_out = tied(come, grad_coarse_qkv, grad_coarse_out)
    fine_pair = jnp.stack([fine_quarter, come[:rows]])
    near_qkv, near_out, dx_coarse = near_step(
        fine_pair, x_coarse[0], coarse_factor, coarse_kept[0], come[rows:]
    )
    far_pair = swapped(fine_pair, "gx", 1)
    far_pair, near_qkv, near_out = tied(far_pair, near_qkv, near_out)
    grad_qkv, grad_out = far_step(far_pair, near_qkv, near_out)
    return (
        dx_picture[None],
        dx_coarse[None],
        grad_qkv,
        grad_out,
        grad_coarse_qkv,
        grad_coarse_out,
    )


def solution(mesh):
    placed = (
        P("batch", "gy", "gx", None),
        P("batch", "gy", "gx", None),
        P("batch", "gy", "gx", None),
        P("batch", "gy", "gx", None),
        P("batch"),
        P(),
        P(),
        P(),
        P(),
        P(None, plane_spec, None),
        P(plane_spec, None),
    )
    return jax.shard_map(
        local,
        mesh=mesh,
        in_specs=placed,
        out_specs=(
            P("batch", "gy", "gx", None),
            P("batch", "gy", "gx", None),
            P(),
            P(),
            P(None, plane_spec, None),
            P(plane_spec, None),
        ),
        check_vma=False,
    )


plane_spec = ("gy", "gx")
```

```python
import math

import jax
import jax.numpy as jnp
import numpy as np
from jax import lax
from jax.experimental import pallas as pl
from jax.experimental.pallas import tpu as pltpu
from jax.sharding import PartitionSpec as P

D_F = 256
H_F = 4
D_C = 1024
HD = 64
RAD = 3
HALO = 2 * RAD

eps = 1e-06
log_span = math.log(1000.0)
side = 8
extent = side + 2 * RAD
lanes_wide = 16
thin = 4
lag = 1
scale = 1.0 / math.sqrt(HD)
vmem_bytes = 48 * 1024 * 1024


def dot(first, second, dims=((1,), (0,))):
    return lax.dot_general(first, second, (dims, ((), ())), preferred_element_type=jnp.float32)


def frequencies(channels):
    steps = np.float32(-log_span) * np.arange(channels, dtype=np.float32) / np.float32(channels)
    return np.exp(steps)[None]


def odd_rank(axis):
    return lax.axis_index(axis) & 1 == 1


def inverse_rms(floats):
    return lax.rsqrt(jnp.mean(floats * floats, axis=-1, keepdims=True) + eps)


def norm_backward(floats, inverse, factor, upstream):
    scaled = upstream * factor
    middle = jnp.mean(floats * scaled, axis=-1, keepdims=True)
    return (inverse * scaled - floats * inverse * inverse * inverse * middle).astype(jnp.bfloat16)


def round_up(value, multiple):
    return -(-value // multiple) * multiple


def in_order(axis, near, far):
    odd = odd_rank(axis)
    first, second = near[...].astype(jnp.float32), far[...].astype(jnp.float32)
    return jnp.where(odd, first, second), jnp.where(odd, second, first)


def fine_body(
    x_ref,
    dy_ref,
    row_far_ref,
    row_near_ref,
    col_far_ref,
    col_near_ref,
    factor_ref,
    qkv_ref,
    out_ref,
    dx_ref,
    keep_ref,
    send_ref,
    x_grid,
    dy_grid,
    k_grid,
    v_grid,
    q_grid,
    u_grid,
    dk_grid,
    dv_grid,
    dq_grid,
    a_grid,
    total_ref,
    *scratch,
):
    height, breadth = x_ref.shape[0], x_ref.shape[1]
    grid_rows, grid_cols = x_grid.shape[0], x_grid.shape[1]
    query_rows = dy_grid.shape[0]
    floats = jnp.float32
    factor = factor_ref[...]

    for grid, rows in ((x_grid, height + 2 * HALO), (dy_grid, height + 2 * RAD)):
        grid[rows:] = jnp.zeros((grid.shape[0] - rows,) + grid.shape[1:], floats)
        cols = breadth + 2 * HALO
        grid[:rows, cols:] = jnp.zeros((rows, grid_cols - cols, D_F), floats)
    dk_grid[...] = jnp.zeros_like(dk_grid)
    dv_grid[...] = jnp.zeros_like(dv_grid)
    inner = slice(HALO, HALO + breadth)
    above, below = in_order("gy", row_near_ref, row_far_ref)
    left, right = in_order("gx", col_near_ref, col_far_ref)
    x_grid[0:HALO, inner] = above[0:HALO]
    x_grid[HALO : HALO + height, inner] = x_ref[...].astype(floats)
    x_grid[HALO + height : HALO + height + HALO, inner] = below[0:HALO]
    dy_grid[0:RAD, inner] = above[HALO : HALO + RAD]
    dy_grid[RAD : RAD + height, inner] = dy_ref[...].astype(floats)
    dy_grid[RAD + height : RAD + height + RAD, inner] = below[HALO : HALO + RAD]
    left, right = left[:, left.shape[1] - HALO :], right[:, :HALO]
    for strip, first in ((left, 0), (right, HALO + breadth)):
        span = slice(first, first + HALO)
        at = 0
        for grid, begin, count in (
            (x_grid, 0, HALO),
            (dy_grid, 0, RAD),
            (x_grid, HALO, height),
            (dy_grid, RAD, height),
            (x_grid, HALO + height, HALO),
            (dy_grid, RAD + height, RAD),
        ):
            grid[begin : begin + count, span] = strip[at : at + count]
            at += count

    tokens = x_grid[...].reshape(grid_rows * grid_cols, D_F)
    normed = (tokens * inverse_rms(tokens) * factor).astype(jnp.bfloat16)
    key_values = dot(normed, qkv_ref[:, D_F:]).astype(jnp.bfloat16).astype(floats)
    k_grid[...] = key_values[:, :D_F].reshape(grid_rows, grid_cols, D_F)
    v_grid[...] = key_values[:, D_F:].reshape(grid_rows, grid_cols, D_F)
    query_tokens = normed[RAD * grid_cols : (RAD + query_rows) * grid_cols]
    queries = dot(query_tokens, qkv_ref[:, :D_F]).astype(jnp.bfloat16).astype(floats) * scale
    q_grid[...] = queries.reshape(query_rows, grid_cols, D_F)
    cotangents = dy_grid[...].reshape(query_rows * grid_cols, D_F).astype(jnp.bfloat16)
    ups = dot(cotangents, out_ref[...], ((1,), (1,))).astype(jnp.bfloat16).astype(floats)
    u_grid[...] = ups.reshape(query_rows, grid_cols, D_F)

    gx, gy = lax.axis_index("gx"), lax.axis_index("gy")
    row_low, col_low = HALO - gy * height, HALO - gx * breadth
    row_high = row_low + lax.axis_size("gy") * height
    col_high = col_low + lax.axis_size("gx") * breadth

    def window_bias(query_rows):
        shape = ((query_rows + 2 * RAD) * lanes_wide, H_F * query_rows * side)
        key_at = lax.broadcasted_iota(jnp.int32, shape, 0)
        query_at = lax.broadcasted_iota(jnp.int32, shape, 1)
        row_gap = (key_at // lanes_wide) - ((query_at // side) % query_rows)
        col_gap = (key_at % lanes_wide) - (query_at % side)
        near = (row_gap >= 0) & (row_gap <= 2 * RAD) & (col_gap >= 0) & (col_gap <= 2 * RAD)
        return jnp.where(near, 0.0, -1e30)

    own_scratch, thin_scratch = scratch[:7], scratch[7:]
    own_scratch[-1][...] = window_bias(side)
    thin_scratch[-1][...] = window_bias(thin)

    def head_of(rows):
        return lax.broadcasted_iota(jnp.int32, (rows, D_F), 1) // HD

    def spread(block):
        block = block.reshape(-1, D_F)
        heads = head_of(block.shape[0])
        return jnp.concatenate(
            [jnp.where(heads == h, block, 0.0).astype(jnp.bfloat16) for h in range(H_F)], axis=0
        )

    def collect(full):
        rows = full.shape[0] // H_F
        heads = head_of(rows)
        total = jnp.where(heads == 0, full[:rows], 0.0)
        for h in range(1, H_F):
            total = jnp.where(heads == h, full[h * rows : (h + 1) * rows], total)
        return total.reshape(rows // side, side, D_F)

    def windows(task):
        top, start, query_rows = task[:3]
        window = (slice(top, top + query_rows + 2 * RAD), slice(start, start + lanes_wide))
        keys = k_grid[window].reshape(-1, D_F).astype(jnp.bfloat16)
        return keys, v_grid[window].reshape(-1, D_F).astype(jnp.bfloat16)

    def begin(task):
        top, start, query_rows, live, scratch, index = task
        score_ref, product_ref, query_ref, up_ref = scratch[:4]
        keys, values = windows(task)
        place = (slice(top, top + query_rows), slice(start + RAD, start + RAD + side))
        wide_queries = spread(q_grid[place])
        ups = u_grid[place]
        if live < query_rows:
            row = lax.broadcasted_iota(jnp.int32, ups.shape, 0)
            ups = jnp.where(row < live, ups, 0.0)
        wide_ups = spread(ups)
        query_ref[index], up_ref[index] = wide_queries, wide_ups
        score_ref[index] = dot(keys, wide_queries, ((1,), (1,)))
        product_ref[index] = dot(values, wide_ups, ((1,), (1,)))

    def share(task):
        top, start, query_rows, live, scratch, index = task
        score_ref, product_ref, _, _, weight_ref, slope_ref, near_bias = scratch
        lone = lax.broadcasted_iota(jnp.int32, ((query_rows + 2 * RAD) * lanes_wide, 1), 0)
        key_row, key_col = lone // lanes_wide + top, lone % lanes_wide + start
        inside = (key_row >= row_low) & (key_row < row_high)
        inside = inside & (key_col >= col_low) & (key_col < col_high)
        scores = score_ref[index] + (near_bias[...] + jnp.where(inside, 0.0, -1e30))
        raised = jnp.exp(scores - jnp.max(scores, axis=0, keepdims=True))
        shares = raised * (1.0 / jnp.sum(raised, axis=0, keepdims=True))
        products = product_ref[index]
        centre = jnp.sum(shares * products, axis=0, keepdims=True)
        slope_ref[index] = (shares * (products - centre)).astype(jnp.bfloat16)
        weight_ref[index] = shares.astype(jnp.bfloat16)

    def finish(task):
        top, start, query_rows, live, scratch, index = task
        query_ref, up_ref, weight_ref, slope_ref = scratch[2:6]
        first, final = max(top, HALO), min(top + query_rows + 2 * RAD, HALO + height)
        kept = slice((first - top) * lanes_wide, (final - top) * lanes_wide)
        target = (slice(first - HALO, final - HALO), slice(start, start + lanes_wide))
        shape = (final - first, lanes_wide, D_F)
        dv_grid[target] += dot(weight_ref[index, kept], up_ref[index]).reshape(shape)
        dk_grid[target] += dot(slope_ref[index, kept], query_ref[index]).reshape(shape)
        if live == side:
            keys, values = windows(task)
            block = (slice(top - RAD, top - RAD + side), slice(start, start + side))
            a_grid[block] = collect(dot(weight_ref[index], values, ((0,), (0,))))
            dq_grid[block] = collect(dot(slope_ref[index], keys, ((0,), (0,))))

    tasks = []
    for start in range(0, grid_cols - side, side):
        for top in range(RAD, RAD + height, side):
            tasks.append((top, start, side, side, own_scratch, len(tasks)))
    for index, start in enumerate(range(0, grid_cols - side, side)):
        tasks.append((0, start, thin, RAD, thin_scratch, 2 * index))
        tasks.append((RAD + height, start, thin, thin, thin_scratch, 2 * index + 1))
    for turn in range(len(tasks) + 2 * lag):
        if turn < len(tasks):
            begin(tasks[turn])
        if 0 <= turn - lag < len(tasks):
            share(tasks[turn - lag])
        if turn >= 2 * lag:
            finish(tasks[turn - 2 * lag])

    count = height * breadth
    own_queries = (slice(0, height), slice(RAD, RAD + breadth))
    own_keys = (slice(0, height), inner)
    attended = a_grid[own_queries].reshape(count, D_F).astype(jnp.bfloat16)
    grad_q = (dq_grid[own_queries].reshape(count, D_F) * scale).astype(jnp.bfloat16)
    grad_k = dk_grid[own_keys].reshape(count, D_F).astype(jnp.bfloat16)
    grad_v = dv_grid[own_keys].reshape(count, D_F).astype(jnp.bfloat16)
    grad_proj = jnp.concatenate([grad_q, grad_k, grad_v], axis=1)
    picture = x_ref[...].reshape(count, D_F).astype(floats)
    inverse = inverse_rms(picture)
    own_normed = (picture * inverse * factor).astype(jnp.bfloat16)
    flat_cot = dy_ref[...].reshape(count, D_F)
    grads = jnp.concatenate(
        [
            dot(own_normed, grad_proj, ((0,), (0,))),
            dot(attended, flat_cot, ((0,), (0,))),
        ],
        axis=1,
    )
    half, columns = keep_ref.shape[0], keep_ref.shape[1]
    total_ref[...] = grads.reshape(total_ref.shape)
    for low in range(2):
        target = (keep_ref, send_ref)[low]
        for high in range(half):
            for row in range(columns):
                block = (gx ^ (2 * high + low)) * columns + row
                target[high, row] = total_ref[block].astype(target.dtype)
    down = dot(grad_proj, qkv_ref[...], ((1,), (1,)))
    dx_ref[...] = norm_backward(picture, inverse, factor, down).reshape(height, breadth, D_F)


def block_scratch(blocks, query_rows):
    keys_count, heads_count = (query_rows + 2 * RAD) * lanes_wide, H_F * query_rows * side
    square = (blocks, keys_count, heads_count)
    wide = (blocks, heads_count, D_F)
    return [
        pltpu.VMEM(square, jnp.float32),
        pltpu.VMEM(square, jnp.float32),
        pltpu.VMEM(wide, jnp.bfloat16),
        pltpu.VMEM(wide, jnp.bfloat16),
        pltpu.VMEM(square, jnp.bfloat16),
        pltpu.VMEM(square, jnp.bfloat16),
        pltpu.VMEM((keys_count, heads_count), jnp.float32),
    ]


def fine_block(peers, picture, *operands):
    height, breadth = picture.shape[0], picture.shape[1]
    query_rows = RAD + height + thin
    query_cols = round_up(breadth + 2 * RAD, side)
    grid_rows, grid_cols = query_rows + 2 * RAD, query_cols + side
    across, down = peers
    rows = D_F // (across * down)
    halves = (across // 2, down, rows, 4 * D_F)
    vmem = pl.BlockSpec(memory_space=pltpu.VMEM)
    wide = pltpu.VMEM((grid_rows, grid_cols, D_F), jnp.float32)
    middle = pltpu.VMEM((query_rows, grid_cols, D_F), jnp.float32)
    small = pltpu.VMEM((height, query_cols, D_F), jnp.float32)
    strip = pltpu.VMEM((height, grid_cols, D_F), jnp.float32)
    return pl.pallas_call(
        fine_body,
        out_shape=(
            jax.ShapeDtypeStruct((height, breadth, D_F), jnp.bfloat16),
            jax.ShapeDtypeStruct(halves, jnp.float32),
            jax.ShapeDtypeStruct(halves, jnp.bfloat16),
        ),
        in_specs=[vmem] * 9,
        out_specs=(vmem, vmem, vmem),
        scratch_shapes=[
            wide,
            middle,
            wide,
            wide,
            middle,
            middle,
            strip,
            strip,
            small,
            small,
            pltpu.VMEM((across * down, rows, 4 * D_F), jnp.float32),
            *block_scratch(query_cols // side * (height // side), side),
            *block_scratch(2 * (query_cols // side), thin),
        ],
        compiler_params=pltpu.CompilerParams(vmem_limit_bytes=vmem_bytes),
        name="fine_block",
    )(picture, *operands)


def coarse_body(
    x_ref,
    dy_ref,
    factor_ref,
    qkv_hbm,
    out_hbm,
    parts_ref,
    grads_ref,
    qkv_ref,
    out_ref,
    arrived,
):
    fetches = [
        pltpu.make_async_copy(qkv_hbm, qkv_ref, arrived.at[0]),
        pltpu.make_async_copy(out_hbm, out_ref, arrived.at[1]),
    ]
    for fetch in fetches:
        fetch.start()
    tokens = x_ref[...].astype(jnp.float32)
    normed = (tokens * inverse_rms(tokens) * factor_ref[...]).astype(jnp.bfloat16)
    cot = dy_ref[...]
    for fetch in fetches:
        fetch.wait()
    flat_qkv = qkv_ref[...].reshape(3 * HD, D_C)
    out_rows = out_ref[...]
    projected = dot(normed, flat_qkv, ((1,), (1,))).astype(jnp.bfloat16)
    queries, keys, values = projected[:, :HD], projected[:, HD : 2 * HD], projected[:, 2 * HD :]
    ups = dot(cot, out_rows, ((1,), (1,))).astype(jnp.bfloat16)
    scores = dot(queries, keys, ((1,), (1,))) * scale
    raised = jnp.exp(scores - jnp.max(scores, axis=-1, keepdims=True))
    shares = raised * (1.0 / jnp.sum(raised, axis=-1, keepdims=True))
    weights = shares.astype(jnp.bfloat16)
    mixed = dot(weights, values).astype(jnp.bfloat16)
    products = dot(ups, values, ((1,), (1,)))
    centre = jnp.sum(shares * products, axis=-1, keepdims=True)
    slopes = (shares * (products - centre)).astype(jnp.bfloat16)
    grad_q = (dot(slopes, keys) * scale).astype(jnp.bfloat16)
    grad_k = (dot(slopes, queries, ((0,), (0,))) * scale).astype(jnp.bfloat16)
    grad_v = dot(weights, ups, ((0,), (0,))).astype(jnp.bfloat16)
    stacked = jnp.concatenate([grad_q, grad_k, grad_v], axis=1)
    parts_ref[...] = dot(stacked, flat_qkv).astype(jnp.bfloat16)
    grads_ref[: 3 * HD] = dot(stacked, normed, ((0,), (0,))).astype(grads_ref.dtype)
    grads_ref[3 * HD :] = dot(mixed, cot, ((0,), (0,))).astype(grads_ref.dtype)


def coarse_block(tokens, cotangents, factor, head_qkv, head_out):
    count = tokens.shape[0]
    vmem = pl.BlockSpec(memory_space=pltpu.VMEM)
    return pl.pallas_call(
        coarse_body,
        out_shape=(
            jax.ShapeDtypeStruct((count, D_C), jnp.bfloat16),
            jax.ShapeDtypeStruct((4 * HD, D_C), jnp.bfloat16),
        ),
        in_specs=[vmem] * 3 + [pl.BlockSpec(memory_space=pltpu.HBM)] * 2,
        out_specs=(vmem, vmem),
        scratch_shapes=[
            pltpu.VMEM(head_qkv.shape, jnp.bfloat16),
            pltpu.VMEM(head_out.shape, jnp.bfloat16),
            pltpu.SemaphoreType.DMA((2,)),
        ],
        compiler_params=pltpu.CompilerParams(vmem_limit_bytes=vmem_bytes),
        name="coarse_block",
    )(tokens, cotangents, factor, head_qkv, head_out)


def row_edges_body(x_low, x_high, dy_low, dy_high, near_ref, far_ref):
    odd = odd_rank("gy")

    def fill(low_ref, high_ref):
        low_ref[:HALO], low_ref[HALO:] = x_low[...], dy_low[...]
        high_ref[:HALO], high_ref[HALO:] = x_high[...], dy_high[...]

    @pl.when(odd)
    def _():
        fill(near_ref, far_ref)

    @pl.when(jnp.logical_not(odd))
    def _():
        fill(far_ref, near_ref)


def row_edges(picture, cotangent):
    vmem = pl.BlockSpec(memory_space=pltpu.VMEM)
    height = picture.shape[0]
    shape = jax.ShapeDtypeStruct((HALO + RAD,) + picture.shape[1:], jnp.bfloat16)
    return pl.pallas_call(
        row_edges_body,
        out_shape=(shape, shape),
        in_specs=[vmem] * 4,
        out_specs=(vmem, vmem),
        compiler_params=pltpu.CompilerParams(vmem_limit_bytes=vmem_bytes),
        name="row_edges",
    )(picture[:HALO], picture[height - HALO :], cotangent[:RAD], cotangent[height - RAD :])


def col_edges_body(x_ref, dy_ref, row_far_ref, row_near_ref, near_ref, far_ref):
    above, below = in_order("gy", row_near_ref, row_far_ref)
    breadth = x_ref.shape[1]
    odd = odd_rank("gx")
    at = 0
    for rows in (above, x_ref[...].astype(jnp.float32), dy_ref[...].astype(jnp.float32), below):
        first, final = rows[:, :side], rows[:, breadth - side :]
        span = slice(at, at + rows.shape[0])
        near_ref[span] = jnp.where(odd, first, final).astype(jnp.bfloat16)
        far_ref[span] = jnp.where(odd, final, first).astype(jnp.bfloat16)
        at += rows.shape[0]


def col_edges(picture, cotangent, row_far, row_near):
    vmem = pl.BlockSpec(memory_space=pltpu.VMEM)
    rows = 2 * (picture.shape[0] + row_near.shape[0])
    shape = jax.ShapeDtypeStruct((rows, side, D_F), jnp.bfloat16)
    return pl.pallas_call(
        col_edges_body,
        out_shape=(shape, shape),
        in_specs=[vmem] * 4,
        out_specs=(vmem, vmem),
        compiler_params=pltpu.CompilerParams(vmem_limit_bytes=vmem_bytes),
        name="col_edges",
    )(picture, cotangent, row_far, row_near)


def pack_body(first, second, x_ref, dy_ref, own_ref):
    own_ref[:, :D_C] = x_ref[...].astype(jnp.float32).reshape(-1, D_C).astype(jnp.bfloat16)
    own_ref[:, D_C:] = dy_ref[...].astype(jnp.float32).reshape(-1, D_C).astype(jnp.bfloat16)


def packed(after, tokens, cotangents):
    vmem = pl.BlockSpec(memory_space=pltpu.VMEM)
    count = tokens.shape[0] * tokens.shape[1]
    return pl.pallas_call(
        pack_body,
        out_shape=jax.ShapeDtypeStruct((count, 2 * D_C), jnp.bfloat16),
        in_specs=[pl.BlockSpec(memory_space=pl.ANY)] * 2 + [vmem] * 2,
        out_specs=vmem,
        compiler_params=pltpu.CompilerParams(vmem_limit_bytes=vmem_bytes),
        name="pack_coarse",
    )(*after, tokens, cotangents)


def factors_body(step, fine_gain, coarse_gain, fine_freq, coarse_freq, fine_ref, coarse_ref):
    time = step[0].astype(jnp.float32)
    fine_ref[...] = fine_gain[...] * (1.0 + 0.5 * jnp.cos(time * fine_freq[...]))
    coarse_ref[...] = coarse_gain[...] * (1.0 + 0.5 * jnp.cos(time * coarse_freq[...]))


def time_factors(step, fine_gain, coarse_gain):
    vmem = pl.BlockSpec(memory_space=pltpu.VMEM)
    return pl.pallas_call(
        factors_body,
        out_shape=(
            jax.ShapeDtypeStruct((1, D_F), jnp.float32),
            jax.ShapeDtypeStruct((1, D_C), jnp.float32),
        ),
        in_specs=[pl.BlockSpec(memory_space=pltpu.SMEM)] + [vmem] * 4,
        out_specs=(vmem, vmem),
        compiler_params=pltpu.CompilerParams(vmem_limit_bytes=vmem_bytes),
        name="time_factors",
    )(step, fine_gain[None], coarse_gain[None], frequencies(D_F), frequencies(D_C))


def pair_sum_body(own, *refs):
    qkv_ref, out_ref = refs[-2:]
    come = jnp.concatenate([ref[...] for ref in refs[:-2]], axis=0)
    for part in range(4):
        rows = slice(part * HD, (part + 1) * HD)
        total = own[rows].astype(jnp.float32) + come[rows].astype(jnp.float32)
        if part < 3:
            qkv_ref[part] = total.astype(jnp.bfloat16)
        else:
            out_ref[...] = total.astype(jnp.bfloat16)


def pair_sum(own, *come):
    vmem = pl.BlockSpec(memory_space=pltpu.VMEM)
    return pl.pallas_call(
        pair_sum_body,
        out_shape=(
            jax.ShapeDtypeStruct((3, HD, D_C), jnp.bfloat16),
            jax.ShapeDtypeStruct((HD, D_C), jnp.bfloat16),
        ),
        in_specs=[vmem] * (1 + len(come)),
        out_specs=(vmem, vmem),
        compiler_params=pltpu.CompilerParams(vmem_limit_bytes=vmem_bytes),
        name="pair_sum",
    )(own, *come)


def block_copies(near_ref, low, qkv_hbm, out_hbm, sems):
    highs, rows = near_ref.shape[0], near_ref.shape[1]
    copies = []
    for high in range(highs):
        block = lax.axis_index("gx") ^ (2 * high + low)
        at = pl.ds(pl.multiple_of(block * rows, rows), rows)
        for part, target in enumerate((qkv_hbm, out_hbm)):
            lanes = (slice(0, 3 * D_F), slice(3 * D_F, 4 * D_F))[part]
            copies.append(
                pltpu.make_async_copy(
                    near_ref.at[high, :, lanes], target.at[at, :], sems.at[high, part]
                )
            )
    for copy in copies:
        copy.start()
    return copies


def near_body(near_ref, x_ref, factor_ref, kept_ref, come_ref, qkv_hbm, out_hbm, dx_ref, sems):
    copies = block_copies(near_ref, 0, qkv_hbm, out_hbm, sems)
    tokens = x_ref[...].astype(jnp.float32).reshape(-1, D_C)
    upstream = kept_ref[...] + come_ref[...].astype(jnp.float32)
    grads = norm_backward(tokens, inverse_rms(tokens), factor_ref[...], upstream)
    dx_ref[...] = grads.astype(jnp.float32).reshape(dx_ref.shape).astype(jnp.bfloat16)
    for copy in copies:
        copy.wait()


def far_body(far_ref, qkv_in, out_in, qkv_hbm, out_hbm, sems):
    for copy in block_copies(far_ref, 1, qkv_hbm, out_hbm, sems):
        copy.wait()


def near_step(near, tokens, *operands):
    vmem = pl.BlockSpec(memory_space=pltpu.VMEM)
    hbm = pl.BlockSpec(memory_space=pltpu.HBM)
    return pl.pallas_call(
        near_body,
        out_shape=(
            jax.ShapeDtypeStruct((D_F, 3 * D_F), jnp.bfloat16),
            jax.ShapeDtypeStruct((D_F, D_F), jnp.bfloat16),
            jax.ShapeDtypeStruct(tokens.shape, jnp.bfloat16),
        ),
        in_specs=[vmem] * 5,
        out_specs=(hbm, hbm, vmem),
        scratch_shapes=[pltpu.SemaphoreType.DMA((near.shape[0], 2))],
        compiler_params=pltpu.CompilerParams(vmem_limit_bytes=vmem_bytes),
        name="near_step",
    )(near, tokens, *operands)


def far_step(far, qkv, out):
    vmem = pl.BlockSpec(memory_space=pltpu.VMEM)
    hbm = pl.BlockSpec(memory_space=pltpu.HBM)
    return pl.pallas_call(
        far_body,
        out_shape=(
            jax.ShapeDtypeStruct(qkv.shape, qkv.dtype),
            jax.ShapeDtypeStruct(out.shape, out.dtype),
        ),
        in_specs=[vmem, hbm, hbm],
        out_specs=(hbm, hbm),
        input_output_aliases={1: 0, 2: 1},
        scratch_shapes=[pltpu.SemaphoreType.DMA((far.shape[0], 2))],
        compiler_params=pltpu.CompilerParams(vmem_limit_bytes=vmem_bytes),
        name="far_step",
    )(far, qkv, out)


def neighbours(to_near, to_far, axis):
    peers = lax.axis_size(axis)
    near = [(i, i ^ 1) for i in range(peers)]
    far = [(i, i + 1 if i % 2 else i - 1) for i in range(1, peers - 1)]
    from_far = lax.ppermute(to_far, axis, far)
    return lax.ppermute(to_near, axis, near), from_far


def swapped(value, axis, mask):
    return lax.ppermute(value, axis, [(i, i ^ mask) for i in range(lax.axis_size(axis))])


def tied(*arrays):
    return lax.optimization_barrier(arrays)


def batch_sum(partial):
    if lax.axis_size("batch") != 2:
        return lax.psum(partial, "batch")
    return wide(partial) + wide(swapped(partial, "batch", 1))


def wide(value):
    return value.astype(jnp.float32)


def narrow(value):
    return value.astype(jnp.bfloat16)


def all_rows(piece):
    downs = lax.axis_size("gy")
    return jnp.stack([piece] + [swapped(piece, "gy", row) for row in range(1, downs)])


def local(
    x_fine,
    dy_fine,
    x_coarse,
    dy_coarse,
    timestep,
    fine_gain,
    coarse_gain,
    fine_qkv,
    fine_out,
    coarse_qkv,
    coarse_out,
):
    picture, cotangent = x_fine[0], dy_fine[0]
    across, downs = lax.axis_size("gx"), lax.axis_size("gy")
    assert across == 4 and downs & (downs - 1) == 0

    payloads = row_edges(picture, cotangent)
    row_near, row_far = neighbours(*payloads, "gy")
    own = packed(payloads, x_coarse[0], dy_coarse[0])
    count = own.shape[0]
    row_group = all_rows(own)
    edges = col_edges(picture, cotangent, row_far, row_near)
    *edges, step, gain_f, gain_c = tied(*edges, timestep, fine_gain, coarse_gain)
    col_near, col_far = neighbours(*edges, "gx")
    factor, coarse_factor = time_factors(step, gain_f, gain_c)
    cross = swapped(row_group, "gx", 2)
    beside = swapped(row_group, "gx", 1)
    col_far, col_near, row_group, factor = tied(col_far, col_near, row_group, factor)
    dx_picture, fine_keep, fine_send = fine_block(
        (across, downs),
        picture,
        cotangent,
        row_far,
        row_near,
        col_far,
        col_near,
        factor,
        fine_qkv,
        fine_out,
    )
    fine_half = fine_keep + wide(swapped(fine_send, "gx", 1))
    opposite = swapped(cross, "gx", 1)
    fine_half, opposite = tied(fine_half, opposite)

    fine_quarter = narrow(fine_half[0] + wide(swapped(narrow(fine_half[1]), "gx", 2)))
    everyone = jnp.stack([row_group, cross, beside, opposite]).reshape(-1, 2 * D_C)
    parts, coarse_partial = coarse_block(
        everyone[:, :D_C], everyone[:, D_C:], coarse_factor, coarse_qkv, coarse_out
    )
    fine_quarter, parts, coarse_partial = tied(fine_quarter, parts, coarse_partial)

    rows = D_F // across
    fine_quarter = narrow(batch_sum(fine_quarter)).reshape(rows, 4 * D_F)
    parts = parts.reshape(2, 2, downs, count, D_C)
    coarse_kept = wide(parts[0]) + wide(swapped(parts[1], "gx", 1))
    fine_quarter, coarse_kept, coarse_partial = tied(fine_quarter, coarse_kept, coarse_partial)

    pair_batch = lax.axis_size("batch") == 2
    cut = 7 * HD // 4
    halves = (coarse_partial[:cut], coarse_partial[cut:])
    others = [swapped(half, "batch", 1) if pair_batch else half for half in halves]
    mask = 1
    while mask < downs:
        last = 2 * mask == downs
        coarse_kept = coarse_kept.reshape(2, -1, 2, count, D_C)
        sent = narrow(coarse_kept[:, :, 1]).reshape(-1, D_C)
        come = swapped(jnp.concatenate([fine_quarter, sent], axis=0), "gy", mask)
        coarse_kept = coarse_kept[:, :, 0]
        coarse_kept = coarse_kept + wide(come[rows:]).reshape(coarse_kept.shape)
        fine_quarter = narrow(wide(fine_quarter) + wide(come[:rows]))
        at = int(last)
        fine_quarter, coarse_kept, others[at] = tied(fine_quarter, coarse_kept, others[at])
        mask *= 2

    coarse_kept = coarse_kept.reshape(2, count, D_C)
    come = swapped(jnp.concatenate([fine_quarter, narrow(coarse_kept[1])], axis=0), "gx", 2)
    if pair_batch:
        grad_coarse_qkv, grad_coarse_out = pair_sum(coarse_partial, *others)
    else:
        coarse_sum = narrow(batch_sum(wide(coarse_partial)))
        grad_coarse_qkv = coarse_sum[: 3 * HD].reshape(coarse_qkv.shape)
        grad_coarse_out = coarse_sum[3 * HD :]
    come, grad_coarse_qkv, grad_coarse_out = tied(come, grad_coarse_qkv, grad_coarse_out)
    fine_pair = jnp.stack([fine_quarter, come[:rows]])
    near_qkv, near_out, dx_coarse = near_step(
        fine_pair, x_coarse[0], coarse_factor, coarse_kept[0], come[rows:]
    )
    far_pair = swapped(fine_pair, "gx", 1)
    far_pair, near_qkv, near_out = tied(far_pair, near_qkv, near_out)
    grad_qkv, grad_out = far_step(far_pair, near_qkv, near_out)
    return (
        dx_picture[None],
        dx_coarse[None],
        grad_qkv,
        grad_out,
        grad_coarse_qkv,
        grad_coarse_out,
    )


def solution(mesh):
    placed = (
        P("batch", "gy", "gx", None),
        P("batch", "gy", "gx", None),
        P("batch", "gy", "gx", None),
        P("batch", "gy", "gx", None),
        P("batch"),
        P(),
        P(),
        P(),
        P(),
        P(None, plane_spec, None),
        P(plane_spec, None),
    )
    return jax.shard_map(
        local,
        mesh=mesh,
        in_specs=placed,
        out_specs=(
            P("batch", "gy", "gx", None),
            P("batch", "gy", "gx", None),
            P(),
            P(),
            P(None, plane_spec, None),
            P(plane_spec, None),
        ),
        check_vma=False,
    )


plane_spec = ("gy", "gx")
```

```python
import math

import jax
import jax.numpy as jnp
import numpy as np
from jax import lax
from jax.experimental import pallas as pl
from jax.experimental.pallas import tpu as pltpu
from jax.sharding import PartitionSpec as P

D_F = 256
H_F = 4
D_C = 1024
HD = 64
RAD = 3
HALO = 2 * RAD

eps = 1e-06
log_span = math.log(1000.0)
side = 8
extent = side + 2 * RAD
lanes_wide = 16
thin = 4
lag = 2
scale = 1.0 / math.sqrt(HD)
vmem_bytes = 48 * 1024 * 1024


def dot(first, second, dims=((1,), (0,))):
    return lax.dot_general(first, second, (dims, ((), ())), preferred_element_type=jnp.float32)


def frequencies(channels):
    steps = np.float32(-log_span) * np.arange(channels, dtype=np.float32) / np.float32(channels)
    return np.exp(steps)[None]


def odd_rank(axis):
    return lax.axis_index(axis) & 1 == 1


def inverse_rms(floats):
    return lax.rsqrt(jnp.mean(floats * floats, axis=-1, keepdims=True) + eps)


def norm_backward(floats, inverse, factor, upstream):
    scaled = upstream * factor
    middle = jnp.mean(floats * scaled, axis=-1, keepdims=True)
    return (inverse * scaled - floats * inverse * inverse * inverse * middle).astype(jnp.bfloat16)


def round_up(value, multiple):
    return -(-value // multiple) * multiple


def in_order(axis, near, far):
    odd = odd_rank(axis)
    first, second = near[...].astype(jnp.float32), far[...].astype(jnp.float32)
    return jnp.where(odd, first, second), jnp.where(odd, second, first)


def fine_body(
    x_ref,
    dy_ref,
    row_far_ref,
    row_near_ref,
    col_far_ref,
    col_near_ref,
    factor_ref,
    qkv_ref,
    out_ref,
    dx_ref,
    keep_ref,
    send_ref,
    x_grid,
    dy_grid,
    k_grid,
    v_grid,
    q_grid,
    u_grid,
    dk_grid,
    dv_grid,
    dq_grid,
    a_grid,
    total_ref,
    *scratch,
):
    height, breadth = x_ref.shape[0], x_ref.shape[1]
    grid_rows, grid_cols = x_grid.shape[0], x_grid.shape[1]
    query_rows = dy_grid.shape[0]
    floats = jnp.float32
    factor = factor_ref[...]

    for grid, rows in ((x_grid, height + 2 * HALO), (dy_grid, height + 2 * RAD)):
        grid[rows:] = jnp.zeros((grid.shape[0] - rows,) + grid.shape[1:], floats)
        cols = breadth + 2 * HALO
        grid[:rows, cols:] = jnp.zeros((rows, grid_cols - cols, D_F), floats)
    dk_grid[...] = jnp.zeros_like(dk_grid)
    dv_grid[...] = jnp.zeros_like(dv_grid)
    inner = slice(HALO, HALO + breadth)
    above, below = in_order("gy", row_near_ref, row_far_ref)
    left, right = in_order("gx", col_near_ref, col_far_ref)
    x_grid[0:HALO, inner] = above[0:HALO]
    x_grid[HALO : HALO + height, inner] = x_ref[...].astype(floats)
    x_grid[HALO + height : HALO + height + HALO, inner] = below[0:HALO]
    dy_grid[0:RAD, inner] = above[HALO : HALO + RAD]
    dy_grid[RAD : RAD + height, inner] = dy_ref[...].astype(floats)
    dy_grid[RAD + height : RAD + height + RAD, inner] = below[HALO : HALO + RAD]
    left, right = left[:, left.shape[1] - HALO :], right[:, :HALO]
    for strip, first in ((left, 0), (right, HALO + breadth)):
        span = slice(first, first + HALO)
        at = 0
        for grid, begin, count in (
            (x_grid, 0, HALO),
            (dy_grid, 0, RAD),
            (x_grid, HALO, height),
            (dy_grid, RAD, height),
            (x_grid, HALO + height, HALO),
            (dy_grid, RAD + height, RAD),
        ):
            grid[begin : begin + count, span] = strip[at : at + count]
            at += count

    tokens = x_grid[...].reshape(grid_rows * grid_cols, D_F)
    normed = (tokens * inverse_rms(tokens) * factor).astype(jnp.bfloat16)
    key_values = dot(normed, qkv_ref[:, D_F:]).astype(jnp.bfloat16).astype(floats)
    k_grid[...] = key_values[:, :D_F].reshape(grid_rows, grid_cols, D_F)
    v_grid[...] = key_values[:, D_F:].reshape(grid_rows, grid_cols, D_F)
    query_tokens = normed[RAD * grid_cols : (RAD + query_rows) * grid_cols]
    queries = dot(query_tokens, qkv_ref[:, :D_F]).astype(jnp.bfloat16).astype(floats) * scale
    q_grid[...] = queries.reshape(query_rows, grid_cols, D_F)
    cotangents = dy_grid[...].reshape(query_rows * grid_cols, D_F).astype(jnp.bfloat16)
    ups = dot(cotangents, out_ref[...], ((1,), (1,))).astype(jnp.bfloat16).astype(floats)
    u_grid[...] = ups.reshape(query_rows, grid_cols, D_F)

    gx, gy = lax.axis_index("gx"), lax.axis_index("gy")
    row_low, col_low = HALO - gy * height, HALO - gx * breadth
    row_high = row_low + lax.axis_size("gy") * height
    col_high = col_low + lax.axis_size("gx") * breadth

    def window_bias(query_rows):
        shape = ((query_rows + 2 * RAD) * lanes_wide, H_F * query_rows * side)
        key_at = lax.broadcasted_iota(jnp.int32, shape, 0)
        query_at = lax.broadcasted_iota(jnp.int32, shape, 1)
        row_gap = (key_at // lanes_wide) - ((query_at // side) % query_rows)
        col_gap = (key_at % lanes_wide) - (query_at % side)
        near = (row_gap >= 0) & (row_gap <= 2 * RAD) & (col_gap >= 0) & (col_gap <= 2 * RAD)
        return jnp.where(near, 0.0, -1e30)

    own_scratch, thin_scratch = scratch[:7], scratch[7:]
    own_scratch[-1][...] = window_bias(side)
    thin_scratch[-1][...] = window_bias(thin)

    def head_of(rows):
        return lax.broadcasted_iota(jnp.int32, (rows, D_F), 1) // HD

    def spread(block):
        block = block.reshape(-1, D_F)
        heads = head_of(block.shape[0])
        return jnp.concatenate(
            [jnp.where(heads == h, block, 0.0).astype(jnp.bfloat16) for h in range(H_F)], axis=0
        )

    def collect(full):
        rows = full.shape[0] // H_F
        heads = head_of(rows)
        total = jnp.where(heads == 0, full[:rows], 0.0)
        for h in range(1, H_F):
            total = jnp.where(heads == h, full[h * rows : (h + 1) * rows], total)
        return total.reshape(rows // side, side, D_F)

    def windows(task):
        top, start, query_rows = task[:3]
        window = (slice(top, top + query_rows + 2 * RAD), slice(start, start + lanes_wide))
        keys = k_grid[window].reshape(-1, D_F).astype(jnp.bfloat16)
        return keys, v_grid[window].reshape(-1, D_F).astype(jnp.bfloat16)

    def begin(task):
        top, start, query_rows, live, scratch, index = task
        score_ref, product_ref, query_ref, up_ref = scratch[:4]
        keys, values = windows(task)
        place = (slice(top, top + query_rows), slice(start + RAD, start + RAD + side))
        wide_queries = spread(q_grid[place])
        ups = u_grid[place]
        if live < query_rows:
            row = lax.broadcasted_iota(jnp.int32, ups.shape, 0)
            ups = jnp.where(row < live, ups, 0.0)
        wide_ups = spread(ups)
        query_ref[index], up_ref[index] = wide_queries, wide_ups
        score_ref[index] = dot(keys, wide_queries, ((1,), (1,)))
        product_ref[index] = dot(values, wide_ups, ((1,), (1,)))

    def share(task):
        top, start, query_rows, live, scratch, index = task
        score_ref, product_ref, _, _, weight_ref, slope_ref, near_bias = scratch
        lone = lax.broadcasted_iota(jnp.int32, ((query_rows + 2 * RAD) * lanes_wide, 1), 0)
        key_row, key_col = lone // lanes_wide + top, lone % lanes_wide + start
        inside = (key_row >= row_low) & (key_row < row_high)
        inside = inside & (key_col >= col_low) & (key_col < col_high)
        scores = score_ref[index] + (near_bias[...] + jnp.where(inside, 0.0, -1e30))
        raised = jnp.exp(scores - jnp.max(scores, axis=0, keepdims=True))
        shares = raised * (1.0 / jnp.sum(raised, axis=0, keepdims=True))
        products = product_ref[index]
        centre = jnp.sum(shares * products, axis=0, keepdims=True)
        slope_ref[index] = (shares * (products - centre)).astype(jnp.bfloat16)
        weight_ref[index] = shares.astype(jnp.bfloat16)

    def finish(task):
        top, start, query_rows, live, scratch, index = task
        query_ref, up_ref, weight_ref, slope_ref = scratch[2:6]
        first, final = max(top, HALO), min(top + query_rows + 2 * RAD, HALO + height)
        kept = slice((first - top) * lanes_wide, (final - top) * lanes_wide)
        target = (slice(first - HALO, final - HALO), slice(start, start + lanes_wide))
        shape = (final - first, lanes_wide, D_F)
        dv_grid[target] += dot(weight_ref[index, kept], up_ref[index]).reshape(shape)
        dk_grid[target] += dot(slope_ref[index, kept], query_ref[index]).reshape(shape)
        if live == side:
            keys, values = windows(task)
            block = (slice(top - RAD, top - RAD + side), slice(start, start + side))
            a_grid[block] = collect(dot(weight_ref[index], values, ((0,), (0,))))
            dq_grid[block] = collect(dot(slope_ref[index], keys, ((0,), (0,))))

    tasks = []
    for start in range(0, grid_cols - side, side):
        for top in range(RAD, RAD + height, side):
            tasks.append((top, start, side, side, own_scratch, len(tasks)))
    for index, start in enumerate(range(0, grid_cols - side, side)):
        tasks.append((0, start, thin, RAD, thin_scratch, 2 * index))
        tasks.append((RAD + height, start, thin, thin, thin_scratch, 2 * index + 1))
    for turn in range(len(tasks) + 2 * lag):
        if turn < len(tasks):
            begin(tasks[turn])
        if 0 <= turn - lag < len(tasks):
            share(tasks[turn - lag])
        if turn >= 2 * lag:
            finish(tasks[turn - 2 * lag])

    count = height * breadth
    own_queries = (slice(0, height), slice(RAD, RAD + breadth))
    own_keys = (slice(0, height), inner)
    attended = a_grid[own_queries].reshape(count, D_F).astype(jnp.bfloat16)
    grad_q = (dq_grid[own_queries].reshape(count, D_F) * scale).astype(jnp.bfloat16)
    grad_k = dk_grid[own_keys].reshape(count, D_F).astype(jnp.bfloat16)
    grad_v = dv_grid[own_keys].reshape(count, D_F).astype(jnp.bfloat16)
    grad_proj = jnp.concatenate([grad_q, grad_k, grad_v], axis=1)
    picture = x_ref[...].reshape(count, D_F).astype(floats)
    inverse = inverse_rms(picture)
    own_normed = (picture * inverse * factor).astype(jnp.bfloat16)
    flat_cot = dy_ref[...].reshape(count, D_F)
    grads = jnp.concatenate(
        [
            dot(own_normed, grad_proj, ((0,), (0,))),
            dot(attended, flat_cot, ((0,), (0,))),
        ],
        axis=1,
    )
    half, columns = keep_ref.shape[0], keep_ref.shape[1]
    total_ref[...] = grads.reshape(total_ref.shape)
    for low in range(2):
        target = (keep_ref, send_ref)[low]
        for high in range(half):
            for row in range(columns):
                block = (gx ^ (2 * high + low)) * columns + row
                target[high, row] = total_ref[block].astype(target.dtype)
    down = dot(grad_proj, qkv_ref[...], ((1,), (1,)))
    dx_ref[...] = norm_backward(picture, inverse, factor, down).reshape(height, breadth, D_F)


def block_scratch(blocks, query_rows):
    keys_count, heads_count = (query_rows + 2 * RAD) * lanes_wide, H_F * query_rows * side
    square = (blocks, keys_count, heads_count)
    wide = (blocks, heads_count, D_F)
    return [
        pltpu.VMEM(square, jnp.float32),
        pltpu.VMEM(square, jnp.float32),
        pltpu.VMEM(wide, jnp.bfloat16),
        pltpu.VMEM(wide, jnp.bfloat16),
        pltpu.VMEM(square, jnp.bfloat16),
        pltpu.VMEM(square, jnp.bfloat16),
        pltpu.VMEM((keys_count, heads_count), jnp.float32),
    ]


def fine_block(peers, picture, *operands):
    height, breadth = picture.shape[0], picture.shape[1]
    query_rows = RAD + height + thin
    query_cols = round_up(breadth + 2 * RAD, side)
    grid_rows, grid_cols = query_rows + 2 * RAD, query_cols + side
    across, down = peers
    rows = D_F // (across * down)
    halves = (across // 2, down, rows, 4 * D_F)
    vmem = pl.BlockSpec(memory_space=pltpu.VMEM)
    wide = pltpu.VMEM((grid_rows, grid_cols, D_F), jnp.float32)
    middle = pltpu.VMEM((query_rows, grid_cols, D_F), jnp.float32)
    small = pltpu.VMEM((height, query_cols, D_F), jnp.float32)
    strip = pltpu.VMEM((height, grid_cols, D_F), jnp.float32)
    return pl.pallas_call(
        fine_body,
        out_shape=(
            jax.ShapeDtypeStruct((height, breadth, D_F), jnp.bfloat16),
            jax.ShapeDtypeStruct(halves, jnp.float32),
            jax.ShapeDtypeStruct(halves, jnp.bfloat16),
        ),
        in_specs=[vmem] * 9,
        out_specs=(vmem, vmem, vmem),
        scratch_shapes=[
            wide,
            middle,
            wide,
            wide,
            middle,
            middle,
            strip,
            strip,
            small,
            small,
            pltpu.VMEM((across * down, rows, 4 * D_F), jnp.float32),
            *block_scratch(query_cols // side * (height // side), side),
            *block_scratch(2 * (query_cols // side), thin),
        ],
        compiler_params=pltpu.CompilerParams(vmem_limit_bytes=vmem_bytes),
        name="fine_block",
    )(picture, *operands)


def coarse_body(
    x_ref,
    dy_ref,
    factor_ref,
    qkv_hbm,
    out_hbm,
    parts_ref,
    grads_ref,
    qkv_ref,
    out_ref,
    arrived,
):
    fetches = [
        pltpu.make_async_copy(qkv_hbm, qkv_ref, arrived.at[0]),
        pltpu.make_async_copy(out_hbm, out_ref, arrived.at[1]),
    ]
    for fetch in fetches:
        fetch.start()
    tokens = x_ref[...].astype(jnp.float32)
    normed = (tokens * inverse_rms(tokens) * factor_ref[...]).astype(jnp.bfloat16)
    cot = dy_ref[...]
    for fetch in fetches:
        fetch.wait()
    flat_qkv = qkv_ref[...].reshape(3 * HD, D_C)
    out_rows = out_ref[...]
    projected = dot(normed, flat_qkv, ((1,), (1,))).astype(jnp.bfloat16)
    queries, keys, values = projected[:, :HD], projected[:, HD : 2 * HD], projected[:, 2 * HD :]
    ups = dot(cot, out_rows, ((1,), (1,))).astype(jnp.bfloat16)
    scores = dot(queries, keys, ((1,), (1,))) * scale
    raised = jnp.exp(scores - jnp.max(scores, axis=-1, keepdims=True))
    shares = raised * (1.0 / jnp.sum(raised, axis=-1, keepdims=True))
    weights = shares.astype(jnp.bfloat16)
    mixed = dot(weights, values).astype(jnp.bfloat16)
    products = dot(ups, values, ((1,), (1,)))
    centre = jnp.sum(shares * products, axis=-1, keepdims=True)
    slopes = (shares * (products - centre)).astype(jnp.bfloat16)
    grad_q = (dot(slopes, keys) * scale).astype(jnp.bfloat16)
    grad_k = (dot(slopes, queries, ((0,), (0,))) * scale).astype(jnp.bfloat16)
    grad_v = dot(weights, ups, ((0,), (0,))).astype(jnp.bfloat16)
    stacked = jnp.concatenate([grad_q, grad_k, grad_v], axis=1)
    parts_ref[...] = dot(stacked, flat_qkv).astype(jnp.bfloat16)
    grads_ref[: 3 * HD] = dot(stacked, normed, ((0,), (0,))).astype(grads_ref.dtype)
    grads_ref[3 * HD :] = dot(mixed, cot, ((0,), (0,))).astype(grads_ref.dtype)


def coarse_block(tokens, cotangents, factor, head_qkv, head_out):
    count = tokens.shape[0]
    vmem = pl.BlockSpec(memory_space=pltpu.VMEM)
    return pl.pallas_call(
        coarse_body,
        out_shape=(
            jax.ShapeDtypeStruct((count, D_C), jnp.bfloat16),
            jax.ShapeDtypeStruct((4 * HD, D_C), jnp.bfloat16),
        ),
        in_specs=[vmem] * 3 + [pl.BlockSpec(memory_space=pltpu.HBM)] * 2,
        out_specs=(vmem, vmem),
        scratch_shapes=[
            pltpu.VMEM(head_qkv.shape, jnp.bfloat16),
            pltpu.VMEM(head_out.shape, jnp.bfloat16),
            pltpu.SemaphoreType.DMA((2,)),
        ],
        compiler_params=pltpu.CompilerParams(vmem_limit_bytes=vmem_bytes),
        name="coarse_block",
    )(tokens, cotangents, factor, head_qkv, head_out)


def row_edges_body(x_low, x_high, dy_low, dy_high, near_ref, far_ref):
    odd = odd_rank("gy")

    def fill(low_ref, high_ref):
        low_ref[:HALO], low_ref[HALO:] = x_low[...], dy_low[...]
        high_ref[:HALO], high_ref[HALO:] = x_high[...], dy_high[...]

    @pl.when(odd)
    def _():
        fill(near_ref, far_ref)

    @pl.when(jnp.logical_not(odd))
    def _():
        fill(far_ref, near_ref)


def row_edges(picture, cotangent):
    vmem = pl.BlockSpec(memory_space=pltpu.VMEM)
    height = picture.shape[0]
    shape = jax.ShapeDtypeStruct((HALO + RAD,) + picture.shape[1:], jnp.bfloat16)
    return pl.pallas_call(
        row_edges_body,
        out_shape=(shape, shape),
        in_specs=[vmem] * 4,
        out_specs=(vmem, vmem),
        compiler_params=pltpu.CompilerParams(vmem_limit_bytes=vmem_bytes),
        name="row_edges",
    )(picture[:HALO], picture[height - HALO :], cotangent[:RAD], cotangent[height - RAD :])


def col_edges_body(x_ref, dy_ref, row_far_ref, row_near_ref, near_ref, far_ref):
    above, below = in_order("gy", row_near_ref, row_far_ref)
    breadth = x_ref.shape[1]
    odd = odd_rank("gx")
    at = 0
    for rows in (above, x_ref[...].astype(jnp.float32), dy_ref[...].astype(jnp.float32), below):
        first, final = rows[:, :side], rows[:, breadth - side :]
        span = slice(at, at + rows.shape[0])
        near_ref[span] = jnp.where(odd, first, final).astype(jnp.bfloat16)
        far_ref[span] = jnp.where(odd, final, first).astype(jnp.bfloat16)
        at += rows.shape[0]


def col_edges(picture, cotangent, row_far, row_near):
    vmem = pl.BlockSpec(memory_space=pltpu.VMEM)
    rows = 2 * (picture.shape[0] + row_near.shape[0])
    shape = jax.ShapeDtypeStruct((rows, side, D_F), jnp.bfloat16)
    return pl.pallas_call(
        col_edges_body,
        out_shape=(shape, shape),
        in_specs=[vmem] * 4,
        out_specs=(vmem, vmem),
        compiler_params=pltpu.CompilerParams(vmem_limit_bytes=vmem_bytes),
        name="col_edges",
    )(picture, cotangent, row_far, row_near)


def pack_body(first, second, x_ref, dy_ref, own_ref):
    own_ref[:, :D_C] = x_ref[...].astype(jnp.float32).reshape(-1, D_C).astype(jnp.bfloat16)
    own_ref[:, D_C:] = dy_ref[...].astype(jnp.float32).reshape(-1, D_C).astype(jnp.bfloat16)


def packed(after, tokens, cotangents):
    vmem = pl.BlockSpec(memory_space=pltpu.VMEM)
    count = tokens.shape[0] * tokens.shape[1]
    return pl.pallas_call(
        pack_body,
        out_shape=jax.ShapeDtypeStruct((count, 2 * D_C), jnp.bfloat16),
        in_specs=[pl.BlockSpec(memory_space=pl.ANY)] * 2 + [vmem] * 2,
        out_specs=vmem,
        compiler_params=pltpu.CompilerParams(vmem_limit_bytes=vmem_bytes),
        name="pack_coarse",
    )(*after, tokens, cotangents)


def factors_body(step, fine_gain, coarse_gain, fine_freq, coarse_freq, fine_ref, coarse_ref):
    time = step[0].astype(jnp.float32)
    fine_ref[...] = fine_gain[...] * (1.0 + 0.5 * jnp.cos(time * fine_freq[...]))
    coarse_ref[...] = coarse_gain[...] * (1.0 + 0.5 * jnp.cos(time * coarse_freq[...]))


def time_factors(step, fine_gain, coarse_gain):
    vmem = pl.BlockSpec(memory_space=pltpu.VMEM)
    return pl.pallas_call(
        factors_body,
        out_shape=(
            jax.ShapeDtypeStruct((1, D_F), jnp.float32),
            jax.ShapeDtypeStruct((1, D_C), jnp.float32),
        ),
        in_specs=[pl.BlockSpec(memory_space=pltpu.SMEM)] + [vmem] * 4,
        out_specs=(vmem, vmem),
        compiler_params=pltpu.CompilerParams(vmem_limit_bytes=vmem_bytes),
        name="time_factors",
    )(step, fine_gain[None], coarse_gain[None], frequencies(D_F), frequencies(D_C))


def pair_sum_body(own, *refs):
    qkv_ref, out_ref = refs[-2:]
    come = jnp.concatenate([ref[...] for ref in refs[:-2]], axis=0)
    for part in range(4):
        rows = slice(part * HD, (part + 1) * HD)
        total = own[rows].astype(jnp.float32) + come[rows].astype(jnp.float32)
        if part < 3:
            qkv_ref[part] = total.astype(jnp.bfloat16)
        else:
            out_ref[...] = total.astype(jnp.bfloat16)


def pair_sum(own, *come):
    vmem = pl.BlockSpec(memory_space=pltpu.VMEM)
    return pl.pallas_call(
        pair_sum_body,
        out_shape=(
            jax.ShapeDtypeStruct((3, HD, D_C), jnp.bfloat16),
            jax.ShapeDtypeStruct((HD, D_C), jnp.bfloat16),
        ),
        in_specs=[vmem] * (1 + len(come)),
        out_specs=(vmem, vmem),
        compiler_params=pltpu.CompilerParams(vmem_limit_bytes=vmem_bytes),
        name="pair_sum",
    )(own, *come)


def block_copies(near_ref, low, qkv_hbm, out_hbm, sems):
    highs, rows = near_ref.shape[0], near_ref.shape[1]
    copies = []
    for high in range(highs):
        block = lax.axis_index("gx") ^ (2 * high + low)
        at = pl.ds(pl.multiple_of(block * rows, rows), rows)
        for part, target in enumerate((qkv_hbm, out_hbm)):
            lanes = (slice(0, 3 * D_F), slice(3 * D_F, 4 * D_F))[part]
            copies.append(
                pltpu.make_async_copy(
                    near_ref.at[high, :, lanes], target.at[at, :], sems.at[high, part]
                )
            )
    for copy in copies:
        copy.start()
    return copies


def near_body(near_ref, x_ref, factor_ref, kept_ref, come_ref, qkv_hbm, out_hbm, dx_ref, sems):
    copies = block_copies(near_ref, 0, qkv_hbm, out_hbm, sems)
    tokens = x_ref[...].astype(jnp.float32).reshape(-1, D_C)
    upstream = kept_ref[...] + come_ref[...].astype(jnp.float32)
    grads = norm_backward(tokens, inverse_rms(tokens), factor_ref[...], upstream)
    dx_ref[...] = grads.astype(jnp.float32).reshape(dx_ref.shape).astype(jnp.bfloat16)
    for copy in copies:
        copy.wait()


def far_body(far_ref, qkv_in, out_in, qkv_hbm, out_hbm, sems):
    for copy in block_copies(far_ref, 1, qkv_hbm, out_hbm, sems):
        copy.wait()


def near_step(near, tokens, *operands):
    vmem = pl.BlockSpec(memory_space=pltpu.VMEM)
    hbm = pl.BlockSpec(memory_space=pltpu.HBM)
    return pl.pallas_call(
        near_body,
        out_shape=(
            jax.ShapeDtypeStruct((D_F, 3 * D_F), jnp.bfloat16),
            jax.ShapeDtypeStruct((D_F, D_F), jnp.bfloat16),
            jax.ShapeDtypeStruct(tokens.shape, jnp.bfloat16),
        ),
        in_specs=[vmem] * 5,
        out_specs=(hbm, hbm, vmem),
        scratch_shapes=[pltpu.SemaphoreType.DMA((near.shape[0], 2))],
        compiler_params=pltpu.CompilerParams(vmem_limit_bytes=vmem_bytes),
        name="near_step",
    )(near, tokens, *operands)


def far_step(far, qkv, out):
    vmem = pl.BlockSpec(memory_space=pltpu.VMEM)
    hbm = pl.BlockSpec(memory_space=pltpu.HBM)
    return pl.pallas_call(
        far_body,
        out_shape=(
            jax.ShapeDtypeStruct(qkv.shape, qkv.dtype),
            jax.ShapeDtypeStruct(out.shape, out.dtype),
        ),
        in_specs=[vmem, hbm, hbm],
        out_specs=(hbm, hbm),
        input_output_aliases={1: 0, 2: 1},
        scratch_shapes=[pltpu.SemaphoreType.DMA((far.shape[0], 2))],
        compiler_params=pltpu.CompilerParams(vmem_limit_bytes=vmem_bytes),
        name="far_step",
    )(far, qkv, out)


def neighbours(to_near, to_far, axis):
    peers = lax.axis_size(axis)
    near = [(i, i ^ 1) for i in range(peers)]
    far = [(i, i + 1 if i % 2 else i - 1) for i in range(1, peers - 1)]
    from_far = lax.ppermute(to_far, axis, far)
    return lax.ppermute(to_near, axis, near), from_far


def swapped(value, axis, mask):
    return lax.ppermute(value, axis, [(i, i ^ mask) for i in range(lax.axis_size(axis))])


def tied(*arrays):
    return lax.optimization_barrier(arrays)


def batch_sum(partial):
    if lax.axis_size("batch") != 2:
        return lax.psum(partial, "batch")
    return wide(partial) + wide(swapped(partial, "batch", 1))


def wide(value):
    return value.astype(jnp.float32)


def narrow(value):
    return value.astype(jnp.bfloat16)


def all_rows(piece):
    downs = lax.axis_size("gy")
    return jnp.stack([piece] + [swapped(piece, "gy", row) for row in range(1, downs)])


def local(
    x_fine,
    dy_fine,
    x_coarse,
    dy_coarse,
    timestep,
    fine_gain,
    coarse_gain,
    fine_qkv,
    fine_out,
    coarse_qkv,
    coarse_out,
):
    picture, cotangent = x_fine[0], dy_fine[0]
    across, downs = lax.axis_size("gx"), lax.axis_size("gy")
    assert across == 4 and downs & (downs - 1) == 0

    payloads = row_edges(picture, cotangent)
    row_near, row_far = neighbours(*payloads, "gy")
    own = packed(payloads, x_coarse[0], dy_coarse[0])
    count = own.shape[0]
    pieces = [own] + [swapped(own, "gy", row) for row in range(1, downs)]
    edges = col_edges(picture, cotangent, row_far, row_near)
    *edges, step, gain_f, gain_c = tied(*edges, timestep, fine_gain, coarse_gain)
    col_near, col_far = neighbours(*edges, "gx")
    factor, coarse_factor = time_factors(step, gain_f, gain_c)
    factor, *pieces = tied(factor, *pieces)
    row_group = jnp.stack(pieces)
    cross = swapped(row_group, "gx", 2)
    beside = swapped(row_group, "gx", 1)
    col_far, col_near, row_group = tied(col_far, col_near, row_group)
    dx_picture, fine_keep, fine_send = fine_block(
        (across, downs),
        picture,
        cotangent,
        row_far,
        row_near,
        col_far,
        col_near,
        factor,
        fine_qkv,
        fine_out,
    )
    fine_half = fine_keep + wide(swapped(fine_send, "gx", 1))
    opposite = swapped(cross, "gx", 1)

    fine_quarter = narrow(fine_half[0] + wide(swapped(narrow(fine_half[1]), "gx", 2)))
    everyone = jnp.stack([row_group, cross, beside, opposite]).reshape(-1, 2 * D_C)
    parts, coarse_partial = coarse_block(
        everyone[:, :D_C], everyone[:, D_C:], coarse_factor, coarse_qkv, coarse_out
    )
    fine_quarter, parts, coarse_partial = tied(fine_quarter, parts, coarse_partial)

    rows = D_F // across
    fine_quarter = narrow(batch_sum(fine_quarter)).reshape(rows, 4 * D_F)
    parts = parts.reshape(2, 2, downs, count, D_C)
    coarse_kept = wide(parts[0]) + wide(swapped(parts[1], "gx", 1))
    fine_quarter, coarse_kept, coarse_partial = tied(fine_quarter, coarse_kept, coarse_partial)

    pair_batch = lax.axis_size("batch") == 2
    cut = 7 * HD // 4
    halves = (coarse_partial[:cut], coarse_partial[cut:])
    others = [swapped(half, "batch", 1) if pair_batch else half for half in halves]
    mask = 1
    while mask < downs:
        last = 2 * mask == downs
        coarse_kept = coarse_kept.reshape(2, -1, 2, count, D_C)
        sent = narrow(coarse_kept[:, :, 1]).reshape(-1, D_C)
        come = swapped(jnp.concatenate([fine_quarter, sent], axis=0), "gy", mask)
        coarse_kept = coarse_kept[:, :, 0]
        coarse_kept = coarse_kept + wide(come[rows:]).reshape(coarse_kept.shape)
        fine_quarter = narrow(wide(fine_quarter) + wide(come[:rows]))
        at = int(last)
        fine_quarter, coarse_kept, others[at] = tied(fine_quarter, coarse_kept, others[at])
        mask *= 2

    coarse_kept = coarse_kept.reshape(2, count, D_C)
    come = swapped(jnp.concatenate([fine_quarter, narrow(coarse_kept[1])], axis=0), "gx", 2)
    if pair_batch:
        grad_coarse_qkv, grad_coarse_out = pair_sum(coarse_partial, *others)
    else:
        coarse_sum = narrow(batch_sum(wide(coarse_partial)))
        grad_coarse_qkv = coarse_sum[: 3 * HD].reshape(coarse_qkv.shape)
        grad_coarse_out = coarse_sum[3 * HD :]
    come, grad_coarse_qkv, grad_coarse_out = tied(come, grad_coarse_qkv, grad_coarse_out)
    fine_pair = jnp.stack([fine_quarter, come[:rows]])
    near_qkv, near_out, dx_coarse = near_step(
        fine_pair, x_coarse[0], coarse_factor, coarse_kept[0], come[rows:]
    )
    far_pair = swapped(fine_pair, "gx", 1)
    far_pair, near_qkv, near_out = tied(far_pair, near_qkv, near_out)
    grad_qkv, grad_out = far_step(far_pair, near_qkv, near_out)
    return (
        dx_picture[None],
        dx_coarse[None],
        grad_qkv,
        grad_out,
        grad_coarse_qkv,
        grad_coarse_out,
    )


def solution(mesh):
    placed = (
        P("batch", "gy", "gx", None),
        P("batch", "gy", "gx", None),
        P("batch", "gy", "gx", None),
        P("batch", "gy", "gx", None),
        P("batch"),
        P(),
        P(),
        P(),
        P(),
        P(None, plane_spec, None),
        P(plane_spec, None),
    )
    return jax.shard_map(
        local,
        mesh=mesh,
        in_specs=placed,
        out_specs=(
            P("batch", "gy", "gx", None),
            P("batch", "gy", "gx", None),
            P(),
            P(),
            P(None, plane_spec, None),
            P(plane_spec, None),
        ),
        check_vma=False,
    )


plane_spec = ("gy", "gx")
```

```python
import math

import jax
import jax.numpy as jnp
import numpy as np
from jax import lax
from jax.experimental import pallas as pl
from jax.experimental.pallas import tpu as pltpu
from jax.sharding import PartitionSpec as P

D_F = 256
H_F = 4
D_C = 1024
HD = 64
RAD = 3
HALO = 2 * RAD

eps = 1e-06
log_span = math.log(1000.0)
side = 8
extent = side + 2 * RAD
lanes_wide = 16
thin = 4
lag = 2
scale = 1.0 / math.sqrt(HD)
vmem_bytes = 48 * 1024 * 1024


def dot(first, second, dims=((1,), (0,))):
    return lax.dot_general(first, second, (dims, ((), ())), preferred_element_type=jnp.float32)


def frequencies(channels):
    steps = np.float32(-log_span) * np.arange(channels, dtype=np.float32) / np.float32(channels)
    return np.exp(steps)[None]


def odd_rank(axis):
    return lax.axis_index(axis) & 1 == 1


def inverse_rms(floats):
    return lax.rsqrt(jnp.mean(floats * floats, axis=-1, keepdims=True) + eps)


def norm_backward(floats, inverse, factor, upstream):
    scaled = upstream * factor
    middle = jnp.mean(floats * scaled, axis=-1, keepdims=True)
    return (inverse * scaled - floats * inverse * inverse * inverse * middle).astype(jnp.bfloat16)


def round_up(value, multiple):
    return -(-value // multiple) * multiple


def in_order(axis, near, far):
    odd = odd_rank(axis)
    first, second = near[...].astype(jnp.float32), far[...].astype(jnp.float32)
    return jnp.where(odd, first, second), jnp.where(odd, second, first)


def fine_body(
    x_ref,
    dy_ref,
    row_far_ref,
    row_near_ref,
    col_far_ref,
    col_near_ref,
    factor_ref,
    qkv_ref,
    out_ref,
    dx_ref,
    keep_ref,
    send_ref,
    x_grid,
    dy_grid,
    k_grid,
    v_grid,
    q_grid,
    u_grid,
    dk_grid,
    dv_grid,
    dq_grid,
    a_grid,
    total_ref,
    *scratch,
):
    height, breadth = x_ref.shape[0], x_ref.shape[1]
    grid_rows, grid_cols = x_grid.shape[0], x_grid.shape[1]
    query_rows = dy_grid.shape[0]
    floats = jnp.float32
    factor = factor_ref[...]

    for grid, rows in ((x_grid, height + 2 * HALO), (dy_grid, height + 2 * RAD)):
        grid[rows:] = jnp.zeros((grid.shape[0] - rows,) + grid.shape[1:], floats)
        cols = HALO + breadth
        grid[:rows, :HALO] = jnp.zeros((rows, HALO, D_F), floats)
        grid[:rows, cols:] = jnp.zeros((rows, grid_cols - cols, D_F), floats)
    dk_grid[...] = jnp.zeros_like(dk_grid)
    dv_grid[...] = jnp.zeros_like(dv_grid)
    inner = slice(HALO, HALO + breadth)
    above, below = in_order("gy", row_near_ref, row_far_ref)
    left, right = in_order("gx", col_near_ref, col_far_ref)
    x_grid[0:HALO, inner] = above[0:HALO]
    x_grid[HALO : HALO + height, inner] = x_ref[...].astype(floats)
    x_grid[HALO + height : HALO + height + HALO, inner] = below[0:HALO]
    dy_grid[0:RAD, inner] = above[HALO : HALO + RAD]
    dy_grid[RAD : RAD + height, inner] = dy_ref[...].astype(floats)
    dy_grid[RAD + height : RAD + height + RAD, inner] = below[HALO : HALO + RAD]
    for strip, x_first, dy_first in (
        (left, 0, RAD),
        (right, HALO + breadth, HALO + breadth),
    ):
        at = 0
        for grid, first, width, rows in (
            (x_grid, x_first, HALO, height + 2 * HALO),
            (dy_grid, dy_first, RAD, height + 2 * RAD),
        ):
            for row in range(rows):
                grid[row, first : first + width] = strip[at : at + width]
                at += width

    tokens = x_grid[...].reshape(grid_rows * grid_cols, D_F)
    normed = (tokens * inverse_rms(tokens) * factor).astype(jnp.bfloat16)
    key_values = dot(normed, qkv_ref[:, D_F:]).astype(jnp.bfloat16).astype(floats)
    k_grid[...] = key_values[:, :D_F].reshape(grid_rows, grid_cols, D_F)
    v_grid[...] = key_values[:, D_F:].reshape(grid_rows, grid_cols, D_F)
    query_tokens = normed[RAD * grid_cols : (RAD + query_rows) * grid_cols]
    queries = dot(query_tokens, qkv_ref[:, :D_F]).astype(jnp.bfloat16).astype(floats) * scale
    q_grid[...] = queries.reshape(query_rows, grid_cols, D_F)
    cotangents = dy_grid[...].reshape(query_rows * grid_cols, D_F).astype(jnp.bfloat16)
    ups = dot(cotangents, out_ref[...], ((1,), (1,))).astype(jnp.bfloat16).astype(floats)
    u_grid[...] = ups.reshape(query_rows, grid_cols, D_F)

    gx, gy = lax.axis_index("gx"), lax.axis_index("gy")
    row_low, col_low = HALO - gy * height, HALO - gx * breadth
    row_high = row_low + lax.axis_size("gy") * height
    col_high = col_low + lax.axis_size("gx") * breadth

    def window_bias(query_rows):
        shape = ((query_rows + 2 * RAD) * lanes_wide, H_F * query_rows * side)
        key_at = lax.broadcasted_iota(jnp.int32, shape, 0)
        query_at = lax.broadcasted_iota(jnp.int32, shape, 1)
        row_gap = (key_at // lanes_wide) - ((query_at // side) % query_rows)
        col_gap = (key_at % lanes_wide) - (query_at % side)
        near = (row_gap >= 0) & (row_gap <= 2 * RAD) & (col_gap >= 0) & (col_gap <= 2 * RAD)
        return jnp.where(near, 0.0, -1e30)

    own_scratch, thin_scratch = scratch[:7], scratch[7:]
    own_scratch[-1][...] = window_bias(side)
    thin_scratch[-1][...] = window_bias(thin)

    def head_of(rows):
        return lax.broadcasted_iota(jnp.int32, (rows, D_F), 1) // HD

    def spread(block):
        block = block.reshape(-1, D_F)
        heads = head_of(block.shape[0])
        return jnp.concatenate(
            [jnp.where(heads == h, block, 0.0).astype(jnp.bfloat16) for h in range(H_F)], axis=0
        )

    def collect(full):
        rows = full.shape[0] // H_F
        heads = head_of(rows)
        total = jnp.where(heads == 0, full[:rows], 0.0)
        for h in range(1, H_F):
            total = jnp.where(heads == h, full[h * rows : (h + 1) * rows], total)
        return total.reshape(rows // side, side, D_F)

    def windows(task):
        top, start, query_rows = task[:3]
        window = (slice(top, top + query_rows + 2 * RAD), slice(start, start + lanes_wide))
        keys = k_grid[window].reshape(-1, D_F).astype(jnp.bfloat16)
        return keys, v_grid[window].reshape(-1, D_F).astype(jnp.bfloat16)

    def begin(task):
        top, start, query_rows, live, scratch, index = task
        score_ref, product_ref, query_ref, up_ref = scratch[:4]
        keys, values = windows(task)
        place = (slice(top, top + query_rows), slice(start + RAD, start + RAD + side))
        wide_queries = spread(q_grid[place])
        ups = u_grid[place]
        if live < query_rows:
            row = lax.broadcasted_iota(jnp.int32, ups.shape, 0)
            ups = jnp.where(row < live, ups, 0.0)
        wide_ups = spread(ups)
        query_ref[index], up_ref[index] = wide_queries, wide_ups
        score_ref[index] = dot(keys, wide_queries, ((1,), (1,)))
        product_ref[index] = dot(values, wide_ups, ((1,), (1,)))

    def share(task):
        top, start, query_rows, live, scratch, index = task
        score_ref, product_ref, _, _, weight_ref, slope_ref, near_bias = scratch
        lone = lax.broadcasted_iota(jnp.int32, ((query_rows + 2 * RAD) * lanes_wide, 1), 0)
        key_row, key_col = lone // lanes_wide + top, lone % lanes_wide + start
        inside = (key_row >= row_low) & (key_row < row_high)
        inside = inside & (key_col >= col_low) & (key_col < col_high)
        scores = score_ref[index] + (near_bias[...] + jnp.where(inside, 0.0, -1e30))
        raised = jnp.exp(scores - jnp.max(scores, axis=0, keepdims=True))
        shares = raised * (1.0 / jnp.sum(raised, axis=0, keepdims=True))
        products = product_ref[index]
        centre = jnp.sum(shares * products, axis=0, keepdims=True)
        slope_ref[index] = (shares * (products - centre)).astype(jnp.bfloat16)
        weight_ref[index] = shares.astype(jnp.bfloat16)

    def finish(task):
        top, start, query_rows, live, scratch, index = task
        query_ref, up_ref, weight_ref, slope_ref = scratch[2:6]
        first, final = max(top, HALO), min(top + query_rows + 2 * RAD, HALO + height)
        kept = slice((first - top) * lanes_wide, (final - top) * lanes_wide)
        target = (slice(first - HALO, final - HALO), slice(start, start + lanes_wide))
        shape = (final - first, lanes_wide, D_F)
        dv_grid[target] += dot(weight_ref[index, kept], up_ref[index]).reshape(shape)
        dk_grid[target] += dot(slope_ref[index, kept], query_ref[index]).reshape(shape)
        if live == side:
            keys, values = windows(task)
            block = (slice(top - RAD, top - RAD + side), slice(start, start + side))
            a_grid[block] = collect(dot(weight_ref[index], values, ((0,), (0,))))
            dq_grid[block] = collect(dot(slope_ref[index], keys, ((0,), (0,))))

    tasks = []
    for start in range(0, grid_cols - side, side):
        for top in range(RAD, RAD + height, side):
            tasks.append((top, start, side, side, own_scratch, len(tasks)))
    for index, start in enumerate(range(0, grid_cols - side, side)):
        tasks.append((0, start, thin, RAD, thin_scratch, 2 * index))
        tasks.append((RAD + height, start, thin, thin, thin_scratch, 2 * index + 1))
    for turn in range(len(tasks) + 2 * lag):
        if turn < len(tasks):
            begin(tasks[turn])
        if 0 <= turn - lag < len(tasks):
            share(tasks[turn - lag])
        if turn >= 2 * lag:
            finish(tasks[turn - 2 * lag])

    count = height * breadth
    own_queries = (slice(0, height), slice(RAD, RAD + breadth))
    own_keys = (slice(0, height), inner)
    attended = a_grid[own_queries].reshape(count, D_F).astype(jnp.bfloat16)
    grad_q = (dq_grid[own_queries].reshape(count, D_F) * scale).astype(jnp.bfloat16)
    grad_k = dk_grid[own_keys].reshape(count, D_F).astype(jnp.bfloat16)
    grad_v = dv_grid[own_keys].reshape(count, D_F).astype(jnp.bfloat16)
    grad_proj = jnp.concatenate([grad_q, grad_k, grad_v], axis=1)
    picture = x_ref[...].reshape(count, D_F).astype(floats)
    inverse = inverse_rms(picture)
    own_normed = (picture * inverse * factor).astype(jnp.bfloat16)
    flat_cot = dy_ref[...].reshape(count, D_F)
    grads = jnp.concatenate(
        [
            dot(own_normed, grad_proj, ((0,), (0,))),
            dot(attended, flat_cot, ((0,), (0,))),
        ],
        axis=1,
    )
    half, columns = keep_ref.shape[0], keep_ref.shape[1]
    total_ref[...] = grads.reshape(total_ref.shape)
    for low in range(2):
        target = (keep_ref, send_ref)[low]
        for high in range(half):
            for row in range(columns):
                block = (gx ^ (2 * high + low)) * columns + row
                target[high, row] = total_ref[block].astype(target.dtype)
    down = dot(grad_proj, qkv_ref[...], ((1,), (1,)))
    dx_ref[...] = norm_backward(picture, inverse, factor, down).reshape(height, breadth, D_F)


def block_scratch(blocks, query_rows):
    keys_count, heads_count = (query_rows + 2 * RAD) * lanes_wide, H_F * query_rows * side
    square = (blocks, keys_count, heads_count)
    wide = (blocks, heads_count, D_F)
    return [
        pltpu.VMEM(square, jnp.float32),
        pltpu.VMEM(square, jnp.float32),
        pltpu.VMEM(wide, jnp.bfloat16),
        pltpu.VMEM(wide, jnp.bfloat16),
        pltpu.VMEM(square, jnp.bfloat16),
        pltpu.VMEM(square, jnp.bfloat16),
        pltpu.VMEM((keys_count, heads_count), jnp.float32),
    ]


def fine_block(peers, picture, *operands):
    height, breadth = picture.shape[0], picture.shape[1]
    query_rows = RAD + height + thin
    query_cols = round_up(breadth + 2 * RAD, side)
    grid_rows, grid_cols = query_rows + 2 * RAD, query_cols + side
    across, down = peers
    rows = D_F // (across * down)
    halves = (across // 2, down, rows, 4 * D_F)
    vmem = pl.BlockSpec(memory_space=pltpu.VMEM)
    wide = pltpu.VMEM((grid_rows, grid_cols, D_F), jnp.float32)
    middle = pltpu.VMEM((query_rows, grid_cols, D_F), jnp.float32)
    small = pltpu.VMEM((height, query_cols, D_F), jnp.float32)
    strip = pltpu.VMEM((height, grid_cols, D_F), jnp.float32)
    return pl.pallas_call(
        fine_body,
        out_shape=(
            jax.ShapeDtypeStruct((height, breadth, D_F), jnp.bfloat16),
            jax.ShapeDtypeStruct(halves, jnp.float32),
            jax.ShapeDtypeStruct(halves, jnp.bfloat16),
        ),
        in_specs=[vmem] * 9,
        out_specs=(vmem, vmem, vmem),
        scratch_shapes=[
            wide,
            middle,
            wide,
            wide,
            middle,
            middle,
            strip,
            strip,
            small,
            small,
            pltpu.VMEM((across * down, rows, 4 * D_F), jnp.float32),
            *block_scratch(query_cols // side * (height // side), side),
            *block_scratch(2 * (query_cols // side), thin),
        ],
        compiler_params=pltpu.CompilerParams(vmem_limit_bytes=vmem_bytes),
        name="fine_block",
    )(picture, *operands)


def coarse_body(
    x_ref,
    dy_ref,
    factor_ref,
    qkv_hbm,
    out_hbm,
    parts_ref,
    grads_ref,
    qkv_ref,
    out_ref,
    arrived,
):
    fetches = [
        pltpu.make_async_copy(qkv_hbm, qkv_ref, arrived.at[0]),
        pltpu.make_async_copy(out_hbm, out_ref, arrived.at[1]),
    ]
    for fetch in fetches:
        fetch.start()
    tokens = x_ref[...].astype(jnp.float32)
    normed = (tokens * inverse_rms(tokens) * factor_ref[...]).astype(jnp.bfloat16)
    cot = dy_ref[...]
    for fetch in fetches:
        fetch.wait()
    flat_qkv = qkv_ref[...].reshape(3 * HD, D_C)
    out_rows = out_ref[...]
    projected = dot(normed, flat_qkv, ((1,), (1,))).astype(jnp.bfloat16)
    queries, keys, values = projected[:, :HD], projected[:, HD : 2 * HD], projected[:, 2 * HD :]
    ups = dot(cot, out_rows, ((1,), (1,))).astype(jnp.bfloat16)
    scores = dot(queries, keys, ((1,), (1,))) * scale
    raised = jnp.exp(scores - jnp.max(scores, axis=-1, keepdims=True))
    shares = raised * (1.0 / jnp.sum(raised, axis=-1, keepdims=True))
    weights = shares.astype(jnp.bfloat16)
    mixed = dot(weights, values).astype(jnp.bfloat16)
    products = dot(ups, values, ((1,), (1,)))
    centre = jnp.sum(shares * products, axis=-1, keepdims=True)
    slopes = (shares * (products - centre)).astype(jnp.bfloat16)
    grad_q = (dot(slopes, keys) * scale).astype(jnp.bfloat16)
    grad_k = (dot(slopes, queries, ((0,), (0,))) * scale).astype(jnp.bfloat16)
    grad_v = dot(weights, ups, ((0,), (0,))).astype(jnp.bfloat16)
    stacked = jnp.concatenate([grad_q, grad_k, grad_v], axis=1)
    parts_ref[...] = dot(stacked, flat_qkv).astype(jnp.bfloat16)
    grads_ref[: 3 * HD] = dot(stacked, normed, ((0,), (0,))).astype(grads_ref.dtype)
    grads_ref[3 * HD :] = dot(mixed, cot, ((0,), (0,))).astype(grads_ref.dtype)


def coarse_block(tokens, cotangents, factor, head_qkv, head_out):
    count = tokens.shape[0]
    vmem = pl.BlockSpec(memory_space=pltpu.VMEM)
    return pl.pallas_call(
        coarse_body,
        out_shape=(
            jax.ShapeDtypeStruct((count, D_C), jnp.bfloat16),
            jax.ShapeDtypeStruct((4 * HD, D_C), jnp.bfloat16),
        ),
        in_specs=[vmem] * 3 + [pl.BlockSpec(memory_space=pltpu.HBM)] * 2,
        out_specs=(vmem, vmem),
        scratch_shapes=[
            pltpu.VMEM(head_qkv.shape, jnp.bfloat16),
            pltpu.VMEM(head_out.shape, jnp.bfloat16),
            pltpu.SemaphoreType.DMA((2,)),
        ],
        compiler_params=pltpu.CompilerParams(vmem_limit_bytes=vmem_bytes),
        name="coarse_block",
    )(tokens, cotangents, factor, head_qkv, head_out)


def row_edges_body(x_low, x_high, dy_low, dy_high, near_ref, far_ref):
    odd = odd_rank("gy")

    def fill(low_ref, high_ref):
        low_ref[:HALO], low_ref[HALO:] = x_low[...], dy_low[...]
        high_ref[:HALO], high_ref[HALO:] = x_high[...], dy_high[...]

    @pl.when(odd)
    def _():
        fill(near_ref, far_ref)

    @pl.when(jnp.logical_not(odd))
    def _():
        fill(far_ref, near_ref)


def row_edges(picture, cotangent):
    vmem = pl.BlockSpec(memory_space=pltpu.VMEM)
    height = picture.shape[0]
    shape = jax.ShapeDtypeStruct((HALO + RAD,) + picture.shape[1:], jnp.bfloat16)
    return pl.pallas_call(
        row_edges_body,
        out_shape=(shape, shape),
        in_specs=[vmem] * 4,
        out_specs=(vmem, vmem),
        compiler_params=pltpu.CompilerParams(vmem_limit_bytes=vmem_bytes),
        name="row_edges",
    )(picture[:HALO], picture[height - HALO :], cotangent[:RAD], cotangent[height - RAD :])


def col_edges_body(x_ref, dy_ref, row_far_ref, row_near_ref, near_ref, far_ref, *scratch):
    above, below = in_order("gy", row_near_ref, row_far_ref)
    breadth = x_ref.shape[1]
    odd = odd_rank("gx")
    x_rows = jnp.concatenate([above[:HALO], x_ref[...].astype(jnp.float32), below[:HALO]], axis=0)
    dy_rows = jnp.concatenate([above[HALO:], dy_ref[...].astype(jnp.float32), below[HALO:]], axis=0)
    at = 0
    for rows, width in ((x_rows, HALO), (dy_rows, RAD)):
        for row in range(rows.shape[0]):
            first, final = rows[row, :width], rows[row, breadth - width :]
            scratch[0][at : at + width] = jnp.where(odd, first, final)
            scratch[1][at : at + width] = jnp.where(odd, final, first)
            at += width
    pad = jnp.zeros((scratch[0].shape[0] - at, D_F), jnp.float32)
    for held, target in zip(scratch, (near_ref, far_ref)):
        held[at:] = pad
        target[...] = held[...].astype(jnp.bfloat16)


def col_edges(picture, cotangent, row_far, row_near):
    vmem = pl.BlockSpec(memory_space=pltpu.VMEM)
    height = picture.shape[0]
    rows = round_up((height + 2 * HALO) * HALO + (height + 2 * RAD) * RAD, 16)
    shape = jax.ShapeDtypeStruct((rows, D_F), jnp.bfloat16)
    return pl.pallas_call(
        col_edges_body,
        out_shape=(shape, shape),
        in_specs=[vmem] * 4,
        out_specs=(vmem, vmem),
        scratch_shapes=[pltpu.VMEM((rows, D_F), jnp.float32)] * 2,
        compiler_params=pltpu.CompilerParams(vmem_limit_bytes=vmem_bytes),
        name="col_edges",
    )(picture, cotangent, row_far, row_near)


def pack_body(first, second, x_ref, dy_ref, own_ref):
    own_ref[:, :D_C] = x_ref[...].astype(jnp.float32).reshape(-1, D_C).astype(jnp.bfloat16)
    own_ref[:, D_C:] = dy_ref[...].astype(jnp.float32).reshape(-1, D_C).astype(jnp.bfloat16)


def packed(after, tokens, cotangents):
    vmem = pl.BlockSpec(memory_space=pltpu.VMEM)
    count = tokens.shape[0] * tokens.shape[1]
    return pl.pallas_call(
        pack_body,
        out_shape=jax.ShapeDtypeStruct((count, 2 * D_C), jnp.bfloat16),
        in_specs=[pl.BlockSpec(memory_space=pl.ANY)] * 2 + [vmem] * 2,
        out_specs=vmem,
        compiler_params=pltpu.CompilerParams(vmem_limit_bytes=vmem_bytes),
        name="pack_coarse",
    )(*after, tokens, cotangents)


def factors_body(step, fine_gain, coarse_gain, fine_freq, coarse_freq, fine_ref, coarse_ref):
    time = step[0].astype(jnp.float32)
    fine_ref[...] = fine_gain[...] * (1.0 + 0.5 * jnp.cos(time * fine_freq[...]))
    coarse_ref[...] = coarse_gain[...] * (1.0 + 0.5 * jnp.cos(time * coarse_freq[...]))


def time_factors(step, fine_gain, coarse_gain):
    vmem = pl.BlockSpec(memory_space=pltpu.VMEM)
    return pl.pallas_call(
        factors_body,
        out_shape=(
            jax.ShapeDtypeStruct((1, D_F), jnp.float32),
            jax.ShapeDtypeStruct((1, D_C), jnp.float32),
        ),
        in_specs=[pl.BlockSpec(memory_space=pltpu.SMEM)] + [vmem] * 4,
        out_specs=(vmem, vmem),
        compiler_params=pltpu.CompilerParams(vmem_limit_bytes=vmem_bytes),
        name="time_factors",
    )(step, fine_gain[None], coarse_gain[None], frequencies(D_F), frequencies(D_C))


def pair_sum_body(own, *refs):
    qkv_ref, out_ref = refs[-2:]
    come = jnp.concatenate([ref[...] for ref in refs[:-2]], axis=0)
    for part in range(4):
        rows = slice(part * HD, (part + 1) * HD)
        total = own[rows].astype(jnp.float32) + come[rows].astype(jnp.float32)
        if part < 3:
            qkv_ref[part] = total.astype(jnp.bfloat16)
        else:
            out_ref[...] = total.astype(jnp.bfloat16)


def pair_sum(own, *come):
    vmem = pl.BlockSpec(memory_space=pltpu.VMEM)
    return pl.pallas_call(
        pair_sum_body,
        out_shape=(
            jax.ShapeDtypeStruct((3, HD, D_C), jnp.bfloat16),
            jax.ShapeDtypeStruct((HD, D_C), jnp.bfloat16),
        ),
        in_specs=[vmem] * (1 + len(come)),
        out_specs=(vmem, vmem),
        compiler_params=pltpu.CompilerParams(vmem_limit_bytes=vmem_bytes),
        name="pair_sum",
    )(own, *come)


def block_copies(near_ref, low, qkv_hbm, out_hbm, sems):
    highs, rows = near_ref.shape[0], near_ref.shape[1]
    copies = []
    for high in range(highs):
        block = lax.axis_index("gx") ^ (2 * high + low)
        at = pl.ds(pl.multiple_of(block * rows, rows), rows)
        for part, target in enumerate((qkv_hbm, out_hbm)):
            lanes = (slice(0, 3 * D_F), slice(3 * D_F, 4 * D_F))[part]
            copies.append(
                pltpu.make_async_copy(
                    near_ref.at[high, :, lanes], target.at[at, :], sems.at[high, part]
                )
            )
    for copy in copies:
        copy.start()
    return copies


def near_body(near_ref, x_ref, factor_ref, kept_ref, come_ref, qkv_hbm, out_hbm, dx_ref, sems):
    copies = block_copies(near_ref, 0, qkv_hbm, out_hbm, sems)
    tokens = x_ref[...].astype(jnp.float32).reshape(-1, D_C)
    upstream = kept_ref[...] + come_ref[...].astype(jnp.float32)
    grads = norm_backward(tokens, inverse_rms(tokens), factor_ref[...], upstream)
    dx_ref[...] = grads.astype(jnp.float32).reshape(dx_ref.shape).astype(jnp.bfloat16)
    for copy in copies:
        copy.wait()


def far_body(far_ref, qkv_in, out_in, qkv_hbm, out_hbm, sems):
    for copy in block_copies(far_ref, 1, qkv_hbm, out_hbm, sems):
        copy.wait()


def near_step(near, tokens, *operands):
    vmem = pl.BlockSpec(memory_space=pltpu.VMEM)
    hbm = pl.BlockSpec(memory_space=pltpu.HBM)
    return pl.pallas_call(
        near_body,
        out_shape=(
            jax.ShapeDtypeStruct((D_F, 3 * D_F), jnp.bfloat16),
            jax.ShapeDtypeStruct((D_F, D_F), jnp.bfloat16),
            jax.ShapeDtypeStruct(tokens.shape, jnp.bfloat16),
        ),
        in_specs=[vmem] * 5,
        out_specs=(hbm, hbm, vmem),
        scratch_shapes=[pltpu.SemaphoreType.DMA((near.shape[0], 2))],
        compiler_params=pltpu.CompilerParams(vmem_limit_bytes=vmem_bytes),
        name="near_step",
    )(near, tokens, *operands)


def far_step(far, qkv, out):
    vmem = pl.BlockSpec(memory_space=pltpu.VMEM)
    hbm = pl.BlockSpec(memory_space=pltpu.HBM)
    return pl.pallas_call(
        far_body,
        out_shape=(
            jax.ShapeDtypeStruct(qkv.shape, qkv.dtype),
            jax.ShapeDtypeStruct(out.shape, out.dtype),
        ),
        in_specs=[vmem, hbm, hbm],
        out_specs=(hbm, hbm),
        input_output_aliases={1: 0, 2: 1},
        scratch_shapes=[pltpu.SemaphoreType.DMA((far.shape[0], 2))],
        compiler_params=pltpu.CompilerParams(vmem_limit_bytes=vmem_bytes),
        name="far_step",
    )(far, qkv, out)


def neighbours(to_near, to_far, axis):
    peers = lax.axis_size(axis)
    near = [(i, i ^ 1) for i in range(peers)]
    far = [(i, i + 1 if i % 2 else i - 1) for i in range(1, peers - 1)]
    from_far = lax.ppermute(to_far, axis, far)
    return lax.ppermute(to_near, axis, near), from_far


def swapped(value, axis, mask):
    return lax.ppermute(value, axis, [(i, i ^ mask) for i in range(lax.axis_size(axis))])


def tied(*arrays):
    return lax.optimization_barrier(arrays)


def batch_sum(partial):
    if lax.axis_size("batch") != 2:
        return lax.psum(partial, "batch")
    return wide(partial) + wide(swapped(partial, "batch", 1))


def wide(value):
    return value.astype(jnp.float32)


def narrow(value):
    return value.astype(jnp.bfloat16)


def all_rows(piece):
    downs = lax.axis_size("gy")
    return jnp.stack([piece] + [swapped(piece, "gy", row) for row in range(1, downs)])


def local(
    x_fine,
    dy_fine,
    x_coarse,
    dy_coarse,
    timestep,
    fine_gain,
    coarse_gain,
    fine_qkv,
    fine_out,
    coarse_qkv,
    coarse_out,
):
    picture, cotangent = x_fine[0], dy_fine[0]
    across, downs = lax.axis_size("gx"), lax.axis_size("gy")
    assert across == 4 and downs & (downs - 1) == 0

    payloads = row_edges(picture, cotangent)
    row_near, row_far = neighbours(*payloads, "gy")
    own = packed(payloads, x_coarse[0], dy_coarse[0])
    count = own.shape[0]
    pieces = [own] + [swapped(own, "gy", row) for row in range(1, downs)]
    edges = col_edges(picture, cotangent, row_far, row_near)
    *edges, step, gain_f, gain_c = tied(*edges, timestep, fine_gain, coarse_gain)
    col_near, col_far = neighbours(*edges, "gx")
    factor, coarse_factor = time_factors(step, gain_f, gain_c)
    factor, *pieces = tied(factor, *pieces)
    row_group = jnp.stack(pieces)
    cross = swapped(row_group, "gx", 2)
    beside = swapped(row_group, "gx", 1)
    col_far, col_near, row_group = tied(col_far, col_near, row_group)
    dx_picture, fine_keep, fine_send = fine_block(
        (across, downs),
        picture,
        cotangent,
        row_far,
        row_near,
        col_far,
        col_near,
        factor,
        fine_qkv,
        fine_out,
    )
    fine_half = fine_keep + wide(swapped(fine_send, "gx", 1))
    opposite = swapped(cross, "gx", 1)
    fine_half, opposite = tied(fine_half, opposite)

    fine_quarter = narrow(fine_half[0] + wide(swapped(narrow(fine_half[1]), "gx", 2)))
    everyone = jnp.stack([row_group, cross, beside, opposite]).reshape(-1, 2 * D_C)
    parts, coarse_partial = coarse_block(
        everyone[:, :D_C], everyone[:, D_C:], coarse_factor, coarse_qkv, coarse_out
    )
    fine_quarter, parts, coarse_partial = tied(fine_quarter, parts, coarse_partial)

    rows = D_F // across
    fine_quarter = narrow(batch_sum(fine_quarter)).reshape(rows, 4 * D_F)
    parts = parts.reshape(2, 2, downs, count, D_C)
    coarse_kept = wide(parts[0]) + wide(swapped(parts[1], "gx", 1))
    fine_quarter, coarse_kept, coarse_partial = tied(fine_quarter, coarse_kept, coarse_partial)

    pair_batch = lax.axis_size("batch") == 2
    cut = 7 * HD // 4
    halves = (coarse_partial[:cut], coarse_partial[cut:])
    others = [swapped(half, "batch", 1) if pair_batch else half for half in halves]
    mask = 1
    while mask < downs:
        last = 2 * mask == downs
        coarse_kept = coarse_kept.reshape(2, -1, 2, count, D_C)
        sent = narrow(coarse_kept[:, :, 1]).reshape(-1, D_C)
        come = swapped(jnp.concatenate([fine_quarter, sent], axis=0), "gy", mask)
        coarse_kept = coarse_kept[:, :, 0]
        coarse_kept = coarse_kept + wide(come[rows:]).reshape(coarse_kept.shape)
        fine_quarter = narrow(wide(fine_quarter) + wide(come[:rows]))
        at = int(last)
        fine_quarter, coarse_kept, others[at] = tied(fine_quarter, coarse_kept, others[at])
        mask *= 2

    coarse_kept = coarse_kept.reshape(2, count, D_C)
    come = swapped(jnp.concatenate([fine_quarter, narrow(coarse_kept[1])], axis=0), "gx", 2)
    if pair_batch:
        grad_coarse_qkv, grad_coarse_out = pair_sum(coarse_partial, *others)
    else:
        coarse_sum = narrow(batch_sum(wide(coarse_partial)))
        grad_coarse_qkv = coarse_sum[: 3 * HD].reshape(coarse_qkv.shape)
        grad_coarse_out = coarse_sum[3 * HD :]
    come, grad_coarse_qkv, grad_coarse_out = tied(come, grad_coarse_qkv, grad_coarse_out)
    fine_pair = jnp.stack([fine_quarter, come[:rows]])
    near_qkv, near_out, dx_coarse = near_step(
        fine_pair, x_coarse[0], coarse_factor, coarse_kept[0], come[rows:]
    )
    far_pair = swapped(fine_pair, "gx", 1)
    far_pair, near_qkv, near_out = tied(far_pair, near_qkv, near_out)
    grad_qkv, grad_out = far_step(far_pair, near_qkv, near_out)
    return (
        dx_picture[None],
        dx_coarse[None],
        grad_qkv,
        grad_out,
        grad_coarse_qkv,
        grad_coarse_out,
    )


def solution(mesh):
    placed = (
        P("batch", "gy", "gx", None),
        P("batch", "gy", "gx", None),
        P("batch", "gy", "gx", None),
        P("batch", "gy", "gx", None),
        P("batch"),
        P(),
        P(),
        P(),
        P(),
        P(None, plane_spec, None),
        P(plane_spec, None),
    )
    return jax.shard_map(
        local,
        mesh=mesh,
        in_specs=placed,
        out_specs=(
            P("batch", "gy", "gx", None),
            P("batch", "gy", "gx", None),
            P(),
            P(),
            P(None, plane_spec, None),
            P(plane_spec, None),
        ),
        check_vma=False,
    )


plane_spec = ("gy", "gx")
```

```python
import math

import jax
import jax.numpy as jnp
import numpy as np
from jax import lax
from jax.experimental import pallas as pl
from jax.experimental.pallas import tpu as pltpu
from jax.sharding import PartitionSpec as P

D_F = 256
H_F = 4
D_C = 1024
HD = 64
RAD = 3
HALO = 2 * RAD

eps = 1e-06
log_span = math.log(1000.0)
side = 8
extent = side + 2 * RAD
lanes_wide = 16
thin = 4
lag = 2
scale = 1.0 / math.sqrt(HD)
vmem_bytes = 48 * 1024 * 1024


def dot(first, second, dims=((1,), (0,))):
    return lax.dot_general(first, second, (dims, ((), ())), preferred_element_type=jnp.float32)


def frequencies(channels):
    steps = np.float32(-log_span) * np.arange(channels, dtype=np.float32) / np.float32(channels)
    return np.exp(steps)[None]


def odd_rank(axis):
    return lax.axis_index(axis) & 1 == 1


def inverse_rms(floats):
    return lax.rsqrt(jnp.mean(floats * floats, axis=-1, keepdims=True) + eps)


def norm_backward(floats, inverse, factor, upstream):
    scaled = upstream * factor
    middle = jnp.mean(floats * scaled, axis=-1, keepdims=True)
    return (inverse * scaled - floats * inverse * inverse * inverse * middle).astype(jnp.bfloat16)


def round_up(value, multiple):
    return -(-value // multiple) * multiple


def in_order(axis, near, far):
    odd = odd_rank(axis)
    first, second = near[...].astype(jnp.float32), far[...].astype(jnp.float32)
    return jnp.where(odd, first, second), jnp.where(odd, second, first)


def fine_body(
    x_ref,
    dy_ref,
    row_far_ref,
    row_near_ref,
    col_far_ref,
    col_near_ref,
    factor_ref,
    qkv_ref,
    out_ref,
    dx_ref,
    keep_ref,
    send_ref,
    x_grid,
    dy_grid,
    k_grid,
    v_grid,
    q_grid,
    u_grid,
    dk_grid,
    dv_grid,
    dq_grid,
    a_grid,
    total_ref,
    *scratch,
):
    height, breadth = x_ref.shape[0], x_ref.shape[1]
    grid_rows, grid_cols = x_grid.shape[0], x_grid.shape[1]
    query_rows = dy_grid.shape[0]
    floats = jnp.float32
    factor = factor_ref[...]

    for grid, rows in ((x_grid, height + 2 * HALO), (dy_grid, height + 2 * RAD)):
        grid[rows:] = jnp.zeros((grid.shape[0] - rows,) + grid.shape[1:], floats)
        cols = breadth + 2 * HALO
        grid[:rows, cols:] = jnp.zeros((rows, grid_cols - cols, D_F), floats)
    dk_grid[...] = jnp.zeros_like(dk_grid)
    dv_grid[...] = jnp.zeros_like(dv_grid)
    inner = slice(HALO, HALO + breadth)
    above, below = in_order("gy", row_near_ref, row_far_ref)
    left, right = in_order("gx", col_near_ref, col_far_ref)
    x_grid[0:HALO, inner] = above[0:HALO]
    x_grid[HALO : HALO + height, inner] = x_ref[...].astype(floats)
    x_grid[HALO + height : HALO + height + HALO, inner] = below[0:HALO]
    dy_grid[0:RAD, inner] = above[HALO : HALO + RAD]
    dy_grid[RAD : RAD + height, inner] = dy_ref[...].astype(floats)
    dy_grid[RAD + height : RAD + height + RAD, inner] = below[HALO : HALO + RAD]
    left, right = left[:, left.shape[1] - HALO :], right[:, :HALO]
    for strip, first in ((left, 0), (right, HALO + breadth)):
        span = slice(first, first + HALO)
        at = 0
        for grid, begin, count in (
            (x_grid, 0, HALO),
            (dy_grid, 0, RAD),
            (x_grid, HALO, height),
            (dy_grid, RAD, height),
            (x_grid, HALO + height, HALO),
            (dy_grid, RAD + height, RAD),
        ):
            grid[begin : begin + count, span] = strip[at : at + count]
            at += count

    tokens = x_grid[...].reshape(grid_rows * grid_cols, D_F)
    normed = (tokens * inverse_rms(tokens) * factor).astype(jnp.bfloat16)
    key_values = dot(normed, qkv_ref[:, D_F:]).astype(jnp.bfloat16).astype(floats)
    k_grid[...] = key_values[:, :D_F].reshape(grid_rows, grid_cols, D_F)
    v_grid[...] = key_values[:, D_F:].reshape(grid_rows, grid_cols, D_F)
    query_tokens = normed[RAD * grid_cols : (RAD + query_rows) * grid_cols]
    queries = dot(query_tokens, qkv_ref[:, :D_F]).astype(jnp.bfloat16).astype(floats) * scale
    q_grid[...] = queries.reshape(query_rows, grid_cols, D_F)
    cotangents = dy_grid[...].reshape(query_rows * grid_cols, D_F).astype(jnp.bfloat16)
    ups = dot(cotangents, out_ref[...], ((1,), (1,))).astype(jnp.bfloat16).astype(floats)
    u_grid[...] = ups.reshape(query_rows, grid_cols, D_F)

    gx, gy = lax.axis_index("gx"), lax.axis_index("gy")
    row_low, col_low = HALO - gy * height, HALO - gx * breadth
    row_high = row_low + lax.axis_size("gy") * height
    col_high = col_low + lax.axis_size("gx") * breadth

    def window_bias(query_rows):
        shape = ((query_rows + 2 * RAD) * lanes_wide, H_F * query_rows * side)
        key_at = lax.broadcasted_iota(jnp.int32, shape, 0)
        query_at = lax.broadcasted_iota(jnp.int32, shape, 1)
        row_gap = (key_at // lanes_wide) - ((query_at // side) % query_rows)
        col_gap = (key_at % lanes_wide) - (query_at % side)
        near = (row_gap >= 0) & (row_gap <= 2 * RAD) & (col_gap >= 0) & (col_gap <= 2 * RAD)
        return jnp.where(near, 0.0, -1e30)

    own_scratch, thin_scratch = scratch[:7], scratch[7:]
    own_scratch[-1][...] = window_bias(side)
    thin_scratch[-1][...] = window_bias(thin)

    def head_of(rows):
        return lax.broadcasted_iota(jnp.int32, (rows, D_F), 1) // HD

    def spread(block):
        block = block.reshape(-1, D_F)
        heads = head_of(block.shape[0])
        return jnp.concatenate(
            [jnp.where(heads == h, block, 0.0).astype(jnp.bfloat16) for h in range(H_F)], axis=0
        )

    def collect(full):
        rows = full.shape[0] // H_F
        heads = head_of(rows)
        total = jnp.where(heads == 0, full[:rows], 0.0)
        for h in range(1, H_F):
            total = jnp.where(heads == h, full[h * rows : (h + 1) * rows], total)
        return total.reshape(rows // side, side, D_F)

    def windows(task):
        top, start, query_rows = task[:3]
        window = (slice(top, top + query_rows + 2 * RAD), slice(start, start + lanes_wide))
        keys = k_grid[window].reshape(-1, D_F).astype(jnp.bfloat16)
        return keys, v_grid[window].reshape(-1, D_F).astype(jnp.bfloat16)

    def begin(task):
        top, start, query_rows, live, scratch, index = task
        score_ref, product_ref, query_ref, up_ref = scratch[:4]
        keys, values = windows(task)
        place = (slice(top, top + query_rows), slice(start + RAD, start + RAD + side))
        wide_queries = spread(q_grid[place])
        ups = u_grid[place]
        if live < query_rows:
            row = lax.broadcasted_iota(jnp.int32, ups.shape, 0)
            ups = jnp.where(row < live, ups, 0.0)
        wide_ups = spread(ups)
        query_ref[index], up_ref[index] = wide_queries, wide_ups
        score_ref[index] = dot(keys, wide_queries, ((1,), (1,)))
        product_ref[index] = dot(values, wide_ups, ((1,), (1,)))

    def share(task):
        top, start, query_rows, live, scratch, index = task
        score_ref, product_ref, _, _, weight_ref, slope_ref, near_bias = scratch
        lone = lax.broadcasted_iota(jnp.int32, ((query_rows + 2 * RAD) * lanes_wide, 1), 0)
        key_row, key_col = lone // lanes_wide + top, lone % lanes_wide + start
        inside = (key_row >= row_low) & (key_row < row_high)
        inside = inside & (key_col >= col_low) & (key_col < col_high)
        scores = score_ref[index] + (near_bias[...] + jnp.where(inside, 0.0, -1e30))
        raised = jnp.exp(scores - jnp.max(scores, axis=0, keepdims=True))
        shares = raised * (1.0 / jnp.sum(raised, axis=0, keepdims=True))
        products = product_ref[index]
        centre = jnp.sum(shares * products, axis=0, keepdims=True)
        slope_ref[index] = (shares * (products - centre)).astype(jnp.bfloat16)
        weight_ref[index] = shares.astype(jnp.bfloat16)

    def finish(task):
        top, start, query_rows, live, scratch, index = task
        query_ref, up_ref, weight_ref, slope_ref = scratch[2:6]
        first, final = max(top, HALO), min(top + query_rows + 2 * RAD, HALO + height)
        kept = slice((first - top) * lanes_wide, (final - top) * lanes_wide)
        target = (slice(first - HALO, final - HALO), slice(start, start + lanes_wide))
        shape = (final - first, lanes_wide, D_F)
        dv_grid[target] += dot(weight_ref[index, kept], up_ref[index]).reshape(shape)
        dk_grid[target] += dot(slope_ref[index, kept], query_ref[index]).reshape(shape)
        if live == side:
            keys, values = windows(task)
            block = (slice(top - RAD, top - RAD + side), slice(start, start + side))
            a_grid[block] = collect(dot(weight_ref[index], values, ((0,), (0,))))
            dq_grid[block] = collect(dot(slope_ref[index], keys, ((0,), (0,))))

    tasks = []
    for start in range(0, grid_cols - side, side):
        for top in range(RAD, RAD + height, side):
            tasks.append((top, start, side, side, own_scratch, len(tasks)))
    for index, start in enumerate(range(0, grid_cols - side, side)):
        tasks.append((0, start, thin, RAD, thin_scratch, 2 * index))
        tasks.append((RAD + height, start, thin, thin, thin_scratch, 2 * index + 1))
    for turn in range(len(tasks) + 2 * lag):
        if turn < len(tasks):
            begin(tasks[turn])
        if 0 <= turn - lag < len(tasks):
            share(tasks[turn - lag])
        if turn >= 2 * lag:
            finish(tasks[turn - 2 * lag])

    count = height * breadth
    own_queries = (slice(0, height), slice(RAD, RAD + breadth))
    own_keys = (slice(0, height), inner)
    attended = a_grid[own_queries].reshape(count, D_F).astype(jnp.bfloat16)
    grad_q = (dq_grid[own_queries].reshape(count, D_F) * scale).astype(jnp.bfloat16)
    grad_k = dk_grid[own_keys].reshape(count, D_F).astype(jnp.bfloat16)
    grad_v = dv_grid[own_keys].reshape(count, D_F).astype(jnp.bfloat16)
    grad_proj = jnp.concatenate([grad_q, grad_k, grad_v], axis=1)
    picture = x_ref[...].reshape(count, D_F).astype(floats)
    inverse = inverse_rms(picture)
    own_normed = (picture * inverse * factor).astype(jnp.bfloat16)
    flat_cot = dy_ref[...].reshape(count, D_F)
    grads = jnp.concatenate(
        [
            dot(own_normed, grad_proj, ((0,), (0,))),
            dot(attended, flat_cot, ((0,), (0,))),
        ],
        axis=1,
    )
    half, columns = keep_ref.shape[0], keep_ref.shape[1]
    total_ref[...] = grads.reshape(total_ref.shape)
    for low in range(2):
        target = (keep_ref, send_ref)[low]
        for high in range(half):
            for row in range(columns):
                block = (gx ^ (2 * high + low)) * columns + row
                target[high, row] = total_ref[block].astype(target.dtype)
    down = dot(grad_proj, qkv_ref[...], ((1,), (1,)))
    dx_ref[...] = norm_backward(picture, inverse, factor, down).reshape(height, breadth, D_F)


def block_scratch(blocks, query_rows):
    keys_count, heads_count = (query_rows + 2 * RAD) * lanes_wide, H_F * query_rows * side
    square = (blocks, keys_count, heads_count)
    wide = (blocks, heads_count, D_F)
    return [
        pltpu.VMEM(square, jnp.float32),
        pltpu.VMEM(square, jnp.float32),
        pltpu.VMEM(wide, jnp.bfloat16),
        pltpu.VMEM(wide, jnp.bfloat16),
        pltpu.VMEM(square, jnp.bfloat16),
        pltpu.VMEM(square, jnp.bfloat16),
        pltpu.VMEM((keys_count, heads_count), jnp.float32),
    ]


def fine_block(peers, picture, *operands):
    height, breadth = picture.shape[0], picture.shape[1]
    query_rows = RAD + height + thin
    query_cols = round_up(breadth + 2 * RAD, side)
    grid_rows, grid_cols = query_rows + 2 * RAD, query_cols + side
    across, down = peers
    rows = D_F // (across * down)
    halves = (across // 2, down, rows, 4 * D_F)
    vmem = pl.BlockSpec(memory_space=pltpu.VMEM)
    wide = pltpu.VMEM((grid_rows, grid_cols, D_F), jnp.float32)
    middle = pltpu.VMEM((query_rows, grid_cols, D_F), jnp.float32)
    small = pltpu.VMEM((height, query_cols, D_F), jnp.float32)
    strip = pltpu.VMEM((height, grid_cols, D_F), jnp.float32)
    return pl.pallas_call(
        fine_body,
        out_shape=(
            jax.ShapeDtypeStruct((height, breadth, D_F), jnp.bfloat16),
            jax.ShapeDtypeStruct(halves, jnp.float32),
            jax.ShapeDtypeStruct(halves, jnp.bfloat16),
        ),
        in_specs=[vmem] * 9,
        out_specs=(vmem, vmem, vmem),
        scratch_shapes=[
            wide,
            middle,
            wide,
            wide,
            middle,
            middle,
            strip,
            strip,
            small,
            small,
            pltpu.VMEM((across * down, rows, 4 * D_F), jnp.float32),
            *block_scratch(query_cols // side * (height // side), side),
            *block_scratch(2 * (query_cols // side), thin),
        ],
        compiler_params=pltpu.CompilerParams(vmem_limit_bytes=vmem_bytes),
        name="fine_block",
    )(picture, *operands)


def coarse_body(
    x_ref,
    dy_ref,
    factor_ref,
    qkv_hbm,
    out_hbm,
    parts_ref,
    grads_ref,
    qkv_ref,
    out_ref,
    arrived,
):
    fetches = [
        pltpu.make_async_copy(qkv_hbm, qkv_ref, arrived.at[0]),
        pltpu.make_async_copy(out_hbm, out_ref, arrived.at[1]),
    ]
    for fetch in fetches:
        fetch.start()
    tokens = x_ref[...].astype(jnp.float32)
    normed = (tokens * inverse_rms(tokens) * factor_ref[...]).astype(jnp.bfloat16)
    cot = dy_ref[...]
    for fetch in fetches:
        fetch.wait()
    flat_qkv = qkv_ref[...].reshape(3 * HD, D_C)
    out_rows = out_ref[...]
    projected = dot(normed, flat_qkv, ((1,), (1,))).astype(jnp.bfloat16)
    queries, keys, values = projected[:, :HD], projected[:, HD : 2 * HD], projected[:, 2 * HD :]
    ups = dot(cot, out_rows, ((1,), (1,))).astype(jnp.bfloat16)
    scores = dot(queries, keys, ((1,), (1,))) * scale
    raised = jnp.exp(scores - jnp.max(scores, axis=-1, keepdims=True))
    shares = raised * (1.0 / jnp.sum(raised, axis=-1, keepdims=True))
    weights = shares.astype(jnp.bfloat16)
    mixed = dot(weights, values).astype(jnp.bfloat16)
    products = dot(ups, values, ((1,), (1,)))
    centre = jnp.sum(shares * products, axis=-1, keepdims=True)
    slopes = (shares * (products - centre)).astype(jnp.bfloat16)
    grad_q = (dot(slopes, keys) * scale).astype(jnp.bfloat16)
    grad_k = (dot(slopes, queries, ((0,), (0,))) * scale).astype(jnp.bfloat16)
    grad_v = dot(weights, ups, ((0,), (0,))).astype(jnp.bfloat16)
    stacked = jnp.concatenate([grad_q, grad_k, grad_v], axis=1)
    parts_ref[...] = dot(stacked, flat_qkv).astype(jnp.bfloat16)
    grads_ref[: 3 * HD] = dot(stacked, normed, ((0,), (0,))).astype(grads_ref.dtype)
    grads_ref[3 * HD :] = dot(mixed, cot, ((0,), (0,))).astype(grads_ref.dtype)


def coarse_block(tokens, cotangents, factor, head_qkv, head_out):
    count = tokens.shape[0]
    vmem = pl.BlockSpec(memory_space=pltpu.VMEM)
    return pl.pallas_call(
        coarse_body,
        out_shape=(
            jax.ShapeDtypeStruct((count, D_C), jnp.bfloat16),
            jax.ShapeDtypeStruct((4 * HD, D_C), jnp.bfloat16),
        ),
        in_specs=[vmem] * 3 + [pl.BlockSpec(memory_space=pltpu.HBM)] * 2,
        out_specs=(vmem, vmem),
        scratch_shapes=[
            pltpu.VMEM(head_qkv.shape, jnp.bfloat16),
            pltpu.VMEM(head_out.shape, jnp.bfloat16),
            pltpu.SemaphoreType.DMA((2,)),
        ],
        compiler_params=pltpu.CompilerParams(vmem_limit_bytes=vmem_bytes),
        name="coarse_block",
    )(tokens, cotangents, factor, head_qkv, head_out)


def row_edges_body(x_low, x_high, dy_low, dy_high, near_ref, far_ref):
    odd = odd_rank("gy")

    def fill(low_ref, high_ref):
        low_ref[:HALO], low_ref[HALO:] = x_low[...], dy_low[...]
        high_ref[:HALO], high_ref[HALO:] = x_high[...], dy_high[...]

    @pl.when(odd)
    def _():
        fill(near_ref, far_ref)

    @pl.when(jnp.logical_not(odd))
    def _():
        fill(far_ref, near_ref)


def row_edges(picture, cotangent):
    vmem = pl.BlockSpec(memory_space=pltpu.VMEM)
    height = picture.shape[0]
    shape = jax.ShapeDtypeStruct((HALO + RAD,) + picture.shape[1:], jnp.bfloat16)
    return pl.pallas_call(
        row_edges_body,
        out_shape=(shape, shape),
        in_specs=[vmem] * 4,
        out_specs=(vmem, vmem),
        compiler_params=pltpu.CompilerParams(vmem_limit_bytes=vmem_bytes),
        name="row_edges",
    )(picture[:HALO], picture[height - HALO :], cotangent[:RAD], cotangent[height - RAD :])


def col_edges_body(x_ref, dy_ref, row_far_ref, row_near_ref, near_ref, far_ref):
    above, below = in_order("gy", row_near_ref, row_far_ref)
    breadth = x_ref.shape[1]
    odd = odd_rank("gx")
    at = 0
    for rows in (above, x_ref[...].astype(jnp.float32), dy_ref[...].astype(jnp.float32), below):
        first, final = rows[:, :side], rows[:, breadth - side :]
        span = slice(at, at + rows.shape[0])
        near_ref[span] = jnp.where(odd, first, final).astype(jnp.bfloat16)
        far_ref[span] = jnp.where(odd, final, first).astype(jnp.bfloat16)
        at += rows.shape[0]


def col_edges(picture, cotangent, row_far, row_near):
    vmem = pl.BlockSpec(memory_space=pltpu.VMEM)
    rows = 2 * (picture.shape[0] + row_near.shape[0])
    shape = jax.ShapeDtypeStruct((rows, side, D_F), jnp.bfloat16)
    return pl.pallas_call(
        col_edges_body,
        out_shape=(shape, shape),
        in_specs=[vmem] * 4,
        out_specs=(vmem, vmem),
        compiler_params=pltpu.CompilerParams(vmem_limit_bytes=vmem_bytes),
        name="col_edges",
    )(picture, cotangent, row_far, row_near)


def pack_body(first, second, x_ref, dy_ref, own_ref):
    own_ref[:, :D_C] = x_ref[...].astype(jnp.float32).reshape(-1, D_C).astype(jnp.bfloat16)
    own_ref[:, D_C:] = dy_ref[...].astype(jnp.float32).reshape(-1, D_C).astype(jnp.bfloat16)


def packed(after, tokens, cotangents):
    vmem = pl.BlockSpec(memory_space=pltpu.VMEM)
    count = tokens.shape[0] * tokens.shape[1]
    return pl.pallas_call(
        pack_body,
        out_shape=jax.ShapeDtypeStruct((count, 2 * D_C), jnp.bfloat16),
        in_specs=[pl.BlockSpec(memory_space=pl.ANY)] * 2 + [vmem] * 2,
        out_specs=vmem,
        compiler_params=pltpu.CompilerParams(vmem_limit_bytes=vmem_bytes),
        name="pack_coarse",
    )(*after, tokens, cotangents)


def factors_body(step, fine_gain, coarse_gain, fine_freq, coarse_freq, fine_ref, coarse_ref):
    time = step[0].astype(jnp.float32)
    fine_ref[...] = fine_gain[...] * (1.0 + 0.5 * jnp.cos(time * fine_freq[...]))
    coarse_ref[...] = coarse_gain[...] * (1.0 + 0.5 * jnp.cos(time * coarse_freq[...]))


def time_factors(step, fine_gain, coarse_gain):
    vmem = pl.BlockSpec(memory_space=pltpu.VMEM)
    return pl.pallas_call(
        factors_body,
        out_shape=(
            jax.ShapeDtypeStruct((1, D_F), jnp.float32),
            jax.ShapeDtypeStruct((1, D_C), jnp.float32),
        ),
        in_specs=[pl.BlockSpec(memory_space=pltpu.SMEM)] + [vmem] * 4,
        out_specs=(vmem, vmem),
        compiler_params=pltpu.CompilerParams(vmem_limit_bytes=vmem_bytes),
        name="time_factors",
    )(step, fine_gain[None], coarse_gain[None], frequencies(D_F), frequencies(D_C))


def pair_sum_body(own, *refs):
    qkv_ref, out_ref = refs[-2:]
    come = jnp.concatenate([ref[...] for ref in refs[:-2]], axis=0)
    for part in range(4):
        rows = slice(part * HD, (part + 1) * HD)
        total = own[rows].astype(jnp.float32) + come[rows].astype(jnp.float32)
        if part < 3:
            qkv_ref[part] = total.astype(jnp.bfloat16)
        else:
            out_ref[...] = total.astype(jnp.bfloat16)


def pair_sum(own, *come):
    vmem = pl.BlockSpec(memory_space=pltpu.VMEM)
    return pl.pallas_call(
        pair_sum_body,
        out_shape=(
            jax.ShapeDtypeStruct((3, HD, D_C), jnp.bfloat16),
            jax.ShapeDtypeStruct((HD, D_C), jnp.bfloat16),
        ),
        in_specs=[vmem] * (1 + len(come)),
        out_specs=(vmem, vmem),
        compiler_params=pltpu.CompilerParams(vmem_limit_bytes=vmem_bytes),
        name="pair_sum",
    )(own, *come)


def block_copies(near_ref, low, qkv_hbm, out_hbm, sems):
    highs, rows = near_ref.shape[0], near_ref.shape[1]
    copies = []
    for high in range(highs):
        block = lax.axis_index("gx") ^ (2 * high + low)
        at = pl.ds(pl.multiple_of(block * rows, rows), rows)
        for part, target in enumerate((qkv_hbm, out_hbm)):
            lanes = (slice(0, 3 * D_F), slice(3 * D_F, 4 * D_F))[part]
            copies.append(
                pltpu.make_async_copy(
                    near_ref.at[high, :, lanes], target.at[at, :], sems.at[high, part]
                )
            )
    for copy in copies:
        copy.start()
    return copies


def near_body(near_ref, x_ref, factor_ref, kept_ref, come_ref, qkv_hbm, out_hbm, dx_ref, sems):
    copies = block_copies(near_ref, 0, qkv_hbm, out_hbm, sems)
    tokens = x_ref[...].astype(jnp.float32).reshape(-1, D_C)
    upstream = kept_ref[...] + come_ref[...].astype(jnp.float32)
    grads = norm_backward(tokens, inverse_rms(tokens), factor_ref[...], upstream)
    dx_ref[...] = grads.astype(jnp.float32).reshape(dx_ref.shape).astype(jnp.bfloat16)
    for copy in copies:
        copy.wait()


def far_body(far_ref, qkv_in, out_in, qkv_hbm, out_hbm, sems):
    for copy in block_copies(far_ref, 1, qkv_hbm, out_hbm, sems):
        copy.wait()


def near_step(near, tokens, *operands):
    vmem = pl.BlockSpec(memory_space=pltpu.VMEM)
    hbm = pl.BlockSpec(memory_space=pltpu.HBM)
    return pl.pallas_call(
        near_body,
        out_shape=(
            jax.ShapeDtypeStruct((D_F, 3 * D_F), jnp.bfloat16),
            jax.ShapeDtypeStruct((D_F, D_F), jnp.bfloat16),
            jax.ShapeDtypeStruct(tokens.shape, jnp.bfloat16),
        ),
        in_specs=[vmem] * 5,
        out_specs=(hbm, hbm, vmem),
        scratch_shapes=[pltpu.SemaphoreType.DMA((near.shape[0], 2))],
        compiler_params=pltpu.CompilerParams(vmem_limit_bytes=vmem_bytes),
        name="near_step",
    )(near, tokens, *operands)


def far_step(far, qkv, out):
    vmem = pl.BlockSpec(memory_space=pltpu.VMEM)
    hbm = pl.BlockSpec(memory_space=pltpu.HBM)
    return pl.pallas_call(
        far_body,
        out_shape=(
            jax.ShapeDtypeStruct(qkv.shape, qkv.dtype),
            jax.ShapeDtypeStruct(out.shape, out.dtype),
        ),
        in_specs=[vmem, hbm, hbm],
        out_specs=(hbm, hbm),
        input_output_aliases={1: 0, 2: 1},
        scratch_shapes=[pltpu.SemaphoreType.DMA((far.shape[0], 2))],
        compiler_params=pltpu.CompilerParams(vmem_limit_bytes=vmem_bytes),
        name="far_step",
    )(far, qkv, out)


def neighbours(to_near, to_far, axis):
    peers = lax.axis_size(axis)
    near = [(i, i ^ 1) for i in range(peers)]
    far = [(i, i + 1 if i % 2 else i - 1) for i in range(1, peers - 1)]
    from_far = lax.ppermute(to_far, axis, far)
    return lax.ppermute(to_near, axis, near), from_far


def swapped(value, axis, mask):
    return lax.ppermute(value, axis, [(i, i ^ mask) for i in range(lax.axis_size(axis))])


def tied(*arrays):
    return lax.optimization_barrier(arrays)


def batch_sum(partial):
    if lax.axis_size("batch") != 2:
        return lax.psum(partial, "batch")
    return wide(partial) + wide(swapped(partial, "batch", 1))


def wide(value):
    return value.astype(jnp.float32)


def narrow(value):
    return value.astype(jnp.bfloat16)


def all_rows(piece):
    downs = lax.axis_size("gy")
    return jnp.stack([piece] + [swapped(piece, "gy", row) for row in range(1, downs)])


def local(
    x_fine,
    dy_fine,
    x_coarse,
    dy_coarse,
    timestep,
    fine_gain,
    coarse_gain,
    fine_qkv,
    fine_out,
    coarse_qkv,
    coarse_out,
):
    picture, cotangent = x_fine[0], dy_fine[0]
    across, downs = lax.axis_size("gx"), lax.axis_size("gy")
    assert across == 4 and downs & (downs - 1) == 0

    payloads = row_edges(picture, cotangent)
    row_near, row_far = neighbours(*payloads, "gy")
    own = packed(payloads, x_coarse[0], dy_coarse[0])
    count = own.shape[0]
    pieces = [own] + [swapped(own, "gy", row) for row in range(1, downs)]
    edges = col_edges(picture, cotangent, row_far, row_near)
    *edges, step, gain_f, gain_c = tied(*edges, timestep, fine_gain, coarse_gain)
    col_near, col_far = neighbours(*edges, "gx")
    factor, coarse_factor = time_factors(step, gain_f, gain_c)
    factor, *pieces = tied(factor, *pieces)
    row_group = jnp.stack(pieces)
    cross = swapped(row_group, "gx", 2)
    beside = swapped(row_group, "gx", 1)
    col_far, col_near, row_group = tied(col_far, col_near, row_group)
    dx_picture, fine_keep, fine_send = fine_block(
        (across, downs),
        picture,
        cotangent,
        row_far,
        row_near,
        col_far,
        col_near,
        factor,
        fine_qkv,
        fine_out,
    )
    fine_half = fine_keep + wide(swapped(fine_send, "gx", 1))
    opposite = swapped(cross, "gx", 1)

    fine_quarter = narrow(fine_half[0] + wide(swapped(narrow(fine_half[1]), "gx", 2)))
    everyone = jnp.stack([row_group, cross, beside, opposite]).reshape(-1, 2 * D_C)
    parts, coarse_partial = coarse_block(
        everyone[:, :D_C], everyone[:, D_C:], coarse_factor, coarse_qkv, coarse_out
    )
    fine_quarter, parts, coarse_partial = tied(fine_quarter, parts, coarse_partial)

    rows = D_F // across
    fine_quarter = narrow(batch_sum(fine_quarter)).reshape(rows, 4 * D_F)
    parts = parts.reshape(2, 2, downs, count, D_C)
    coarse_kept = wide(parts[0]) + wide(swapped(parts[1], "gx", 1))
    fine_quarter, coarse_kept, coarse_partial = tied(fine_quarter, coarse_kept, coarse_partial)

    pair_batch = lax.axis_size("batch") == 2
    cut = 7 * HD // 4
    halves = (coarse_partial[:cut], coarse_partial[cut:])
    others = [swapped(half, "batch", 1) if pair_batch else half for half in halves]
    masks = [1 << bit for bit in range(downs.bit_length() - 1)]
    for mask in masks:
        fine_quarter = narrow(wide(fine_quarter) + wide(swapped(fine_quarter, "gy", mask)))
    for turn, mask in enumerate(masks):
        coarse_kept = coarse_kept.reshape(2, -1, 2, count, D_C)
        come = swapped(narrow(coarse_kept[:, :, 1]), "gy", mask)
        coarse_kept = coarse_kept[:, :, 0] + wide(come)
        at = min(turn, 1)
        coarse_kept, others[at] = tied(coarse_kept, others[at])
    coarse_kept = coarse_kept.reshape(2, count, D_C)
    come = swapped(narrow(coarse_kept[1]), "gx", 2)
    if pair_batch:
        grad_coarse_qkv, grad_coarse_out = pair_sum(coarse_partial, *others)
    else:
        coarse_sum = narrow(lax.psum(wide(coarse_partial), "batch"))
        grad_coarse_qkv = coarse_sum[: 3 * HD].reshape(coarse_qkv.shape)
        grad_coarse_out = coarse_sum[3 * HD :]
    fine_other = swapped(fine_quarter, "gx", 2)
    fine_other, come, grad_coarse_qkv, grad_coarse_out = tied(
        fine_other, come, grad_coarse_qkv, grad_coarse_out
    )
    fine_pair = jnp.stack([fine_quarter, fine_other])
    near_qkv, near_out, dx_coarse = near_step(
        fine_pair, x_coarse[0], coarse_factor, coarse_kept[0], come
    )
    far_pair = swapped(fine_pair, "gx", 1)
    far_pair, near_qkv, near_out = tied(far_pair, near_qkv, near_out)
    grad_qkv, grad_out = far_step(far_pair, near_qkv, near_out)
    return (
        dx_picture[None],
        dx_coarse[None],
        grad_qkv,
        grad_out,
        grad_coarse_qkv,
        grad_coarse_out,
    )


def solution(mesh):
    placed = (
        P("batch", "gy", "gx", None),
        P("batch", "gy", "gx", None),
        P("batch", "gy", "gx", None),
        P("batch", "gy", "gx", None),
        P("batch"),
        P(),
        P(),
        P(),
        P(),
        P(None, plane_spec, None),
        P(plane_spec, None),
    )
    return jax.shard_map(
        local,
        mesh=mesh,
        in_specs=placed,
        out_specs=(
            P("batch", "gy", "gx", None),
            P("batch", "gy", "gx", None),
            P(),
            P(),
            P(None, plane_spec, None),
            P(plane_spec, None),
        ),
        check_vma=False,
    )


plane_spec = ("gy", "gx")
```

```python
import math

import jax
import jax.numpy as jnp
import numpy as np
from jax import lax
from jax.experimental import pallas as pl
from jax.experimental.pallas import tpu as pltpu
from jax.sharding import PartitionSpec as P

D_F = 256
H_F = 4
D_C = 1024
HD = 64
RAD = 3
HALO = 2 * RAD

eps = 1e-06
log_span = math.log(1000.0)
side = 8
extent = side + 2 * RAD
lanes_wide = 16
thin = 4
lag = 2
scale = 1.0 / math.sqrt(HD)
vmem_bytes = 48 * 1024 * 1024


def dot(first, second, dims=((1,), (0,))):
    return lax.dot_general(first, second, (dims, ((), ())), preferred_element_type=jnp.float32)


def frequencies(channels):
    steps = np.float32(-log_span) * np.arange(channels, dtype=np.float32) / np.float32(channels)
    return np.exp(steps)[None]


def odd_rank(axis):
    return lax.axis_index(axis) & 1 == 1


def inverse_rms(floats):
    return lax.rsqrt(jnp.mean(floats * floats, axis=-1, keepdims=True) + eps)


def norm_backward(floats, inverse, factor, upstream):
    scaled = upstream * factor
    middle = jnp.mean(floats * scaled, axis=-1, keepdims=True)
    return (inverse * scaled - floats * inverse * inverse * inverse * middle).astype(jnp.bfloat16)


def round_up(value, multiple):
    return -(-value // multiple) * multiple


def in_order(axis, near, far):
    odd = odd_rank(axis)
    first, second = near[...].astype(jnp.float32), far[...].astype(jnp.float32)
    return jnp.where(odd, first, second), jnp.where(odd, second, first)


def fine_body(
    x_ref,
    dy_ref,
    row_far_ref,
    row_near_ref,
    col_far_ref,
    col_near_ref,
    factor_ref,
    qkv_ref,
    out_ref,
    dx_ref,
    keep_ref,
    send_ref,
    x_grid,
    dy_grid,
    k_grid,
    v_grid,
    q_grid,
    u_grid,
    dk_grid,
    dv_grid,
    dq_grid,
    a_grid,
    total_ref,
    *scratch,
):
    height, breadth = x_ref.shape[0], x_ref.shape[1]
    grid_rows, grid_cols = x_grid.shape[0], x_grid.shape[1]
    query_rows = dy_grid.shape[0]
    floats = jnp.float32
    factor = factor_ref[...]

    for grid, rows in ((x_grid, height + 2 * HALO), (dy_grid, height + 2 * RAD)):
        grid[rows:] = jnp.zeros((grid.shape[0] - rows,) + grid.shape[1:], floats)
        cols = breadth + 2 * HALO
        grid[:rows, cols:] = jnp.zeros((rows, grid_cols - cols, D_F), floats)
    dk_grid[...] = jnp.zeros_like(dk_grid)
    dv_grid[...] = jnp.zeros_like(dv_grid)
    inner = slice(HALO, HALO + breadth)
    above, below = in_order("gy", row_near_ref, row_far_ref)
    left, right = in_order("gx", col_near_ref, col_far_ref)
    x_grid[0:HALO, inner] = above[0:HALO]
    x_grid[HALO : HALO + height, inner] = x_ref[...].astype(floats)
    x_grid[HALO + height : HALO + height + HALO, inner] = below[0:HALO]
    dy_grid[0:RAD, inner] = above[HALO : HALO + RAD]
    dy_grid[RAD : RAD + height, inner] = dy_ref[...].astype(floats)
    dy_grid[RAD + height : RAD + height + RAD, inner] = below[HALO : HALO + RAD]
    left, right = left[:, left.shape[1] - HALO :], right[:, :HALO]
    for strip, first in ((left, 0), (right, HALO + breadth)):
        span = slice(first, first + HALO)
        at = 0
        for grid, begin, count in (
            (x_grid, 0, HALO),
            (dy_grid, 0, RAD),
            (x_grid, HALO, height),
            (dy_grid, RAD, height),
            (x_grid, HALO + height, HALO),
            (dy_grid, RAD + height, RAD),
        ):
            grid[begin : begin + count, span] = strip[at : at + count]
            at += count

    tokens = x_grid[...].reshape(grid_rows * grid_cols, D_F)
    normed = (tokens * inverse_rms(tokens) * factor).astype(jnp.bfloat16)
    key_values = dot(normed, qkv_ref[:, D_F:]).astype(jnp.bfloat16).astype(floats)
    k_grid[...] = key_values[:, :D_F].reshape(grid_rows, grid_cols, D_F)
    v_grid[...] = key_values[:, D_F:].reshape(grid_rows, grid_cols, D_F)
    query_tokens = normed[RAD * grid_cols : (RAD + query_rows) * grid_cols]
    queries = dot(query_tokens, qkv_ref[:, :D_F]).astype(jnp.bfloat16).astype(floats) * scale
    q_grid[...] = queries.reshape(query_rows, grid_cols, D_F)
    cotangents = dy_grid[...].reshape(query_rows * grid_cols, D_F).astype(jnp.bfloat16)
    ups = dot(cotangents, out_ref[...], ((1,), (1,))).astype(jnp.bfloat16).astype(floats)
    u_grid[...] = ups.reshape(query_rows, grid_cols, D_F)

    gx, gy = lax.axis_index("gx"), lax.axis_index("gy")
    row_low, col_low = HALO - gy * height, HALO - gx * breadth
    row_high = row_low + lax.axis_size("gy") * height
    col_high = col_low + lax.axis_size("gx") * breadth

    def window_bias(query_rows):
        shape = ((query_rows + 2 * RAD) * lanes_wide, H_F * query_rows * side)
        key_at = lax.broadcasted_iota(jnp.int32, shape, 0)
        query_at = lax.broadcasted_iota(jnp.int32, shape, 1)
        row_gap = (key_at // lanes_wide) - ((query_at // side) % query_rows)
        col_gap = (key_at % lanes_wide) - (query_at % side)
        near = (row_gap >= 0) & (row_gap <= 2 * RAD) & (col_gap >= 0) & (col_gap <= 2 * RAD)
        return jnp.where(near, 0.0, -1e30)

    own_scratch, thin_scratch = scratch[:7], scratch[7:]
    own_scratch[-1][...] = window_bias(side)
    thin_scratch[-1][...] = window_bias(thin)

    def head_of(rows):
        return lax.broadcasted_iota(jnp.int32, (rows, D_F), 1) // HD

    def spread(block):
        block = block.reshape(-1, D_F)
        heads = head_of(block.shape[0])
        return jnp.concatenate(
            [jnp.where(heads == h, block, 0.0).astype(jnp.bfloat16) for h in range(H_F)], axis=0
        )

    def collect(full):
        rows = full.shape[0] // H_F
        heads = head_of(rows)
        total = jnp.where(heads == 0, full[:rows], 0.0)
        for h in range(1, H_F):
            total = jnp.where(heads == h, full[h * rows : (h + 1) * rows], total)
        return total.reshape(rows // side, side, D_F)

    def windows(task):
        top, start, query_rows = task[:3]
        window = (slice(top, top + query_rows + 2 * RAD), slice(start, start + lanes_wide))
        keys = k_grid[window].reshape(-1, D_F).astype(jnp.bfloat16)
        return keys, v_grid[window].reshape(-1, D_F).astype(jnp.bfloat16)

    def begin(task):
        top, start, query_rows, live, scratch, index = task
        score_ref, product_ref, query_ref, up_ref = scratch[:4]
        keys, values = windows(task)
        place = (slice(top, top + query_rows), slice(start + RAD, start + RAD + side))
        wide_queries = spread(q_grid[place])
        ups = u_grid[place]
        if live < query_rows:
            row = lax.broadcasted_iota(jnp.int32, ups.shape, 0)
            ups = jnp.where(row < live, ups, 0.0)
        wide_ups = spread(ups)
        query_ref[index], up_ref[index] = wide_queries, wide_ups
        score_ref[index] = dot(keys, wide_queries, ((1,), (1,)))
        product_ref[index] = dot(values, wide_ups, ((1,), (1,)))

    def share(task):
        top, start, query_rows, live, scratch, index = task
        score_ref, product_ref, _, _, weight_ref, slope_ref, near_bias = scratch
        lone = lax.broadcasted_iota(jnp.int32, ((query_rows + 2 * RAD) * lanes_wide, 1), 0)
        key_row, key_col = lone // lanes_wide + top, lone % lanes_wide + start
        inside = (key_row >= row_low) & (key_row < row_high)
        inside = inside & (key_col >= col_low) & (key_col < col_high)
        scores = score_ref[index] + (near_bias[...] + jnp.where(inside, 0.0, -1e30))
        raised = jnp.exp(scores - jnp.max(scores, axis=0, keepdims=True))
        shares = raised * (1.0 / jnp.sum(raised, axis=0, keepdims=True))
        products = product_ref[index]
        centre = jnp.sum(shares * products, axis=0, keepdims=True)
        slope_ref[index] = (shares * (products - centre)).astype(jnp.bfloat16)
        weight_ref[index] = shares.astype(jnp.bfloat16)

    def finish(task):
        top, start, query_rows, live, scratch, index = task
        query_ref, up_ref, weight_ref, slope_ref = scratch[2:6]
        first, final = max(top, HALO), min(top + query_rows + 2 * RAD, HALO + height)
        kept = slice((first - top) * lanes_wide, (final - top) * lanes_wide)
        target = (slice(first - HALO, final - HALO), slice(start, start + lanes_wide))
        shape = (final - first, lanes_wide, D_F)
        dv_grid[target] += dot(weight_ref[index, kept], up_ref[index]).reshape(shape)
        dk_grid[target] += dot(slope_ref[index, kept], query_ref[index]).reshape(shape)
        if live == side:
            keys, values = windows(task)
            block = (slice(top - RAD, top - RAD + side), slice(start, start + side))
            a_grid[block] = collect(dot(weight_ref[index], values, ((0,), (0,))))
            dq_grid[block] = collect(dot(slope_ref[index], keys, ((0,), (0,))))

    tasks = []
    for start in range(0, grid_cols - side, side):
        for top in range(RAD, RAD + height, side):
            tasks.append((top, start, side, side, own_scratch, len(tasks)))
    for index, start in enumerate(range(0, grid_cols - side, side)):
        tasks.append((0, start, thin, RAD, thin_scratch, 2 * index))
        tasks.append((RAD + height, start, thin, thin, thin_scratch, 2 * index + 1))
    for turn in range(len(tasks) + 2 * lag):
        if turn < len(tasks):
            begin(tasks[turn])
        if 0 <= turn - lag < len(tasks):
            share(tasks[turn - lag])
        if turn >= 2 * lag:
            finish(tasks[turn - 2 * lag])

    count = height * breadth
    own_queries = (slice(0, height), slice(RAD, RAD + breadth))
    own_keys = (slice(0, height), inner)
    attended = a_grid[own_queries].reshape(count, D_F).astype(jnp.bfloat16)
    grad_q = (dq_grid[own_queries].reshape(count, D_F) * scale).astype(jnp.bfloat16)
    grad_k = dk_grid[own_keys].reshape(count, D_F).astype(jnp.bfloat16)
    grad_v = dv_grid[own_keys].reshape(count, D_F).astype(jnp.bfloat16)
    grad_proj = jnp.concatenate([grad_q, grad_k, grad_v], axis=1)
    picture = x_ref[...].reshape(count, D_F).astype(floats)
    inverse = inverse_rms(picture)
    own_normed = (picture * inverse * factor).astype(jnp.bfloat16)
    flat_cot = dy_ref[...].reshape(count, D_F)
    grads = jnp.concatenate(
        [
            dot(own_normed, grad_proj, ((0,), (0,))),
            dot(attended, flat_cot, ((0,), (0,))),
        ],
        axis=1,
    )
    half, columns = keep_ref.shape[0], keep_ref.shape[1]
    total_ref[...] = grads.reshape(total_ref.shape)
    for low in range(2):
        target = (keep_ref, send_ref)[low]
        for high in range(half):
            for row in range(columns):
                block = (gx ^ (2 * high + low)) * columns + row
                target[high, row] = total_ref[block].astype(target.dtype)
    down = dot(grad_proj, qkv_ref[...], ((1,), (1,)))
    dx_ref[...] = norm_backward(picture, inverse, factor, down).reshape(height, breadth, D_F)


def block_scratch(blocks, query_rows):
    keys_count, heads_count = (query_rows + 2 * RAD) * lanes_wide, H_F * query_rows * side
    square = (blocks, keys_count, heads_count)
    wide = (blocks, heads_count, D_F)
    return [
        pltpu.VMEM(square, jnp.float32),
        pltpu.VMEM(square, jnp.float32),
        pltpu.VMEM(wide, jnp.bfloat16),
        pltpu.VMEM(wide, jnp.bfloat16),
        pltpu.VMEM(square, jnp.bfloat16),
        pltpu.VMEM(square, jnp.bfloat16),
        pltpu.VMEM((keys_count, heads_count), jnp.float32),
    ]


def fine_block(peers, picture, *operands):
    height, breadth = picture.shape[0], picture.shape[1]
    query_rows = RAD + height + thin
    query_cols = round_up(breadth + 2 * RAD, side)
    grid_rows, grid_cols = query_rows + 2 * RAD, query_cols + side
    across, down = peers
    rows = D_F // (across * down)
    halves = (across // 2, down, rows, 4 * D_F)
    vmem = pl.BlockSpec(memory_space=pltpu.VMEM)
    wide = pltpu.VMEM((grid_rows, grid_cols, D_F), jnp.float32)
    middle = pltpu.VMEM((query_rows, grid_cols, D_F), jnp.float32)
    small = pltpu.VMEM((height, query_cols, D_F), jnp.float32)
    strip = pltpu.VMEM((height, grid_cols, D_F), jnp.float32)
    return pl.pallas_call(
        fine_body,
        out_shape=(
            jax.ShapeDtypeStruct((height, breadth, D_F), jnp.bfloat16),
            jax.ShapeDtypeStruct(halves, jnp.float32),
            jax.ShapeDtypeStruct(halves, jnp.bfloat16),
        ),
        in_specs=[vmem] * 9,
        out_specs=(vmem, vmem, vmem),
        scratch_shapes=[
            wide,
            middle,
            wide,
            wide,
            middle,
            middle,
            strip,
            strip,
            small,
            small,
            pltpu.VMEM((across * down, rows, 4 * D_F), jnp.float32),
            *block_scratch(query_cols // side * (height // side), side),
            *block_scratch(2 * (query_cols // side), thin),
        ],
        compiler_params=pltpu.CompilerParams(vmem_limit_bytes=vmem_bytes),
        name="fine_block",
    )(picture, *operands)


def coarse_body(
    x_ref,
    dy_ref,
    factor_ref,
    qkv_hbm,
    out_hbm,
    parts_ref,
    grads_ref,
    qkv_ref,
    out_ref,
    arrived,
):
    fetches = [
        pltpu.make_async_copy(qkv_hbm, qkv_ref, arrived.at[0]),
        pltpu.make_async_copy(out_hbm, out_ref, arrived.at[1]),
    ]
    for fetch in fetches:
        fetch.start()
    tokens = x_ref[...].astype(jnp.float32)
    normed = (tokens * inverse_rms(tokens) * factor_ref[...]).astype(jnp.bfloat16)
    cot = dy_ref[...]
    for fetch in fetches:
        fetch.wait()
    flat_qkv = qkv_ref[...].reshape(3 * HD, D_C)
    out_rows = out_ref[...]
    projected = dot(normed, flat_qkv, ((1,), (1,))).astype(jnp.bfloat16)
    queries, keys, values = projected[:, :HD], projected[:, HD : 2 * HD], projected[:, 2 * HD :]
    ups = dot(cot, out_rows, ((1,), (1,))).astype(jnp.bfloat16)
    scores = dot(queries, keys, ((1,), (1,))) * scale
    raised = jnp.exp(scores - jnp.max(scores, axis=-1, keepdims=True))
    shares = raised * (1.0 / jnp.sum(raised, axis=-1, keepdims=True))
    weights = shares.astype(jnp.bfloat16)
    mixed = dot(weights, values).astype(jnp.bfloat16)
    products = dot(ups, values, ((1,), (1,)))
    centre = jnp.sum(shares * products, axis=-1, keepdims=True)
    slopes = (shares * (products - centre)).astype(jnp.bfloat16)
    grad_q = (dot(slopes, keys) * scale).astype(jnp.bfloat16)
    grad_k = (dot(slopes, queries, ((0,), (0,))) * scale).astype(jnp.bfloat16)
    grad_v = dot(weights, ups, ((0,), (0,))).astype(jnp.bfloat16)
    stacked = jnp.concatenate([grad_q, grad_k, grad_v], axis=1)
    parts_ref[...] = dot(stacked, flat_qkv).astype(jnp.bfloat16)
    grads_ref[: 3 * HD] = dot(stacked, normed, ((0,), (0,))).astype(grads_ref.dtype)
    grads_ref[3 * HD :] = dot(mixed, cot, ((0,), (0,))).astype(grads_ref.dtype)


def coarse_block(tokens, cotangents, factor, head_qkv, head_out):
    count = tokens.shape[0]
    vmem = pl.BlockSpec(memory_space=pltpu.VMEM)
    return pl.pallas_call(
        coarse_body,
        out_shape=(
            jax.ShapeDtypeStruct((count, D_C), jnp.bfloat16),
            jax.ShapeDtypeStruct((4 * HD, D_C), jnp.bfloat16),
        ),
        in_specs=[vmem] * 3 + [pl.BlockSpec(memory_space=pltpu.HBM)] * 2,
        out_specs=(vmem, vmem),
        scratch_shapes=[
            pltpu.VMEM(head_qkv.shape, jnp.bfloat16),
            pltpu.VMEM(head_out.shape, jnp.bfloat16),
            pltpu.SemaphoreType.DMA((2,)),
        ],
        compiler_params=pltpu.CompilerParams(vmem_limit_bytes=vmem_bytes),
        name="coarse_block",
    )(tokens, cotangents, factor, head_qkv, head_out)


def row_edges_body(x_low, x_high, dy_low, dy_high, near_ref, far_ref):
    odd = odd_rank("gy")

    def fill(low_ref, high_ref):
        low_ref[:HALO], low_ref[HALO:] = x_low[...], dy_low[...]
        high_ref[:HALO], high_ref[HALO:] = x_high[...], dy_high[...]

    @pl.when(odd)
    def _():
        fill(near_ref, far_ref)

    @pl.when(jnp.logical_not(odd))
    def _():
        fill(far_ref, near_ref)


def row_edges(picture, cotangent):
    vmem = pl.BlockSpec(memory_space=pltpu.VMEM)
    height = picture.shape[0]
    shape = jax.ShapeDtypeStruct((HALO + RAD,) + picture.shape[1:], jnp.bfloat16)
    return pl.pallas_call(
        row_edges_body,
        out_shape=(shape, shape),
        in_specs=[vmem] * 4,
        out_specs=(vmem, vmem),
        compiler_params=pltpu.CompilerParams(vmem_limit_bytes=vmem_bytes),
        name="row_edges",
    )(picture[:HALO], picture[height - HALO :], cotangent[:RAD], cotangent[height - RAD :])


def col_edges_body(x_ref, dy_ref, row_far_ref, row_near_ref, near_ref, far_ref):
    above, below = in_order("gy", row_near_ref, row_far_ref)
    breadth = x_ref.shape[1]
    odd = odd_rank("gx")
    at = 0
    for rows in (above, x_ref[...].astype(jnp.float32), dy_ref[...].astype(jnp.float32), below):
        first, final = rows[:, :side], rows[:, breadth - side :]
        span = slice(at, at + rows.shape[0])
        near_ref[span] = jnp.where(odd, first, final).astype(jnp.bfloat16)
        far_ref[span] = jnp.where(odd, final, first).astype(jnp.bfloat16)
        at += rows.shape[0]


def col_edges(picture, cotangent, row_far, row_near):
    vmem = pl.BlockSpec(memory_space=pltpu.VMEM)
    rows = 2 * (picture.shape[0] + row_near.shape[0])
    shape = jax.ShapeDtypeStruct((rows, side, D_F), jnp.bfloat16)
    return pl.pallas_call(
        col_edges_body,
        out_shape=(shape, shape),
        in_specs=[vmem] * 4,
        out_specs=(vmem, vmem),
        compiler_params=pltpu.CompilerParams(vmem_limit_bytes=vmem_bytes),
        name="col_edges",
    )(picture, cotangent, row_far, row_near)


def pack_body(first, second, x_ref, dy_ref, own_ref):
    own_ref[:, :D_C] = x_ref[...].astype(jnp.float32).reshape(-1, D_C).astype(jnp.bfloat16)
    own_ref[:, D_C:] = dy_ref[...].astype(jnp.float32).reshape(-1, D_C).astype(jnp.bfloat16)


def packed(after, tokens, cotangents):
    vmem = pl.BlockSpec(memory_space=pltpu.VMEM)
    count = tokens.shape[0] * tokens.shape[1]
    return pl.pallas_call(
        pack_body,
        out_shape=jax.ShapeDtypeStruct((count, 2 * D_C), jnp.bfloat16),
        in_specs=[pl.BlockSpec(memory_space=pl.ANY)] * 2 + [vmem] * 2,
        out_specs=vmem,
        compiler_params=pltpu.CompilerParams(vmem_limit_bytes=vmem_bytes),
        name="pack_coarse",
    )(*after, tokens, cotangents)


def factors_body(step, fine_gain, coarse_gain, fine_freq, coarse_freq, fine_ref, coarse_ref):
    time = step[0].astype(jnp.float32)
    fine_ref[...] = fine_gain[...] * (1.0 + 0.5 * jnp.cos(time * fine_freq[...]))
    coarse_ref[...] = coarse_gain[...] * (1.0 + 0.5 * jnp.cos(time * coarse_freq[...]))


def time_factors(step, fine_gain, coarse_gain):
    vmem = pl.BlockSpec(memory_space=pltpu.VMEM)
    return pl.pallas_call(
        factors_body,
        out_shape=(
            jax.ShapeDtypeStruct((1, D_F), jnp.float32),
            jax.ShapeDtypeStruct((1, D_C), jnp.float32),
        ),
        in_specs=[pl.BlockSpec(memory_space=pltpu.SMEM)] + [vmem] * 4,
        out_specs=(vmem, vmem),
        compiler_params=pltpu.CompilerParams(vmem_limit_bytes=vmem_bytes),
        name="time_factors",
    )(step, fine_gain[None], coarse_gain[None], frequencies(D_F), frequencies(D_C))


def pair_sum_body(own, *refs):
    qkv_ref, out_ref = refs[-2:]
    come = jnp.concatenate([ref[...] for ref in refs[:-2]], axis=0)
    for part in range(4):
        rows = slice(part * HD, (part + 1) * HD)
        total = own[rows].astype(jnp.float32) + come[rows].astype(jnp.float32)
        if part < 3:
            qkv_ref[part] = total.astype(jnp.bfloat16)
        else:
            out_ref[...] = total.astype(jnp.bfloat16)


def pair_sum(own, *come):
    vmem = pl.BlockSpec(memory_space=pltpu.VMEM)
    return pl.pallas_call(
        pair_sum_body,
        out_shape=(
            jax.ShapeDtypeStruct((3, HD, D_C), jnp.bfloat16),
            jax.ShapeDtypeStruct((HD, D_C), jnp.bfloat16),
        ),
        in_specs=[vmem] * (1 + len(come)),
        out_specs=(vmem, vmem),
        compiler_params=pltpu.CompilerParams(vmem_limit_bytes=vmem_bytes),
        name="pair_sum",
    )(own, *come)


def block_copies(near_ref, low, qkv_hbm, out_hbm, sems):
    highs, rows = near_ref.shape[0], near_ref.shape[1]
    copies = []
    for high in range(highs):
        block = lax.axis_index("gx") ^ (2 * high + low)
        at = pl.ds(pl.multiple_of(block * rows, rows), rows)
        for part, target in enumerate((qkv_hbm, out_hbm)):
            lanes = (slice(0, 3 * D_F), slice(3 * D_F, 4 * D_F))[part]
            copies.append(
                pltpu.make_async_copy(
                    near_ref.at[high, :, lanes], target.at[at, :], sems.at[high, part]
                )
            )
    for copy in copies:
        copy.start()
    return copies


def near_body(near_ref, x_ref, factor_ref, kept_ref, come_ref, qkv_hbm, out_hbm, dx_ref, sems):
    copies = block_copies(near_ref, 0, qkv_hbm, out_hbm, sems)
    tokens = x_ref[...].astype(jnp.float32).reshape(-1, D_C)
    upstream = kept_ref[...] + come_ref[...].astype(jnp.float32)
    grads = norm_backward(tokens, inverse_rms(tokens), factor_ref[...], upstream)
    dx_ref[...] = grads.astype(jnp.float32).reshape(dx_ref.shape).astype(jnp.bfloat16)
    for copy in copies:
        copy.wait()


def far_body(far_ref, qkv_in, out_in, qkv_hbm, out_hbm, sems):
    for copy in block_copies(far_ref, 1, qkv_hbm, out_hbm, sems):
        copy.wait()


def near_step(near, tokens, *operands):
    vmem = pl.BlockSpec(memory_space=pltpu.VMEM)
    hbm = pl.BlockSpec(memory_space=pltpu.HBM)
    return pl.pallas_call(
        near_body,
        out_shape=(
            jax.ShapeDtypeStruct((D_F, 3 * D_F), jnp.bfloat16),
            jax.ShapeDtypeStruct((D_F, D_F), jnp.bfloat16),
            jax.ShapeDtypeStruct(tokens.shape, jnp.bfloat16),
        ),
        in_specs=[vmem] * 5,
        out_specs=(hbm, hbm, vmem),
        scratch_shapes=[pltpu.SemaphoreType.DMA((near.shape[0], 2))],
        compiler_params=pltpu.CompilerParams(vmem_limit_bytes=vmem_bytes),
        name="near_step",
    )(near, tokens, *operands)


def far_step(far, qkv, out):
    vmem = pl.BlockSpec(memory_space=pltpu.VMEM)
    hbm = pl.BlockSpec(memory_space=pltpu.HBM)
    return pl.pallas_call(
        far_body,
        out_shape=(
            jax.ShapeDtypeStruct(qkv.shape, qkv.dtype),
            jax.ShapeDtypeStruct(out.shape, out.dtype),
        ),
        in_specs=[vmem, hbm, hbm],
        out_specs=(hbm, hbm),
        input_output_aliases={1: 0, 2: 1},
        scratch_shapes=[pltpu.SemaphoreType.DMA((far.shape[0], 2))],
        compiler_params=pltpu.CompilerParams(vmem_limit_bytes=vmem_bytes),
        name="far_step",
    )(far, qkv, out)


def neighbours(to_near, to_far, axis):
    peers = lax.axis_size(axis)
    near = [(i, i ^ 1) for i in range(peers)]
    far = [(i, i + 1 if i % 2 else i - 1) for i in range(1, peers - 1)]
    from_far = lax.ppermute(to_far, axis, far)
    return lax.ppermute(to_near, axis, near), from_far


def swapped(value, axis, mask):
    return lax.ppermute(value, axis, [(i, i ^ mask) for i in range(lax.axis_size(axis))])


def tied(*arrays):
    return lax.optimization_barrier(arrays)


def batch_sum(partial):
    if lax.axis_size("batch") != 2:
        return lax.psum(partial, "batch")
    return wide(partial) + wide(swapped(partial, "batch", 1))


def wide(value):
    return value.astype(jnp.float32)


def narrow(value):
    return value.astype(jnp.bfloat16)


def all_rows(piece):
    downs = lax.axis_size("gy")
    return jnp.stack([piece] + [swapped(piece, "gy", row) for row in range(1, downs)])


def local(
    x_fine,
    dy_fine,
    x_coarse,
    dy_coarse,
    timestep,
    fine_gain,
    coarse_gain,
    fine_qkv,
    fine_out,
    coarse_qkv,
    coarse_out,
):
    picture, cotangent = x_fine[0], dy_fine[0]
    across, downs = lax.axis_size("gx"), lax.axis_size("gy")
    assert across == 4 and downs & (downs - 1) == 0

    payloads = row_edges(picture, cotangent)
    row_near, row_far = neighbours(*payloads, "gy")
    own = packed(payloads, x_coarse[0], dy_coarse[0])
    count = own.shape[0]
    pieces = [own] + [swapped(own, "gy", row) for row in range(1, downs)]
    edges = col_edges(picture, cotangent, row_far, row_near)
    *edges, step, gain_f, gain_c = tied(*edges, timestep, fine_gain, coarse_gain)
    col_near, col_far = neighbours(*edges, "gx")
    factor, coarse_factor = time_factors(step, gain_f, gain_c)
    factor, *pieces = tied(factor, *pieces)
    row_group = jnp.stack(pieces)
    cross = swapped(row_group, "gx", 2)
    beside = swapped(row_group, "gx", 1)
    col_far, col_near, row_group = tied(col_far, col_near, row_group)
    dx_picture, fine_keep, fine_send = fine_block(
        (across, downs),
        picture,
        cotangent,
        row_far,
        row_near,
        col_far,
        col_near,
        factor,
        fine_qkv,
        fine_out,
    )
    fine_half = fine_keep + wide(swapped(fine_send, "gx", 1))
    opposite = swapped(cross, "gx", 1)

    fine_quarter = narrow(fine_half[0] + wide(swapped(narrow(fine_half[1]), "gx", 2)))
    everyone = jnp.stack([row_group, cross, beside, opposite]).reshape(-1, 2 * D_C)
    parts, coarse_partial = coarse_block(
        everyone[:, :D_C], everyone[:, D_C:], coarse_factor, coarse_qkv, coarse_out
    )
    fine_quarter, parts, coarse_partial = tied(fine_quarter, parts, coarse_partial)

    rows = D_F // across
    fine_quarter = narrow(batch_sum(fine_quarter)).reshape(rows, 4 * D_F)
    parts = parts.reshape(2, 2, downs, count, D_C)
    coarse_kept = wide(parts[0]) + wide(swapped(parts[1], "gx", 1))
    fine_quarter, coarse_kept, coarse_partial = tied(fine_quarter, coarse_kept, coarse_partial)

    pair_batch = lax.axis_size("batch") == 2
    cut = 6 * HD // 4
    halves = (coarse_partial[:cut], coarse_partial[cut:])
    others = [swapped(half, "batch", 1) if pair_batch else half for half in halves]
    masks = [1 << bit for bit in range(downs.bit_length() - 1)]
    for mask in masks:
        fine_quarter = narrow(wide(fine_quarter) + wide(swapped(fine_quarter, "gy", mask)))
    for turn, mask in enumerate(masks):
        coarse_kept = coarse_kept.reshape(2, -1, 2, count, D_C)
        come = swapped(narrow(coarse_kept[:, :, 1]), "gy", mask)
        coarse_kept = coarse_kept[:, :, 0] + wide(come)
        if turn == 0:
            coarse_kept, others[0] = tied(coarse_kept, others[0])
    coarse_kept = coarse_kept.reshape(2, count, D_C)
    come = swapped(narrow(coarse_kept[1]), "gx", 2)
    if pair_batch:
        grad_coarse_qkv, grad_coarse_out = pair_sum(coarse_partial, *others)
    else:
        coarse_sum = narrow(lax.psum(wide(coarse_partial), "batch"))
        grad_coarse_qkv = coarse_sum[: 3 * HD].reshape(coarse_qkv.shape)
        grad_coarse_out = coarse_sum[3 * HD :]
    fine_other = swapped(fine_quarter, "gx", 2)
    fine_other, come, grad_coarse_qkv, grad_coarse_out = tied(
        fine_other, come, grad_coarse_qkv, grad_coarse_out
    )
    fine_pair = jnp.stack([fine_quarter, fine_other])
    near_qkv, near_out, dx_coarse = near_step(
        fine_pair, x_coarse[0], coarse_factor, coarse_kept[0], come
    )
    far_pair = swapped(fine_pair, "gx", 1)
    far_pair, near_qkv, near_out = tied(far_pair, near_qkv, near_out)
    grad_qkv, grad_out = far_step(far_pair, near_qkv, near_out)
    return (
        dx_picture[None],
        dx_coarse[None],
        grad_qkv,
        grad_out,
        grad_coarse_qkv,
        grad_coarse_out,
    )


def solution(mesh):
    placed = (
        P("batch", "gy", "gx", None),
        P("batch", "gy", "gx", None),
        P("batch", "gy", "gx", None),
        P("batch", "gy", "gx", None),
        P("batch"),
        P(),
        P(),
        P(),
        P(),
        P(None, plane_spec, None),
        P(plane_spec, None),
    )
    return jax.shard_map(
        local,
        mesh=mesh,
        in_specs=placed,
        out_specs=(
            P("batch", "gy", "gx", None),
            P("batch", "gy", "gx", None),
            P(),
            P(),
            P(None, plane_spec, None),
            P(plane_spec, None),
        ),
        check_vma=False,
    )


plane_spec = ("gy", "gx")
```

```python
import math

import jax
import jax.numpy as jnp
import numpy as np
from jax import lax
from jax.experimental import pallas as pl
from jax.experimental.pallas import tpu as pltpu
from jax.sharding import PartitionSpec as P

D_F = 256
H_F = 4
D_C = 1024
HD = 64
RAD = 3
HALO = 2 * RAD

eps = 1e-06
log_span = math.log(1000.0)
side = 8
extent = side + 2 * RAD
lanes_wide = 16
thin = 4
lag = 2
scale = 1.0 / math.sqrt(HD)
vmem_bytes = 48 * 1024 * 1024


def dot(first, second, dims=((1,), (0,))):
    return lax.dot_general(first, second, (dims, ((), ())), preferred_element_type=jnp.float32)


def frequencies(channels):
    steps = np.float32(-log_span) * np.arange(channels, dtype=np.float32) / np.float32(channels)
    return np.exp(steps)[None]


def odd_rank(axis):
    return lax.axis_index(axis) & 1 == 1


def inverse_rms(floats):
    return lax.rsqrt(jnp.mean(floats * floats, axis=-1, keepdims=True) + eps)


def norm_backward(floats, inverse, factor, upstream):
    scaled = upstream * factor
    middle = jnp.mean(floats * scaled, axis=-1, keepdims=True)
    return (inverse * scaled - floats * inverse * inverse * inverse * middle).astype(jnp.bfloat16)


def round_up(value, multiple):
    return -(-value // multiple) * multiple


def in_order(axis, near, far):
    odd = odd_rank(axis)
    first, second = near[...].astype(jnp.float32), far[...].astype(jnp.float32)
    return jnp.where(odd, first, second), jnp.where(odd, second, first)


def fine_body(
    x_ref,
    dy_ref,
    row_far_ref,
    row_near_ref,
    col_far_ref,
    col_near_ref,
    factor_ref,
    qkv_ref,
    out_ref,
    dx_ref,
    keep_ref,
    send_ref,
    x_grid,
    dy_grid,
    k_grid,
    v_grid,
    q_grid,
    u_grid,
    dk_grid,
    dv_grid,
    dq_grid,
    a_grid,
    total_ref,
    *scratch,
):
    height, breadth = x_ref.shape[0], x_ref.shape[1]
    grid_rows, grid_cols = x_grid.shape[0], x_grid.shape[1]
    query_rows = dy_grid.shape[0]
    floats = jnp.float32
    factor = factor_ref[...]

    for grid, rows in ((x_grid, height + 2 * HALO), (dy_grid, height + 2 * RAD)):
        grid[rows:] = jnp.zeros((grid.shape[0] - rows,) + grid.shape[1:], floats)
        cols = breadth + 2 * HALO
        grid[:rows, cols:] = jnp.zeros((rows, grid_cols - cols, D_F), floats)
    dk_grid[...] = jnp.zeros_like(dk_grid)
    dv_grid[...] = jnp.zeros_like(dv_grid)
    inner = slice(HALO, HALO + breadth)
    above, below = in_order("gy", row_near_ref, row_far_ref)
    left, right = in_order("gx", col_near_ref, col_far_ref)
    x_grid[0:HALO, inner] = above[0:HALO]
    x_grid[HALO : HALO + height, inner] = x_ref[...].astype(floats)
    x_grid[HALO + height : HALO + height + HALO, inner] = below[0:HALO]
    dy_grid[0:RAD, inner] = above[HALO : HALO + RAD]
    dy_grid[RAD : RAD + height, inner] = dy_ref[...].astype(floats)
    dy_grid[RAD + height : RAD + height + RAD, inner] = below[HALO : HALO + RAD]
    left, right = left[:, left.shape[1] - HALO :], right[:, :HALO]
    for strip, first in ((left, 0), (right, HALO + breadth)):
        span = slice(first, first + HALO)
        at = 0
        for grid, begin, count in (
            (x_grid, 0, HALO),
            (dy_grid, 0, RAD),
            (x_grid, HALO, height),
            (dy_grid, RAD, height),
            (x_grid, HALO + height, HALO),
            (dy_grid, RAD + height, RAD),
        ):
            grid[begin : begin + count, span] = strip[at : at + count]
            at += count

    tokens = x_grid[...].reshape(grid_rows * grid_cols, D_F)
    normed = (tokens * inverse_rms(tokens) * factor).astype(jnp.bfloat16)
    key_values = dot(normed, qkv_ref[:, D_F:]).astype(jnp.bfloat16).astype(floats)
    k_grid[...] = key_values[:, :D_F].reshape(grid_rows, grid_cols, D_F)
    v_grid[...] = key_values[:, D_F:].reshape(grid_rows, grid_cols, D_F)
    query_tokens = normed[RAD * grid_cols : (RAD + query_rows) * grid_cols]
    queries = dot(query_tokens, qkv_ref[:, :D_F]).astype(jnp.bfloat16).astype(floats) * scale
    q_grid[...] = queries.reshape(query_rows, grid_cols, D_F)
    cotangents = dy_grid[...].reshape(query_rows * grid_cols, D_F).astype(jnp.bfloat16)
    ups = dot(cotangents, out_ref[...], ((1,), (1,))).astype(jnp.bfloat16).astype(floats)
    u_grid[...] = ups.reshape(query_rows, grid_cols, D_F)

    gx, gy = lax.axis_index("gx"), lax.axis_index("gy")
    row_low, col_low = HALO - gy * height, HALO - gx * breadth
    row_high = row_low + lax.axis_size("gy") * height
    col_high = col_low + lax.axis_size("gx") * breadth

    def window_bias(query_rows):
        shape = ((query_rows + 2 * RAD) * lanes_wide, H_F * query_rows * side)
        key_at = lax.broadcasted_iota(jnp.int32, shape, 0)
        query_at = lax.broadcasted_iota(jnp.int32, shape, 1)
        row_gap = (key_at // lanes_wide) - ((query_at // side) % query_rows)
        col_gap = (key_at % lanes_wide) - (query_at % side)
        near = (row_gap >= 0) & (row_gap <= 2 * RAD) & (col_gap >= 0) & (col_gap <= 2 * RAD)
        return jnp.where(near, 0.0, -1e30)

    own_scratch, thin_scratch = scratch[:7], scratch[7:]
    own_scratch[-1][...] = window_bias(side)
    thin_scratch[-1][...] = window_bias(thin)

    def head_of(rows):
        return lax.broadcasted_iota(jnp.int32, (rows, D_F), 1) // HD

    def spread(block):
        block = block.reshape(-1, D_F)
        heads = head_of(block.shape[0])
        return jnp.concatenate(
            [jnp.where(heads == h, block, 0.0).astype(jnp.bfloat16) for h in range(H_F)], axis=0
        )

    def collect(full):
        rows = full.shape[0] // H_F
        heads = head_of(rows)
        total = jnp.where(heads == 0, full[:rows], 0.0)
        for h in range(1, H_F):
            total = jnp.where(heads == h, full[h * rows : (h + 1) * rows], total)
        return total.reshape(rows // side, side, D_F)

    def windows(task):
        top, start, query_rows = task[:3]
        window = (slice(top, top + query_rows + 2 * RAD), slice(start, start + lanes_wide))
        keys = k_grid[window].reshape(-1, D_F).astype(jnp.bfloat16)
        return keys, v_grid[window].reshape(-1, D_F).astype(jnp.bfloat16)

    def begin(task):
        top, start, query_rows, live, scratch, index = task
        score_ref, product_ref, query_ref, up_ref = scratch[:4]
        keys, values = windows(task)
        place = (slice(top, top + query_rows), slice(start + RAD, start + RAD + side))
        wide_queries = spread(q_grid[place])
        ups = u_grid[place]
        if live < query_rows:
            row = lax.broadcasted_iota(jnp.int32, ups.shape, 0)
            ups = jnp.where(row < live, ups, 0.0)
        wide_ups = spread(ups)
        query_ref[index], up_ref[index] = wide_queries, wide_ups
        score_ref[index] = dot(keys, wide_queries, ((1,), (1,)))
        product_ref[index] = dot(values, wide_ups, ((1,), (1,)))

    def share(task):
        top, start, query_rows, live, scratch, index = task
        score_ref, product_ref, _, _, weight_ref, slope_ref, near_bias = scratch
        lone = lax.broadcasted_iota(jnp.int32, ((query_rows + 2 * RAD) * lanes_wide, 1), 0)
        key_row, key_col = lone // lanes_wide + top, lone % lanes_wide + start
        inside = (key_row >= row_low) & (key_row < row_high)
        inside = inside & (key_col >= col_low) & (key_col < col_high)
        scores = score_ref[index] + (near_bias[...] + jnp.where(inside, 0.0, -1e30))
        raised = jnp.exp(scores - jnp.max(scores, axis=0, keepdims=True))
        shares = raised * (1.0 / jnp.sum(raised, axis=0, keepdims=True))
        products = product_ref[index]
        centre = jnp.sum(shares * products, axis=0, keepdims=True)
        slope_ref[index] = (shares * (products - centre)).astype(jnp.bfloat16)
        weight_ref[index] = shares.astype(jnp.bfloat16)

    def finish(task):
        top, start, query_rows, live, scratch, index = task
        query_ref, up_ref, weight_ref, slope_ref = scratch[2:6]
        first, final = max(top, HALO), min(top + query_rows + 2 * RAD, HALO + height)
        kept = slice((first - top) * lanes_wide, (final - top) * lanes_wide)
        target = (slice(first - HALO, final - HALO), slice(start, start + lanes_wide))
        shape = (final - first, lanes_wide, D_F)
        dv_grid[target] += dot(weight_ref[index, kept], up_ref[index]).reshape(shape)
        dk_grid[target] += dot(slope_ref[index, kept], query_ref[index]).reshape(shape)
        if live == side:
            keys, values = windows(task)
            block = (slice(top - RAD, top - RAD + side), slice(start, start + side))
            a_grid[block] = collect(dot(weight_ref[index], values, ((0,), (0,))))
            dq_grid[block] = collect(dot(slope_ref[index], keys, ((0,), (0,))))

    tasks = []
    for start in range(0, grid_cols - side, side):
        for top in range(RAD, RAD + height, side):
            tasks.append((top, start, side, side, own_scratch, len(tasks)))
    for index, start in enumerate(range(0, grid_cols - side, side)):
        tasks.append((0, start, thin, RAD, thin_scratch, 2 * index))
        tasks.append((RAD + height, start, thin, thin, thin_scratch, 2 * index + 1))
    for turn in range(len(tasks) + 2 * lag):
        if turn < len(tasks):
            begin(tasks[turn])
        if 0 <= turn - lag < len(tasks):
            share(tasks[turn - lag])
        if turn >= 2 * lag:
            finish(tasks[turn - 2 * lag])

    count = height * breadth
    own_queries = (slice(0, height), slice(RAD, RAD + breadth))
    own_keys = (slice(0, height), inner)
    attended = a_grid[own_queries].reshape(count, D_F).astype(jnp.bfloat16)
    grad_q = (dq_grid[own_queries].reshape(count, D_F) * scale).astype(jnp.bfloat16)
    grad_k = dk_grid[own_keys].reshape(count, D_F).astype(jnp.bfloat16)
    grad_v = dv_grid[own_keys].reshape(count, D_F).astype(jnp.bfloat16)
    grad_proj = jnp.concatenate([grad_q, grad_k, grad_v], axis=1)
    picture = x_ref[...].reshape(count, D_F).astype(floats)
    inverse = inverse_rms(picture)
    own_normed = (picture * inverse * factor).astype(jnp.bfloat16)
    flat_cot = dy_ref[...].reshape(count, D_F)
    grads = jnp.concatenate(
        [
            dot(own_normed, grad_proj, ((0,), (0,))),
            dot(attended, flat_cot, ((0,), (0,))),
        ],
        axis=1,
    )
    half, columns = keep_ref.shape[0], keep_ref.shape[1]
    total_ref[...] = grads.reshape(total_ref.shape)
    for low in range(2):
        target = (keep_ref, send_ref)[low]
        for high in range(half):
            for row in range(columns):
                block = (gx ^ (2 * high + low)) * columns + row
                target[high, row] = total_ref[block].astype(target.dtype)
    down = dot(grad_proj, qkv_ref[...], ((1,), (1,)))
    dx_ref[...] = norm_backward(picture, inverse, factor, down).reshape(height, breadth, D_F)


def block_scratch(blocks, query_rows):
    keys_count, heads_count = (query_rows + 2 * RAD) * lanes_wide, H_F * query_rows * side
    square = (blocks, keys_count, heads_count)
    wide = (blocks, heads_count, D_F)
    return [
        pltpu.VMEM(square, jnp.float32),
        pltpu.VMEM(square, jnp.float32),
        pltpu.VMEM(wide, jnp.bfloat16),
        pltpu.VMEM(wide, jnp.bfloat16),
        pltpu.VMEM(square, jnp.bfloat16),
        pltpu.VMEM(square, jnp.bfloat16),
        pltpu.VMEM((keys_count, heads_count), jnp.float32),
    ]


def fine_block(peers, picture, *operands):
    height, breadth = picture.shape[0], picture.shape[1]
    query_rows = RAD + height + thin
    query_cols = round_up(breadth + 2 * RAD, side)
    grid_rows, grid_cols = query_rows + 2 * RAD, query_cols + side
    across, down = peers
    rows = D_F // (across * down)
    halves = (across // 2, down, rows, 4 * D_F)
    vmem = pl.BlockSpec(memory_space=pltpu.VMEM)
    wide = pltpu.VMEM((grid_rows, grid_cols, D_F), jnp.float32)
    middle = pltpu.VMEM((query_rows, grid_cols, D_F), jnp.float32)
    small = pltpu.VMEM((height, query_cols, D_F), jnp.float32)
    strip = pltpu.VMEM((height, grid_cols, D_F), jnp.float32)
    return pl.pallas_call(
        fine_body,
        out_shape=(
            jax.ShapeDtypeStruct((height, breadth, D_F), jnp.bfloat16),
            jax.ShapeDtypeStruct(halves, jnp.float32),
            jax.ShapeDtypeStruct(halves, jnp.bfloat16),
        ),
        in_specs=[vmem] * 9,
        out_specs=(vmem, vmem, vmem),
        scratch_shapes=[
            wide,
            middle,
            wide,
            wide,
            middle,
            middle,
            strip,
            strip,
            small,
            small,
            pltpu.VMEM((across * down, rows, 4 * D_F), jnp.float32),
            *block_scratch(query_cols // side * (height // side), side),
            *block_scratch(2 * (query_cols // side), thin),
        ],
        compiler_params=pltpu.CompilerParams(vmem_limit_bytes=vmem_bytes),
        name="fine_block",
    )(picture, *operands)


def coarse_body(
    x_ref,
    dy_ref,
    factor_ref,
    qkv_hbm,
    out_hbm,
    parts_ref,
    grads_ref,
    qkv_ref,
    out_ref,
    arrived,
):
    fetches = [
        pltpu.make_async_copy(qkv_hbm, qkv_ref, arrived.at[0]),
        pltpu.make_async_copy(out_hbm, out_ref, arrived.at[1]),
    ]
    for fetch in fetches:
        fetch.start()
    tokens = x_ref[...].astype(jnp.float32)
    normed = (tokens * inverse_rms(tokens) * factor_ref[...]).astype(jnp.bfloat16)
    cot = dy_ref[...]
    for fetch in fetches:
        fetch.wait()
    flat_qkv = qkv_ref[...].reshape(3 * HD, D_C)
    out_rows = out_ref[...]
    projected = dot(normed, flat_qkv, ((1,), (1,))).astype(jnp.bfloat16)
    queries, keys, values = projected[:, :HD], projected[:, HD : 2 * HD], projected[:, 2 * HD :]
    ups = dot(cot, out_rows, ((1,), (1,))).astype(jnp.bfloat16)
    scores = dot(queries, keys, ((1,), (1,))) * scale
    raised = jnp.exp(scores - jnp.max(scores, axis=-1, keepdims=True))
    shares = raised * (1.0 / jnp.sum(raised, axis=-1, keepdims=True))
    weights = shares.astype(jnp.bfloat16)
    mixed = dot(weights, values).astype(jnp.bfloat16)
    products = dot(ups, values, ((1,), (1,)))
    centre = jnp.sum(shares * products, axis=-1, keepdims=True)
    slopes = (shares * (products - centre)).astype(jnp.bfloat16)
    grad_q = (dot(slopes, keys) * scale).astype(jnp.bfloat16)
    grad_k = (dot(slopes, queries, ((0,), (0,))) * scale).astype(jnp.bfloat16)
    grad_v = dot(weights, ups, ((0,), (0,))).astype(jnp.bfloat16)
    stacked = jnp.concatenate([grad_q, grad_k, grad_v], axis=1)
    parts_ref[...] = dot(stacked, flat_qkv).astype(jnp.bfloat16)
    grads_ref[: 3 * HD] = dot(stacked, normed, ((0,), (0,))).astype(grads_ref.dtype)
    grads_ref[3 * HD :] = dot(mixed, cot, ((0,), (0,))).astype(grads_ref.dtype)


def coarse_block(tokens, cotangents, factor, head_qkv, head_out):
    count = tokens.shape[0]
    vmem = pl.BlockSpec(memory_space=pltpu.VMEM)
    return pl.pallas_call(
        coarse_body,
        out_shape=(
            jax.ShapeDtypeStruct((count, D_C), jnp.bfloat16),
            jax.ShapeDtypeStruct((4 * HD, D_C), jnp.bfloat16),
        ),
        in_specs=[vmem] * 3 + [pl.BlockSpec(memory_space=pltpu.HBM)] * 2,
        out_specs=(vmem, vmem),
        scratch_shapes=[
            pltpu.VMEM(head_qkv.shape, jnp.bfloat16),
            pltpu.VMEM(head_out.shape, jnp.bfloat16),
            pltpu.SemaphoreType.DMA((2,)),
        ],
        compiler_params=pltpu.CompilerParams(vmem_limit_bytes=vmem_bytes),
        name="coarse_block",
    )(tokens, cotangents, factor, head_qkv, head_out)


def row_edges_body(x_low, x_high, dy_low, dy_high, near_ref, far_ref):
    odd = odd_rank("gy")

    def fill(low_ref, high_ref):
        low_ref[:HALO], low_ref[HALO:] = x_low[...], dy_low[...]
        high_ref[:HALO], high_ref[HALO:] = x_high[...], dy_high[...]

    @pl.when(odd)
    def _():
        fill(near_ref, far_ref)

    @pl.when(jnp.logical_not(odd))
    def _():
        fill(far_ref, near_ref)


def row_edges(picture, cotangent):
    vmem = pl.BlockSpec(memory_space=pltpu.VMEM)
    height = picture.shape[0]
    shape = jax.ShapeDtypeStruct((HALO + RAD,) + picture.shape[1:], jnp.bfloat16)
    return pl.pallas_call(
        row_edges_body,
        out_shape=(shape, shape),
        in_specs=[vmem] * 4,
        out_specs=(vmem, vmem),
        compiler_params=pltpu.CompilerParams(vmem_limit_bytes=vmem_bytes),
        name="row_edges",
    )(picture[:HALO], picture[height - HALO :], cotangent[:RAD], cotangent[height - RAD :])


def col_edges_body(x_ref, dy_ref, row_far_ref, row_near_ref, near_ref, far_ref):
    above, below = in_order("gy", row_near_ref, row_far_ref)
    breadth = x_ref.shape[1]
    odd = odd_rank("gx")
    at = 0
    for rows in (above, x_ref[...].astype(jnp.float32), dy_ref[...].astype(jnp.float32), below):
        first, final = rows[:, :side], rows[:, breadth - side :]
        span = slice(at, at + rows.shape[0])
        near_ref[span] = jnp.where(odd, first, final).astype(jnp.bfloat16)
        far_ref[span] = jnp.where(odd, final, first).astype(jnp.bfloat16)
        at += rows.shape[0]


def col_edges(picture, cotangent, row_far, row_near):
    vmem = pl.BlockSpec(memory_space=pltpu.VMEM)
    rows = 2 * (picture.shape[0] + row_near.shape[0])
    shape = jax.ShapeDtypeStruct((rows, side, D_F), jnp.bfloat16)
    return pl.pallas_call(
        col_edges_body,
        out_shape=(shape, shape),
        in_specs=[vmem] * 4,
        out_specs=(vmem, vmem),
        compiler_params=pltpu.CompilerParams(vmem_limit_bytes=vmem_bytes),
        name="col_edges",
    )(picture, cotangent, row_far, row_near)


def pack_body(first, second, x_ref, dy_ref, own_ref):
    own_ref[:, :D_C] = x_ref[...].astype(jnp.float32).reshape(-1, D_C).astype(jnp.bfloat16)
    own_ref[:, D_C:] = dy_ref[...].astype(jnp.float32).reshape(-1, D_C).astype(jnp.bfloat16)


def packed(after, tokens, cotangents):
    vmem = pl.BlockSpec(memory_space=pltpu.VMEM)
    count = tokens.shape[0] * tokens.shape[1]
    return pl.pallas_call(
        pack_body,
        out_shape=jax.ShapeDtypeStruct((count, 2 * D_C), jnp.bfloat16),
        in_specs=[pl.BlockSpec(memory_space=pl.ANY)] * 2 + [vmem] * 2,
        out_specs=vmem,
        compiler_params=pltpu.CompilerParams(vmem_limit_bytes=vmem_bytes),
        name="pack_coarse",
    )(*after, tokens, cotangents)


def factors_body(step, fine_gain, coarse_gain, fine_freq, coarse_freq, fine_ref, coarse_ref):
    time = step[0].astype(jnp.float32)
    fine_ref[...] = fine_gain[...] * (1.0 + 0.5 * jnp.cos(time * fine_freq[...]))
    coarse_ref[...] = coarse_gain[...] * (1.0 + 0.5 * jnp.cos(time * coarse_freq[...]))


def time_factors(step, fine_gain, coarse_gain):
    vmem = pl.BlockSpec(memory_space=pltpu.VMEM)
    return pl.pallas_call(
        factors_body,
        out_shape=(
            jax.ShapeDtypeStruct((1, D_F), jnp.float32),
            jax.ShapeDtypeStruct((1, D_C), jnp.float32),
        ),
        in_specs=[pl.BlockSpec(memory_space=pltpu.SMEM)] + [vmem] * 4,
        out_specs=(vmem, vmem),
        compiler_params=pltpu.CompilerParams(vmem_limit_bytes=vmem_bytes),
        name="time_factors",
    )(step, fine_gain[None], coarse_gain[None], frequencies(D_F), frequencies(D_C))


def pair_sum_body(own, *refs):
    qkv_ref, out_ref = refs[-2:]
    come = jnp.concatenate([ref[...] for ref in refs[:-2]], axis=0)
    for part in range(4):
        rows = slice(part * HD, (part + 1) * HD)
        total = own[rows].astype(jnp.float32) + come[rows].astype(jnp.float32)
        if part < 3:
            qkv_ref[part] = total.astype(jnp.bfloat16)
        else:
            out_ref[...] = total.astype(jnp.bfloat16)


def pair_sum(own, *come):
    vmem = pl.BlockSpec(memory_space=pltpu.VMEM)
    return pl.pallas_call(
        pair_sum_body,
        out_shape=(
            jax.ShapeDtypeStruct((3, HD, D_C), jnp.bfloat16),
            jax.ShapeDtypeStruct((HD, D_C), jnp.bfloat16),
        ),
        in_specs=[vmem] * (1 + len(come)),
        out_specs=(vmem, vmem),
        compiler_params=pltpu.CompilerParams(vmem_limit_bytes=vmem_bytes),
        name="pair_sum",
    )(own, *come)


def block_copies(near_ref, low, qkv_hbm, out_hbm, sems):
    highs, rows = near_ref.shape[0], near_ref.shape[1]
    copies = []
    for high in range(highs):
        block = lax.axis_index("gx") ^ (2 * high + low)
        at = pl.ds(pl.multiple_of(block * rows, rows), rows)
        for part, target in enumerate((qkv_hbm, out_hbm)):
            lanes = (slice(0, 3 * D_F), slice(3 * D_F, 4 * D_F))[part]
            copies.append(
                pltpu.make_async_copy(
                    near_ref.at[high, :, lanes], target.at[at, :], sems.at[high, part]
                )
            )
    for copy in copies:
        copy.start()
    return copies


def near_body(near_ref, x_ref, factor_ref, kept_ref, come_ref, qkv_hbm, out_hbm, dx_ref, sems):
    copies = block_copies(near_ref, 0, qkv_hbm, out_hbm, sems)
    tokens = x_ref[...].astype(jnp.float32).reshape(-1, D_C)
    upstream = kept_ref[...] + come_ref[...].astype(jnp.float32)
    grads = norm_backward(tokens, inverse_rms(tokens), factor_ref[...], upstream)
    dx_ref[...] = grads.astype(jnp.float32).reshape(dx_ref.shape).astype(jnp.bfloat16)
    for copy in copies:
        copy.wait()


def far_body(far_ref, qkv_in, out_in, qkv_hbm, out_hbm, sems):
    for copy in block_copies(far_ref, 1, qkv_hbm, out_hbm, sems):
        copy.wait()


def near_step(near, tokens, *operands):
    vmem = pl.BlockSpec(memory_space=pltpu.VMEM)
    hbm = pl.BlockSpec(memory_space=pltpu.HBM)
    return pl.pallas_call(
        near_body,
        out_shape=(
            jax.ShapeDtypeStruct((D_F, 3 * D_F), jnp.bfloat16),
            jax.ShapeDtypeStruct((D_F, D_F), jnp.bfloat16),
            jax.ShapeDtypeStruct(tokens.shape, jnp.bfloat16),
        ),
        in_specs=[vmem] * 5,
        out_specs=(hbm, hbm, vmem),
        scratch_shapes=[pltpu.SemaphoreType.DMA((near.shape[0], 2))],
        compiler_params=pltpu.CompilerParams(vmem_limit_bytes=vmem_bytes),
        name="near_step",
    )(near, tokens, *operands)


def far_step(far, qkv, out):
    vmem = pl.BlockSpec(memory_space=pltpu.VMEM)
    hbm = pl.BlockSpec(memory_space=pltpu.HBM)
    return pl.pallas_call(
        far_body,
        out_shape=(
            jax.ShapeDtypeStruct(qkv.shape, qkv.dtype),
            jax.ShapeDtypeStruct(out.shape, out.dtype),
        ),
        in_specs=[vmem, hbm, hbm],
        out_specs=(hbm, hbm),
        input_output_aliases={1: 0, 2: 1},
        scratch_shapes=[pltpu.SemaphoreType.DMA((far.shape[0], 2))],
        compiler_params=pltpu.CompilerParams(vmem_limit_bytes=vmem_bytes),
        name="far_step",
    )(far, qkv, out)


def neighbours(to_near, to_far, axis):
    peers = lax.axis_size(axis)
    near = [(i, i ^ 1) for i in range(peers)]
    far = [(i, i + 1 if i % 2 else i - 1) for i in range(1, peers - 1)]
    from_far = lax.ppermute(to_far, axis, far)
    return lax.ppermute(to_near, axis, near), from_far


def swapped(value, axis, mask):
    return lax.ppermute(value, axis, [(i, i ^ mask) for i in range(lax.axis_size(axis))])


def tied(*arrays):
    return lax.optimization_barrier(arrays)


def batch_sum(partial):
    if lax.axis_size("batch") != 2:
        return lax.psum(partial, "batch")
    return wide(partial) + wide(swapped(partial, "batch", 1))


def wide(value):
    return value.astype(jnp.float32)


def narrow(value):
    return value.astype(jnp.bfloat16)


def all_rows(piece):
    downs = lax.axis_size("gy")
    return jnp.stack([piece] + [swapped(piece, "gy", row) for row in range(1, downs)])


def local(
    x_fine,
    dy_fine,
    x_coarse,
    dy_coarse,
    timestep,
    fine_gain,
    coarse_gain,
    fine_qkv,
    fine_out,
    coarse_qkv,
    coarse_out,
):
    picture, cotangent = x_fine[0], dy_fine[0]
    across, downs = lax.axis_size("gx"), lax.axis_size("gy")
    assert across == 4 and downs & (downs - 1) == 0

    payloads = row_edges(picture, cotangent)
    row_near, row_far = neighbours(*payloads, "gy")
    own = packed(payloads, x_coarse[0], dy_coarse[0])
    count = own.shape[0]
    pieces = [own] + [swapped(own, "gy", row) for row in range(1, downs)]
    edges = col_edges(picture, cotangent, row_far, row_near)
    *edges, step, gain_f, gain_c = tied(*edges, timestep, fine_gain, coarse_gain)
    col_near, col_far = neighbours(*edges, "gx")
    factor, coarse_factor = time_factors(step, gain_f, gain_c)
    factor, *pieces = tied(factor, *pieces)
    row_group = jnp.stack(pieces)
    cross = swapped(row_group, "gx", 2)
    beside = swapped(row_group, "gx", 1)
    col_far, col_near, row_group = tied(col_far, col_near, row_group)
    dx_picture, fine_keep, fine_send = fine_block(
        (across, downs),
        picture,
        cotangent,
        row_far,
        row_near,
        col_far,
        col_near,
        factor,
        fine_qkv,
        fine_out,
    )
    fine_half = fine_keep + wide(swapped(fine_send, "gx", 1))
    opposite = swapped(cross, "gx", 1)

    fine_quarter = narrow(fine_half[0] + wide(swapped(narrow(fine_half[1]), "gx", 2)))
    everyone = jnp.stack([row_group, cross, beside, opposite]).reshape(-1, 2 * D_C)
    parts, coarse_partial = coarse_block(
        everyone[:, :D_C], everyone[:, D_C:], coarse_factor, coarse_qkv, coarse_out
    )
    fine_quarter, parts, coarse_partial = tied(fine_quarter, parts, coarse_partial)

    rows = D_F // across
    fine_quarter = narrow(batch_sum(fine_quarter)).reshape(rows, 4 * D_F)
    parts = parts.reshape(2, 2, downs, count, D_C)
    coarse_kept = wide(parts[0]) + wide(swapped(parts[1], "gx", 1))
    fine_quarter, coarse_kept, coarse_partial = tied(fine_quarter, coarse_kept, coarse_partial)

    pair_batch = lax.axis_size("batch") == 2
    cut = 6 * HD // 4
    halves = (coarse_partial[:cut], coarse_partial[cut:])
    others = [swapped(half, "batch", 1) if pair_batch else half for half in halves]
    masks = [1 << bit for bit in range(downs.bit_length() - 1)]
    for mask in masks:
        fine_quarter = narrow(wide(fine_quarter) + wide(swapped(fine_quarter, "gy", mask)))
    for turn, mask in enumerate(masks):
        coarse_kept = coarse_kept.reshape(2, -1, 2, count, D_C)
        come = swapped(narrow(coarse_kept[:, :, 1]), "gy", mask)
        coarse_kept = coarse_kept[:, :, 0] + wide(come)
    coarse_kept = coarse_kept.reshape(2, count, D_C)
    come = swapped(narrow(coarse_kept[1]), "gx", 2)
    if pair_batch:
        grad_coarse_qkv, grad_coarse_out = pair_sum(coarse_partial, *others)
    else:
        coarse_sum = narrow(lax.psum(wide(coarse_partial), "batch"))
        grad_coarse_qkv = coarse_sum[: 3 * HD].reshape(coarse_qkv.shape)
        grad_coarse_out = coarse_sum[3 * HD :]
    fine_other = swapped(fine_quarter, "gx", 2)
    fine_other, come, grad_coarse_qkv, grad_coarse_out = tied(
        fine_other, come, grad_coarse_qkv, grad_coarse_out
    )
    fine_pair = jnp.stack([fine_quarter, fine_other])
    near_qkv, near_out, dx_coarse = near_step(
        fine_pair, x_coarse[0], coarse_factor, coarse_kept[0], come
    )
    far_pair = swapped(fine_pair, "gx", 1)
    far_pair, near_qkv, near_out = tied(far_pair, near_qkv, near_out)
    grad_qkv, grad_out = far_step(far_pair, near_qkv, near_out)
    return (
        dx_picture[None],
        dx_coarse[None],
        grad_qkv,
        grad_out,
        grad_coarse_qkv,
        grad_coarse_out,
    )


def solution(mesh):
    placed = (
        P("batch", "gy", "gx", None),
        P("batch", "gy", "gx", None),
        P("batch", "gy", "gx", None),
        P("batch", "gy", "gx", None),
        P("batch"),
        P(),
        P(),
        P(),
        P(),
        P(None, plane_spec, None),
        P(plane_spec, None),
    )
    return jax.shard_map(
        local,
        mesh=mesh,
        in_specs=placed,
        out_specs=(
            P("batch", "gy", "gx", None),
            P("batch", "gy", "gx", None),
            P(),
            P(),
            P(None, plane_spec, None),
            P(plane_spec, None),
        ),
        check_vma=False,
    )


plane_spec = ("gy", "gx")
```
